32 devices in a mesh: shard: 8 (over z, x), dp: 4 (over y, core).
Axes of the slice: x: 2, y: 2, z: 4, core: 2. Of those that a mesh axis runs over, the one named last changes fastest.
Arguments:
- source: float32 [384, 6, 6, 512], P(('shard', 'dp')), may hold values from -6 to 6
- index_map: int32 [384], P(('shard', 'dp')), may hold values from 0 to 11
- crop_offsets: int32 [384, 2], P(('shard', 'dp')), may hold values from 0 to 2
- flip_flags: int32 [384], P(('shard', 'dp')), may hold values from 0 to 1
- labels: int32 [384], P(('shard', 'dp')), may hold values from 0 to 9
- valid_mask: int32 [384], P(('shard', 'dp')), may hold values from 0 to 1, as said below
- conv_weights: float32 [2, 512, 4608], P(None, 'shard'), may hold values from -0.09375 to 0.09375
- norm_params: float32 [4, 512], P(None, 'shard'), may hold values from -2 to 2, as said below
- head_weights: float32 [512, 10], P('shard'), may hold values from -0.75 to 0.75
- decay_rates: float32 [2, 512, 4608], P(None, 'shard'), may hold values from 0.01 to 0.08
- conv_first: float32 [2, 512, 4608], P(None, 'shard'), may hold values from -0.0390625 to 0.0390625
- conv_second: float32 [2, 512, 4608], P(None, 'shard'), may hold values from 6.457908e-06 to 2.5831632e-05
- norm_first: float32 [4, 512], P(None, 'shard'), may hold values from -0.03125 to 0.03125
- norm_second: float32 [4, 512], P(None, 'shard'), may hold values from 4.1666667e-06 to 1.6666667e-05
- head_first: float32 [512, 10], P('shard'), may hold values from -0.5 to 0.5
- head_second: float32 [512, 10], P('shard'), may hold values from 0.0014648438 to 0.005859375
Outputs:
- loss_sum: float32 [], replicated
- label_total: float32 [], replicated
- conv_updated: float32 [2, 512, 4608], P(None, 'shard')
- conv_moment_one: float32 [2, 512, 4608], P(None, 'shard')
- conv_moment_two: float32 [2, 512, 4608], P(None, 'shard')
- norm_updated: float32 [4, 512], P(None, 'shard')
- norm_moment_one: float32 [4, 512], P(None, 'shard')
- norm_moment_two: float32 [4, 512], P(None, 'shard')
- head_updated: float32 [512, 10], P('shard')
- head_moment_one: float32 [512, 10], P('shard')
- head_moment_two: float32 [512, 10], P('shard')
- hyper_gradient: float32 [2, 512, 4608], P(None, 'shard')
The draws below stay inside these ranges and needn't reach their ends.
Inputs may be any that keep to these rules, and one draw needn't show every extreme that they name: `valid_mask`: the last image always counts. `norm_params`: rows 0 and 2 are gains, rows 1 and 3 biases.
All inputs are finite; a program needn't handle non-finite values.
Results may differ from the reference program's by a relative error of at most 0.0003.
Values sent between devices are 32-bit elements; how exact they have to be, the bound alone decides.
A program may use at most 256 MiB of HBM per device.

```python
import math
import jax
import jax.numpy as jnp
from jax import lax

C = 512
CLASSES = 10
MAP = 4
IMG_DEV = 12
NEUMANN = 3
STEP = 5
IMAGES = 384


def draw_valid_mask(key, part):
    key = jax.random.fold_in(key, 11)
    positions = jnp.arange(IMAGES, dtype=jnp.int32)
    threshold = 25 + 50 * positions // IMAGES
    random_rolls = jax.random.randint(key, (IMAGES,), 0, 100)
    flags = (random_rolls < threshold).astype(jnp.int32)
    return jnp.where(positions == IMAGES - 1, 1, flags).astype(jnp.int32)


def draw_norm_params(key, part):
    key = jax.random.fold_in(key, 23)
    key_gain, key_shift = jax.random.split(key)
    gains = jax.random.uniform(key_gain, (2, C), jnp.float32, 0.5, 1.5)
    shifts = jnp.clip(0.3 * jax.random.normal(key_shift, (2, C), jnp.float32), -1.5, 1.5)
    return jnp.stack([gains[0], shifts[0], gains[1], shifts[1]]).astype(jnp.float32)


def place_ends(result, rng, smallest, largest):
    index_at = [jax.random.randint(jax.random.fold_in(rng, axis), (), 0, length) for axis, length in enumerate(result.shape)]
    main_axis = result.shape.index(max(result.shape))
    neighbour = index_at[:main_axis] + [(index_at[main_axis] + 1) % result.shape[main_axis]] + index_at[main_axis + 1:]
    return result.at[tuple(index_at)].set(smallest).at[tuple(neighbour)].set(largest)


def steps_of(key, extent, cuts, low, high):
    factor_of, own = 1.0, jax.random.fold_in(key, 6)
    for dim, shards_of in cuts:
        draws = jnp.exp(jax.random.uniform(jax.random.fold_in(own, dim), (shards_of,), jnp.float32, low / len(cuts), high / len(cuts)))
        factor_of = factor_of * jnp.repeat(draws, extent[dim] // shards_of).reshape([-1 if axis == dim else 1 for axis in range(len(extent))])
    return factor_of


def normal_values(key, extent, deviation, bound, pieces=(), kind=jnp.bfloat16):
    result = deviation * jax.random.normal(key, extent, jnp.float32)
    if pieces:
        result = result * steps_of(key, extent, pieces, -0.22, 0.18)
    return jnp.clip(result, -bound, bound).astype(kind)


def setup_inputs(seed: int = 0) -> dict:
    keys = jax.random.split(jax.random.key(seed), 17)
    source = normal_values(keys[0], (IMAGES, MAP + 2, MAP + 2, C), 1.0, 6.0, ((0, 32),), jnp.float32)
    index_map = place_ends(jax.random.randint(keys[1], (IMAGES,), 0, IMG_DEV), jax.random.fold_in(keys[1], 1), 0, IMG_DEV - 1).astype(jnp.int32)
    crop_offsets = place_ends(jax.random.randint(keys[2], (IMAGES, 2), 0, 3), jax.random.fold_in(keys[2], 1), 0, 2).astype(jnp.int32)
    flip_flags = place_ends(jax.random.randint(keys[3], (IMAGES,), 0, 2), jax.random.fold_in(keys[3], 1), 0, 1).astype(jnp.int32)
    labels = place_ends(jax.random.randint(keys[4], (IMAGES,), 0, CLASSES), jax.random.fold_in(keys[4], 1), 0, CLASSES - 1).astype(jnp.int32)
    valid_mask = draw_valid_mask(jax.random.fold_in(keys[16], 71), 0)
    conv_weights = normal_values(keys[6], (2, C, 9 * C), (9 * C) ** -0.5, 0.09375, ((1, 8),), jnp.float32)
    norm_params = draw_norm_params(jax.random.fold_in(keys[16], 71), 0)
    head_weights = normal_values(keys[8], (C, CLASSES), (C // 9) ** -0.5, 0.75, ((0, 8),), jnp.float32)
    decay_rates = jnp.clip(jnp.exp(math.log(0.08) - 2.0794415 * jax.random.uniform(keys[9], (2, C, 9 * C), jnp.float32) ** steps_of(keys[9], (2, C, 9 * C), ((1, 8),), -0.2, 0.2)), 0.01, 0.08)
    conv_first = normal_values(keys[10], (2, C, 9 * C), (0.04 * IMAGES ** -0.5 + 0.0005), 0.0390625, ((1, 8),), jnp.float32)
    conv_second = jnp.clip(6.457908057200257e-06 + 1.937372417160077e-05 * jax.random.uniform(keys[11], (2, C, 9 * C), jnp.float32) ** steps_of(keys[11], (2, C, 9 * C), ((1, 8),), -0.2, 0.2), 6.457908057200257e-06, 2.5831632228801027e-05)
    norm_first = normal_values(keys[12], (4, C), (0.04 * IMAGES ** -0.5), 0.03125, ((1, 8),), jnp.float32)
    norm_second = jnp.clip(4.1666667129902635e-06 + 1.250000013897079e-05 * jax.random.uniform(keys[13], (4, C), jnp.float32) ** steps_of(keys[13], (4, C), ((1, 8),), -0.2, 0.2), 4.1666667129902635e-06, 1.6666666851961054e-05)
    head_first = normal_values(keys[14], (C, CLASSES), (0.75 * IMAGES ** -0.5), 0.5, ((0, 8),), jnp.float32)
    head_second = jnp.clip(0.0014648438 + 0.0043945312 * jax.random.uniform(keys[15], (C, CLASSES), jnp.float32) ** steps_of(keys[15], (C, CLASSES), ((0, 8),), -0.2, 0.2), 0.0014648438, 0.005859375)
    return dict(source=source, index_map=index_map, crop_offsets=crop_offsets, flip_flags=flip_flags, labels=labels, valid_mask=valid_mask, conv_weights=conv_weights, norm_params=norm_params, head_weights=head_weights, decay_rates=decay_rates, conv_first=conv_first, conv_second=conv_second, norm_first=norm_first, norm_second=norm_second, head_first=head_first, head_second=head_second)


@jax.custom_vjp
def low(v):
    return lax.optimization_barrier(v.astype(jnp.bfloat16)).astype(jnp.float32)

@jax.custom_vjp
def low_back(v):
    return v

def low_keep(v):
    return (low(v), None)

def low_pass(kept, grad):
    return (grad,)

def back_keep(v):
    return (v, None)

def back_low(kept, grad):
    return (low(grad),)
low.defvjp(low_keep, low_pass)
low_back.defvjp(back_keep, back_low)
norm_eps = 1e-05
neumann_rate = 10.0
beta_first = 0.5
beta_second = 0.5
adam_eps = 1e-08
decoupled = 0.01

def crop_image(single, offsets, flipped):
    window = lax.dynamic_slice(single, (offsets[0].astype(jnp.int32), offsets[1].astype(jnp.int32), jnp.int32(0)), (MAP, MAP, single.shape[2]))
    return jnp.where(flipped == 1, window[:, ::-1, :], window)

def convolve(inputs, kernel):
    padded = jnp.pad(inputs, ((0, 0), (1, 1), (1, 1), (0, 0)))
    taps = [padded[:, shift_y:shift_y + MAP, shift_x:shift_x + MAP, :] for shift_y in range(3) for shift_x in range(3)]
    patches = jnp.concatenate(taps, axis=3)
    return jnp.einsum('bhwk,ck->bhwc', patches, kernel, precision=lax.Precision.HIGHEST)

def channel_sums(hidden):
    return jnp.stack([lax.optimization_barrier(jnp.sum(hidden, axis=(0, 1, 2))), lax.optimization_barrier(jnp.sum(hidden * hidden, axis=(0, 1, 2)))])

def normalize(hidden, totals, gain, shift, count_rows):
    average = totals[0] / count_rows
    spread = totals[1] / count_rows - average * average
    return (hidden - average) * lax.rsqrt(spread + norm_eps) * gain + shift

def cross_terms(head_matrix, params, hidden, totals, images, labels, valid, count_rows):
    block = jax.nn.silu(normalize(hidden, totals, params[2], params[3], count_rows) + images)
    pooled = lax.optimization_barrier(jnp.mean(block, axis=(1, 2)))
    logits = jnp.dot(pooled, head_matrix, precision=lax.Precision.HIGHEST)
    highest = lax.optimization_barrier(jnp.max(logits, axis=1, keepdims=True))
    logsum = highest[:, 0] + jnp.log(lax.optimization_barrier(jnp.sum(jnp.exp(logits - highest), axis=1)))
    classes = jnp.arange(logits.shape[1], dtype=jnp.int32)
    target = lax.optimization_barrier(jnp.sum(jnp.where(labels[:, None] == classes[None, :], logits, 0.0), axis=1))
    return jnp.sum(valid * (logsum - target))

def forward_terms(params, images, labels, valid, count_rows):
    conv_all, norm_all, head_all = params
    hidden_one = convolve(images, conv_all[0])
    activated = jax.nn.silu(normalize(hidden_one, channel_sums(hidden_one), norm_all[0], norm_all[1], count_rows))
    hidden_two = convolve(activated, conv_all[1])
    return cross_terms(head_all, norm_all, hidden_two, channel_sums(hidden_two), images, labels, valid, count_rows)

def adamw(weight, grad, first, second, rate):
    first = beta_first * first + (1.0 - beta_first) * grad
    second = beta_second * second + (1.0 - beta_second) * grad * grad
    first_hat = first / (1.0 - beta_first ** STEP)
    second_hat = second / (1.0 - beta_second ** STEP)
    update = first_hat / (jnp.sqrt(second_hat) + adam_eps) + decoupled * weight
    return (weight - rate * update, first, second)

def reference(source, index_map, crop_offsets, flip_flags, labels, valid_mask, conv_weights, norm_params, head_weights, decay_rates, conv_first, conv_second, norm_first, norm_second, head_first, head_second):
    owners = jnp.arange(source.shape[0], dtype=jnp.int32) // IMG_DEV * IMG_DEV
    picked = source[owners + index_map.astype(jnp.int32)]
    images = jax.vmap(crop_image)(picked, crop_offsets, flip_flags)
    valid = valid_mask.astype(jnp.float32)
    label_total = jnp.sum(valid)
    count_rows = float(images.shape[0] * MAP * MAP)

    def objective(params):
        cross = forward_terms(params, images, labels, valid, count_rows)
        return (cross / label_total + 0.5 * jnp.sum(decay_rates * params[0] * params[0]), cross)

    def gradient(params):
        value, pull, cross = jax.vjp(objective, params, has_aux=True)
        return (pull(jnp.ones_like(value))[0], cross)
    params = (conv_weights, norm_params, head_weights)
    grads, loss_sum = gradient(params)
    vector = grads
    series = grads
    for turn in range(NEUMANN):
        product = jax.jvp(lambda point: gradient(point)[0], (params,), (vector,))[1]
        vector = jax.tree.map(lambda previous, change: previous - neumann_rate * change, vector, product)
        series = jax.tree.map(lambda summed, change: summed + change, series, vector)
    hyper_gradient = -neumann_rate * conv_weights * series[0]
    conv_new, conv_one, conv_two = adamw(conv_weights, grads[0], conv_first, conv_second, 0.015)
    norm_new, norm_one, norm_two = adamw(norm_params, grads[1], norm_first, norm_second, 0.3)
    head_new, head_one, head_two = adamw(head_weights, grads[2], head_first, head_second, 0.13)
    return (loss_sum, label_total, conv_new, conv_one, conv_two, norm_new, norm_one, norm_two, head_new, head_one, head_two, hyper_gradient)
```

```python
import jax
import jax.numpy as jnp
from jax import lax
from jax.sharding import PartitionSpec as P

MAP = 4
NEUMANN = 3
STEP = 5
TAPS = 9

norm_eps = 1e-05
neumann_rate = 10.0
beta_first = 0.5
beta_second = 0.5
adam_eps = 1e-08
decoupled = 0.01
HIGH = lax.Precision.HIGH


def crop_image(single, offsets, flipped):
    window = lax.dynamic_slice(
        single, (offsets[0], offsets[1], jnp.int32(0)), (MAP, MAP, single.shape[2])
    )
    return jnp.where(flipped == 1, window[:, ::-1, :], window)


def patches(maps):
    count, width = maps.shape[2:]
    padded = jnp.pad(maps, ((1, 1), (1, 1), (0, 0), (0, 0)))
    taps = [padded[dy : dy + MAP, dx : dx + MAP] for dy in range(3) for dx in range(3)]
    return jnp.concatenate(taps, axis=3).reshape(MAP * MAP * count, TAPS * width)


def fold(columns, count):
    width = columns.shape[1] // TAPS
    whole = columns.reshape(MAP, MAP, count, TAPS, width)
    padded = jnp.pad(whole, ((1, 1), (1, 1), (0, 0), (0, 0), (0, 0)))
    total = 0.0
    for dy in range(3):
        for dx in range(3):
            total = total + padded[2 - dy : 2 - dy + MAP, 2 - dx : 2 - dx + MAP, :, dy * 3 + dx]
    return total.reshape(MAP * MAP * count, width)


def dot(left, right, dims):
    return lax.dot_general(
        left, right, ((dims[0], dims[1]), ((), ())), precision=HIGH, preferred_element_type=jnp.float32
    )


def adamw(weight, grad, first, second, rate):
    first = beta_first * first + (1.0 - beta_first) * grad
    second = beta_second * second + (1.0 - beta_second) * grad * grad
    first_hat = first / (1.0 - beta_first**STEP)
    second_hat = second / (1.0 - beta_second**STEP)
    update = first_hat / (jnp.sqrt(second_hat) + adam_eps) + decoupled * weight
    return (weight - rate * update, first, second)


def silu_parts(value):
    gate = jax.nn.sigmoid(value)
    slope = gate * (1.0 - gate)
    first = gate + value * slope
    second = slope * (2.0 + value * (1.0 - 2.0 * gate))
    return value * gate, first, second


class Links:
    def __init__(self):
        self.shards = lax.axis_size("shard")
        self.copies = lax.axis_size("dp")
        self.parts = 4 if self.shards % 4 == 0 else 1
        self.members = self.shards // self.parts
        index = lax.axis_index("shard")
        self.part = index // self.members
        self.member = index % self.members
        self.across = [
            [p * self.members + m for p in range(self.parts)] for m in range(self.members)
        ]
        self.within = [
            [p * self.members + m for m in range(self.members)] for p in range(self.parts)
        ]

    def sum_rows(self, value):
        value = lax.psum(value, "dp")
        gathered = lax.all_gather(value, "shard", axis_index_groups=self.within)
        return jnp.sum(gathered, axis=0)

    def sum_parts(self, value):
        return jnp.sum(lax.all_gather(value, "shard", axis_index_groups=self.across), axis=0)

    def gather_parts(self, value, axis):
        return lax.all_gather(value, "shard", axis_index_groups=self.across, axis=axis, tiled=True)

    def gather_members(self, value, axis):
        return lax.all_gather(value, "shard", axis_index_groups=self.within, axis=axis, tiled=True)

    def scatter_parts(self, value, axis):
        return lax.psum_scatter(
            value, "shard", axis_index_groups=self.across, scatter_dimension=axis, tiled=True
        )

    def to_inner(self, value):
        rows, channels = value.shape[0], value.shape[1] // TAPS
        width = channels // self.parts
        cut = value.reshape(rows, TAPS, self.parts, width).transpose(2, 0, 1, 3)
        moved = lax.all_to_all(cut, "shard", 0, 0, axis_index_groups=self.across, tiled=True)
        whole = self.gather_members(moved, 1)
        return whole.reshape(channels, TAPS * width)

    def to_outer(self, value):
        channels, width = value.shape[0], value.shape[1] // TAPS
        rows = channels // self.shards
        cut = value.reshape(self.parts, self.members, rows, TAPS * width)
        cut = lax.dynamic_index_in_dim(cut, self.member, 1, keepdims=False)
        moved = lax.all_to_all(cut, "shard", 0, 0, axis_index_groups=self.across, tiled=True)
        moved = moved.reshape(self.parts, rows, TAPS, width).transpose(1, 2, 0, 3)
        return moved.reshape(rows, TAPS * channels)

    def own_rows(self, value, axis=0):
        size = value.shape[axis] // self.members
        return lax.dynamic_slice_in_dim(value, self.member * size, size, axis)


def moments(hidden, rows, links):
    totals = links.sum_rows(jnp.stack([jnp.sum(hidden, axis=0), jnp.sum(hidden * hidden, axis=0)]))
    average = totals[0] / rows
    scale = lax.rsqrt(totals[1] / rows - average * average + norm_eps)
    return (hidden - average) * scale, scale


def moments_tangent(normal, scale, tangent, rows, links):
    totals = links.sum_rows(
        jnp.stack([jnp.sum(tangent, axis=0), jnp.sum(tangent * normal, axis=0)])
    )
    average, cross = totals[0] / rows, totals[1] / rows
    return scale * (tangent - average - normal * cross), -scale * scale * cross


def shards(
    source,
    index_map,
    crop_offsets,
    flip_flags,
    labels,
    valid_mask,
    conv_weights,
    norm_params,
    head_weights,
    decay_rates,
    conv_first,
    conv_second,
    norm_first,
    norm_second,
    head_first,
    head_second,
):
    links = Links()
    own_images = source.shape[0]
    channels = source.shape[3]
    rows = float(own_images * MAP * MAP * links.shards * links.copies)
    count = own_images * links.parts
    width = channels // links.parts
    first_column = links.part * width

    picked = source[index_map]
    images = jax.vmap(crop_image)(picked, crop_offsets, flip_flags)
    images = images.transpose(1, 2, 0, 3)
    images = links.gather_parts(images, 2)
    labels = links.gather_parts(labels, 0)
    valid = links.gather_parts(valid_mask.astype(jnp.float32), 0)
    label_total = lax.psum(jnp.sum(valid_mask.astype(jnp.float32)), ("shard", "dp"))

    kernel_one = links.gather_members(conv_weights[0], 0)
    kernel_two = links.to_inner(conv_weights[1])
    decay_one = links.gather_members(decay_rates[0], 0)
    decay_two = links.to_inner(decay_rates[1])
    norms = links.gather_members(norm_params, 1)
    head = links.gather_members(head_weights, 0)
    gain_one, shift_one, gain_two, shift_two = norms[0], norms[1], norms[2], norms[3]

    def pool(value):
        return jnp.sum(value.reshape(MAP * MAP, count, width), axis=0) / (MAP * MAP)

    def spread(value):
        whole = jnp.broadcast_to(value[None] / (MAP * MAP), (MAP * MAP, count, width))
        return whole.reshape(MAP * MAP * count, width)

    columns = patches(images)
    own_columns = lax.dynamic_slice_in_dim(
        images.reshape(MAP * MAP * count, channels), first_column, width, 1
    )

    hidden_one = dot(columns, kernel_one, ((1,), (1,)))
    normal_one, scale_one = moments(hidden_one, rows, links)
    active, slope_one, bend_one = silu_parts(normal_one * gain_one + shift_one)
    active_columns = patches(active.reshape(MAP, MAP, count, width))
    hidden_two = links.scatter_parts(dot(active_columns, kernel_two, ((1,), (1,))), 1)
    normal_two, scale_two = moments(hidden_two, rows, links)
    block, slope_two, bend_two = silu_parts(normal_two * gain_two + shift_two + own_columns)
    pooled = pool(block)
    logits = links.sum_parts(dot(pooled, head, ((1,), (0,))))
    highest = jnp.max(logits, axis=1, keepdims=True)
    powers = jnp.exp(logits - highest)
    total = jnp.sum(powers, axis=1, keepdims=True)
    chances = powers / total
    classes = jnp.arange(logits.shape[1], dtype=jnp.int32)
    chosen = (labels[:, None] == classes[None, :]).astype(jnp.float32)
    cross = highest[:, 0] + jnp.log(total[:, 0]) - jnp.sum(chosen * logits, axis=1)
    loss_sum = links.sum_rows(jnp.sum(valid * cross)[None])[0]
    weights = (valid / label_total)[:, None]
    pull_logits = weights * (chances - chosen)
    grad_head = dot(pooled, pull_logits, ((0,), (0,)))
    pull_block = spread(dot(pull_logits, head, ((1,), (1,))))
    pull_two = pull_block * slope_two
    sums_two = links.sum_rows(
        jnp.stack([jnp.sum(pull_two * normal_two, axis=0), jnp.sum(pull_two, axis=0)])
    )
    centred_two = pull_two - sums_two[1] / rows - normal_two * (sums_two[0] / rows)
    factor_two = scale_two * gain_two
    pull_hidden_two = links.gather_parts(factor_two * centred_two, 1)
    grad_two = dot(pull_hidden_two, active_columns, ((0,), (0,)))
    pull_active = fold(dot(pull_hidden_two, kernel_two, ((1,), (0,))), count)
    pull_one = pull_active * slope_one
    sums_one = links.sum_rows(
        jnp.stack([jnp.sum(pull_one * normal_one, axis=0), jnp.sum(pull_one, axis=0)])
    )
    centred_one = pull_one - sums_one[1] / rows - normal_one * (sums_one[0] / rows)
    factor_one = scale_one * gain_one
    grad_one = dot(factor_one * centred_one, columns, ((0,), (0,)))

    grad_one = links.sum_rows(grad_one) + decay_one * kernel_one
    grad_two = links.sum_rows(grad_two) + decay_two * kernel_two
    grad_head = links.sum_rows(grad_head)
    grad_norm = jnp.concatenate([sums_one, sums_two])

    def product(vector):
        move_one, move_two, move_norm, move_head = vector
        tan_hidden = dot(columns, move_one, ((1,), (1,)))
        tan_normal_one, tan_scale_one = moments_tangent(
            normal_one, scale_one, tan_hidden, rows, links
        )
        tan_inner = move_norm[0] * normal_one + gain_one * tan_normal_one + move_norm[1]
        tan_active = slope_one * tan_inner
        tan_columns = patches(tan_active.reshape(MAP, MAP, count, width))
        tan_hidden = links.scatter_parts(
            dot(tan_columns, kernel_two, ((1,), (1,))) + dot(active_columns, move_two, ((1,), (1,))),
            1,
        )
        tan_normal_two, tan_scale_two = moments_tangent(
            normal_two, scale_two, tan_hidden, rows, links
        )
        tan_outer = move_norm[2] * normal_two + gain_two * tan_normal_two + move_norm[3]
        tan_pooled = pool(slope_two * tan_outer)
        tan_logits = links.sum_parts(
            dot(tan_pooled, head, ((1,), (0,))) + dot(pooled, move_head, ((1,), (0,)))
        )
        tan_chances = chances * (tan_logits - jnp.sum(chances * tan_logits, axis=1, keepdims=True))
        tan_pull = weights * tan_chances
        out_head = dot(tan_pooled, pull_logits, ((0,), (0,))) + dot(pooled, tan_pull, ((0,), (0,)))
        tan_block = spread(
            dot(tan_pull, head, ((1,), (1,))) + dot(pull_logits, move_head, ((1,), (1,)))
        )
        tan_two = tan_block * slope_two + pull_block * bend_two * tan_outer
        tan_sums_two = links.sum_rows(
            jnp.stack(
                [
                    jnp.sum(tan_two * normal_two + pull_two * tan_normal_two, axis=0),
                    jnp.sum(tan_two, axis=0),
                ]
            )
        )
        tan_factor = tan_scale_two * gain_two + scale_two * move_norm[2]
        tan_hidden = tan_factor * centred_two + factor_two * (
            tan_two
            - tan_sums_two[1] / rows
            - tan_normal_two * (sums_two[0] / rows)
            - normal_two * (tan_sums_two[0] / rows)
        )
        tan_hidden = links.gather_parts(tan_hidden, 1)
        out_two = dot(tan_hidden, active_columns, ((0,), (0,))) + dot(
            pull_hidden_two, tan_columns, ((0,), (0,))
        )
        tan_pull_active = fold(
            dot(tan_hidden, kernel_two, ((1,), (0,))) + dot(pull_hidden_two, move_two, ((1,), (0,))),
            count,
        )
        tan_one = tan_pull_active * slope_one + pull_active * bend_one * tan_inner
        tan_sums_one = links.sum_rows(
            jnp.stack(
                [
                    jnp.sum(tan_one * normal_one + pull_one * tan_normal_one, axis=0),
                    jnp.sum(tan_one, axis=0),
                ]
            )
        )
        tan_factor = tan_scale_one * gain_one + scale_one * move_norm[0]
        tan_hidden = tan_factor * centred_one + factor_one * (
            tan_one
            - tan_sums_one[1] / rows
            - tan_normal_one * (sums_one[0] / rows)
            - normal_one * (tan_sums_one[0] / rows)
        )
        out_one = dot(tan_hidden, columns, ((0,), (0,)))
        return (
            links.sum_rows(out_one) + decay_one * move_one,
            links.sum_rows(out_two) + decay_two * move_two,
            jnp.concatenate([tan_sums_one, tan_sums_two]),
            links.sum_rows(out_head),
        )

    vector = (grad_one, grad_two, grad_norm, grad_head)
    series_one, series_two = grad_one, grad_two
    for turn in range(NEUMANN):
        change = product(vector)
        vector = tuple(
            previous - neumann_rate * moved for previous, moved in zip(vector, change)
        )
        series_one, series_two = series_one + vector[0], series_two + vector[1]

    series = jnp.stack([links.own_rows(series_one), links.to_outer(series_two)])
    hyper_gradient = -neumann_rate * conv_weights * series
    grads = jnp.stack([links.own_rows(grad_one), links.to_outer(grad_two)])
    conv_new, conv_one, conv_two = adamw(conv_weights, grads, conv_first, conv_second, 0.015)
    norm_new, norm_one, norm_two = adamw(
        norm_params, links.own_rows(grad_norm, 1), norm_first, norm_second, 0.3
    )
    head_new, head_one, head_two = adamw(
        head_weights, links.own_rows(grad_head), head_first, head_second, 0.13
    )
    return (
        loss_sum,
        label_total,
        conv_new,
        conv_one,
        conv_two,
        norm_new,
        norm_one,
        norm_two,
        head_new,
        head_one,
        head_two,
        hyper_gradient,
    )


def solution(mesh):
    images = P(("shard", "dp"))
    rows = P(None, "shard")
    head = P("shard")
    in_specs = (images,) * 6 + (rows, rows, head, rows, rows, rows, rows, rows, head, head)
    out_specs = (P(), P()) + (rows,) * 6 + (head,) * 3 + (rows,)
    return jax.shard_map(shards, mesh=mesh, in_specs=in_specs, out_specs=out_specs, check_vma=False)
```

```python
import functools

import jax
import jax.numpy as jnp
from jax import lax
from jax.experimental import pallas as pl
from jax.experimental.pallas import tpu as pltpu
from jax.sharding import PartitionSpec as P

MAP = 4
NEUMANN = 3
STEP = 5
TAPS = 9

norm_eps = 1e-05
neumann_rate = 10.0
beta_first = 0.5
beta_second = 0.5
adam_eps = 1e-08
decoupled = 0.01
HIGH = lax.Precision.HIGH


def crop_image(single, offsets, flipped):
    window = lax.dynamic_slice(
        single, (offsets[0], offsets[1], jnp.int32(0)), (MAP, MAP, single.shape[2])
    )
    return jnp.where(flipped == 1, window[:, ::-1, :], window)


def patches(maps):
    count, width = maps.shape[2:]
    padded = jnp.pad(maps, ((1, 1), (1, 1), (0, 0), (0, 0)))
    taps = [padded[dy : dy + MAP, dx : dx + MAP] for dy in range(3) for dx in range(3)]
    return jnp.concatenate(taps, axis=3).reshape(MAP * MAP * count, TAPS * width)


def fold(columns, count):
    width = columns.shape[1] // TAPS
    whole = columns.reshape(MAP, MAP, count, TAPS, width)
    padded = jnp.pad(whole, ((1, 1), (1, 1), (0, 0), (0, 0), (0, 0)))
    total = 0.0
    for dy in range(3):
        for dx in range(3):
            total = total + padded[2 - dy : 2 - dy + MAP, 2 - dx : 2 - dx + MAP, :, dy * 3 + dx]
    return total.reshape(MAP * MAP * count, width)


def dot(left, right, dims):
    return lax.dot_general(
        left, right, ((dims[0], dims[1]), ((), ())), precision=HIGH, preferred_element_type=jnp.float32
    )


MESH_ID = pl.DeviceIdType.MESH
LANES = 128


def halves(value):
    high = value.astype(jnp.bfloat16)
    return high, (value - high.astype(jnp.float32)).astype(jnp.bfloat16)


def halves_outside(value):
    high = lax.reduce_precision(value, 8, 7)
    return high.astype(jnp.bfloat16), (value - high).astype(jnp.bfloat16)


def mul(left, right, dims=((1,), (0,))):
    return lax.dot_general(left, right, (dims, ((), ())), preferred_element_type=jnp.float32)


def mul_exact(left, right, dims=((1,), (0,))):
    return lax.dot_general(
        left,
        right,
        (dims, ((), ())),
        precision=lax.Precision.HIGHEST,
        preferred_element_type=jnp.float32,
    )


def neumann_kernel(
    rows,
    members,
    copies,
    x_hi,
    x_lo,
    k_hi,
    k_lo,
    a_hi,
    a_lo,
    g_hi,
    g_lo,
    gt_hi,
    gt_lo,
    v1_in,
    v2_in,
    decay_one,
    decay_two,
    move_norm_in,
    move_head_in,
    head,
    n1,
    s1,
    pb1,
    pull1,
    c1,
    n2,
    s2,
    pb2,
    pull2,
    c2,
    pooled,
    chances,
    weights,
    pull_logits,
    channel,
    series_one,
    gathered_two,
    series_two,
    v1,
    v2,
    v1_hi,
    v1_lo,
    v2_hi,
    v2_lo,
    b_hi,
    b_lo,
    t_hi,
    t_lo,
    tt_hi,
    tt_lo,
    slots,
    partial,
    from_low,
    from_high,
    flow,
    nt1,
    in1,
    nt2,
    in2,
    fold_sum,
    sum_one,
    sum_two,
    half_one,
    half_two,
    piece_one,
    piece_two,
    stats_box,
    stats_own,
    logit_box,
    logit_own,
    turned_hi,
    turned_lo,
    move_norm,
    move_head,
    load_sem,
    stats_send,
    stats_recv,
    logit_send,
    logit_recv,
    up_send,
    up_recv,
    down_send,
    down_recv,
    ring_send,
    ring_recv,
    pair_send,
    pair_recv,
    plane_send,
    plane_recv,
    back_send,
    back_recv,
    swap_send,
    swap_recv,
    last_send,
    last_recv,
):
    shard = lax.axis_index("shard")
    copy = lax.axis_index("dp")
    part = shard // members
    me = (shard % members) * copies + copy
    place, core = me // 2, me % 2
    last_part = 3

    def row_peer(other):
        return (part * members + other // copies, other % copies)

    def part_peer(other):
        return (other * members + shard % members, copy)

    owns = shard == me

    def owner(other):
        return (me, other)

    def holder(other):
        return (other * members + shard // copies, shard % copies)

    barrier = pltpu.get_barrier_semaphore()
    for step in range(1, 8):
        pl.semaphore_signal(barrier, inc=1, device_id=row_peer(me ^ step), device_id_type=MESH_ID)
    for step in range(1, 4):
        pl.semaphore_signal(barrier, inc=1, device_id=part_peer(part ^ step), device_id_type=MESH_ID)
    for step in range(4):
        target, source = owner(step), holder(step)

        @pl.when(jnp.logical_not(owns))
        def _():
            pl.semaphore_signal(barrier, inc=1, device_id=target, device_id_type=MESH_ID)
            pl.semaphore_signal(barrier, inc=1, device_id=source, device_id_type=MESH_ID)

        @pl.when(owns & (step != copy))
        def _():
            pl.semaphore_signal(barrier, inc=1, device_id=target, device_id_type=MESH_ID)

        @pl.when(owns & (step != part))
        def _():
            pl.semaphore_signal(barrier, inc=1, device_id=source, device_id_type=MESH_ID)

    loads = [
        pltpu.make_async_copy(v1_in, v1, load_sem.at[0]),
        pltpu.make_async_copy(v2_in, v2, load_sem.at[1]),
    ]
    for load in loads:
        load.start()
    move_norm[...] = move_norm_in[...]
    move_head[...] = move_head_in[...]
    stats_own[...] = jnp.zeros_like(stats_own)
    b_hi[...] = jnp.zeros_like(b_hi)
    b_lo[...] = jnp.zeros_like(b_lo)
    for load in loads:
        load.wait()
    pl.semaphore_wait(barrier, 18 - 2 * owns.astype(jnp.int32))

    def remote(source, target, send, recv, device):
        return pltpu.make_async_remote_copy(
            src_ref=source,
            dst_ref=target,
            send_sem=send,
            recv_sem=recv,
            device_id=device,
            device_id_type=MESH_ID,
        )

    def sum_members(site, size):
        moves = []
        for step in range(1, 8):
            move = remote(
                stats_own.at[site, pl.ds(0, size)],
                stats_box.at[site, step, pl.ds(0, size)],
                stats_send.at[site, step],
                stats_recv.at[site, step],
                row_peer(me ^ step),
            )
            move.start()
            moves.append(move)
        stats_box[site, 0, pl.ds(0, size)] = stats_own[site, pl.ds(0, size)]
        for move in moves:
            move.wait()
        total = stats_box[site, me, pl.ds(0, size)]
        for other in range(1, 8):
            total = total + stats_box[site, other ^ me, pl.ds(0, size)]
        return total

    def each_cell(body, init=None):
        return lax.fori_loop(0, 16, body, init)

    def window(ref, tap):
        part_of = ref[pl.ds(tap // 3, 4), pl.ds(tap % 3, 4)]
        return part_of.reshape(16 * part_of.shape[2], part_of.shape[3])

    def row(ref, index):
        return ref[index : index + 1, :]

    count = n1.shape[1]
    zero = jnp.zeros((count, LANES), jnp.float32)

    def put_sums(site, first, second):
        stats_own[site, 0:1, :] = jnp.sum(first, axis=0, keepdims=True)
        stats_own[site, 1:2, :] = jnp.sum(second, axis=0, keepdims=True)

    series_one[...] = v1[:, place, core]
    series_two[...] = v2[me]

    def turn_body(turn, nothing):
        def split_one(tap, _):
            for place_of in range(4):
                for core_of in range(2):
                    high, low = halves(v1[tap, place_of, core_of])
                    start = (place_of * 2 + core_of) * 16
                    v1_hi[tap, start : start + 16] = high
                    v1_lo[tap, start : start + 16] = low

        lax.fori_loop(0, 9, split_one, None)

        def split_two(block, _):
            at = pl.ds(pl.multiple_of(block * 64, 64), 64)
            v2_hi[at], v2_lo[at] = halves(v2[block])

        lax.fori_loop(0, 8, split_two, None)

        def tap_one(tap, _):
            weight = jnp.concatenate([v1_hi[tap], v1_lo[tap]], axis=0)
            out = mul(window(x_hi, tap), weight, ((1,), (1,)))
            out = out[:, :LANES] + out[:, LANES:] + mul(window(x_lo, tap), v1_hi[tap], ((1,), (1,)))
            flow[...] += out.reshape(flow.shape)

        flow[...] = jnp.zeros_like(flow)
        lax.fori_loop(0, 9, tap_one, None)

        def sums_forward(normal):
            def body(cell, carry):
                value = flow[cell]
                return carry[0] + value, carry[1] + value * normal[cell]

            return each_cell(body, (zero, zero))

        put_sums(0, *sums_forward(n1))
        total = sum_members(0, 8) * (1.0 / rows)
        average, cross = total[0:1], total[1:2]
        scale, gain = row(channel, 0), row(channel, 1)
        tan_scale_one = -scale * scale * cross
        move_gain, move_shift = row(move_norm, 0), row(move_norm, 1)

        def forward_one(cell, _):
            normal = n1[cell]
            tangent = scale * (flow[cell] - average - normal * cross)
            inner = move_gain * normal + gain * tangent + move_shift
            nt1[cell] = tangent
            in1[cell] = inner
            high, low = halves(s1[cell] * inner)
            b_hi[cell // 4 + 1, cell % 4 + 1] = high
            b_lo[cell // 4 + 1, cell % 4 + 1] = low

        each_cell(forward_one)

        def half_of(half, _):
            at = pl.ds(pl.multiple_of(half * 256, 256), 256)

            def tap_two(tap, _):
                lanes = pl.ds(pl.multiple_of(tap * LANES, LANES), LANES)
                left_hi = jnp.concatenate([window(b_hi, tap), window(a_hi, tap)], axis=1)
                left_lo = jnp.concatenate([window(b_lo, tap), window(a_lo, tap)], axis=1)
                right_hi = jnp.concatenate([k_hi[at, lanes], v2_hi[at, lanes]], axis=1)
                right_lo = jnp.concatenate([k_lo[at, lanes], v2_lo[at, lanes]], axis=1)
                out = mul(
                    jnp.concatenate([left_hi, left_hi, left_lo], axis=1),
                    jnp.concatenate([right_hi, right_lo, right_hi], axis=1),
                    ((1,), (1,)),
                )
                partial[half * 2] += out[:, :LANES].reshape(flow.shape)
                partial[half * 2 + 1] += out[:, LANES:].reshape(flow.shape)

            lax.fori_loop(0, 9, tap_two, None)

        partial[...] = jnp.zeros_like(partial)
        lax.fori_loop(0, 2, half_of, None)

        for target in (3, 2, 1):

            @pl.when(part < target)
            def _():
                @pl.when(part > 0)
                def _():
                    remote(
                        from_low.at[target],
                        from_low.at[target],
                        up_send.at[target],
                        up_recv.at[target],
                        part_peer(part - 1),
                    ).wait_recv()
                    partial[target] += from_low[target]

                remote(
                    partial.at[target],
                    from_low.at[target],
                    up_send.at[target],
                    up_recv.at[target],
                    part_peer(part + 1),
                ).start()

            @pl.when(part > last_part - target)
            def _():
                goal = last_part - target

                @pl.when(part < last_part)
                def _():
                    remote(
                        from_high.at[goal],
                        from_high.at[goal],
                        down_send.at[goal],
                        down_recv.at[goal],
                        part_peer(part + 1),
                    ).wait_recv()
                    partial[goal] += from_high[goal]

                remote(
                    partial.at[goal],
                    from_high.at[goal],
                    down_send.at[goal],
                    down_recv.at[goal],
                    part_peer(part - 1),
                ).start()

        for target in range(4):

            @pl.when(part == target)
            def _():
                total = partial[target]
                if target > 0:
                    remote(
                        from_low.at[target],
                        from_low.at[target],
                        up_send.at[target],
                        up_recv.at[target],
                        part_peer(target - 1),
                    ).wait_recv()
                    total = total + from_low[target]
                if target < last_part:
                    remote(
                        from_high.at[target],
                        from_high.at[target],
                        down_send.at[target],
                        down_recv.at[target],
                        part_peer(target + 1),
                    ).wait_recv()
                    total = total + from_high[target]
                flow[...] = total

        for target in (3, 2, 1):

            @pl.when(part < target)
            def _():
                remote(
                    partial.at[target],
                    from_low.at[target],
                    up_send.at[target],
                    up_recv.at[target],
                    part_peer(part + 1),
                ).wait_send()

            @pl.when(part > last_part - target)
            def _():
                goal = last_part - target
                remote(
                    partial.at[goal],
                    from_high.at[goal],
                    down_send.at[goal],
                    down_recv.at[goal],
                    part_peer(part - 1),
                ).wait_send()

        put_sums(1, *sums_forward(n2))
        total = sum_members(1, 8) * (1.0 / rows)
        average2, cross2 = total[0:1], total[1:2]
        scale2, gain2 = row(channel, 2), row(channel, 3)
        tan_scale_two = -scale2 * scale2 * cross2
        move_gain2, move_shift2 = row(move_norm, 2), row(move_norm, 3)

        def forward_two(cell, carry):
            normal = n2[cell]
            tangent = scale2 * (flow[cell] - average2 - normal * cross2)
            inner = move_gain2 * normal + gain2 * tangent + move_shift2
            nt2[cell] = tangent
            in2[cell] = inner
            return carry + s2[cell] * inner

        tan_pooled = each_cell(forward_two, zero) * (1.0 / 16.0)
        logit_own[...] = mul_exact(tan_pooled, head[...], ((1,), (1,))) + mul_exact(
            pooled[...], move_head[...], ((1,), (1,))
        )
        moves = []
        for step in range(1, 4):
            move = remote(
                logit_own,
                logit_box.at[step],
                logit_send.at[step],
                logit_recv.at[step],
                part_peer(part ^ step),
            )
            move.start()
            moves.append(move)
        logit_box[0] = logit_own[...]
        for move in moves:
            move.wait()
        tan_logits = logit_box[part]
        for other in range(1, 4):
            tan_logits = tan_logits + logit_box[other ^ part]
        chance = chances[...]
        tan_pull = (
            weights[...]
            * chance
            * (tan_logits - jnp.sum(chance * tan_logits, axis=1, keepdims=True))
        )
        out_head = mul_exact(pull_logits[...], tan_pooled, ((0,), (0,))) + mul_exact(
            tan_pull, pooled[...], ((0,), (0,))
        )
        tan_block = (
            mul_exact(tan_pull, head[...]) + mul_exact(pull_logits[...], move_head[...])
        ) * (1.0 / 16.0)

        def back_two(cell, carry):
            tangent = tan_block * s2[cell] + pb2[cell] * in2[cell]
            flow[cell] = tangent
            return (
                carry[0] + tangent * n2[cell] + pull2[cell] * nt2[cell],
                carry[1] + tangent,
            )

        put_sums(2, *each_cell(back_two, (zero, zero)))
        stats_own[2, 8:24, :] = out_head[0:16]
        total = sum_members(2, 24)
        out_gain2, out_shift2 = total[0:1], total[1:2]
        move_head_new = move_head[0:16] - neumann_rate * total[8:24]
        factor2 = scale2 * gain2
        tan_factor2 = tan_scale_two * gain2 + scale2 * move_gain2
        inverse = 1.0 / rows

        def pull_two_body(cell, _):
            slots[part, cell] = tan_factor2 * c2[cell] + factor2 * (
                flow[cell]
                - out_shift2 * inverse
                - nt2[cell] * row(channel, 6)
                - n2[cell] * (out_gain2 * inverse)
            )

        each_cell(pull_two_body)

        def ring_up(block):
            return remote(
                slots.at[block],
                slots.at[block],
                ring_send.at[0, part - block],
                ring_recv.at[block],
                part_peer(part + 1),
            )

        def ring_down(block):
            return remote(
                slots.at[block],
                slots.at[block],
                ring_send.at[1, block - part],
                ring_recv.at[block],
                part_peer(part - 1),
            )

        @pl.when(part < last_part)
        def _():
            ring_up(part).start()

        @pl.when(part > 0)
        def _():
            ring_down(part).start()

        for step in range(1, 4):

            @pl.when(part >= step)
            def _():
                remote(
                    slots.at[part - step],
                    slots.at[part - step],
                    ring_send.at[0, 0],
                    ring_recv.at[part - step],
                    part_peer(part - 1),
                ).wait_recv()

                @pl.when(part < last_part)
                def _():
                    ring_up(part - step).start()

            @pl.when(part + step <= last_part)
            def _():
                remote(
                    slots.at[part + step],
                    slots.at[part + step],
                    ring_send.at[0, 0],
                    ring_recv.at[part + step],
                    part_peer(part + 1),
                ).wait_recv()

                @pl.when(part > 0)
                def _():
                    ring_down(part + step).start()

        for step in range(0, 4):

            @pl.when((part >= step) & (part < last_part))
            def _():
                ring_up(part - step).wait_send()

            @pl.when((part + step <= last_part) & (part > 0))
            def _():
                ring_down(part + step).wait_send()

        for block in range(4):
            at = slice(block * LANES, (block + 1) * LANES)
            value = slots[block].reshape(16 * count, LANES)
            t_hi[:, at], t_lo[:, at] = halves(value)
            tt_hi[at, :], tt_lo[at, :] = halves(value.T)

        fold_sum[...] = jnp.zeros_like(fold_sum)

        def tap_back(tap, _):
            lanes = pl.ds(pl.multiple_of(tap * LANES, LANES), LANES)
            active_hi, active_lo = window(a_hi, tap), window(a_lo, tap)
            moved_hi, moved_lo = window(b_hi, tap), window(b_lo, tap)
            left = jnp.concatenate([tt_hi[...], gt_hi[...]], axis=1)
            right = jnp.concatenate(
                [
                    jnp.concatenate([active_hi, active_lo], axis=1),
                    jnp.concatenate([moved_hi, moved_lo], axis=1),
                ],
                axis=0,
            )
            out = mul(left, right)
            left = jnp.concatenate([tt_lo[...], gt_lo[...]], axis=1)
            right = jnp.concatenate([active_hi, moved_hi], axis=0)
            out = out[:, :LANES] + out[:, LANES:] + mul(left, right)
            sum_two[:, :, :, lanes] = out.reshape(4, 2, 64, LANES)
            left = jnp.concatenate([t_hi[...], g_hi[...]], axis=1)
            right = jnp.concatenate(
                [
                    jnp.concatenate([k_hi[:, lanes], k_lo[:, lanes]], axis=1),
                    jnp.concatenate([v2_hi[:, lanes], v2_lo[:, lanes]], axis=1),
                ],
                axis=0,
            )
            out = mul(left, right)
            left = jnp.concatenate([t_lo[...], g_lo[...]], axis=1)
            right = jnp.concatenate([k_hi[:, lanes], v2_hi[:, lanes]], axis=0)
            out = out[:, :LANES] + out[:, LANES:] + mul(left, right)
            fold_sum[pl.ds(tap // 3, 4), pl.ds(tap % 3, 4)] += out.reshape(4, 4, count, LANES)

        lax.fori_loop(0, 9, tap_back, None)

        def back_one(cell, carry):
            pull = fold_sum[cell // 4 + 1, cell % 4 + 1]
            tangent = pull * s1[cell] + pb1[cell] * in1[cell]
            flow[cell] = tangent
            return (
                carry[0] + tangent * n1[cell] + pull1[cell] * nt1[cell],
                carry[1] + tangent,
            )

        put_sums(3, *each_cell(back_one, (zero, zero)))
        total = sum_members(3, 8)
        out_gain, out_shift = total[0:1], total[1:2]
        factor = scale * gain
        tan_factor = tan_scale_one * gain + scale * move_gain

        def pull_one_body(cell, _):
            flow[cell] = tan_factor * c1[cell] + factor * (
                flow[cell]
                - out_shift * inverse
                - nt1[cell] * row(channel, 4)
                - n1[cell] * (out_gain * inverse)
            )

        each_cell(pull_one_body)
        turned_hi[...], turned_lo[...] = halves(flow[...].reshape(16 * count, LANES).T)

        def tap_weight(tap, _):
            left = jnp.concatenate([turned_hi[...], turned_lo[...]], axis=0)
            out = mul(left, window(x_hi, tap))
            out = out[:LANES] + out[LANES:] + mul(turned_hi[...], window(x_lo, tap))
            sum_one[tap] = out.reshape(sum_one.shape[1:])

        lax.fori_loop(0, 9, tap_weight, None)

        pair = row_peer(me ^ 1)
        moves = [
            remote(
                sum_one.at[:, :, 1 - core], half_one, pair_send.at[0], pair_recv.at[0], pair
            ),
            remote(sum_two.at[:, 1 - core], half_two, pair_send.at[1], pair_recv.at[1], pair),
        ]
        for move in moves:
            move.start()
        for move in moves:
            move.wait()

        def add_one(tap, _):
            for place_of in range(4):
                half_one[tap, place_of] += sum_one[tap, place_of, core]

        lax.fori_loop(0, 9, add_one, None)
        for place_of in range(4):
            half_two[place_of] += sum_two[place_of, core]
        moves = []
        for step in range(1, 4):
            other = place ^ step
            device = row_peer(other * 2 + core)
            moves.append(
                remote(
                    half_one.at[:, other],
                    piece_one.at[step],
                    plane_send.at[0, step],
                    plane_recv.at[0, step],
                    device,
                )
            )
            moves.append(
                remote(
                    half_two.at[other],
                    piece_two.at[step],
                    plane_send.at[1, step],
                    plane_recv.at[1, step],
                    device,
                )
            )
        for move in moves:
            move.start()
        for move in moves:
            move.wait()

        def step_one(tap, _):
            change = half_one[tap, place] + piece_one[1, tap] + piece_one[2, tap] + piece_one[3, tap]
            old = v1[tap, place, core]
            new = old - neumann_rate * (change + decay_one[tap] * old)
            v1[tap, place, core] = new
            series_one[tap] += new

        lax.fori_loop(0, 9, step_one, None)
        change = half_two[place] + piece_two[1] + piece_two[2] + piece_two[3]
        old = v2[me]
        new = old - neumann_rate * (change + decay_two[...] * old)
        v2[me] = new
        series_two[...] += new
        move_norm[0:1, :] = move_gain - neumann_rate * out_gain
        move_norm[1:2, :] = move_shift - neumann_rate * out_shift
        move_norm[2:3, :] = move_gain2 - neumann_rate * out_gain2
        move_norm[3:4, :] = move_shift2 - neumann_rate * out_shift2
        move_head[0:16, :] = move_head_new

        @pl.when(turn < NEUMANN - 1)
        def _():
            def piece_of(which, other):
                if which == 0:
                    return v1.at[:, other // 2, other % 2]
                return v2.at[other]

            def to_plane(which, step):
                return remote(
                    piece_of(which, me),
                    piece_of(which, me),
                    back_send.at[which, step],
                    back_recv.at[which, step],
                    row_peer(me ^ (2 * step)),
                )

            def to_pair(which, step):
                piece = piece_of(which, me ^ (2 * step))
                return remote(
                    piece, piece, swap_send.at[which, step], swap_recv.at[which, step], pair
                )

            for which in range(2):
                for step in range(1, 4):
                    to_plane(which, step).start()
                to_pair(which, 0).start()
            for which in range(2):
                for step in range(1, 4):
                    piece = piece_of(which, me ^ (2 * step))
                    remote(
                        piece,
                        piece,
                        back_send.at[which, step],
                        back_recv.at[which, step],
                        row_peer(me ^ (2 * step)),
                    ).wait_recv()
                    to_pair(which, step).start()
            for which in range(2):
                for step in range(1, 4):
                    to_plane(which, step).wait_send()
                for step in range(0, 4):
                    to_pair(which, step).wait_send()
                    piece = piece_of(which, me ^ 1 ^ (2 * step))
                    remote(
                        piece, piece, swap_send.at[which, step], swap_recv.at[which, step], pair
                    ).wait_recv()

    lax.fori_loop(0, NEUMANN, turn_body, None)

    for other in range(4):

        @pl.when(jnp.logical_not(owns & (copy == other)))
        def _():
            remote(
                series_two,
                gathered_two.at[part],
                last_send.at[other],
                last_recv.at[part],
                owner(other),
            ).start()

    @pl.when(owns)
    def _():
        gathered_two[part] = series_two[...]

    for other in range(4):

        @pl.when(jnp.logical_not(owns & (copy == other)))
        def _():
            remote(
                series_two,
                gathered_two.at[part],
                last_send.at[other],
                last_recv.at[part],
                owner(other),
            ).wait_send()

        @pl.when(jnp.logical_not(owns & (part == other)))
        def _():
            remote(
                series_two,
                gathered_two.at[other],
                last_send.at[other],
                last_recv.at[other],
                owner(other),
            ).wait_recv()


def neumann_fused(
    links, rows, images, kernel_two, decay, vector, head, active, pull_hidden_two, maps, small, channel
):
    cells, count, channels = images.shape
    width = active.shape[1]
    me = links.member * links.copies + lax.axis_index("dp")
    group = links.members * links.copies
    piece, block = width // group, channels // group

    def padded(value):
        value = value.reshape(MAP, MAP, count, value.shape[-1])
        return halves_outside(jnp.pad(value, ((1, 1), (1, 1), (0, 0), (0, 0))))

    def fill(value, shape):
        return jnp.pad(value, [(0, new - old) for new, old in zip(shape, value.shape)])

    by_tap = vector[0].reshape(width, TAPS, channels).transpose(1, 0, 2)
    decay_one = lax.dynamic_slice_in_dim(decay[0], me * piece, piece, 0)
    decay_one = decay_one.reshape(piece, TAPS, channels).transpose(1, 0, 2)
    decay_two = lax.dynamic_slice_in_dim(decay[1], me * block, block, 0)
    pull_hi, pull_lo = halves_outside(pull_hidden_two)
    operands = (
        *padded(images),
        *halves_outside(kernel_two),
        *padded(active),
        pull_hi,
        pull_lo,
        pull_hi.T,
        pull_lo.T,
        by_tap.reshape(TAPS, 4, 2, piece, channels),
        vector[1].reshape(group, block, TAPS * width),
        decay_one,
        decay_two,
        fill(vector[2], (8, width)),
        fill(vector[3].T, (LANES, width)),
        fill(head.T, (LANES, width)),
        *(value.reshape(cells, count, width) for value in maps),
        *(fill(value, (count, LANES)) for value in small),
        channel,
    )
    vmem = pl.BlockSpec(memory_space=pltpu.VMEM)
    anywhere = pl.BlockSpec(memory_space=pl.ANY)
    in_specs = [vmem] * len(operands)
    in_specs[10] = in_specs[11] = anywhere
    f32, b16 = jnp.float32, jnp.bfloat16
    row_map = pltpu.VMEM((cells, count, width), f32)
    dma = pltpu.SemaphoreType.DMA
    scratch = [
        pltpu.VMEM((block, TAPS * width), f32),
        pltpu.VMEM((TAPS, 4, 2, piece, channels), f32),
        pltpu.VMEM((group, block, TAPS * width), f32),
        pltpu.VMEM((TAPS, width, channels), b16),
        pltpu.VMEM((TAPS, width, channels), b16),
        pltpu.VMEM((channels, TAPS * width), b16),
        pltpu.VMEM((channels, TAPS * width), b16),
        pltpu.VMEM((MAP + 2, MAP + 2, count, width), b16),
        pltpu.VMEM((MAP + 2, MAP + 2, count, width), b16),
        pltpu.VMEM((cells * count, channels), b16),
        pltpu.VMEM((cells * count, channels), b16),
        pltpu.VMEM((channels, cells * count), b16),
        pltpu.VMEM((channels, cells * count), b16),
        pltpu.VMEM((4, cells, count, width), f32),
        pltpu.VMEM((4, cells, count, width), f32),
        pltpu.VMEM((4, cells, count, width), f32),
        pltpu.VMEM((4, cells, count, width), f32),
        row_map,
        row_map,
        row_map,
        row_map,
        row_map,
        pltpu.VMEM((MAP + 2, MAP + 2, count, width), f32),
        pltpu.VMEM((TAPS, 4, 2, piece, channels), f32),
        pltpu.VMEM((4, 2, block, TAPS * width), f32),
        pltpu.VMEM((TAPS, 4, piece, channels), f32),
        pltpu.VMEM((4, block, TAPS * width), f32),
        pltpu.VMEM((4, TAPS, piece, channels), f32),
        pltpu.VMEM((4, block, TAPS * width), f32),
        pltpu.VMEM((4, 8, 24, width), f32),
        pltpu.VMEM((4, 24, width), f32),
        pltpu.VMEM((4, count, LANES), f32),
        pltpu.VMEM((count, LANES), f32),
        pltpu.VMEM((width, cells * count), b16),
        pltpu.VMEM((width, cells * count), b16),
        pltpu.VMEM((8, width), f32),
        pltpu.VMEM((LANES, width), f32),
        dma((2,)),
        dma((4, 8)),
        dma((4, 8)),
        dma((4,)),
        dma((4,)),
        dma((4,)),
        dma((4,)),
        dma((4,)),
        dma((4,)),
        dma((2, 4)),
        dma((4,)),
        dma((2,)),
        dma((2,)),
        dma((2, 4)),
        dma((2, 4)),
        dma((2, 4)),
        dma((2, 4)),
        dma((2, 4)),
        dma((2, 4)),
        dma((4,)),
        dma((4,)),
    ]
    series_one, series_two = pl.pallas_call(
        functools.partial(neumann_kernel, rows, links.members, links.copies),
        out_shape=(
            jax.ShapeDtypeStruct((TAPS, piece, channels), f32),
            jax.ShapeDtypeStruct((4, block, TAPS * width), f32),
        ),
        in_specs=in_specs,
        out_specs=(vmem, vmem),
        scratch_shapes=scratch,
        compiler_params=pltpu.CompilerParams(
            collective_id=1, has_side_effects=True, vmem_limit_bytes=63 * 1024 * 1024
        ),
        name="neumann",
    )(*operands)
    series_one = lax.all_gather(series_one, "dp").transpose(0, 2, 1, 3)
    series_one = series_one.reshape(-1, TAPS * channels)
    series_two = series_two.reshape(4, block, TAPS, width).transpose(1, 2, 0, 3)
    return jnp.stack([series_one, series_two.reshape(block, TAPS * channels)])


def adamw(weight, grad, first, second, rate):
    first = beta_first * first + (1.0 - beta_first) * grad
    second = beta_second * second + (1.0 - beta_second) * grad * grad
    first_hat = first / (1.0 - beta_first**STEP)
    second_hat = second / (1.0 - beta_second**STEP)
    update = first_hat / (jnp.sqrt(second_hat) + adam_eps) + decoupled * weight
    return (weight - rate * update, first, second)


def silu_parts(value):
    gate = jax.nn.sigmoid(value)
    slope = gate * (1.0 - gate)
    first = gate + value * slope
    second = slope * (2.0 + value * (1.0 - 2.0 * gate))
    return value * gate, first, second


class Links:
    def __init__(self):
        self.shards = lax.axis_size("shard")
        self.copies = lax.axis_size("dp")
        self.parts = 4 if self.shards % 4 == 0 else 1
        self.members = self.shards // self.parts
        index = lax.axis_index("shard")
        self.part = index // self.members
        self.member = index % self.members
        self.across = [
            [p * self.members + m for p in range(self.parts)] for m in range(self.members)
        ]
        self.within = [
            [p * self.members + m for m in range(self.members)] for p in range(self.parts)
        ]

    def sum_rows(self, value):
        value = lax.psum(value, "dp")
        gathered = lax.all_gather(value, "shard", axis_index_groups=self.within)
        return jnp.sum(gathered, axis=0)

    def sum_parts(self, value):
        return jnp.sum(lax.all_gather(value, "shard", axis_index_groups=self.across), axis=0)

    def gather_parts(self, value, axis):
        return lax.all_gather(value, "shard", axis_index_groups=self.across, axis=axis, tiled=True)

    def gather_members(self, value, axis):
        return lax.all_gather(value, "shard", axis_index_groups=self.within, axis=axis, tiled=True)

    def scatter_parts(self, value, axis):
        return lax.psum_scatter(
            value, "shard", axis_index_groups=self.across, scatter_dimension=axis, tiled=True
        )

    def to_inner(self, value):
        rows, channels = value.shape[0], value.shape[1] // TAPS
        width = channels // self.parts
        cut = value.reshape(rows, TAPS, self.parts, width).transpose(2, 0, 1, 3)
        moved = lax.all_to_all(cut, "shard", 0, 0, axis_index_groups=self.across, tiled=True)
        whole = self.gather_members(moved, 1)
        return whole.reshape(channels, TAPS * width)

    def to_outer(self, value):
        channels, width = value.shape[0], value.shape[1] // TAPS
        rows = channels // self.shards
        cut = value.reshape(self.parts, self.members, rows, TAPS * width)
        cut = lax.dynamic_index_in_dim(cut, self.member, 1, keepdims=False)
        moved = lax.all_to_all(cut, "shard", 0, 0, axis_index_groups=self.across, tiled=True)
        moved = moved.reshape(self.parts, rows, TAPS, width).transpose(1, 2, 0, 3)
        return moved.reshape(rows, TAPS * channels)

    def own_rows(self, value, axis=0):
        size = value.shape[axis] // self.members
        return lax.dynamic_slice_in_dim(value, self.member * size, size, axis)


def moments(hidden, rows, links):
    totals = links.sum_rows(jnp.stack([jnp.sum(hidden, axis=0), jnp.sum(hidden * hidden, axis=0)]))
    average = totals[0] / rows
    scale = lax.rsqrt(totals[1] / rows - average * average + norm_eps)
    return (hidden - average) * scale, scale


def moments_tangent(normal, scale, tangent, rows, links):
    totals = links.sum_rows(
        jnp.stack([jnp.sum(tangent, axis=0), jnp.sum(tangent * normal, axis=0)])
    )
    average, cross = totals[0] / rows, totals[1] / rows
    return scale * (tangent - average - normal * cross), -scale * scale * cross


def shards(
    source,
    index_map,
    crop_offsets,
    flip_flags,
    labels,
    valid_mask,
    conv_weights,
    norm_params,
    head_weights,
    decay_rates,
    conv_first,
    conv_second,
    norm_first,
    norm_second,
    head_first,
    head_second,
):
    links = Links()
    own_images = source.shape[0]
    channels = source.shape[3]
    rows = float(own_images * MAP * MAP * links.shards * links.copies)
    count = own_images * links.parts
    width = channels // links.parts
    first_column = links.part * width

    picked = source[index_map]
    images = jax.vmap(crop_image)(picked, crop_offsets, flip_flags)
    images = images.transpose(1, 2, 0, 3)
    images = links.gather_parts(images, 2)
    labels = links.gather_parts(labels, 0)
    valid = links.gather_parts(valid_mask.astype(jnp.float32), 0)
    label_total = lax.psum(jnp.sum(valid_mask.astype(jnp.float32)), ("shard", "dp"))

    kernel_one = links.gather_members(conv_weights[0], 0)
    kernel_two = links.to_inner(conv_weights[1])
    decay_one = links.gather_members(decay_rates[0], 0)
    decay_two = links.to_inner(decay_rates[1])
    norms = links.gather_members(norm_params, 1)
    head = links.gather_members(head_weights, 0)
    gain_one, shift_one, gain_two, shift_two = norms[0], norms[1], norms[2], norms[3]

    def pool(value):
        return jnp.sum(value.reshape(MAP * MAP, count, width), axis=0) / (MAP * MAP)

    def spread(value):
        whole = jnp.broadcast_to(value[None] / (MAP * MAP), (MAP * MAP, count, width))
        return whole.reshape(MAP * MAP * count, width)

    columns = patches(images)
    own_columns = lax.dynamic_slice_in_dim(
        images.reshape(MAP * MAP * count, channels), first_column, width, 1
    )

    hidden_one = dot(columns, kernel_one, ((1,), (1,)))
    normal_one, scale_one = moments(hidden_one, rows, links)
    active, slope_one, bend_one = silu_parts(normal_one * gain_one + shift_one)
    active_columns = patches(active.reshape(MAP, MAP, count, width))
    hidden_two = links.scatter_parts(dot(active_columns, kernel_two, ((1,), (1,))), 1)
    normal_two, scale_two = moments(hidden_two, rows, links)
    block, slope_two, bend_two = silu_parts(normal_two * gain_two + shift_two + own_columns)
    pooled = pool(block)
    logits = links.sum_parts(dot(pooled, head, ((1,), (0,))))
    highest = jnp.max(logits, axis=1, keepdims=True)
    powers = jnp.exp(logits - highest)
    total = jnp.sum(powers, axis=1, keepdims=True)
    chances = powers / total
    classes = jnp.arange(logits.shape[1], dtype=jnp.int32)
    chosen = (labels[:, None] == classes[None, :]).astype(jnp.float32)
    cross = highest[:, 0] + jnp.log(total[:, 0]) - jnp.sum(chosen * logits, axis=1)
    loss_sum = links.sum_rows(jnp.sum(valid * cross)[None])[0]
    weights = (valid / label_total)[:, None]
    pull_logits = weights * (chances - chosen)
    grad_head = dot(pooled, pull_logits, ((0,), (0,)))
    pull_block = spread(dot(pull_logits, head, ((1,), (1,))))
    pull_two = pull_block * slope_two
    sums_two = links.sum_rows(
        jnp.stack([jnp.sum(pull_two * normal_two, axis=0), jnp.sum(pull_two, axis=0)])
    )
    centred_two = pull_two - sums_two[1] / rows - normal_two * (sums_two[0] / rows)
    factor_two = scale_two * gain_two
    pull_hidden_two = links.gather_parts(factor_two * centred_two, 1)
    grad_two = dot(pull_hidden_two, active_columns, ((0,), (0,)))
    pull_active = fold(dot(pull_hidden_two, kernel_two, ((1,), (0,))), count)
    pull_one = pull_active * slope_one
    sums_one = links.sum_rows(
        jnp.stack([jnp.sum(pull_one * normal_one, axis=0), jnp.sum(pull_one, axis=0)])
    )
    centred_one = pull_one - sums_one[1] / rows - normal_one * (sums_one[0] / rows)
    factor_one = scale_one * gain_one
    grad_one = dot(factor_one * centred_one, columns, ((0,), (0,)))

    grad_one = links.sum_rows(grad_one) + decay_one * kernel_one
    grad_two = links.sum_rows(grad_two) + decay_two * kernel_two
    grad_head = links.sum_rows(grad_head)
    grad_norm = jnp.concatenate([sums_one, sums_two])

    def product(vector):
        move_one, move_two, move_norm, move_head = vector
        tan_hidden = dot(columns, move_one, ((1,), (1,)))
        tan_normal_one, tan_scale_one = moments_tangent(
            normal_one, scale_one, tan_hidden, rows, links
        )
        tan_inner = move_norm[0] * normal_one + gain_one * tan_normal_one + move_norm[1]
        tan_active = slope_one * tan_inner
        tan_columns = patches(tan_active.reshape(MAP, MAP, count, width))
        tan_hidden = links.scatter_parts(
            dot(tan_columns, kernel_two, ((1,), (1,))) + dot(active_columns, move_two, ((1,), (1,))),
            1,
        )
        tan_normal_two, tan_scale_two = moments_tangent(
            normal_two, scale_two, tan_hidden, rows, links
        )
        tan_outer = move_norm[2] * normal_two + gain_two * tan_normal_two + move_norm[3]
        tan_pooled = pool(slope_two * tan_outer)
        tan_logits = links.sum_parts(
            dot(tan_pooled, head, ((1,), (0,))) + dot(pooled, move_head, ((1,), (0,)))
        )
        tan_chances = chances * (tan_logits - jnp.sum(chances * tan_logits, axis=1, keepdims=True))
        tan_pull = weights * tan_chances
        out_head = dot(tan_pooled, pull_logits, ((0,), (0,))) + dot(pooled, tan_pull, ((0,), (0,)))
        tan_block = spread(
            dot(tan_pull, head, ((1,), (1,))) + dot(pull_logits, move_head, ((1,), (1,)))
        )
        tan_two = tan_block * slope_two + pull_block * bend_two * tan_outer
        tan_sums_two = links.sum_rows(
            jnp.stack(
                [
                    jnp.sum(tan_two * normal_two + pull_two * tan_normal_two, axis=0),
                    jnp.sum(tan_two, axis=0),
                ]
            )
        )
        tan_factor = tan_scale_two * gain_two + scale_two * move_norm[2]
        tan_hidden = tan_factor * centred_two + factor_two * (
            tan_two
            - tan_sums_two[1] / rows
            - tan_normal_two * (sums_two[0] / rows)
            - normal_two * (tan_sums_two[0] / rows)
        )
        tan_hidden = links.gather_parts(tan_hidden, 1)
        out_two = dot(tan_hidden, active_columns, ((0,), (0,))) + dot(
            pull_hidden_two, tan_columns, ((0,), (0,))
        )
        tan_pull_active = fold(
            dot(tan_hidden, kernel_two, ((1,), (0,))) + dot(pull_hidden_two, move_two, ((1,), (0,))),
            count,
        )
        tan_one = tan_pull_active * slope_one + pull_active * bend_one * tan_inner
        tan_sums_one = links.sum_rows(
            jnp.stack(
                [
                    jnp.sum(tan_one * normal_one + pull_one * tan_normal_one, axis=0),
                    jnp.sum(tan_one, axis=0),
                ]
            )
        )
        tan_factor = tan_scale_one * gain_one + scale_one * move_norm[0]
        tan_hidden = tan_factor * centred_one + factor_one * (
            tan_one
            - tan_sums_one[1] / rows
            - tan_normal_one * (sums_one[0] / rows)
            - normal_one * (tan_sums_one[0] / rows)
        )
        out_one = dot(tan_hidden, columns, ((0,), (0,)))
        return (
            links.sum_rows(out_one) + decay_one * move_one,
            links.sum_rows(out_two) + decay_two * move_two,
            jnp.concatenate([tan_sums_one, tan_sums_two]),
            links.sum_rows(out_head),
        )

    if links.members * links.copies == 8 and links.parts == 4:
        series = neumann_fused(
            links,
            rows,
            images=images.reshape(MAP * MAP, count, channels),
            kernel_two=kernel_two,
            decay=(decay_one, decay_two),
            vector=(grad_one, grad_two, grad_norm, grad_head),
            head=head,
            active=active,
            pull_hidden_two=pull_hidden_two,
            maps=(
                normal_one,
                slope_one,
                pull_active * bend_one,
                pull_one,
                centred_one,
                normal_two,
                slope_two,
                pull_block * bend_two,
                pull_two,
                centred_two,
            ),
            small=(pooled, chances, jnp.broadcast_to(weights, chances.shape), pull_logits),
            channel=jnp.stack(
                [
                    scale_one,
                    gain_one,
                    scale_two,
                    gain_two,
                    sums_one[0] / rows,
                    sums_one[1] / rows,
                    sums_two[0] / rows,
                    sums_two[1] / rows,
                ]
            ),
        )
    else:
        vector = (grad_one, grad_two, grad_norm, grad_head)
        series_one, series_two = grad_one, grad_two
        for turn in range(NEUMANN):
            change = product(vector)
            vector = tuple(
                previous - neumann_rate * moved for previous, moved in zip(vector, change)
            )
            series_one, series_two = series_one + vector[0], series_two + vector[1]
        series = jnp.stack([links.own_rows(series_one), links.to_outer(series_two)])

    hyper_gradient = -neumann_rate * conv_weights * series
    grads = jnp.stack([links.own_rows(grad_one), links.to_outer(grad_two)])
    conv_new, conv_one, conv_two = adamw(conv_weights, grads, conv_first, conv_second, 0.015)
    norm_new, norm_one, norm_two = adamw(
        norm_params, links.own_rows(grad_norm, 1), norm_first, norm_second, 0.3
    )
    head_new, head_one, head_two = adamw(
        head_weights, links.own_rows(grad_head), head_first, head_second, 0.13
    )
    return (
        loss_sum,
        label_total,
        conv_new,
        conv_one,
        conv_two,
        norm_new,
        norm_one,
        norm_two,
        head_new,
        head_one,
        head_two,
        hyper_gradient,
    )


def solution(mesh):
    images = P(("shard", "dp"))
    rows = P(None, "shard")
    head = P("shard")
    in_specs = (images,) * 6 + (rows, rows, head, rows, rows, rows, rows, rows, head, head)
    out_specs = (P(), P()) + (rows,) * 6 + (head,) * 3 + (rows,)
    return jax.shard_map(shards, mesh=mesh, in_specs=in_specs, out_specs=out_specs, check_vma=False)
```

```python
import functools

import jax
import jax.numpy as jnp
from jax import lax
from jax.experimental import pallas as pl
from jax.experimental.pallas import tpu as pltpu
from jax.sharding import PartitionSpec as P

MAP = 4
NEUMANN = 3
STEP = 5
TAPS = 9

norm_eps = 1e-05
neumann_rate = 10.0
beta_first = 0.5
beta_second = 0.5
adam_eps = 1e-08
decoupled = 0.01
HIGH = lax.Precision.HIGH


def crop_image(single, offsets, flipped):
    window = lax.dynamic_slice(
        single, (offsets[0], offsets[1], jnp.int32(0)), (MAP, MAP, single.shape[2])
    )
    return jnp.where(flipped == 1, window[:, ::-1, :], window)


def patches(maps):
    count, width = maps.shape[2:]
    padded = jnp.pad(maps, ((1, 1), (1, 1), (0, 0), (0, 0)))
    taps = [padded[dy : dy + MAP, dx : dx + MAP] for dy in range(3) for dx in range(3)]
    return jnp.concatenate(taps, axis=3).reshape(MAP * MAP * count, TAPS * width)


def fold(columns, count):
    width = columns.shape[1] // TAPS
    whole = columns.reshape(MAP, MAP, count, TAPS, width)
    padded = jnp.pad(whole, ((1, 1), (1, 1), (0, 0), (0, 0), (0, 0)))
    total = 0.0
    for dy in range(3):
        for dx in range(3):
            total = total + padded[2 - dy : 2 - dy + MAP, 2 - dx : 2 - dx + MAP, :, dy * 3 + dx]
    return total.reshape(MAP * MAP * count, width)


def dot(left, right, dims):
    return lax.dot_general(
        left, right, ((dims[0], dims[1]), ((), ())), precision=HIGH, preferred_element_type=jnp.float32
    )


MESH_ID = pl.DeviceIdType.MESH
LANES = 128
GROUPS = 3


def halves(value):
    high = value.astype(jnp.bfloat16)
    return high, (value - high.astype(jnp.float32)).astype(jnp.bfloat16)


def mul(left, right, dims=((1,), (0,))):
    return lax.dot_general(left, right, (dims, ((), ())), preferred_element_type=jnp.float32)


def mul_exact(left, right, dims=((1,), (0,))):
    return lax.dot_general(
        left,
        right,
        (dims, ((), ())),
        precision=lax.Precision.HIGHEST,
        preferred_element_type=jnp.float32,
    )


def silu_pieces(value):
    gate = 1.0 / (1.0 + jnp.exp(-value))
    slope = gate * (1.0 - gate)
    return value * gate, gate + value * slope, slope * (2.0 + value * (1.0 - 2.0 * gate))


def step_kernel(
    rows,
    members,
    copies,
    classes,
    x_in,
    k1_in,
    k2_in,
    d2_in,
    d1,
    pair_in,
    label_in,
    series_one,
    gathered_two,
    grad_one,
    grad_two,
    grad_small,
    series_two,
    grad_source,
    d2,
    v1,
    v2,
    v1_hi,
    v1_lo,
    v2_hi,
    v2_lo,
    k_hi,
    k_lo,
    x_box,
    x_row,
    x_both,
    x_own,
    a_both,
    b_both,
    g_left,
    g_turned,
    t_left,
    t_turned,
    slots,
    partial,
    from_low,
    from_high,
    flow,
    n1,
    s1,
    pb1,
    pull1,
    c1,
    n2,
    s2,
    pb2,
    pull2,
    c2,
    nt1,
    in1,
    nt2,
    in2,
    fold_sum,
    sum_one,
    sum_two,
    half_one,
    half_two,
    piece_one,
    piece_two,
    stats_box,
    stats_own,
    logit_box,
    logit_own,
    pair_box,
    label_box,
    turned,
    channel,
    move_norm,
    move_head,
    head,
    pooled,
    chances,
    weights,
    pull_logits,
    load_sem,
    k1_load,
    k1_send,
    k1_recv,
    first_send,
    first_recv,
    label_send,
    label_recv,
    x_send,
    x_recv,
    stats_send,
    stats_recv,
    logit_send,
    logit_recv,
    up_send,
    up_recv,
    down_send,
    down_recv,
    ring_send,
    ring_recv,
    pair_send,
    pair_recv,
    plane_send,
    plane_recv,
    back_send,
    back_recv,
    swap_send,
    swap_recv,
    grad_send,
    grad_recv,
    last_send,
    last_recv,
):
    shard = lax.axis_index("shard")
    copy = lax.axis_index("dp")
    part = shard // members
    member = shard % members
    me = member * copies + copy
    place, core = me // 2, me % 2
    last = 3
    count = flow.shape[1]
    own_count = x_in.shape[1]
    inverse = 1.0 / rows
    zero = jnp.zeros((count, LANES), jnp.float32)

    def row_peer(other):
        return (part * members + other // copies, other % copies)

    def part_peer(other):
        return (other * members + member, copy)

    def owner(other):
        return (me, other)

    def holder(other):
        return (other * members + shard // copies, shard % copies)

    owns = shard == me

    def remote(source, target, send, recv, device):
        return pltpu.make_async_remote_copy(
            src_ref=source,
            dst_ref=target,
            send_sem=send,
            recv_sem=recv,
            device_id=device,
            device_id_type=MESH_ID,
        )

    def greet(device):
        pl.semaphore_signal(barrier, inc=1, device_id=device, device_id_type=MESH_ID)

    barrier = pltpu.get_barrier_semaphore()
    for step in range(1, 8):
        greet(row_peer(me ^ step))
    for step in range(1, 4):
        greet(part_peer(part ^ step))
    for step in range(4):

        @pl.when(jnp.logical_not(owns & (step == copy)))
        def _():
            greet(owner(step))

        @pl.when(jnp.logical_not(owns & (step == part)))
        def _():
            greet(holder(step))

    own_places = pl.ds(pl.multiple_of(member * 2, 2), 2)

    def tap_lanes(tap, width):
        return pl.ds(pl.multiple_of(tap * width, width), width)

    channels = x_in.shape[2]
    x_load = pltpu.make_async_copy(x_in, x_box.at[part], load_sem.at[0])
    x_load.start()
    k1_loads = [
        pltpu.make_async_copy(
            k1_in.at[:, :, :, pl.ds(tap * channels, channels)], v1.at[tap, own_places], k1_load.at[tap]
        )
        for tap in range(TAPS)
    ]
    for load in k1_loads:
        load.start()
    stats_own[...] = jnp.zeros_like(stats_own)
    channel[...] = jnp.zeros_like(channel)
    x_both[...] = jnp.zeros_like(x_both)
    a_both[...] = jnp.zeros_like(a_both)
    b_both[...] = jnp.zeros_like(b_both)
    label_box[0] = label_in[...]
    x_load.wait()
    pl.semaphore_wait(barrier, 18 - 2 * owns.astype(jnp.int32))

    def ring_move(box, send, recv, block, step, way):
        return remote(
            box.at[block],
            box.at[block],
            send.at[0 if way > 0 else 1, step],
            recv.at[block],
            part_peer(part + way),
        )

    def ring_start(box, send, recv):
        @pl.when(part < last)
        def _():
            ring_move(box, send, recv, part, 0, 1).start()

        @pl.when(part > 0)
        def _():
            ring_move(box, send, recv, part, 0, -1).start()

    def ring_step(box, send, recv, step, use=None):
        @pl.when(part >= step)
        def _():
            ring_move(box, send, recv, part - step, step, -1).wait_recv()

            @pl.when(part < last)
            def _():
                ring_move(box, send, recv, part - step, step, 1).start()

        @pl.when(part + step <= last)
        def _():
            ring_move(box, send, recv, part + step, step, 1).wait_recv()

            @pl.when(part > 0)
            def _():
                ring_move(box, send, recv, part + step, step, -1).start()

        if use is not None:

            @pl.when(part >= step)
            def _():
                use(part - step)

            @pl.when(part + step <= last)
            def _():
                use(part + step)

    def ring_end(box, send, recv):
        for step in range(0, 3):

            @pl.when((part >= step) & (part < last))
            def _():
                ring_move(box, send, recv, part - step, step, 1).wait_send()

            @pl.when((part + step <= last) & (part > 0))
            def _():
                ring_move(box, send, recv, part + step, step, -1).wait_send()

    ring_start(x_box, x_send, x_recv)
    partner = row_peer(me ^ copies)
    k1_moves = [
        remote(
            k1_in.at[:, :, :, pl.ds(tap * channels, channels)],
            v1.at[tap, own_places],
            k1_send.at[tap],
            k1_recv.at[tap],
            partner,
        )
        for tap in range(TAPS)
    ]
    for move in k1_moves:
        move.start()

    target = holder(copy)
    own_piece = owns & (part == copy)
    k2_move = remote(k2_in, v2.at[shard], first_send.at[0], first_recv.at[0], target)
    d2_move = remote(d2_in, d2, first_send.at[1], first_recv.at[1], target)
    k2_here = pltpu.make_async_copy(k2_in, v2.at[shard], load_sem.at[1])
    d2_here = pltpu.make_async_copy(d2_in, d2, load_sem.at[2])

    @pl.when(own_piece)
    def _():
        k2_here.start()
        d2_here.start()

    @pl.when(jnp.logical_not(own_piece))
    def _():
        k2_move.start()
        d2_move.start()

    pair_move = remote(pair_in, pair_box, first_send.at[2], first_recv.at[2], partner)
    pair_move.start()
    label_moves = [
        remote(
            label_in,
            label_box.at[step],
            label_send.at[step],
            label_recv.at[step],
            part_peer(part ^ step),
        )
        for step in range(1, 4)
    ]
    for move in label_moves:
        move.start()

    pair = row_peer(me ^ 1)

    def piece_of(which, other):
        if which < GROUPS:
            return v1.at[pl.ds(which * 3, 3), other // 2, other % 2]
        return v2.at[other]

    def to_plane(which, step):
        piece = piece_of(which, me)
        return remote(
            piece, piece, back_send.at[which, step], back_recv.at[which, step], row_peer(me ^ (2 * step))
        )

    def to_pair(which, step):
        piece = piece_of(which, me ^ (2 * step))
        return remote(piece, piece, swap_send.at[which, step], swap_recv.at[which, step], pair)

    def back_start(which):
        for step in range(1, 4):
            to_plane(which, step).start()
        to_pair(which, 0).start()

    def back_forward(which):
        for step in range(1, 4):
            piece = piece_of(which, me ^ (2 * step))
            remote(
                piece, piece, back_send.at[which, step], back_recv.at[which, step], pair
            ).wait_recv()
            to_pair(which, step).start()

    def back_arrived(which):
        for step in range(0, 4):
            piece = piece_of(which, me ^ 1 ^ (2 * step))
            remote(
                piece, piece, swap_send.at[which, step], swap_recv.at[which, step], pair
            ).wait_recv()

    def back_end(which):
        for step in range(1, 4):
            to_plane(which, step).wait_send()
        for step in range(0, 4):
            to_pair(which, step).wait_send()

    @pl.when(own_piece)
    def _():
        k2_here.wait()
        d2_here.wait()

    @pl.when(jnp.logical_not(own_piece))
    def _():
        k2_move.wait_send()
        d2_move.wait_send()
        remote(k2_in, v2.at[me], first_send.at[0], first_recv.at[0], target).wait_recv()
        d2_move.wait_recv()

    back_start(GROUPS)

    pair_move.wait()
    small = pair_in[...] + pair_box[...]
    move_norm[...] = small[0:8]
    head[...] = jnp.zeros_like(head)
    move_head[...] = jnp.zeros_like(move_head)
    head[0:16] = small[8:24]
    for move in label_moves:
        move.wait()
    tags = label_box[0] + label_box[1] + label_box[2] + label_box[3]
    chosen, valid = tags[:count], tags[count:]

    def each_cell(body, init=None):
        return lax.fori_loop(0, 16, body, init)

    def window(ref, tap, lanes=slice(None)):
        seen = ref[pl.ds(tap // 3, 4), pl.ds(tap % 3, 4), :, lanes]
        return seen.reshape(16 * seen.shape[2], seen.shape[3])

    def row(ref, index):
        return ref[index : index + 1, :]

    def put_sums(site, first, second):
        stats_own[site, 0:1, :] = jnp.sum(first, axis=0, keepdims=True)
        stats_own[site, 1:2, :] = jnp.sum(second, axis=0, keepdims=True)

    def sum_start(site, size):
        moves = []
        for step in range(1, 8):
            move = remote(
                stats_own.at[site, pl.ds(0, size)],
                stats_box.at[site, step, pl.ds(0, size)],
                stats_send.at[site, step],
                stats_recv.at[site, step],
                row_peer(me ^ step),
            )
            move.start()
            moves.append(move)
        stats_box[site, 0, pl.ds(0, size)] = stats_own[site, pl.ds(0, size)]
        return moves

    def sum_end(site, size, moves):
        for move in moves:
            move.wait()
        total = stats_box[site, me, pl.ds(0, size)]
        for other in range(1, 8):
            total = total + stats_box[site, other ^ me, pl.ds(0, size)]
        return total

    def sum_parts(value):
        logit_own[...] = value
        moves = []
        for step in range(1, 4):
            move = remote(
                logit_own,
                logit_box.at[step],
                logit_send.at[step],
                logit_recv.at[step],
                part_peer(part ^ step),
            )
            move.start()
            moves.append(move)
        logit_box[0] = value
        for move in moves:
            move.wait()
        total = logit_box[part]
        for other in range(1, 4):
            total = total + logit_box[other ^ part]
        return total

    def split_one(tap, _):
        for place_of in range(4):
            for core_of in range(2):
                start = (place_of * 2 + core_of) * 16
                v1_hi[tap, start : start + 16], v1_lo[tap, start : start + 16] = halves(
                    v1[tap, place_of, core_of]
                )

    def split_two(high, low):
        def body(block, _):
            at = pl.ds(pl.multiple_of(block * 64, 64), 64)
            high[at], low[at] = halves(v2[block])

        lax.fori_loop(0, 8, body, None)

    def tap_forward(tap, _):
        weight = jnp.concatenate([v1_hi[tap], v1_lo[tap]], axis=0)
        weight = jnp.concatenate([weight, weight], axis=1)
        out = mul(window(x_both, tap), weight, ((1,), (1,)))
        flow[...] += (out[:, :LANES] + out[:, LANES:]).reshape(flow.shape)

    def part_of_second(maps, high, low, half):
        at = pl.ds(pl.multiple_of(half * 256, 256), 256)

        def body(tap, _):
            lanes = tap_lanes(tap, LANES)
            left = window(maps, tap)
            weight_hi, weight_lo = high[at, lanes], low[at, lanes]
            out = mul(
                jnp.concatenate([left, left], axis=1),
                jnp.concatenate([weight_hi, weight_hi, weight_lo, weight_lo], axis=1),
                ((1,), (1,)),
            )
            partial[half * 2] += out[:, :LANES].reshape(flow.shape)
            partial[half * 2 + 1] += out[:, LANES:].reshape(flow.shape)

        lax.fori_loop(0, TAPS, body, None)

    def up(block):
        return remote(
            partial.at[block], from_low.at[block], up_send.at[block], up_recv.at[block], part_peer(part + 1)
        )

    def down(block):
        return remote(
            partial.at[block],
            from_high.at[block],
            down_send.at[block],
            down_recv.at[block],
            part_peer(part - 1),
        )

    def scatter(maps, high, low, aside):
        near = jnp.where(part < 2, 1, 0)
        part_of_second(maps, high, low, near)

        @pl.when(part == 0)
        def _():
            up(3).start()
            up(2).start()

        @pl.when(part == last)
        def _():
            down(0).start()
            down(1).start()

        part_of_second(maps, high, low, 1 - near)
        for block in (3, 2, 1):
            goal = last - block

            @pl.when((part < block) & (part > 0))
            def _():
                up(block).wait_recv()
                partial[block] += from_low[block]
                up(block).start()

            @pl.when((part > goal) & (part < last))
            def _():
                down(goal).wait_recv()
                partial[goal] += from_high[goal]
                down(goal).start()

            if block == 1:

                @pl.when(part == 0)
                def _():
                    up(1).start()

                @pl.when(part == last)
                def _():
                    down(2).start()

            aside(3 - block)
        aside(3)
        for block in range(4):

            @pl.when(part == block)
            def _():
                total = partial[block]
                if block > 0:
                    up(block).wait_recv()
                    total = total + from_low[block]
                if block < last:
                    down(block).wait_recv()
                    total = total + from_high[block]
                flow[...] = total

        for block in (3, 2, 1):
            goal = last - block

            @pl.when(part < block)
            def _():
                up(block).wait_send()

            @pl.when(part > goal)
            def _():
                down(goal).wait_send()

    def turn_block(block, left, turned_block):
        value = slots[block].reshape(16 * count, LANES)
        left[...] = jnp.concatenate(halves(value), axis=1)
        turned_block[...] = jnp.concatenate(halves(value.T), axis=0)

    def use_block(block, left, turned_block, high, low, maps):
        at = pl.ds(pl.multiple_of(block * LANES, LANES), LANES)

        def body(tap, _):
            lanes = tap_lanes(tap, LANES)
            weight = jnp.concatenate([high[at, lanes], low[at, lanes]], axis=1)
            out = mul(left[...], jnp.concatenate([weight, weight], axis=0))
            out = out[:, :LANES] + out[:, LANES:]
            fold_sum[pl.ds(tap // 3, 4), pl.ds(tap % 3, 4)] += out.reshape(4, 4, count, LANES)
            out = mul(turned_block[...], window(maps, tap))
            out = (out[:LANES, :LANES] + out[LANES:, :LANES]) + (
                out[:LANES, LANES:] + out[LANES:, LANES:]
            )
            sum_two[block, :, :, lanes] += out.reshape(2, 64, LANES)

        lax.fori_loop(0, TAPS, body, None)

    def gather_and_use(block_of):
        ring_start(slots, ring_send, ring_recv)
        block_of(part)
        for step in range(1, 4):
            ring_step(slots, ring_send, ring_recv, step, block_of)
        ring_end(slots, ring_send, ring_recv)

    def pair_two():
        return remote(sum_two.at[:, 1 - core], half_two, pair_send.at[GROUPS], pair_recv.at[GROUPS], pair)

    def pair_one(group):
        return remote(
            sum_one.at[pl.ds(group * 3, 3), :, 1 - core],
            half_one.at[pl.ds(group * 3, 3)],
            pair_send.at[group],
            pair_recv.at[group],
            pair,
        )

    def plane_two(step):
        other = place ^ step
        return remote(
            half_two.at[other],
            piece_two.at[step],
            plane_send.at[GROUPS, step],
            plane_recv.at[GROUPS, step],
            row_peer(other * 2 + core),
        )

    def plane_one(group, step):
        other = place ^ step
        return remote(
            half_one.at[pl.ds(group * 3, 3), other],
            piece_one.at[step, pl.ds(group * 3, 3)],
            plane_send.at[group, step],
            plane_recv.at[group, step],
            row_peer(other * 2 + core),
        )

    def finish_gradients(new_of):
        pair_two().wait()
        for place_of in range(4):
            half_two[place_of] += sum_two[place_of, core]
        for step in range(1, 4):
            plane_two(step).start()

        def tap_weight(tap, _):
            out = mul(turned[...], window(x_both, tap, slice(0, channels)))
            out = out + mul(turned[...], window(x_both, tap, slice(channels, 2 * channels)))
            sum_one[tap] = (out[:LANES] + out[LANES:]).reshape(sum_one.shape[1:])

        def plane_go(group):
            pair_one(group).wait()

            def body(tap, _):
                for place_of in range(4):
                    half_one[tap, place_of] += sum_one[tap, place_of, core]

            lax.fori_loop(group * 3, group * 3 + 3, body, None)
            for step in range(1, 4):
                plane_one(group, step).start()

        for group in range(GROUPS):
            lax.fori_loop(group * 3, group * 3 + 3, tap_weight, None)
            pair_one(group).start()
            if group > 0:
                plane_go(group - 1)
        plane_go(GROUPS - 1)
        for step in range(1, 4):
            plane_two(step).wait()
        change = half_two[place] + piece_two[1] + piece_two[2] + piece_two[3]
        new = new_of(v2[me], change, d2[...])
        v2[me] = new
        series_two[...] += new
        return new

    def step_group(group, new_of):
        for step in range(1, 4):
            plane_one(group, step).wait()

        def body(tap, _):
            change = (
                half_one[tap, place] + piece_one[1, tap] + piece_one[2, tap] + piece_one[3, tap]
            )
            new = new_of(v1[tap, place, core], change, d1[tap])
            v1[tap, place, core] = new
            series_one[tap] += new

        lax.fori_loop(group * 3, group * 3 + 3, body, None)

    def no_aside(index):
        pass

    for load in k1_loads:
        load.wait()
    for move in k1_moves:
        move.wait()
    lax.fori_loop(0, TAPS, split_one, None)
    for step in range(1, 4):
        ring_step(x_box, x_send, x_recv, step)
    ring_end(x_box, x_send, x_recv)

    def place_images(cell, _):
        for block in range(4):
            x_row[block * own_count : (block + 1) * own_count] = x_box[block, cell]
        high, low = halves(x_row[...])
        x_both[cell // 4 + 1, cell % 4 + 1, :, 0:channels] = high
        x_both[cell // 4 + 1, cell % 4 + 1, :, channels : 2 * channels] = low
        x_own[cell] = x_row[:, pl.ds(pl.multiple_of(part * LANES, LANES), LANES)]

    each_cell(place_images)
    flow[...] = jnp.zeros_like(flow)
    lax.fori_loop(0, TAPS, tap_forward, None)

    def sums_primal(cell, carry):
        value = flow[cell]
        return carry[0] + value, carry[1] + value * value

    put_sums(0, *each_cell(sums_primal, (zero, zero)))
    stats_own[0, 2:3, :] = jnp.sum(valid, axis=0, keepdims=True)
    moves = sum_start(0, 8)
    back_forward(GROUPS)
    back_arrived(GROUPS)
    back_end(GROUPS)
    split_two(k_hi, k_lo)
    partial[...] = jnp.zeros_like(partial)
    total = sum_end(0, 8, moves)
    label_total = total[2:3]
    average = total[0:1] * inverse
    scale = lax.rsqrt(total[1:2] * inverse - average * average + norm_eps)
    gain, shift = row(move_norm, 0), row(move_norm, 1)
    gain2, shift2 = row(move_norm, 2), row(move_norm, 3)

    def first_primal(cell, _):
        normal = (flow[cell] - average) * scale
        value, slope, bend = silu_pieces(normal * gain + shift)
        n1[cell] = normal
        s1[cell] = slope
        pb1[cell] = bend
        a_both[cell // 4 + 1, cell % 4 + 1] = jnp.concatenate(halves(value), axis=1)

    each_cell(first_primal)
    scatter(a_both, k_hi, k_lo, no_aside)
    put_sums(1, *each_cell(sums_primal, (zero, zero)))
    total = sum_end(1, 8, sum_start(1, 8))
    average = total[0:1] * inverse
    scale2 = lax.rsqrt(total[1:2] * inverse - average * average + norm_eps)

    def second_primal(cell, carry):
        normal = (flow[cell] - average) * scale2
        value, slope, bend = silu_pieces(normal * gain2 + shift2 + x_own[cell])
        n2[cell] = normal
        s2[cell] = slope
        pb2[cell] = bend
        return carry + value

    pooled[...] = each_cell(second_primal, zero) * (1.0 / 16.0)
    logits = sum_parts(mul_exact(pooled[...], head[...], ((1,), (1,))))
    real = lax.broadcasted_iota(jnp.int32, logits.shape, 1) < classes
    highest = jnp.max(jnp.where(real, logits, -jnp.inf), axis=1, keepdims=True)
    powers = jnp.where(real, jnp.exp(logits - highest), 0.0)
    sum_powers = jnp.sum(powers, axis=1, keepdims=True)
    chances[...] = powers / sum_powers
    target_logit = jnp.sum(chosen * logits, axis=1, keepdims=True)
    cross = (highest + jnp.log(sum_powers) - target_logit) * valid
    weights[...] = valid / label_total
    pull_logits[...] = weights[...] * (chances[...] - chosen)
    out_head = mul_exact(pull_logits[...], pooled[...], ((0,), (0,)))
    pull_block = mul_exact(pull_logits[...], head[...]) * (1.0 / 16.0)

    def back_two_primal(cell, carry):
        pull = pull_block * s2[cell]
        pull2[cell] = pull
        pb2[cell] = pull_block * pb2[cell]
        return carry[0] + pull * n2[cell], carry[1] + pull

    put_sums(2, *each_cell(back_two_primal, (zero, zero)))
    stats_own[2, 2:3, :] = jnp.sum(cross, axis=0, keepdims=True)
    stats_own[2, 8:24, :] = out_head[0:16]
    total = sum_end(2, 24, sum_start(2, 24))
    grad_small[0:1, :] = total[2:3]
    grad_small[1:2, :] = label_total
    grad_small[2:8, :] = jnp.zeros((6, LANES), jnp.float32)
    grad_small[16:32, :] = total[8:24]
    out_gain2, out_shift2 = total[0:1], total[1:2]
    factor2 = scale2 * gain2

    def pull_two_primal(cell, _):
        centred = pull2[cell] - out_shift2 * inverse - n2[cell] * (out_gain2 * inverse)
        c2[cell] = centred
        slots[part, cell] = factor2 * centred

    each_cell(pull_two_primal)
    fold_sum[...] = jnp.zeros_like(fold_sum)
    sum_two[...] = jnp.zeros_like(sum_two)

    def primal_block(block):
        turn_block(block, g_left.at[block], g_turned.at[block])
        use_block(block, g_left.at[block], g_turned.at[block], k_hi, k_lo, a_both)

    gather_and_use(primal_block)
    pair_two().start()

    def back_one_primal(cell, carry):
        seen = fold_sum[cell // 4 + 1, cell % 4 + 1]
        pull = seen * s1[cell]
        pull1[cell] = pull
        pb1[cell] = seen * pb1[cell]
        return carry[0] + pull * n1[cell], carry[1] + pull

    put_sums(3, *each_cell(back_one_primal, (zero, zero)))
    total = sum_end(3, 8, sum_start(3, 8))
    out_gain, out_shift = total[0:1], total[1:2]
    factor = scale * gain

    def pull_one_primal(cell, _):
        centred = pull1[cell] - out_shift * inverse - n1[cell] * (out_gain * inverse)
        c1[cell] = centred
        flow[cell] = factor * centred

    each_cell(pull_one_primal)
    turned[...] = jnp.concatenate(halves(flow[...].reshape(16 * count, LANES).T), axis=0)

    channel[0:1, :] = scale
    channel[1:2, :] = gain
    channel[2:3, :] = scale2
    channel[3:4, :] = gain2
    channel[4:5, :] = out_gain * inverse
    channel[5:6, :] = out_gain2 * inverse
    move_norm[0:1, :] = out_gain
    move_norm[1:2, :] = out_shift
    move_norm[2:3, :] = out_gain2
    move_norm[3:4, :] = out_shift2
    grad_small[8:16, :] = move_norm[...]
    move_head[0:16] = grad_small[16:32, :]

    series_one[...] = jnp.zeros_like(series_one)
    series_two[...] = jnp.zeros_like(series_two)

    def first_vector(old, change, decay):
        return change + decay * old

    def next_vector(old, change, decay):
        return old - neumann_rate * (change + decay * old)

    grad_source[...] = finish_gradients(first_vector)

    def grad_move(other):
        return remote(
            grad_source, grad_two.at[part], grad_send.at[other], grad_recv.at[part], owner(other)
        )

    for other in range(4):

        @pl.when(jnp.logical_not(owns & (copy == other)))
        def _():
            grad_move(other).start()

    @pl.when(owns)
    def _():
        grad_two[part] = grad_source[...]

    for group in range(GROUPS):
        step_group(group, first_vector)
        back_start(group)

    def turn_body(turn, nothing):
        for group in range(GROUPS):
            back_forward(group)
        back_start(GROUPS)
        flow[...] = jnp.zeros_like(flow)
        for group in range(GROUPS):
            back_arrived(group)
            lax.fori_loop(group * 3, group * 3 + 3, split_one, None)
            lax.fori_loop(group * 3, group * 3 + 3, tap_forward, None)
        for group in range(GROUPS):
            back_end(group)

        @pl.when(turn == 0)
        def _():
            grad_one[...] = v1[:, own_places]

        def sums_forward(normal):
            def body(cell, carry):
                value = flow[cell]
                return carry[0] + value, carry[1] + value * normal[cell]

            return each_cell(body, (zero, zero))

        put_sums(0, *sums_forward(n1))
        moves = sum_start(0, 8)
        back_forward(GROUPS)
        partial[...] = jnp.zeros_like(partial)
        fold_sum[...] = jnp.zeros_like(fold_sum)
        sum_two[...] = jnp.zeros_like(sum_two)
        back_arrived(GROUPS)
        back_end(GROUPS)
        split_two(v2_hi, v2_lo)
        part_of_second(a_both, v2_hi, v2_lo, 0)
        part_of_second(a_both, v2_hi, v2_lo, 1)
        total = sum_end(0, 8, moves) * inverse
        average, cross = total[0:1], total[1:2]
        scale, gain = row(channel, 0), row(channel, 1)
        tan_scale_one = -scale * scale * cross
        move_gain, move_shift = row(move_norm, 0), row(move_norm, 1)

        def forward_one(cell, _):
            normal = n1[cell]
            tangent = scale * (flow[cell] - average - normal * cross)
            inner = move_gain * normal + gain * tangent + move_shift
            nt1[cell] = tangent
            in1[cell] = inner
            b_both[cell // 4 + 1, cell % 4 + 1] = jnp.concatenate(halves(s1[cell] * inner), axis=1)

        each_cell(forward_one)

        def aside(block):
            use_block(block, g_left.at[block], g_turned.at[block], v2_hi, v2_lo, b_both)

        scatter(b_both, k_hi, k_lo, aside)

        put_sums(1, *sums_forward(n2))
        total = sum_end(1, 8, sum_start(1, 8)) * inverse
        average2, cross2 = total[0:1], total[1:2]
        scale2, gain2 = row(channel, 2), row(channel, 3)
        tan_scale_two = -scale2 * scale2 * cross2
        move_gain2, move_shift2 = row(move_norm, 2), row(move_norm, 3)

        def forward_two(cell, carry):
            normal = n2[cell]
            tangent = scale2 * (flow[cell] - average2 - normal * cross2)
            inner = move_gain2 * normal + gain2 * tangent + move_shift2
            nt2[cell] = tangent
            in2[cell] = inner
            return carry + s2[cell] * inner

        tan_pooled = each_cell(forward_two, zero) * (1.0 / 16.0)
        tan_logits = sum_parts(
            mul_exact(tan_pooled, head[...], ((1,), (1,)))
            + mul_exact(pooled[...], move_head[...], ((1,), (1,)))
        )
        chance = chances[...]
        tan_pull = (
            weights[...]
            * chance
            * (tan_logits - jnp.sum(chance * tan_logits, axis=1, keepdims=True))
        )
        out_head = mul_exact(pull_logits[...], tan_pooled, ((0,), (0,))) + mul_exact(
            tan_pull, pooled[...], ((0,), (0,))
        )
        tan_block = (
            mul_exact(tan_pull, head[...]) + mul_exact(pull_logits[...], move_head[...])
        ) * (1.0 / 16.0)

        def back_two(cell, carry):
            tangent = tan_block * s2[cell] + pb2[cell] * in2[cell]
            flow[cell] = tangent
            return (
                carry[0] + tangent * n2[cell] + pull2[cell] * nt2[cell],
                carry[1] + tangent,
            )

        put_sums(2, *each_cell(back_two, (zero, zero)))
        stats_own[2, 8:24, :] = out_head[0:16]
        total = sum_end(2, 24, sum_start(2, 24))
        out_gain2, out_shift2 = total[0:1], total[1:2]
        move_head[0:16] = move_head[0:16] - neumann_rate * total[8:24]
        factor2 = scale2 * gain2
        tan_factor2 = tan_scale_two * gain2 + scale2 * move_gain2

        def pull_two_body(cell, _):
            slots[part, cell] = tan_factor2 * c2[cell] + factor2 * (
                flow[cell]
                - out_shift2 * inverse
                - nt2[cell] * row(channel, 5)
                - n2[cell] * (out_gain2 * inverse)
            )

        each_cell(pull_two_body)

        def turn_of_block(block):
            turn_block(block, t_left, t_turned)
            use_block(block, t_left, t_turned, k_hi, k_lo, a_both)

        gather_and_use(turn_of_block)
        pair_two().start()

        def back_one(cell, carry):
            pull = fold_sum[cell // 4 + 1, cell % 4 + 1]
            tangent = pull * s1[cell] + pb1[cell] * in1[cell]
            flow[cell] = tangent
            return (
                carry[0] + tangent * n1[cell] + pull1[cell] * nt1[cell],
                carry[1] + tangent,
            )

        put_sums(3, *each_cell(back_one, (zero, zero)))
        total = sum_end(3, 8, sum_start(3, 8))
        out_gain, out_shift = total[0:1], total[1:2]
        factor = scale * gain
        tan_factor = tan_scale_one * gain + scale * move_gain

        def pull_one_body(cell, _):
            flow[cell] = tan_factor * c1[cell] + factor * (
                flow[cell]
                - out_shift * inverse
                - nt1[cell] * row(channel, 4)
                - n1[cell] * (out_gain * inverse)
            )

        each_cell(pull_one_body)
        turned[...] = jnp.concatenate(halves(flow[...].reshape(16 * count, LANES).T), axis=0)
        move_norm[0:1, :] = move_gain - neumann_rate * out_gain
        move_norm[1:2, :] = move_shift - neumann_rate * out_shift
        move_norm[2:3, :] = move_gain2 - neumann_rate * out_gain2
        move_norm[3:4, :] = move_shift2 - neumann_rate * out_shift2
        finish_gradients(next_vector)
        for group in range(GROUPS):
            step_group(group, next_vector)

            @pl.when(turn < NEUMANN - 1)
            def _():
                back_start(group)

    lax.fori_loop(0, NEUMANN, turn_body, None)

    def last_move(other):
        return remote(
            series_two, gathered_two.at[part], last_send.at[other], last_recv.at[part], owner(other)
        )

    for other in range(4):

        @pl.when(jnp.logical_not(owns & (copy == other)))
        def _():
            last_move(other).start()

    @pl.when(owns)
    def _():
        gathered_two[part] = series_two[...]

    for other in range(4):

        @pl.when(jnp.logical_not(owns & (copy == other)))
        def _():
            grad_move(other).wait_send()
            last_move(other).wait_send()

        @pl.when(jnp.logical_not(owns & (part == other)))
        def _():
            for box, send, recv in ((grad_two, grad_send, grad_recv), (gathered_two, last_send, last_recv)):
                remote(
                    series_two, box.at[other], send.at[other], recv.at[other], owner(other)
                ).wait_recv()


def step_fused(links, rows, images, conv_weights, decay_rates, norm_params, head_weights, labels, valid):
    own_count, channels = images.shape[2:]
    cells, count = MAP * MAP, own_count * 4
    width, group = channels // 4, 8
    piece, block = width // group, channels // group
    classes = head_weights.shape[1]
    copy = lax.axis_index("dp")
    f32, b16 = jnp.float32, jnp.bfloat16

    def inner(value):
        cut = value.reshape(block, TAPS, 4, width)
        return lax.dynamic_index_in_dim(cut, copy, 2, keepdims=False).reshape(block, TAPS * width)

    d1 = lax.dynamic_slice_in_dim(decay_rates[0], copy * piece, piece, 0)
    d1 = d1.reshape(piece, TAPS, channels).transpose(1, 0, 2)
    small = jnp.zeros((24, width), f32)
    lane = links.member * block
    small = lax.dynamic_update_slice(small, norm_params, (0, lane))
    small = lax.dynamic_update_slice(small, head_weights.T, (8, lane))
    chosen = (labels[:, None] == jnp.arange(LANES, dtype=jnp.int32)[None, :]).astype(f32)
    tags = jnp.zeros((2, count, LANES), f32)
    tags = lax.dynamic_update_slice(
        tags,
        jnp.stack([chosen, jnp.broadcast_to(valid[:, None], chosen.shape)]),
        (0, links.part * own_count, 0),
    )
    operands = (
        images.reshape(cells, own_count, channels),
        conv_weights[0].reshape(2, 2, piece, TAPS * channels),
        inner(conv_weights[1]),
        inner(decay_rates[1]),
        d1,
        small,
        tags.reshape(2 * count, LANES),
    )
    vmem = pl.BlockSpec(memory_space=pltpu.VMEM)
    anywhere = pl.BlockSpec(memory_space=pl.ANY)
    row_map = pltpu.VMEM((cells, count, width), f32)
    four_maps = pltpu.VMEM((4, cells, count, width), f32)
    whole_one = pltpu.VMEM((TAPS, 4, 2, piece, channels), f32)
    inner_piece = pltpu.VMEM((block, TAPS * width), f32)
    inner_half = pltpu.VMEM((4, block, TAPS * width), f32)
    inner_part = pltpu.VMEM((channels, TAPS * width), b16)
    outer_part = pltpu.VMEM((TAPS, width, channels), b16)
    both = pltpu.VMEM((MAP + 2, MAP + 2, count, 2 * width), b16)
    logit = pltpu.VMEM((count, LANES), f32)
    dma = pltpu.SemaphoreType.DMA
    scratch = [
        inner_piece,
        inner_piece,
        inner_piece,
        whole_one,
        pltpu.VMEM((group, block, TAPS * width), f32),
        outer_part,
        outer_part,
        inner_part,
        inner_part,
        inner_part,
        inner_part,
        pltpu.VMEM((4, cells, own_count, channels), f32),
        pltpu.VMEM((count, channels), f32),
        pltpu.VMEM((MAP + 2, MAP + 2, count, 2 * channels), b16),
        row_map,
        both,
        both,
        pltpu.VMEM((4, cells * count, 2 * width), b16),
        pltpu.VMEM((4, 2 * width, cells * count), b16),
        pltpu.VMEM((cells * count, 2 * width), b16),
        pltpu.VMEM((2 * width, cells * count), b16),
        four_maps,
        four_maps,
        four_maps,
        four_maps,
        *[row_map] * 15,
        pltpu.VMEM((MAP + 2, MAP + 2, count, width), f32),
        whole_one,
        pltpu.VMEM((4, 2, block, TAPS * width), f32),
        pltpu.VMEM((TAPS, 4, piece, channels), f32),
        inner_half,
        pltpu.VMEM((4, TAPS, piece, channels), f32),
        inner_half,
        pltpu.VMEM((4, 8, 24, width), f32),
        pltpu.VMEM((4, 24, width), f32),
        pltpu.VMEM((4, count, LANES), f32),
        logit,
        pltpu.VMEM((24, width), f32),
        pltpu.VMEM((4, 2 * count, LANES), f32),
        pltpu.VMEM((2 * width, cells * count), b16),
        pltpu.VMEM((8, width), f32),
        pltpu.VMEM((8, width), f32),
        pltpu.VMEM((LANES, width), f32),
        pltpu.VMEM((LANES, width), f32),
        logit,
        logit,
        logit,
        logit,
        dma((3,)),
        dma((TAPS,)),
        dma((TAPS,)),
        dma((TAPS,)),
        dma((3,)),
        dma((3,)),
        dma((4,)),
        dma((4,)),
        dma((2, 4)),
        dma((4,)),
        dma((4, 8)),
        dma((4, 8)),
        dma((4,)),
        dma((4,)),
        dma((4,)),
        dma((4,)),
        dma((4,)),
        dma((4,)),
        dma((2, 4)),
        dma((4,)),
        dma((GROUPS + 1,)),
        dma((GROUPS + 1,)),
        dma((GROUPS + 1, 4)),
        dma((GROUPS + 1, 4)),
        dma((GROUPS + 1, 4)),
        dma((GROUPS + 1, 4)),
        dma((GROUPS + 1, 4)),
        dma((GROUPS + 1, 4)),
        dma((4,)),
        dma((4,)),
        dma((4,)),
        dma((4,)),
    ]
    series_one, series_two, grad_one, grad_two, grad_small = pl.pallas_call(
        functools.partial(step_kernel, rows, links.members, links.copies, classes),
        out_shape=(
            jax.ShapeDtypeStruct((TAPS, piece, channels), f32),
            jax.ShapeDtypeStruct((4, block, TAPS * width), f32),
            jax.ShapeDtypeStruct((TAPS, 2, 2, piece, channels), f32),
            jax.ShapeDtypeStruct((4, block, TAPS * width), f32),
            jax.ShapeDtypeStruct((32, width), f32),
        ),
        in_specs=[anywhere] * 4 + [vmem] * 3,
        out_specs=(vmem,) * 5,
        scratch_shapes=scratch,
        compiler_params=pltpu.CompilerParams(
            collective_id=1, has_side_effects=True, vmem_limit_bytes=63 * 1024 * 1024
        ),
        name="train_step",
    )(*operands)

    def outer(value):
        value = value.reshape(4, block, TAPS, width).transpose(1, 2, 0, 3)
        return value.reshape(block, TAPS * channels)

    series_one = lax.all_gather(series_one, "dp").transpose(0, 2, 1, 3)
    series = jnp.stack([series_one.reshape(block, TAPS * channels), outer(series_two)])
    grad_one = grad_one.reshape(TAPS, block, channels).transpose(1, 0, 2)
    grads = jnp.stack([grad_one.reshape(block, TAPS * channels), outer(grad_two)])
    own = lax.dynamic_slice_in_dim(grad_small, lane, block, 1)
    return grad_small[0, 0], grad_small[1, 0], grads, own[8:12], own[16 : 16 + classes].T, series


def adamw(weight, grad, first, second, rate):
    first = beta_first * first + (1.0 - beta_first) * grad
    second = beta_second * second + (1.0 - beta_second) * grad * grad
    first_hat = first / (1.0 - beta_first**STEP)
    second_hat = second / (1.0 - beta_second**STEP)
    update = first_hat / (jnp.sqrt(second_hat) + adam_eps) + decoupled * weight
    return (weight - rate * update, first, second)


def silu_parts(value):
    gate = jax.nn.sigmoid(value)
    slope = gate * (1.0 - gate)
    first = gate + value * slope
    second = slope * (2.0 + value * (1.0 - 2.0 * gate))
    return value * gate, first, second


class Links:
    def __init__(self):
        self.shards = lax.axis_size("shard")
        self.copies = lax.axis_size("dp")
        self.parts = 4 if self.shards % 4 == 0 else 1
        self.members = self.shards // self.parts
        index = lax.axis_index("shard")
        self.part = index // self.members
        self.member = index % self.members
        self.across = [
            [p * self.members + m for p in range(self.parts)] for m in range(self.members)
        ]
        self.within = [
            [p * self.members + m for m in range(self.members)] for p in range(self.parts)
        ]

    def sum_rows(self, value):
        value = lax.psum(value, "dp")
        gathered = lax.all_gather(value, "shard", axis_index_groups=self.within)
        return jnp.sum(gathered, axis=0)

    def sum_parts(self, value):
        return jnp.sum(lax.all_gather(value, "shard", axis_index_groups=self.across), axis=0)

    def gather_parts(self, value, axis):
        return lax.all_gather(value, "shard", axis_index_groups=self.across, axis=axis, tiled=True)

    def gather_members(self, value, axis):
        return lax.all_gather(value, "shard", axis_index_groups=self.within, axis=axis, tiled=True)

    def scatter_parts(self, value, axis):
        return lax.psum_scatter(
            value, "shard", axis_index_groups=self.across, scatter_dimension=axis, tiled=True
        )

    def to_inner(self, value):
        rows, channels = value.shape[0], value.shape[1] // TAPS
        width = channels // self.parts
        cut = value.reshape(rows, TAPS, self.parts, width).transpose(2, 0, 1, 3)
        moved = lax.all_to_all(cut, "shard", 0, 0, axis_index_groups=self.across, tiled=True)
        whole = self.gather_members(moved, 1)
        return whole.reshape(channels, TAPS * width)

    def to_outer(self, value):
        channels, width = value.shape[0], value.shape[1] // TAPS
        rows = channels // self.shards
        cut = value.reshape(self.parts, self.members, rows, TAPS * width)
        cut = lax.dynamic_index_in_dim(cut, self.member, 1, keepdims=False)
        moved = lax.all_to_all(cut, "shard", 0, 0, axis_index_groups=self.across, tiled=True)
        moved = moved.reshape(self.parts, rows, TAPS, width).transpose(1, 2, 0, 3)
        return moved.reshape(rows, TAPS * channels)

    def own_rows(self, value, axis=0):
        size = value.shape[axis] // self.members
        return lax.dynamic_slice_in_dim(value, self.member * size, size, axis)


def moments(hidden, rows, links):
    totals = links.sum_rows(jnp.stack([jnp.sum(hidden, axis=0), jnp.sum(hidden * hidden, axis=0)]))
    average = totals[0] / rows
    scale = lax.rsqrt(totals[1] / rows - average * average + norm_eps)
    return (hidden - average) * scale, scale


def moments_tangent(normal, scale, tangent, rows, links):
    totals = links.sum_rows(
        jnp.stack([jnp.sum(tangent, axis=0), jnp.sum(tangent * normal, axis=0)])
    )
    average, cross = totals[0] / rows, totals[1] / rows
    return scale * (tangent - average - normal * cross), -scale * scale * cross


def step_general(
    links, rows, images, conv_weights, decay_rates, norm_params, head_weights, labels, valid
):
    own_images, channels = images.shape[2:]
    count = own_images * links.parts
    width = channels // links.parts
    first_column = links.part * width
    label_total = lax.psum(jnp.sum(valid), ("shard", "dp"))
    images = links.gather_parts(images, 2)
    labels = links.gather_parts(labels, 0)
    valid = links.gather_parts(valid, 0)

    kernel_one = links.gather_members(conv_weights[0], 0)
    kernel_two = links.to_inner(conv_weights[1])
    decay_one = links.gather_members(decay_rates[0], 0)
    decay_two = links.to_inner(decay_rates[1])
    norms = links.gather_members(norm_params, 1)
    head = links.gather_members(head_weights, 0)
    gain_one, shift_one, gain_two, shift_two = norms[0], norms[1], norms[2], norms[3]

    def pool(value):
        return jnp.sum(value.reshape(MAP * MAP, count, width), axis=0) / (MAP * MAP)

    def spread(value):
        whole = jnp.broadcast_to(value[None] / (MAP * MAP), (MAP * MAP, count, width))
        return whole.reshape(MAP * MAP * count, width)

    columns = patches(images)
    own_columns = lax.dynamic_slice_in_dim(
        images.reshape(MAP * MAP * count, channels), first_column, width, 1
    )

    hidden_one = dot(columns, kernel_one, ((1,), (1,)))
    normal_one, scale_one = moments(hidden_one, rows, links)
    active, slope_one, bend_one = silu_parts(normal_one * gain_one + shift_one)
    active_columns = patches(active.reshape(MAP, MAP, count, width))
    hidden_two = links.scatter_parts(dot(active_columns, kernel_two, ((1,), (1,))), 1)
    normal_two, scale_two = moments(hidden_two, rows, links)
    block, slope_two, bend_two = silu_parts(normal_two * gain_two + shift_two + own_columns)
    pooled = pool(block)
    logits = links.sum_parts(dot(pooled, head, ((1,), (0,))))
    highest = jnp.max(logits, axis=1, keepdims=True)
    powers = jnp.exp(logits - highest)
    total = jnp.sum(powers, axis=1, keepdims=True)
    chances = powers / total
    classes = jnp.arange(logits.shape[1], dtype=jnp.int32)
    chosen = (labels[:, None] == classes[None, :]).astype(jnp.float32)
    cross = highest[:, 0] + jnp.log(total[:, 0]) - jnp.sum(chosen * logits, axis=1)
    loss_sum = links.sum_rows(jnp.sum(valid * cross)[None])[0]
    weights = (valid / label_total)[:, None]
    pull_logits = weights * (chances - chosen)
    grad_head = dot(pooled, pull_logits, ((0,), (0,)))
    pull_block = spread(dot(pull_logits, head, ((1,), (1,))))
    pull_two = pull_block * slope_two
    sums_two = links.sum_rows(
        jnp.stack([jnp.sum(pull_two * normal_two, axis=0), jnp.sum(pull_two, axis=0)])
    )
    centred_two = pull_two - sums_two[1] / rows - normal_two * (sums_two[0] / rows)
    factor_two = scale_two * gain_two
    pull_hidden_two = links.gather_parts(factor_two * centred_two, 1)
    grad_two = dot(pull_hidden_two, active_columns, ((0,), (0,)))
    pull_active = fold(dot(pull_hidden_two, kernel_two, ((1,), (0,))), count)
    pull_one = pull_active * slope_one
    sums_one = links.sum_rows(
        jnp.stack([jnp.sum(pull_one * normal_one, axis=0), jnp.sum(pull_one, axis=0)])
    )
    centred_one = pull_one - sums_one[1] / rows - normal_one * (sums_one[0] / rows)
    factor_one = scale_one * gain_one
    grad_one = dot(factor_one * centred_one, columns, ((0,), (0,)))

    grad_one = links.sum_rows(grad_one) + decay_one * kernel_one
    grad_two = links.sum_rows(grad_two) + decay_two * kernel_two
    grad_head = links.sum_rows(grad_head)
    grad_norm = jnp.concatenate([sums_one, sums_two])

    def product(vector):
        move_one, move_two, move_norm, move_head = vector
        tan_hidden = dot(columns, move_one, ((1,), (1,)))
        tan_normal_one, tan_scale_one = moments_tangent(
            normal_one, scale_one, tan_hidden, rows, links
        )
        tan_inner = move_norm[0] * normal_one + gain_one * tan_normal_one + move_norm[1]
        tan_active = slope_one * tan_inner
        tan_columns = patches(tan_active.reshape(MAP, MAP, count, width))
        tan_hidden = links.scatter_parts(
            dot(tan_columns, kernel_two, ((1,), (1,))) + dot(active_columns, move_two, ((1,), (1,))),
            1,
        )
        tan_normal_two, tan_scale_two = moments_tangent(
            normal_two, scale_two, tan_hidden, rows, links
        )
        tan_outer = move_norm[2] * normal_two + gain_two * tan_normal_two + move_norm[3]
        tan_pooled = pool(slope_two * tan_outer)
        tan_logits = links.sum_parts(
            dot(tan_pooled, head, ((1,), (0,))) + dot(pooled, move_head, ((1,), (0,)))
        )
        tan_chances = chances * (tan_logits - jnp.sum(chances * tan_logits, axis=1, keepdims=True))
        tan_pull = weights * tan_chances
        out_head = dot(tan_pooled, pull_logits, ((0,), (0,))) + dot(pooled, tan_pull, ((0,), (0,)))
        tan_block = spread(
            dot(tan_pull, head, ((1,), (1,))) + dot(pull_logits, move_head, ((1,), (1,)))
        )
        tan_two = tan_block * slope_two + pull_block * bend_two * tan_outer
        tan_sums_two = links.sum_rows(
            jnp.stack(
                [
                    jnp.sum(tan_two * normal_two + pull_two * tan_normal_two, axis=0),
                    jnp.sum(tan_two, axis=0),
                ]
            )
        )
        tan_factor = tan_scale_two * gain_two + scale_two * move_norm[2]
        tan_hidden = tan_factor * centred_two + factor_two * (
            tan_two
            - tan_sums_two[1] / rows
            - tan_normal_two * (sums_two[0] / rows)
            - normal_two * (tan_sums_two[0] / rows)
        )
        tan_hidden = links.gather_parts(tan_hidden, 1)
        out_two = dot(tan_hidden, active_columns, ((0,), (0,))) + dot(
            pull_hidden_two, tan_columns, ((0,), (0,))
        )
        tan_pull_active = fold(
            dot(tan_hidden, kernel_two, ((1,), (0,))) + dot(pull_hidden_two, move_two, ((1,), (0,))),
            count,
        )
        tan_one = tan_pull_active * slope_one + pull_active * bend_one * tan_inner
        tan_sums_one = links.sum_rows(
            jnp.stack(
                [
                    jnp.sum(tan_one * normal_one + pull_one * tan_normal_one, axis=0),
                    jnp.sum(tan_one, axis=0),
                ]
            )
        )
        tan_factor = tan_scale_one * gain_one + scale_one * move_norm[0]
        tan_hidden = tan_factor * centred_one + factor_one * (
            tan_one
            - tan_sums_one[1] / rows
            - tan_normal_one * (sums_one[0] / rows)
            - normal_one * (tan_sums_one[0] / rows)
        )
        out_one = dot(tan_hidden, columns, ((0,), (0,)))
        return (
            links.sum_rows(out_one) + decay_one * move_one,
            links.sum_rows(out_two) + decay_two * move_two,
            jnp.concatenate([tan_sums_one, tan_sums_two]),
            links.sum_rows(out_head),
        )

    vector = (grad_one, grad_two, grad_norm, grad_head)
    series_one, series_two = grad_one, grad_two
    for turn in range(NEUMANN):
        change = product(vector)
        vector = tuple(
            previous - neumann_rate * moved for previous, moved in zip(vector, change)
        )
        series_one, series_two = series_one + vector[0], series_two + vector[1]

    series = jnp.stack([links.own_rows(series_one), links.to_outer(series_two)])
    grads = jnp.stack([links.own_rows(grad_one), links.to_outer(grad_two)])
    return (
        loss_sum,
        label_total,
        grads,
        links.own_rows(grad_norm, 1),
        links.own_rows(grad_head),
        series,
    )


def shards(
    source,
    index_map,
    crop_offsets,
    flip_flags,
    labels,
    valid_mask,
    conv_weights,
    norm_params,
    head_weights,
    decay_rates,
    conv_first,
    conv_second,
    norm_first,
    norm_second,
    head_first,
    head_second,
):
    links = Links()
    rows = float(source.shape[0] * MAP * MAP * links.shards * links.copies)
    picked = source[index_map]
    images = jax.vmap(crop_image)(picked, crop_offsets, flip_flags)
    images = images.transpose(1, 2, 0, 3)
    fused = links.members * links.copies == 8 and links.parts == 4
    loss_sum, label_total, grads, grad_norm, grad_head, series = (
        step_fused if fused else step_general
    )(
        links,
        rows,
        images,
        conv_weights,
        decay_rates,
        norm_params,
        head_weights,
        labels,
        valid_mask.astype(jnp.float32),
    )
    hyper_gradient = -neumann_rate * conv_weights * series
    conv_new, conv_one, conv_two = adamw(conv_weights, grads, conv_first, conv_second, 0.015)
    norm_new, norm_one, norm_two = adamw(
        norm_params, grad_norm, norm_first, norm_second, 0.3
    )
    head_new, head_one, head_two = adamw(
        head_weights, grad_head, head_first, head_second, 0.13
    )
    return (
        loss_sum,
        label_total,
        conv_new,
        conv_one,
        conv_two,
        norm_new,
        norm_one,
        norm_two,
        head_new,
        head_one,
        head_two,
        hyper_gradient,
    )


def solution(mesh):
    images = P(("shard", "dp"))
    rows = P(None, "shard")
    head = P("shard")
    in_specs = (images,) * 6 + (rows, rows, head, rows, rows, rows, rows, rows, head, head)
    out_specs = (P(), P()) + (rows,) * 6 + (head,) * 3 + (rows,)
    return jax.shard_map(shards, mesh=mesh, in_specs=in_specs, out_specs=out_specs, check_vma=False)
```

```python
import functools

import jax
import jax.numpy as jnp
from jax import lax
from jax.experimental import pallas as pl
from jax.experimental.pallas import tpu as pltpu
from jax.sharding import PartitionSpec as P

MAP = 4
NEUMANN = 3
STEP = 5
TAPS = 9

norm_eps = 1e-05
neumann_rate = 10.0
beta_first = 0.5
beta_second = 0.5
adam_eps = 1e-08
decoupled = 0.01
HIGH = lax.Precision.HIGH


def crop_image(single, offsets, flipped):
    window = lax.dynamic_slice(
        single, (offsets[0], offsets[1], jnp.int32(0)), (MAP, MAP, single.shape[2])
    )
    return jnp.where(flipped == 1, window[:, ::-1, :], window)


def patches(maps):
    count, width = maps.shape[2:]
    padded = jnp.pad(maps, ((1, 1), (1, 1), (0, 0), (0, 0)))
    taps = [padded[dy : dy + MAP, dx : dx + MAP] for dy in range(3) for dx in range(3)]
    return jnp.concatenate(taps, axis=3).reshape(MAP * MAP * count, TAPS * width)


def fold(columns, count):
    width = columns.shape[1] // TAPS
    whole = columns.reshape(MAP, MAP, count, TAPS, width)
    padded = jnp.pad(whole, ((1, 1), (1, 1), (0, 0), (0, 0), (0, 0)))
    total = 0.0
    for dy in range(3):
        for dx in range(3):
            total = total + padded[2 - dy : 2 - dy + MAP, 2 - dx : 2 - dx + MAP, :, dy * 3 + dx]
    return total.reshape(MAP * MAP * count, width)


def dot(left, right, dims):
    return lax.dot_general(
        left, right, ((dims[0], dims[1]), ((), ())), precision=HIGH, preferred_element_type=jnp.float32
    )


MESH_ID = pl.DeviceIdType.MESH
LANES = 128
GROUPS = 3


def halves(value):
    high = value.astype(jnp.bfloat16)
    return high, (value - high.astype(jnp.float32)).astype(jnp.bfloat16)


def mul(left, right, dims=((1,), (0,))):
    return lax.dot_general(left, right, (dims, ((), ())), preferred_element_type=jnp.float32)


def mul_exact(left, right, dims=((1,), (0,))):
    return lax.dot_general(
        left,
        right,
        (dims, ((), ())),
        precision=lax.Precision.HIGHEST,
        preferred_element_type=jnp.float32,
    )


def silu_pieces(value):
    gate = 1.0 / (1.0 + jnp.exp(-value))
    slope = gate * (1.0 - gate)
    return value * gate, gate + value * slope, slope * (2.0 + value * (1.0 - 2.0 * gate))


def step_kernel(
    rows,
    members,
    copies,
    classes,
    x_in,
    weights_in,
    decay_in,
    pair_in,
    label_in,
    grads,
    series,
    grad_small,
    series_one,
    series_two,
    grad_source,
    row_parts,
    row_box,
    cut_box,
    d1,
    d2,
    v1,
    v2,
    v1_hi,
    v1_lo,
    v2_hi,
    v2_lo,
    k_hi,
    k_lo,
    x_box,
    x_row,
    x_both,
    x_own,
    a_both,
    b_both,
    g_left,
    g_turned,
    t_left,
    t_turned,
    slots,
    partial,
    from_low,
    from_high,
    flow,
    n1,
    s1,
    pb1,
    pull1,
    c1,
    n2,
    s2,
    pb2,
    pull2,
    c2,
    nt1,
    in1,
    nt2,
    in2,
    fold_sum,
    sum_one,
    sum_two,
    half_one,
    half_two,
    piece_one,
    piece_two,
    stats_box,
    stats_own,
    logit_box,
    logit_own,
    pair_box,
    label_box,
    turned,
    channel,
    move_norm,
    move_head,
    head,
    pooled,
    chances,
    weights,
    pull_logits,
    x_load,
    pair_sem,
    cut_load,
    k1_load,
    d1_load,
    k1_send,
    k1_recv,
    first_send,
    first_recv,
    label_send,
    label_recv,
    x_send,
    x_recv,
    stats_send,
    stats_recv,
    logit_send,
    logit_recv,
    up_send,
    up_recv,
    down_send,
    down_recv,
    ring_send,
    ring_recv,
    pair_send,
    pair_recv,
    plane_send,
    plane_recv,
    back_send,
    back_recv,
    swap_send,
    swap_recv,
    row_send,
    row_recv,
    own_send,
    own_recv,
):
    shard = lax.axis_index("shard")
    copy = lax.axis_index("dp")
    part = shard // members
    member = shard % members
    me = member * copies + copy
    place, core = me // 2, me % 2
    last = 3
    count = flow.shape[1]
    own_count = x_in.shape[1]
    inverse = 1.0 / rows
    zero = jnp.zeros((count, LANES), jnp.float32)

    def row_peer(other):
        return (part * members + other // copies, other % copies)

    def part_peer(other):
        return (other * members + member, copy)

    def remote(source, target, send, recv, device):
        return pltpu.make_async_remote_copy(
            src_ref=source,
            dst_ref=target,
            send_sem=send,
            recv_sem=recv,
            device_id=device,
            device_id_type=MESH_ID,
        )

    def greet(device):
        pl.semaphore_signal(barrier, inc=1, device_id=device, device_id_type=MESH_ID)

    barrier = pltpu.get_barrier_semaphore()
    for step in range(1, 8):
        greet(row_peer(me ^ step))
    for step in range(1, 4):
        greet(part_peer(part ^ step))
    channels = x_in.shape[2]
    own_pieces = pl.ds(pl.multiple_of(member * 4, 4), 4)

    def tap_lanes(tap, width):
        return pl.ds(pl.multiple_of(tap * width, width), width)

    x_here = pltpu.make_async_copy(x_in, x_box.at[part], x_load)
    x_here.start()
    k1_loads = [
        pltpu.make_async_copy(
            weights_in.at[0, :, :, pl.ds(tap * channels, channels)],
            v1.at[tap, own_pieces],
            k1_load.at[tap],
        )
        for tap in range(TAPS)
    ]
    d1_loads = [
        pltpu.make_async_copy(
            decay_in.at[0, copy, :, pl.ds(tap * channels, channels)], d1.at[tap], d1_load.at[tap]
        )
        for tap in range(TAPS)
    ]
    cut_loads = [
        pltpu.make_async_copy(weights_in.at[1, copy], row_box.at[0], cut_load.at[0]),
        pltpu.make_async_copy(decay_in.at[1, copy], row_box.at[1], cut_load.at[1]),
    ]
    for load in cut_loads + k1_loads + d1_loads:
        load.start()
    stats_own[...] = jnp.zeros_like(stats_own)
    channel[...] = jnp.zeros_like(channel)
    x_both[...] = jnp.zeros_like(x_both)
    a_both[...] = jnp.zeros_like(a_both)
    b_both[...] = jnp.zeros_like(b_both)
    label_box[0] = label_in[...]
    x_here.wait()
    pl.semaphore_wait(barrier, 10)

    def ring_move(box, send, recv, block, step, way, half):
        at = pl.ds(half * 8, 8)
        return remote(
            box.at[block, at],
            box.at[block, at],
            send.at[0 if way > 0 else 1, step, half],
            recv.at[block, half],
            part_peer(part + way),
        )

    def ring_start(box, send, recv):
        for half in range(2):

            @pl.when(part < last)
            def _():
                ring_move(box, send, recv, part, 0, 1, half).start()

            @pl.when(part > 0)
            def _():
                ring_move(box, send, recv, part, 0, -1, half).start()

    def ring_step(box, send, recv, step):
        for half in range(2):

            @pl.when(part >= step)
            def _():
                ring_move(box, send, recv, part - step, step, -1, half).wait_recv()

                @pl.when(part < last)
                def _():
                    ring_move(box, send, recv, part - step, step, 1, half).start()

            @pl.when(part + step <= last)
            def _():
                ring_move(box, send, recv, part + step, step, 1, half).wait_recv()

                @pl.when(part > 0)
                def _():
                    ring_move(box, send, recv, part + step, step, -1, half).start()

    def ring_end(box, send, recv):
        for step in range(0, 3):
            for half in range(2):

                @pl.when((part >= step) & (part < last))
                def _():
                    ring_move(box, send, recv, part - step, step, 1, half).wait_send()

                @pl.when((part + step <= last) & (part > 0))
                def _():
                    ring_move(box, send, recv, part + step, step, -1, half).wait_send()

    order = (
        part,
        jnp.where(part == 0, 1, part - 1),
        jnp.where(part == 3, 1, jnp.where(part == 2, 3, 2)),
        jnp.where(part < 2, 3, 0),
    )

    ring_start(x_box, x_send, x_recv)
    partner = row_peer(me ^ copies)
    k1_moves = [
        remote(
            weights_in.at[0, :, :, pl.ds(tap * channels, channels)],
            v1.at[tap, own_pieces],
            k1_send.at[tap],
            k1_recv.at[tap],
            partner,
        )
        for tap in range(TAPS)
    ]
    for move in k1_moves:
        move.start()

    def cut_move(which, other):
        box = v2.at[me, part] if which == 0 else d2.at[part]
        return remote(
            cut_box.at[which, other],
            box,
            first_send.at[which, other],
            first_recv.at[which, part],
            part_peer(other),
        )

    def cut_start(which):
        for other in range(4):
            for tap in range(TAPS):
                start = tap * channels + other * LANES
                cut_box[which, other, :, tap * LANES : (tap + 1) * LANES] = row_box[
                    which, :, start : start + LANES
                ]
        for other in range(4):

            @pl.when(part != other)
            def _():
                cut_move(which, other).start()

        if which == 0:
            v2[me, part] = cut_box[which, part]
        else:
            d2[part] = cut_box[which, part]

    def cut_end(which):
        for other in range(4):

            @pl.when(part != other)
            def _():
                cut_move(which, other).wait_send()
                box = v2.at[me, other] if which == 0 else d2.at[other]
                remote(
                    cut_box.at[which, other],
                    box,
                    first_send.at[which, other],
                    first_recv.at[which, other],
                    part_peer(other),
                ).wait_recv()

    pair_move = remote(pair_in, pair_box, pair_sem.at[0], pair_sem.at[1], partner)
    pair_move.start()
    label_moves = [
        remote(
            label_in,
            label_box.at[step],
            label_send.at[step],
            label_recv.at[step],
            part_peer(part ^ step),
        )
        for step in range(1, 4)
    ]
    for move in label_moves:
        move.start()

    pair = row_peer(me ^ 1)

    def piece_of(which, other):
        if isinstance(which, int):
            return v1.at[pl.ds(which * 3, 3), other]
        return v2.at[other, which[0]]

    def lane_of(which):
        return which if isinstance(which, int) else GROUPS + which[0]

    def to_plane(which, step):
        piece, at = piece_of(which, me), lane_of(which)
        return remote(
            piece, piece, back_send.at[at, step], back_recv.at[at, step], row_peer(me ^ (2 * step))
        )

    def from_plane(which, step):
        piece, at = piece_of(which, me ^ (2 * step)), lane_of(which)
        return remote(piece, piece, back_send.at[at, step], back_recv.at[at, step], pair)

    def to_pair(which, step):
        piece, at = piece_of(which, me ^ (2 * step)), lane_of(which)
        return remote(piece, piece, swap_send.at[at, step], swap_recv.at[at, step], pair)

    def from_pair(which, step):
        piece, at = piece_of(which, me ^ 1 ^ (2 * step)), lane_of(which)
        return remote(piece, piece, swap_send.at[at, step], swap_recv.at[at, step], pair)

    def back_start(which):
        for step in range(1, 4):
            to_plane(which, step).start()
        to_pair(which, 0).start()

    def back_forward(which):
        for step in range(1, 4):
            from_plane(which, step).wait_recv()
            to_pair(which, step).start()

    def back_arrived(which):
        for step in range(0, 4):
            from_pair(which, step).wait_recv()

    def back_end(which):
        for step in range(1, 4):
            to_plane(which, step).wait_send()
        for step in range(0, 4):
            to_pair(which, step).wait_send()

    for load in cut_loads:
        load.wait()
    cut_start(0)
    ring_step(x_box, x_send, x_recv, 1)
    cut_start(1)
    pair_move.wait()
    small = pair_in[...] + pair_box[...]
    move_norm[...] = small[0:8]
    head[...] = jnp.zeros_like(head)
    move_head[...] = jnp.zeros_like(move_head)
    head[0:16] = small[8:24]
    for move in label_moves:
        move.wait()
    tags = label_box[0] + label_box[1] + label_box[2] + label_box[3]
    chosen, valid = tags[:count], tags[count:]

    def each_cell(body, init=None):
        return lax.fori_loop(0, 16, body, init)

    def window(ref, tap, lanes=slice(None)):
        seen = ref[pl.ds(tap // 3, 4), pl.ds(tap % 3, 4), :, lanes]
        return seen.reshape(16 * seen.shape[2], seen.shape[3])

    def row(ref, index):
        return ref[index : index + 1, :]

    def put_sums(site, first, second):
        stats_own[site, 0:1, :] = jnp.sum(first, axis=0, keepdims=True)
        stats_own[site, 1:2, :] = jnp.sum(second, axis=0, keepdims=True)

    def sum_start(site, size):
        moves = []
        for step in range(1, 8):
            move = remote(
                stats_own.at[site, pl.ds(0, size)],
                stats_box.at[site, step, pl.ds(0, size)],
                stats_send.at[site, step],
                stats_recv.at[site, step],
                row_peer(me ^ step),
            )
            move.start()
            moves.append(move)
        stats_box[site, 0, pl.ds(0, size)] = stats_own[site, pl.ds(0, size)]
        return moves

    def sum_end(site, size, moves):
        for move in moves:
            move.wait()
        total = stats_box[site, me, pl.ds(0, size)]
        for other in range(1, 8):
            total = total + stats_box[site, other ^ me, pl.ds(0, size)]
        return total

    def sum_parts(value):
        logit_own[...] = value
        moves = []
        for step in range(1, 4):
            move = remote(
                logit_own,
                logit_box.at[step],
                logit_send.at[step],
                logit_recv.at[step],
                part_peer(part ^ step),
            )
            move.start()
            moves.append(move)
        logit_box[0] = value
        for move in moves:
            move.wait()
        total = logit_box[part]
        for other in range(1, 4):
            total = total + logit_box[other ^ part]
        return total

    def split_one(tap, _):
        for other in range(8):
            at = slice(other * 16, other * 16 + 16)
            v1_hi[tap, at], v1_lo[tap, at] = halves(v1[tap, other])

    def split_two(high, low):
        def body(other, _):
            for block in range(4):
                at = pl.ds(pl.multiple_of(block * LANES + other * 16, 16), 16)
                high[at], low[at] = halves(v2[other, block])

        lax.fori_loop(0, 8, body, None)

    def tap_forward(tap, _):
        weight = jnp.concatenate([v1_hi[tap], v1_lo[tap]], axis=0)
        weight = jnp.concatenate([weight, weight], axis=1)
        out = mul(window(x_both, tap), weight, ((1,), (1,)))
        flow[...] += (out[:, :LANES] + out[:, LANES:]).reshape(flow.shape)

    def part_of_second(maps, high, low, half):
        at = pl.ds(pl.multiple_of(half * 256, 256), 256)

        def body(tap, _):
            lanes = tap_lanes(tap, LANES)
            left = window(maps, tap)
            weight_hi, weight_lo = high[at, lanes], low[at, lanes]
            out = mul(
                jnp.concatenate([left, left], axis=1),
                jnp.concatenate([weight_hi, weight_hi, weight_lo, weight_lo], axis=1),
                ((1,), (1,)),
            )
            partial[half * 2] += out[:, :LANES].reshape(flow.shape)
            partial[half * 2 + 1] += out[:, LANES:].reshape(flow.shape)

        lax.fori_loop(0, TAPS, body, None)

    def up(block, half):
        at = pl.ds(half * 8, 8)
        return remote(
            partial.at[block, at],
            from_low.at[block, at],
            up_send.at[block, half],
            up_recv.at[block, half],
            part_peer(part + 1),
        )

    def down(block, half):
        at = pl.ds(half * 8, 8)
        return remote(
            partial.at[block, at],
            from_high.at[block, at],
            down_send.at[block, half],
            down_recv.at[block, half],
            part_peer(part - 1),
        )

    def scatter(maps, high, low, aside):
        near = jnp.where(part < 2, 1, 0)
        part_of_second(maps, high, low, near)

        @pl.when(part == 0)
        def _():
            for block in (3, 2):
                for half in range(2):
                    up(block, half).start()

        @pl.when(part == last)
        def _():
            for block in (0, 1):
                for half in range(2):
                    down(block, half).start()

        part_of_second(maps, high, low, 1 - near)
        for block in (3, 2, 1):
            goal = last - block

            for half in range(2):
                at = slice(half * 8, half * 8 + 8)

                @pl.when((part < block) & (part > 0))
                def _():
                    up(block, half).wait_recv()
                    partial[block, at] += from_low[block, at]
                    up(block, half).start()

                @pl.when((part > goal) & (part < last))
                def _():
                    down(goal, half).wait_recv()
                    partial[goal, at] += from_high[goal, at]
                    down(goal, half).start()

                if block == 1:

                    @pl.when(part == 0)
                    def _():
                        up(1, half).start()

                    @pl.when(part == last)
                    def _():
                        down(2, half).start()

            aside(3 - block)
        aside(3)
        for block in range(4):

            @pl.when(part == block)
            def _():
                for half in range(2):
                    at = slice(half * 8, half * 8 + 8)
                    total = partial[block, at]
                    if block > 0:
                        up(block, half).wait_recv()
                        total = total + from_low[block, at]
                    if block < last:
                        down(block, half).wait_recv()
                        total = total + from_high[block, at]
                    flow[at] = total

        for block in (3, 2, 1):
            goal = last - block
            for half in range(2):

                @pl.when(part < block)
                def _():
                    up(block, half).wait_send()

                @pl.when(part > goal)
                def _():
                    down(goal, half).wait_send()

    def turn_block(block, left, turned_block):
        value = slots[block].reshape(16 * count, LANES)
        left[...] = jnp.concatenate(halves(value), axis=1)
        turned_block[...] = jnp.concatenate(halves(value.T), axis=0)

    def use_block(block, left, turned_block, high, low, maps):
        at = pl.ds(pl.multiple_of(block * LANES, LANES), LANES)

        def body(tap, _):
            lanes = tap_lanes(tap, LANES)
            weight = jnp.concatenate([high[at, lanes], low[at, lanes]], axis=1)
            out = mul(left[...], jnp.concatenate([weight, weight], axis=0))
            out = out[:, :LANES] + out[:, LANES:]
            fold_sum[pl.ds(tap // 3, 4), pl.ds(tap % 3, 4)] += out.reshape(4, 4, count, LANES)
            out = mul(turned_block[...], window(maps, tap))
            out = (out[:LANES, :LANES] + out[LANES:, :LANES]) + (
                out[:LANES, LANES:] + out[LANES:, LANES:]
            )
            sum_two[block, :, :, :, lanes] += out.reshape(4, 2, 16, LANES)

        lax.fori_loop(0, TAPS, body, None)

    def pair_two(block):
        return remote(
            sum_two.at[block, :, 1 - core],
            half_two.at[block],
            pair_send.at[GROUPS + block],
            pair_recv.at[GROUPS + block],
            pair,
        )

    def plane_two(block, step):
        other = place ^ step
        return remote(
            half_two.at[block, other],
            piece_two.at[step, block],
            plane_send.at[GROUPS + block, step],
            plane_recv.at[GROUPS + block, step],
            row_peer(other * 2 + core),
        )

    def plane_two_go(block):
        pair_two(block).wait()
        for place_of in range(4):
            half_two[block, place_of] += sum_two[block, place_of, core]
        for step in range(1, 4):
            plane_two(block, step).start()

    def step_two(block, new_of, more):
        for step in range(1, 4):
            plane_two(block, step).wait()
        change = half_two[block, place] + piece_two[1, block] + piece_two[2, block] + piece_two[3, block]
        new = new_of(v2[me, block], change, d2[block])
        v2[me, block] = new
        series_two[block] += new

        @pl.when(more)
        def _():
            back_start((block,))

    def back_forward_when(block, more):
        @pl.when(more)
        def _():
            back_forward((block,))

    def gather_and_use(block_of, new_of, more):
        ring_start(slots, ring_send, ring_recv)
        block_of(order[0])
        pair_two(order[0]).start()
        ring_step(slots, ring_send, ring_recv, 1)
        block_of(order[1])
        pair_two(order[1]).start()
        plane_two_go(order[0])
        ring_step(slots, ring_send, ring_recv, 2)
        step_two(order[0], new_of, more)
        block_of(order[2])
        pair_two(order[2]).start()
        plane_two_go(order[1])
        ring_step(slots, ring_send, ring_recv, 3)
        step_two(order[1], new_of, more)
        block_of(order[3])
        pair_two(order[3]).start()
        plane_two_go(order[2])
        back_forward_when(order[0], more)
        ring_end(slots, ring_send, ring_recv)

    def rest_of_two(new_of, more):
        plane_two_go(order[3])
        step_two(order[2], new_of, more)
        back_forward_when(order[1], more)

    def end_of_two(new_of, more):
        step_two(order[3], new_of, more)
        back_forward_when(order[2], more)

    def pair_one(group):
        return remote(
            sum_one.at[pl.ds(group * 3, 3), :, 1 - core],
            half_one.at[pl.ds(group * 3, 3)],
            pair_send.at[group],
            pair_recv.at[group],
            pair,
        )

    def plane_one(group, step):
        other = place ^ step
        return remote(
            half_one.at[pl.ds(group * 3, 3), other],
            piece_one.at[step, pl.ds(group * 3, 3)],
            plane_send.at[group, step],
            plane_recv.at[group, step],
            row_peer(other * 2 + core),
        )

    def first_gradient():
        def tap_weight(tap, _):
            out = mul(turned[...], window(x_both, tap, slice(0, channels)))
            out = out + mul(turned[...], window(x_both, tap, slice(channels, 2 * channels)))
            sum_one[tap] = (out[:LANES] + out[LANES:]).reshape(sum_one.shape[1:])

        def plane_go(group):
            pair_one(group).wait()

            def body(tap, _):
                for place_of in range(4):
                    half_one[tap, place_of] += sum_one[tap, place_of, core]

            lax.fori_loop(group * 3, group * 3 + 3, body, None)
            for step in range(1, 4):
                plane_one(group, step).start()

        for group in range(GROUPS):
            lax.fori_loop(group * 3, group * 3 + 3, tap_weight, None)
            pair_one(group).start()
            if group > 0:
                plane_go(group - 1)
        plane_go(GROUPS - 1)

    def step_group(group, new_of):
        for step in range(1, 4):
            plane_one(group, step).wait()

        def body(tap, _):
            change = (
                half_one[tap, place] + piece_one[1, tap] + piece_one[2, tap] + piece_one[3, tap]
            )
            new = new_of(v1[tap, me], change, d1[tap])
            v1[tap, me] = new
            series_one[:, tap_lanes(tap, channels)] += new

        lax.fori_loop(group * 3, group * 3 + 3, body, None)

    def no_aside(index):
        pass

    series_one[...] = jnp.zeros_like(series_one)
    series_two[...] = jnp.zeros_like(series_two)

    def first_vector(old, change, decay):
        return change + decay * old

    def next_vector(old, change, decay):
        return old - neumann_rate * (change + decay * old)

    for load in k1_loads + d1_loads:
        load.wait()
    for move in k1_moves:
        move.wait()
    lax.fori_loop(0, TAPS, split_one, None)
    ring_step(x_box, x_send, x_recv, 2)
    cut_end(0)
    for block in range(4):
        back_start((block,))
    ring_step(x_box, x_send, x_recv, 3)
    ring_end(x_box, x_send, x_recv)

    def place_images(cell, _):
        for block in range(4):
            x_row[block * own_count : (block + 1) * own_count] = x_box[block, cell]
        high, low = halves(x_row[...])
        x_both[cell // 4 + 1, cell % 4 + 1, :, 0:channels] = high
        x_both[cell // 4 + 1, cell % 4 + 1, :, channels : 2 * channels] = low
        x_own[cell] = x_row[:, pl.ds(pl.multiple_of(part * LANES, LANES), LANES)]

    each_cell(place_images)
    flow[...] = jnp.zeros_like(flow)
    lax.fori_loop(0, TAPS, tap_forward, None)

    def sums_primal(cell, carry):
        value = flow[cell]
        return carry[0] + value, carry[1] + value * value

    put_sums(0, *each_cell(sums_primal, (zero, zero)))
    stats_own[0, 2:3, :] = jnp.sum(valid, axis=0, keepdims=True)
    moves = sum_start(0, 8)
    for block in range(4):
        back_forward((block,))
    cut_end(1)
    for block in range(4):
        back_arrived((block,))
        back_end((block,))
    split_two(k_hi, k_lo)
    partial[...] = jnp.zeros_like(partial)
    total = sum_end(0, 8, moves)
    label_total = total[2:3]
    average = total[0:1] * inverse
    scale = lax.rsqrt(total[1:2] * inverse - average * average + norm_eps)
    gain, shift = row(move_norm, 0), row(move_norm, 1)
    gain2, shift2 = row(move_norm, 2), row(move_norm, 3)

    def first_primal(cell, _):
        normal = (flow[cell] - average) * scale
        value, slope, bend = silu_pieces(normal * gain + shift)
        n1[cell] = normal
        s1[cell] = slope
        pb1[cell] = bend
        a_both[cell // 4 + 1, cell % 4 + 1] = jnp.concatenate(halves(value), axis=1)

    each_cell(first_primal)
    scatter(a_both, k_hi, k_lo, no_aside)
    put_sums(1, *each_cell(sums_primal, (zero, zero)))
    total = sum_end(1, 8, sum_start(1, 8))
    average = total[0:1] * inverse
    scale2 = lax.rsqrt(total[1:2] * inverse - average * average + norm_eps)

    def second_primal(cell, carry):
        normal = (flow[cell] - average) * scale2
        value, slope, bend = silu_pieces(normal * gain2 + shift2 + x_own[cell])
        n2[cell] = normal
        s2[cell] = slope
        pb2[cell] = bend
        return carry + value

    pooled[...] = each_cell(second_primal, zero) * (1.0 / 16.0)
    logits = sum_parts(mul_exact(pooled[...], head[...], ((1,), (1,))))
    real = lax.broadcasted_iota(jnp.int32, logits.shape, 1) < classes
    highest = jnp.max(jnp.where(real, logits, -jnp.inf), axis=1, keepdims=True)
    powers = jnp.where(real, jnp.exp(logits - highest), 0.0)
    sum_powers = jnp.sum(powers, axis=1, keepdims=True)
    chances[...] = powers / sum_powers
    target_logit = jnp.sum(chosen * logits, axis=1, keepdims=True)
    cross = (highest + jnp.log(sum_powers) - target_logit) * valid
    weights[...] = valid / label_total
    pull_logits[...] = weights[...] * (chances[...] - chosen)
    out_head = mul_exact(pull_logits[...], pooled[...], ((0,), (0,)))
    pull_block = mul_exact(pull_logits[...], head[...]) * (1.0 / 16.0)

    def back_two_primal(cell, carry):
        pull = pull_block * s2[cell]
        pull2[cell] = pull
        pb2[cell] = pull_block * pb2[cell]
        return carry[0] + pull * n2[cell], carry[1] + pull

    put_sums(2, *each_cell(back_two_primal, (zero, zero)))
    stats_own[2, 2:3, :] = jnp.sum(cross, axis=0, keepdims=True)
    stats_own[2, 8:24, :] = out_head[0:16]
    total = sum_end(2, 24, sum_start(2, 24))
    grad_small[0:1, :] = total[2:3]
    grad_small[1:2, :] = label_total
    grad_small[2:8, :] = jnp.zeros((6, LANES), jnp.float32)
    grad_small[16:32, :] = total[8:24]
    out_gain2, out_shift2 = total[0:1], total[1:2]
    factor2 = scale2 * gain2

    def pull_two_primal(cell, _):
        centred = pull2[cell] - out_shift2 * inverse - n2[cell] * (out_gain2 * inverse)
        c2[cell] = centred
        slots[part, cell] = factor2 * centred

    each_cell(pull_two_primal)
    fold_sum[...] = jnp.zeros_like(fold_sum)
    sum_two[...] = jnp.zeros_like(sum_two)

    def primal_block(block):
        turn_block(block, g_left.at[block], g_turned.at[block])
        use_block(block, g_left.at[block], g_turned.at[block], k_hi, k_lo, a_both)

    gather_and_use(primal_block, first_vector, True)

    def back_one_primal(cell, carry):
        seen = fold_sum[cell // 4 + 1, cell % 4 + 1]
        pull = seen * s1[cell]
        pull1[cell] = pull
        pb1[cell] = seen * pb1[cell]
        return carry[0] + pull * n1[cell], carry[1] + pull

    put_sums(3, *each_cell(back_one_primal, (zero, zero)))
    moves = sum_start(3, 8)
    rest_of_two(first_vector, True)
    total = sum_end(3, 8, moves)
    out_gain, out_shift = total[0:1], total[1:2]
    factor = scale * gain

    def pull_one_primal(cell, _):
        centred = pull1[cell] - out_shift * inverse - n1[cell] * (out_gain * inverse)
        c1[cell] = centred
        flow[cell] = factor * centred

    each_cell(pull_one_primal)
    turned[...] = jnp.concatenate(halves(flow[...].reshape(16 * count, LANES).T), axis=0)

    channel[0:1, :] = scale
    channel[1:2, :] = gain
    channel[2:3, :] = scale2
    channel[3:4, :] = gain2
    channel[4:5, :] = out_gain * inverse
    channel[5:6, :] = out_gain2 * inverse
    move_norm[0:1, :] = out_gain
    move_norm[1:2, :] = out_shift
    move_norm[2:3, :] = out_gain2
    move_norm[3:4, :] = out_shift2
    grad_small[8:16, :] = move_norm[...]
    move_head[0:16] = grad_small[16:32, :]

    first_gradient()
    end_of_two(first_vector, True)
    back_forward((order[3],))

    def deliver_move(which, source, other):
        return remote(
            source.at[other],
            row_parts.at[which, part],
            row_send.at[which, other],
            row_recv.at[which, part],
            part_peer(other),
        )

    def deliver_start(which, source):
        for other in range(4):

            @pl.when(part != other)
            def _():
                deliver_move(which, source, other).start()

        row_parts[which, part] = source[part]

    def deliver_end(which, source, result):
        for other in range(4):

            @pl.when(part != other)
            def _():
                deliver_move(which, source, other).wait_send()
                remote(
                    source.at[other],
                    row_parts.at[which, other],
                    row_send.at[which, other],
                    row_recv.at[which, other],
                    part_peer(other),
                ).wait_recv()

        for other in range(4):
            for tap in range(TAPS):
                start = tap * channels + other * LANES
                result[copy, :, start : start + LANES] = row_parts[
                    which, other, :, tap * LANES : (tap + 1) * LANES
                ]

    across, corner = row_peer(me ^ 2), copy ^ 2

    def spread_move(which, result, step, block, device):
        return remote(
            result.at[block], result.at[block], own_send.at[which, step], own_recv.at[which, step], device
        )

    def spread_start(which, result):
        spread_move(which, result, 0, copy, across).start()
        spread_move(which, result, 1, copy, pair).start()

    def spread_forward(which, result):
        spread_move(which, result, 0, corner, across).wait_recv()
        spread_move(which, result, 2, corner, pair).start()

    def spread_end(which, result):
        spread_move(which, result, 1, copy ^ 1, pair).wait_recv()
        spread_move(which, result, 2, copy ^ 3, pair).wait_recv()
        spread_move(which, result, 0, copy, across).wait_send()
        spread_move(which, result, 1, copy, pair).wait_send()
        spread_move(which, result, 2, corner, pair).wait_send()

    grad_source[...] = series_two[...]
    deliver_start(0, grad_source)
    for group in range(GROUPS):
        step_group(group, first_vector)
        back_start(group)

    def turn_body(turn, nothing):
        for group in range(GROUPS):
            back_forward(group)
        flow[...] = jnp.zeros_like(flow)
        for group in range(GROUPS):
            back_arrived(group)
            lax.fori_loop(group * 3, group * 3 + 3, split_one, None)
            lax.fori_loop(group * 3, group * 3 + 3, tap_forward, None)
        for group in range(GROUPS):
            back_end(group)

        @pl.when(turn == 0)
        def _():
            for tap in range(TAPS):
                grads[0, :, :, tap * channels : (tap + 1) * channels] = v1[tap, own_pieces]

        def sums_forward(normal):
            def body(cell, carry):
                value = flow[cell]
                return carry[0] + value, carry[1] + value * normal[cell]

            return each_cell(body, (zero, zero))

        put_sums(0, *sums_forward(n1))
        moves = sum_start(0, 8)
        partial[...] = jnp.zeros_like(partial)
        fold_sum[...] = jnp.zeros_like(fold_sum)
        sum_two[...] = jnp.zeros_like(sum_two)
        for block in range(4):
            back_arrived((block,))
            back_end((block,))
        split_two(v2_hi, v2_lo)
        part_of_second(a_both, v2_hi, v2_lo, 0)
        part_of_second(a_both, v2_hi, v2_lo, 1)
        total = sum_end(0, 8, moves) * inverse
        average, cross = total[0:1], total[1:2]
        scale, gain = row(channel, 0), row(channel, 1)
        tan_scale_one = -scale * scale * cross
        move_gain, move_shift = row(move_norm, 0), row(move_norm, 1)

        def forward_one(cell, _):
            normal = n1[cell]
            tangent = scale * (flow[cell] - average - normal * cross)
            inner = move_gain * normal + gain * tangent + move_shift
            nt1[cell] = tangent
            in1[cell] = inner
            b_both[cell // 4 + 1, cell % 4 + 1] = jnp.concatenate(halves(s1[cell] * inner), axis=1)

        each_cell(forward_one)

        def aside(block):
            use_block(block, g_left.at[block], g_turned.at[block], v2_hi, v2_lo, b_both)

        scatter(b_both, k_hi, k_lo, aside)

        @pl.when(turn == 0)
        def _():
            deliver_end(0, grad_source, grads.at[1])
            spread_start(0, grads.at[1])

        @pl.when(turn == 1)
        def _():
            spread_forward(0, grads.at[1])


        put_sums(1, *sums_forward(n2))
        total = sum_end(1, 8, sum_start(1, 8)) * inverse
        average2, cross2 = total[0:1], total[1:2]
        scale2, gain2 = row(channel, 2), row(channel, 3)
        tan_scale_two = -scale2 * scale2 * cross2
        move_gain2, move_shift2 = row(move_norm, 2), row(move_norm, 3)

        def forward_two(cell, carry):
            normal = n2[cell]
            tangent = scale2 * (flow[cell] - average2 - normal * cross2)
            inner = move_gain2 * normal + gain2 * tangent + move_shift2
            nt2[cell] = tangent
            in2[cell] = inner
            return carry + s2[cell] * inner

        tan_pooled = each_cell(forward_two, zero) * (1.0 / 16.0)
        tan_logits = sum_parts(
            mul_exact(tan_pooled, head[...], ((1,), (1,)))
            + mul_exact(pooled[...], move_head[...], ((1,), (1,)))
        )
        chance = chances[...]
        tan_pull = (
            weights[...]
            * chance
            * (tan_logits - jnp.sum(chance * tan_logits, axis=1, keepdims=True))
        )
        out_head = mul_exact(pull_logits[...], tan_pooled, ((0,), (0,))) + mul_exact(
            tan_pull, pooled[...], ((0,), (0,))
        )
        tan_block = (
            mul_exact(tan_pull, head[...]) + mul_exact(pull_logits[...], move_head[...])
        ) * (1.0 / 16.0)

        def back_two(cell, carry):
            tangent = tan_block * s2[cell] + pb2[cell] * in2[cell]
            flow[cell] = tangent
            return (
                carry[0] + tangent * n2[cell] + pull2[cell] * nt2[cell],
                carry[1] + tangent,
            )

        put_sums(2, *each_cell(back_two, (zero, zero)))
        stats_own[2, 8:24, :] = out_head[0:16]
        total = sum_end(2, 24, sum_start(2, 24))
        out_gain2, out_shift2 = total[0:1], total[1:2]
        move_head[0:16] = move_head[0:16] - neumann_rate * total[8:24]
        factor2 = scale2 * gain2
        tan_factor2 = tan_scale_two * gain2 + scale2 * move_gain2

        def pull_two_body(cell, _):
            slots[part, cell] = tan_factor2 * c2[cell] + factor2 * (
                flow[cell]
                - out_shift2 * inverse
                - nt2[cell] * row(channel, 5)
                - n2[cell] * (out_gain2 * inverse)
            )

        each_cell(pull_two_body)

        def turn_of_block(block):
            turn_block(block, t_left, t_turned)
            use_block(block, t_left, t_turned, k_hi, k_lo, a_both)

        more = turn < NEUMANN - 1
        gather_and_use(turn_of_block, next_vector, more)

        def back_one(cell, carry):
            pull = fold_sum[cell // 4 + 1, cell % 4 + 1]
            tangent = pull * s1[cell] + pb1[cell] * in1[cell]
            flow[cell] = tangent
            return (
                carry[0] + tangent * n1[cell] + pull1[cell] * nt1[cell],
                carry[1] + tangent,
            )

        put_sums(3, *each_cell(back_one, (zero, zero)))
        moves = sum_start(3, 8)
        rest_of_two(next_vector, more)
        total = sum_end(3, 8, moves)
        out_gain, out_shift = total[0:1], total[1:2]
        factor = scale * gain
        tan_factor = tan_scale_one * gain + scale * move_gain

        def pull_one_body(cell, _):
            flow[cell] = tan_factor * c1[cell] + factor * (
                flow[cell]
                - out_shift * inverse
                - nt1[cell] * row(channel, 4)
                - n1[cell] * (out_gain * inverse)
            )

        each_cell(pull_one_body)
        turned[...] = jnp.concatenate(halves(flow[...].reshape(16 * count, LANES).T), axis=0)
        move_norm[0:1, :] = move_gain - neumann_rate * out_gain
        move_norm[1:2, :] = move_shift - neumann_rate * out_shift
        move_norm[2:3, :] = move_gain2 - neumann_rate * out_gain2
        move_norm[3:4, :] = move_shift2 - neumann_rate * out_shift2
        first_gradient()
        end_of_two(next_vector, more)
        back_forward_when(order[3], more)

        @pl.when(turn == NEUMANN - 1)
        def _():
            deliver_start(1, series_two)

        for group in range(GROUPS):
            step_group(group, next_vector)

            @pl.when(more)
            def _():
                back_start(group)

    lax.fori_loop(0, NEUMANN, turn_body, None)

    series[0, copy] = series_one[...]
    spread_start(1, series.at[0])
    deliver_end(1, series_two, series.at[1])
    spread_start(2, series.at[1])
    spread_forward(1, series.at[0])
    spread_forward(2, series.at[1])
    spread_end(0, grads.at[1])
    spread_end(1, series.at[0])
    spread_end(2, series.at[1])


def step_fused(links, rows, images, conv_weights, decay_rates, norm_params, head_weights, labels, valid):
    own_count, channels = images.shape[2:]
    cells, count = MAP * MAP, own_count * 4
    width, group = channels // 4, 8
    piece, block = width // group, channels // group
    classes = head_weights.shape[1]
    f32, b16 = jnp.float32, jnp.bfloat16

    small = jnp.zeros((24, width), f32)
    lane = links.member * block
    small = lax.dynamic_update_slice(small, norm_params, (0, lane))
    small = lax.dynamic_update_slice(small, head_weights.T, (8, lane))
    chosen = (labels[:, None] == jnp.arange(LANES, dtype=jnp.int32)[None, :]).astype(f32)
    tags = jnp.zeros((2, count, LANES), f32)
    tags = lax.dynamic_update_slice(
        tags,
        jnp.stack([chosen, jnp.broadcast_to(valid[:, None], chosen.shape)]),
        (0, links.part * own_count, 0),
    )
    operands = (
        images.reshape(cells, own_count, channels),
        conv_weights.reshape(2, 4, piece, TAPS * channels),
        decay_rates.reshape(2, 4, piece, TAPS * channels),
        small,
        tags.reshape(2 * count, LANES),
    )
    vmem = pl.BlockSpec(memory_space=pltpu.VMEM)
    anywhere = pl.BlockSpec(memory_space=pl.ANY)
    row_map = pltpu.VMEM((cells, count, width), f32)
    four_maps = pltpu.VMEM((4, cells, count, width), f32)
    inner_piece = pltpu.VMEM((4, piece, TAPS * width), f32)
    inner_half = pltpu.VMEM((4, 4, piece, TAPS * width), f32)
    inner_part = pltpu.VMEM((channels, TAPS * width), b16)
    outer_part = pltpu.VMEM((TAPS, width, channels), b16)
    both = pltpu.VMEM((MAP + 2, MAP + 2, count, 2 * width), b16)
    logit = pltpu.VMEM((count, LANES), f32)
    dma = pltpu.SemaphoreType.DMA
    scratch = [
        pltpu.VMEM((piece, TAPS * channels), f32),
        inner_piece,
        inner_piece,
        pltpu.VMEM((2, 4, piece, TAPS * width), f32),
        pltpu.VMEM((2, piece, TAPS * channels), f32),
        pltpu.VMEM((2, 4, piece, TAPS * width), f32),
        pltpu.VMEM((TAPS, piece, channels), f32),
        inner_piece,
        pltpu.VMEM((TAPS, group, piece, channels), f32),
        pltpu.VMEM((group, 4, piece, TAPS * width), f32),
        outer_part,
        outer_part,
        inner_part,
        inner_part,
        inner_part,
        inner_part,
        pltpu.VMEM((4, cells, own_count, channels), f32),
        pltpu.VMEM((count, channels), f32),
        pltpu.VMEM((MAP + 2, MAP + 2, count, 2 * channels), b16),
        row_map,
        both,
        both,
        pltpu.VMEM((4, cells * count, 2 * width), b16),
        pltpu.VMEM((4, 2 * width, cells * count), b16),
        pltpu.VMEM((cells * count, 2 * width), b16),
        pltpu.VMEM((2 * width, cells * count), b16),
        four_maps,
        four_maps,
        four_maps,
        four_maps,
        *[row_map] * 15,
        pltpu.VMEM((MAP + 2, MAP + 2, count, width), f32),
        pltpu.VMEM((TAPS, 4, 2, piece, channels), f32),
        pltpu.VMEM((4, 4, 2, piece, TAPS * width), f32),
        pltpu.VMEM((TAPS, 4, piece, channels), f32),
        inner_half,
        pltpu.VMEM((4, TAPS, piece, channels), f32),
        inner_half,
        pltpu.VMEM((4, 8, 24, width), f32),
        pltpu.VMEM((4, 24, width), f32),
        pltpu.VMEM((4, count, LANES), f32),
        logit,
        pltpu.VMEM((24, width), f32),
        pltpu.VMEM((4, 2 * count, LANES), f32),
        pltpu.VMEM((2 * width, cells * count), b16),
        pltpu.VMEM((8, width), f32),
        pltpu.VMEM((8, width), f32),
        pltpu.VMEM((LANES, width), f32),
        pltpu.VMEM((LANES, width), f32),
        logit,
        logit,
        logit,
        logit,
        dma(()),
        dma((2,)),
        dma((2,)),
        dma((TAPS,)),
        dma((TAPS,)),
        dma((TAPS,)),
        dma((TAPS,)),
        dma((2, 4)),
        dma((2, 4)),
        dma((4,)),
        dma((4,)),
        dma((2, 4, 2)),
        dma((4, 2)),
        dma((4, 8)),
        dma((4, 8)),
        dma((4,)),
        dma((4,)),
        dma((4, 2)),
        dma((4, 2)),
        dma((4, 2)),
        dma((4, 2)),
        dma((2, 4, 2)),
        dma((4, 2)),
        dma((GROUPS + 4,)),
        dma((GROUPS + 4,)),
        dma((GROUPS + 4, 4)),
        dma((GROUPS + 4, 4)),
        dma((GROUPS + 4, 4)),
        dma((GROUPS + 4, 4)),
        dma((GROUPS + 4, 4)),
        dma((GROUPS + 4, 4)),
        dma((2, 4)),
        dma((2, 4)),
        dma((3, 3)),
        dma((3, 3)),
    ]
    result = jax.ShapeDtypeStruct((2, 4, piece, TAPS * channels), f32)
    grads, series, grad_small = pl.pallas_call(
        functools.partial(step_kernel, rows, links.members, links.copies, classes),
        out_shape=(result, result, jax.ShapeDtypeStruct((32, width), f32)),
        in_specs=[anywhere] * 3 + [vmem] * 2,
        out_specs=(vmem,) * 3,
        scratch_shapes=scratch,
        compiler_params=pltpu.CompilerParams(
            collective_id=1, has_side_effects=True, vmem_limit_bytes=63 * 1024 * 1024
        ),
        name="train_step",
    )(*operands)
    own = lax.dynamic_slice_in_dim(grad_small, lane, block, 1)
    return (
        grad_small[0, 0],
        grad_small[1, 0],
        grads.reshape(conv_weights.shape),
        own[8:12],
        own[16 : 16 + classes].T,
        series.reshape(conv_weights.shape),
    )


def adamw(weight, grad, first, second, rate):
    first = beta_first * first + (1.0 - beta_first) * grad
    second = beta_second * second + (1.0 - beta_second) * grad * grad
    first_hat = first / (1.0 - beta_first**STEP)
    second_hat = second / (1.0 - beta_second**STEP)
    update = first_hat / (jnp.sqrt(second_hat) + adam_eps) + decoupled * weight
    return (weight - rate * update, first, second)


def silu_parts(value):
    gate = jax.nn.sigmoid(value)
    slope = gate * (1.0 - gate)
    first = gate + value * slope
    second = slope * (2.0 + value * (1.0 - 2.0 * gate))
    return value * gate, first, second


class Links:
    def __init__(self):
        self.shards = lax.axis_size("shard")
        self.copies = lax.axis_size("dp")
        self.parts = 4 if self.shards % 4 == 0 else 1
        self.members = self.shards // self.parts
        index = lax.axis_index("shard")
        self.part = index // self.members
        self.member = index % self.members
        self.across = [
            [p * self.members + m for p in range(self.parts)] for m in range(self.members)
        ]
        self.within = [
            [p * self.members + m for m in range(self.members)] for p in range(self.parts)
        ]

    def sum_rows(self, value):
        value = lax.psum(value, "dp")
        gathered = lax.all_gather(value, "shard", axis_index_groups=self.within)
        return jnp.sum(gathered, axis=0)

    def sum_parts(self, value):
        return jnp.sum(lax.all_gather(value, "shard", axis_index_groups=self.across), axis=0)

    def gather_parts(self, value, axis):
        return lax.all_gather(value, "shard", axis_index_groups=self.across, axis=axis, tiled=True)

    def gather_members(self, value, axis):
        return lax.all_gather(value, "shard", axis_index_groups=self.within, axis=axis, tiled=True)

    def scatter_parts(self, value, axis):
        return lax.psum_scatter(
            value, "shard", axis_index_groups=self.across, scatter_dimension=axis, tiled=True
        )

    def to_inner(self, value):
        rows, channels = value.shape[0], value.shape[1] // TAPS
        width = channels // self.parts
        cut = value.reshape(rows, TAPS, self.parts, width).transpose(2, 0, 1, 3)
        moved = lax.all_to_all(cut, "shard", 0, 0, axis_index_groups=self.across, tiled=True)
        whole = self.gather_members(moved, 1)
        return whole.reshape(channels, TAPS * width)

    def to_outer(self, value):
        channels, width = value.shape[0], value.shape[1] // TAPS
        rows = channels // self.shards
        cut = value.reshape(self.parts, self.members, rows, TAPS * width)
        cut = lax.dynamic_index_in_dim(cut, self.member, 1, keepdims=False)
        moved = lax.all_to_all(cut, "shard", 0, 0, axis_index_groups=self.across, tiled=True)
        moved = moved.reshape(self.parts, rows, TAPS, width).transpose(1, 2, 0, 3)
        return moved.reshape(rows, TAPS * channels)

    def own_rows(self, value, axis=0):
        size = value.shape[axis] // self.members
        return lax.dynamic_slice_in_dim(value, self.member * size, size, axis)


def moments(hidden, rows, links):
    totals = links.sum_rows(jnp.stack([jnp.sum(hidden, axis=0), jnp.sum(hidden * hidden, axis=0)]))
    average = totals[0] / rows
    scale = lax.rsqrt(totals[1] / rows - average * average + norm_eps)
    return (hidden - average) * scale, scale


def moments_tangent(normal, scale, tangent, rows, links):
    totals = links.sum_rows(
        jnp.stack([jnp.sum(tangent, axis=0), jnp.sum(tangent * normal, axis=0)])
    )
    average, cross = totals[0] / rows, totals[1] / rows
    return scale * (tangent - average - normal * cross), -scale * scale * cross


def step_general(
    links, rows, images, conv_weights, decay_rates, norm_params, head_weights, labels, valid
):
    own_images, channels = images.shape[2:]
    count = own_images * links.parts
    width = channels // links.parts
    first_column = links.part * width
    label_total = lax.psum(jnp.sum(valid), ("shard", "dp"))
    images = links.gather_parts(images, 2)
    labels = links.gather_parts(labels, 0)
    valid = links.gather_parts(valid, 0)

    kernel_one = links.gather_members(conv_weights[0], 0)
    kernel_two = links.to_inner(conv_weights[1])
    decay_one = links.gather_members(decay_rates[0], 0)
    decay_two = links.to_inner(decay_rates[1])
    norms = links.gather_members(norm_params, 1)
    head = links.gather_members(head_weights, 0)
    gain_one, shift_one, gain_two, shift_two = norms[0], norms[1], norms[2], norms[3]

    def pool(value):
        return jnp.sum(value.reshape(MAP * MAP, count, width), axis=0) / (MAP * MAP)

    def spread(value):
        whole = jnp.broadcast_to(value[None] / (MAP * MAP), (MAP * MAP, count, width))
        return whole.reshape(MAP * MAP * count, width)

    columns = patches(images)
    own_columns = lax.dynamic_slice_in_dim(
        images.reshape(MAP * MAP * count, channels), first_column, width, 1
    )

    hidden_one = dot(columns, kernel_one, ((1,), (1,)))
    normal_one, scale_one = moments(hidden_one, rows, links)
    active, slope_one, bend_one = silu_parts(normal_one * gain_one + shift_one)
    active_columns = patches(active.reshape(MAP, MAP, count, width))
    hidden_two = links.scatter_parts(dot(active_columns, kernel_two, ((1,), (1,))), 1)
    normal_two, scale_two = moments(hidden_two, rows, links)
    block, slope_two, bend_two = silu_parts(normal_two * gain_two + shift_two + own_columns)
    pooled = pool(block)
    logits = links.sum_parts(dot(pooled, head, ((1,), (0,))))
    highest = jnp.max(logits, axis=1, keepdims=True)
    powers = jnp.exp(logits - highest)
    total = jnp.sum(powers, axis=1, keepdims=True)
    chances = powers / total
    classes = jnp.arange(logits.shape[1], dtype=jnp.int32)
    chosen = (labels[:, None] == classes[None, :]).astype(jnp.float32)
    cross = highest[:, 0] + jnp.log(total[:, 0]) - jnp.sum(chosen * logits, axis=1)
    loss_sum = links.sum_rows(jnp.sum(valid * cross)[None])[0]
    weights = (valid / label_total)[:, None]
    pull_logits = weights * (chances - chosen)
    grad_head = dot(pooled, pull_logits, ((0,), (0,)))
    pull_block = spread(dot(pull_logits, head, ((1,), (1,))))
    pull_two = pull_block * slope_two
    sums_two = links.sum_rows(
        jnp.stack([jnp.sum(pull_two * normal_two, axis=0), jnp.sum(pull_two, axis=0)])
    )
    centred_two = pull_two - sums_two[1] / rows - normal_two * (sums_two[0] / rows)
    factor_two = scale_two * gain_two
    pull_hidden_two = links.gather_parts(factor_two * centred_two, 1)
    grad_two = dot(pull_hidden_two, active_columns, ((0,), (0,)))
    pull_active = fold(dot(pull_hidden_two, kernel_two, ((1,), (0,))), count)
    pull_one = pull_active * slope_one
    sums_one = links.sum_rows(
        jnp.stack([jnp.sum(pull_one * normal_one, axis=0), jnp.sum(pull_one, axis=0)])
    )
    centred_one = pull_one - sums_one[1] / rows - normal_one * (sums_one[0] / rows)
    factor_one = scale_one * gain_one
    grad_one = dot(factor_one * centred_one, columns, ((0,), (0,)))

    grad_one = links.sum_rows(grad_one) + decay_one * kernel_one
    grad_two = links.sum_rows(grad_two) + decay_two * kernel_two
    grad_head = links.sum_rows(grad_head)
    grad_norm = jnp.concatenate([sums_one, sums_two])

    def product(vector):
        move_one, move_two, move_norm, move_head = vector
        tan_hidden = dot(columns, move_one, ((1,), (1,)))
        tan_normal_one, tan_scale_one = moments_tangent(
            normal_one, scale_one, tan_hidden, rows, links
        )
        tan_inner = move_norm[0] * normal_one + gain_one * tan_normal_one + move_norm[1]
        tan_active = slope_one * tan_inner
        tan_columns = patches(tan_active.reshape(MAP, MAP, count, width))
        tan_hidden = links.scatter_parts(
            dot(tan_columns, kernel_two, ((1,), (1,))) + dot(active_columns, move_two, ((1,), (1,))),
            1,
        )
        tan_normal_two, tan_scale_two = moments_tangent(
            normal_two, scale_two, tan_hidden, rows, links
        )
        tan_outer = move_norm[2] * normal_two + gain_two * tan_normal_two + move_norm[3]
        tan_pooled = pool(slope_two * tan_outer)
        tan_logits = links.sum_parts(
            dot(tan_pooled, head, ((1,), (0,))) + dot(pooled, move_head, ((1,), (0,)))
        )
        tan_chances = chances * (tan_logits - jnp.sum(chances * tan_logits, axis=1, keepdims=True))
        tan_pull = weights * tan_chances
        out_head = dot(tan_pooled, pull_logits, ((0,), (0,))) + dot(pooled, tan_pull, ((0,), (0,)))
        tan_block = spread(
            dot(tan_pull, head, ((1,), (1,))) + dot(pull_logits, move_head, ((1,), (1,)))
        )
        tan_two = tan_block * slope_two + pull_block * bend_two * tan_outer
        tan_sums_two = links.sum_rows(
            jnp.stack(
                [
                    jnp.sum(tan_two * normal_two + pull_two * tan_normal_two, axis=0),
                    jnp.sum(tan_two, axis=0),
                ]
            )
        )
        tan_factor = tan_scale_two * gain_two + scale_two * move_norm[2]
        tan_hidden = tan_factor * centred_two + factor_two * (
            tan_two
            - tan_sums_two[1] / rows
            - tan_normal_two * (sums_two[0] / rows)
            - normal_two * (tan_sums_two[0] / rows)
        )
        tan_hidden = links.gather_parts(tan_hidden, 1)
        out_two = dot(tan_hidden, active_columns, ((0,), (0,))) + dot(
            pull_hidden_two, tan_columns, ((0,), (0,))
        )
        tan_pull_active = fold(
            dot(tan_hidden, kernel_two, ((1,), (0,))) + dot(pull_hidden_two, move_two, ((1,), (0,))),
            count,
        )
        tan_one = tan_pull_active * slope_one + pull_active * bend_one * tan_inner
        tan_sums_one = links.sum_rows(
            jnp.stack(
                [
                    jnp.sum(tan_one * normal_one + pull_one * tan_normal_one, axis=0),
                    jnp.sum(tan_one, axis=0),
                ]
            )
        )
        tan_factor = tan_scale_one * gain_one + scale_one * move_norm[0]
        tan_hidden = tan_factor * centred_one + factor_one * (
            tan_one
            - tan_sums_one[1] / rows
            - tan_normal_one * (sums_one[0] / rows)
            - normal_one * (tan_sums_one[0] / rows)
        )
        out_one = dot(tan_hidden, columns, ((0,), (0,)))
        return (
            links.sum_rows(out_one) + decay_one * move_one,
            links.sum_rows(out_two) + decay_two * move_two,
            jnp.concatenate([tan_sums_one, tan_sums_two]),
            links.sum_rows(out_head),
        )

    vector = (grad_one, grad_two, grad_norm, grad_head)
    series_one, series_two = grad_one, grad_two
    for turn in range(NEUMANN):
        change = product(vector)
        vector = tuple(
            previous - neumann_rate * moved for previous, moved in zip(vector, change)
        )
        series_one, series_two = series_one + vector[0], series_two + vector[1]

    series = jnp.stack([links.own_rows(series_one), links.to_outer(series_two)])
    grads = jnp.stack([links.own_rows(grad_one), links.to_outer(grad_two)])
    return (
        loss_sum,
        label_total,
        grads,
        links.own_rows(grad_norm, 1),
        links.own_rows(grad_head),
        series,
    )


def shards(
    source,
    index_map,
    crop_offsets,
    flip_flags,
    labels,
    valid_mask,
    conv_weights,
    norm_params,
    head_weights,
    decay_rates,
    conv_first,
    conv_second,
    norm_first,
    norm_second,
    head_first,
    head_second,
):
    links = Links()
    rows = float(source.shape[0] * MAP * MAP * links.shards * links.copies)
    picked = source[index_map]
    images = jax.vmap(crop_image)(picked, crop_offsets, flip_flags)
    images = images.transpose(1, 2, 0, 3)
    fused = links.members * links.copies == 8 and links.parts == 4
    loss_sum, label_total, grads, grad_norm, grad_head, series = (
        step_fused if fused else step_general
    )(
        links,
        rows,
        images,
        conv_weights,
        decay_rates,
        norm_params,
        head_weights,
        labels,
        valid_mask.astype(jnp.float32),
    )
    hyper_gradient = -neumann_rate * conv_weights * series
    conv_new, conv_one, conv_two = adamw(conv_weights, grads, conv_first, conv_second, 0.015)
    norm_new, norm_one, norm_two = adamw(
        norm_params, grad_norm, norm_first, norm_second, 0.3
    )
    head_new, head_one, head_two = adamw(
        head_weights, grad_head, head_first, head_second, 0.13
    )
    return (
        loss_sum,
        label_total,
        conv_new,
        conv_one,
        conv_two,
        norm_new,
        norm_one,
        norm_two,
        head_new,
        head_one,
        head_two,
        hyper_gradient,
    )


def solution(mesh):
    images = P(("shard", "dp"))
    rows = P(None, "shard")
    head = P("shard")
    in_specs = (images,) * 6 + (rows, rows, head, rows, rows, rows, rows, rows, head, head)
    out_specs = (P(), P()) + (rows,) * 6 + (head,) * 3 + (rows,)
    return jax.shard_map(shards, mesh=mesh, in_specs=in_specs, out_specs=out_specs, check_vma=False)
```

```python
import functools

import jax
import jax.numpy as jnp
from jax import lax
from jax.experimental import pallas as pl
from jax.experimental.pallas import tpu as pltpu
from jax.sharding import PartitionSpec as P

MAP = 4
NEUMANN = 3
STEP = 5
TAPS = 9

norm_eps = 1e-05
neumann_rate = 10.0
beta_first = 0.5
beta_second = 0.5
adam_eps = 1e-08
decoupled = 0.01
HIGH = lax.Precision.HIGH


def crop_image(single, offsets, flipped):
    window = lax.dynamic_slice(
        single, (offsets[0], offsets[1], jnp.int32(0)), (MAP, MAP, single.shape[2])
    )
    return jnp.where(flipped == 1, window[:, ::-1, :], window)


def patches(maps):
    count, width = maps.shape[2:]
    padded = jnp.pad(maps, ((1, 1), (1, 1), (0, 0), (0, 0)))
    taps = [padded[dy : dy + MAP, dx : dx + MAP] for dy in range(3) for dx in range(3)]
    return jnp.concatenate(taps, axis=3).reshape(MAP * MAP * count, TAPS * width)


def fold(columns, count):
    width = columns.shape[1] // TAPS
    whole = columns.reshape(MAP, MAP, count, TAPS, width)
    padded = jnp.pad(whole, ((1, 1), (1, 1), (0, 0), (0, 0), (0, 0)))
    total = 0.0
    for dy in range(3):
        for dx in range(3):
            total = total + padded[2 - dy : 2 - dy + MAP, 2 - dx : 2 - dx + MAP, :, dy * 3 + dx]
    return total.reshape(MAP * MAP * count, width)


def dot(left, right, dims):
    return lax.dot_general(
        left, right, ((dims[0], dims[1]), ((), ())), precision=HIGH, preferred_element_type=jnp.float32
    )


MESH_ID = pl.DeviceIdType.MESH
LANES = 128
GROUPS = 3


def halves(value):
    high = value.astype(jnp.bfloat16)
    return high, (value - high.astype(jnp.float32)).astype(jnp.bfloat16)


def mul(left, right, dims=((1,), (0,))):
    return lax.dot_general(left, right, (dims, ((), ())), preferred_element_type=jnp.float32)


def mul_exact(left, right, dims=((1,), (0,))):
    return lax.dot_general(
        left,
        right,
        (dims, ((), ())),
        precision=lax.Precision.HIGHEST,
        preferred_element_type=jnp.float32,
    )


def silu_pieces(value):
    gate = 1.0 / (1.0 + jnp.exp(-value))
    slope = gate * (1.0 - gate)
    return value * gate, gate + value * slope, slope * (2.0 + value * (1.0 - 2.0 * gate))


def step_kernel(
    rows,
    members,
    copies,
    classes,
    source,
    index_map,
    crop_offsets,
    flip_flags,
    labels,
    valid_mask,
    weights_in,
    decay_in,
    pair_in,
    grads,
    series,
    grad_small,
    series_one,
    series_two,
    grad_source,
    row_parts,
    row_box,
    cut_box,
    d1,
    d2,
    v1,
    v2,
    v1_hi,
    v1_lo,
    v2_hi,
    v2_lo,
    k_hi,
    k_lo,
    source_box,
    x_box,
    x_row,
    x_both,
    x_own,
    a_both,
    b_both,
    g_left,
    g_turned,
    t_left,
    t_turned,
    slots,
    partial,
    from_low,
    from_high,
    flow,
    n1,
    s1,
    pb1,
    pull1,
    c1,
    n2,
    s2,
    pb2,
    pull2,
    c2,
    nt1,
    in1,
    nt2,
    in2,
    fold_sum,
    sum_one,
    sum_two,
    half_one,
    half_two,
    first_low,
    first_up,
    second_low,
    second_up,
    piece_two,
    stats_box,
    stats_own,
    logit_box,
    logit_own,
    pair_box,
    label_box,
    turned,
    channel,
    move_norm,
    move_head,
    head,
    pooled,
    chances,
    weights,
    pull_logits,
    x_load,
    pair_sem,
    cut_load,
    k1_load,
    d1_load,
    k1_send,
    k1_recv,
    first_send,
    first_recv,
    label_send,
    label_recv,
    x_send,
    x_recv,
    stats_send,
    stats_recv,
    logit_send,
    logit_recv,
    up_send,
    up_recv,
    down_send,
    down_recv,
    ring_send,
    ring_recv,
    pair_send,
    pair_recv,
    plane_send,
    plane_recv,
    back_send,
    back_recv,
    swap_send,
    swap_recv,
    fold_send,
    fold_recv,
    open_send,
    open_recv,
    share_send,
    share_recv,
    row_send,
    row_recv,
    own_send,
    own_recv,
):
    shard = lax.axis_index("shard")
    copy = lax.axis_index("dp")
    part = shard // members
    member = shard % members
    me = member * copies + copy
    place, line, core = me // 2, (me // 2) % 2, me % 2
    last = 3
    count = flow.shape[1]
    own_count = source.shape[0]
    inverse = 1.0 / rows
    zero = jnp.zeros((count, LANES), jnp.float32)

    def row_peer(other):
        return (part * members + other // copies, other % copies)

    def part_peer(other):
        return (other * members + member, copy)

    def remote(source, target, send, recv, device):
        return pltpu.make_async_remote_copy(
            src_ref=source,
            dst_ref=target,
            send_sem=send,
            recv_sem=recv,
            device_id=device,
            device_id_type=MESH_ID,
        )

    def greet(device):
        pl.semaphore_signal(barrier, inc=1, device_id=device, device_id_type=MESH_ID)

    barrier = pltpu.get_barrier_semaphore()
    for step in range(1, 8):
        greet(row_peer(me ^ step))
    for step in range(1, 4):
        greet(part_peer(part ^ step))
    channels = source.shape[3]

    def tap_lanes(tap, width):
        return pl.ds(pl.multiple_of(tap * width, width), width)

    source_load = pltpu.make_async_copy(source, source_box, x_load)
    source_load.start()
    k1_loads = [
        pltpu.make_async_copy(
            weights_in.at[0, :, :, :, pl.ds(tap * channels, channels)],
            v1.at[tap, member],
            k1_load.at[tap],
        )
        for tap in range(TAPS)
    ]
    d1_loads = [
        pltpu.make_async_copy(
            decay_in.at[0, line, core, :, pl.ds(tap * channels, channels)], d1.at[tap], d1_load.at[tap]
        )
        for tap in range(TAPS)
    ]
    cut_loads = [
        pltpu.make_async_copy(weights_in.at[1, line, core], row_box.at[0], cut_load.at[0]),
        pltpu.make_async_copy(decay_in.at[1, line, core], row_box.at[1], cut_load.at[1]),
    ]
    for load in cut_loads + k1_loads + d1_loads:
        load.start()
    stats_own[...] = jnp.zeros_like(stats_own)
    channel[...] = jnp.zeros_like(channel)
    x_both[...] = jnp.zeros_like(x_both)
    a_both[...] = jnp.zeros_like(a_both)
    b_both[...] = jnp.zeros_like(b_both)
    label_box[0] = jnp.zeros(label_box.shape[1:], jnp.float32)
    lane = lax.broadcasted_iota(jnp.int32, (1, LANES), 1)

    def tag_image(image, _):
        at = part * own_count + image
        label_box[0, pl.ds(at, 1), :] = (lane == labels[image]).astype(jnp.float32)
        label_box[0, pl.ds(count + at, 1), :] = jnp.full(
            (1, LANES), valid_mask[image].astype(jnp.float32)
        )

    lax.fori_loop(0, own_count, tag_image, None)
    source_load.wait()

    def crop(image, _):
        picked, flipped = index_map[image], flip_flags[image]
        top, left = crop_offsets[image, 0], crop_offsets[image, 1]
        for cell in range(16):
            column = left + jnp.where(flipped == 1, 3 - cell % 4, cell % 4)
            x_box[part, cell, pl.ds(image, 1), :] = source_box[
                picked, top + cell // 4, pl.ds(column, 1), :
            ]

    lax.fori_loop(0, own_count, crop, None)
    pl.semaphore_wait(barrier, 10)

    def ring_move(box, send, recv, block, step, way, half):
        at = pl.ds(half * 8, 8)
        return remote(
            box.at[block, at],
            box.at[block, at],
            send.at[0 if way > 0 else 1, step, half],
            recv.at[block, half],
            part_peer(part + way),
        )

    def ring_start(box, send, recv):
        for half in range(2):

            @pl.when(part < last)
            def _():
                ring_move(box, send, recv, part, 0, 1, half).start()

            @pl.when(part > 0)
            def _():
                ring_move(box, send, recv, part, 0, -1, half).start()

    def ring_step(box, send, recv, step):
        for half in range(2):

            @pl.when(part >= step)
            def _():
                ring_move(box, send, recv, part - step, step, -1, half).wait_recv()

                @pl.when(part < last)
                def _():
                    ring_move(box, send, recv, part - step, step, 1, half).start()

            @pl.when(part + step <= last)
            def _():
                ring_move(box, send, recv, part + step, step, 1, half).wait_recv()

                @pl.when(part > 0)
                def _():
                    ring_move(box, send, recv, part + step, step, -1, half).start()

    def ring_end(box, send, recv):
        for step in range(0, 3):
            for half in range(2):

                @pl.when((part >= step) & (part < last))
                def _():
                    ring_move(box, send, recv, part - step, step, 1, half).wait_send()

                @pl.when((part + step <= last) & (part > 0))
                def _():
                    ring_move(box, send, recv, part + step, step, -1, half).wait_send()

    order = (
        part,
        jnp.where(part == 0, 1, part - 1),
        jnp.where(part == 3, 1, jnp.where(part == 2, 3, 2)),
        jnp.where(part < 2, 3, 0),
    )

    ring_start(x_box, x_send, x_recv)
    partner = row_peer(me ^ copies)
    k1_moves = [
        remote(
            weights_in.at[0, :, :, :, pl.ds(tap * channels, channels)],
            v1.at[tap, member],
            k1_send.at[tap],
            k1_recv.at[tap],
            partner,
        )
        for tap in range(TAPS)
    ]
    for move in k1_moves:
        move.start()

    def cut_move(which, other):
        box = v2.at[me, part] if which == 0 else d2.at[part]
        return remote(
            cut_box.at[which, other],
            box,
            first_send.at[which, other],
            first_recv.at[which, part],
            part_peer(other),
        )

    def cut_start(which):
        for other in range(4):
            for tap in range(TAPS):
                start = tap * channels + other * LANES
                cut_box[which, other, :, tap * LANES : (tap + 1) * LANES] = row_box[
                    which, :, start : start + LANES
                ]
        for other in range(4):

            @pl.when(part != other)
            def _():
                cut_move(which, other).start()

        if which == 0:
            v2[me, part] = cut_box[which, part]
        else:
            d2[part] = cut_box[which, part]

    def cut_end(which):
        for other in range(4):

            @pl.when(part != other)
            def _():
                cut_move(which, other).wait_send()
                box = v2.at[me, other] if which == 0 else d2.at[other]
                remote(
                    cut_box.at[which, other],
                    box,
                    first_send.at[which, other],
                    first_recv.at[which, other],
                    part_peer(other),
                ).wait_recv()

    pair_move = remote(pair_in, pair_box, pair_sem.at[0], pair_sem.at[1], partner)
    pair_move.start()
    label_moves = [
        remote(
            label_box.at[0],
            label_box.at[step],
            label_send.at[step],
            label_recv.at[step],
            part_peer(part ^ step),
        )
        for step in range(1, 4)
    ]
    for move in label_moves:
        move.start()

    pair = row_peer(me ^ 1)

    def piece_of(which, other):
        return v2.at[other, which[0]]

    def lane_of(which):
        return which[0]

    def to_plane(which, step):
        piece, at = piece_of(which, me), lane_of(which)
        return remote(
            piece, piece, back_send.at[at, step], back_recv.at[at, step], row_peer(me ^ (2 * step))
        )

    def from_plane(which, step):
        piece, at = piece_of(which, me ^ (2 * step)), lane_of(which)
        return remote(piece, piece, back_send.at[at, step], back_recv.at[at, step], pair)

    def to_pair(which, step):
        piece, at = piece_of(which, me ^ (2 * step)), lane_of(which)
        return remote(piece, piece, swap_send.at[at, step], swap_recv.at[at, step], pair)

    def from_pair(which, step):
        piece, at = piece_of(which, me ^ 1 ^ (2 * step)), lane_of(which)
        return remote(piece, piece, swap_send.at[at, step], swap_recv.at[at, step], pair)

    def back_start(which):
        for step in range(1, 4):
            to_plane(which, step).start()
        to_pair(which, 0).start()

    def back_forward(which):
        for step in range(1, 4):
            from_plane(which, step).wait_recv()
            to_pair(which, step).start()

    def back_arrived(which):
        for step in range(0, 4):
            from_pair(which, step).wait_recv()

    def back_end(which):
        for step in range(1, 4):
            to_plane(which, step).wait_send()
        for step in range(0, 4):
            to_pair(which, step).wait_send()

    for load in cut_loads:
        load.wait()
    cut_start(0)
    ring_step(x_box, x_send, x_recv, 1)
    cut_start(1)
    pair_move.wait()
    small = pair_in[...] + pair_box[...]
    move_norm[...] = small[0:8]
    head[...] = jnp.zeros_like(head)
    move_head[...] = jnp.zeros_like(move_head)
    head[0:16] = small[8:24]
    for move in label_moves:
        move.wait()
    tags = label_box[0] + label_box[1] + label_box[2] + label_box[3]
    chosen, valid = tags[:count], tags[count:]

    def each_cell(body, init=None):
        return lax.fori_loop(0, 16, body, init)

    def window(ref, down, right, lanes=slice(None)):
        seen = ref[pl.ds(down, 4), right : right + 4, :, lanes]
        return seen.reshape(16 * seen.shape[2], seen.shape[3])

    def row(ref, index):
        return ref[index : index + 1, :]

    def put_sums(site, first, second):
        stats_own[site, 0:1, :] = jnp.sum(first, axis=0, keepdims=True)
        stats_own[site, 1:2, :] = jnp.sum(second, axis=0, keepdims=True)

    def sum_start(site, size):
        moves = []
        for step in range(1, 8):
            move = remote(
                stats_own.at[site, pl.ds(0, size)],
                stats_box.at[site, step, pl.ds(0, size)],
                stats_send.at[site, step],
                stats_recv.at[site, step],
                row_peer(me ^ step),
            )
            move.start()
            moves.append(move)
        stats_box[site, 0, pl.ds(0, size)] = stats_own[site, pl.ds(0, size)]
        return moves

    def sum_end(site, size, moves):
        for move in moves:
            move.wait()
        total = stats_box[site, me, pl.ds(0, size)]
        for other in range(1, 8):
            total = total + stats_box[site, other ^ me, pl.ds(0, size)]
        return total

    def sum_parts(value):
        logit_own[...] = value
        moves = []
        for step in range(1, 4):
            move = remote(
                logit_own,
                logit_box.at[step],
                logit_send.at[step],
                logit_recv.at[step],
                part_peer(part ^ step),
            )
            move.start()
            moves.append(move)
        logit_box[0] = value
        for move in moves:
            move.wait()
        total = logit_box[part]
        for other in range(1, 4):
            total = total + logit_box[other ^ part]
        return total

    def split_one(tap, _):
        for other in range(8):
            at = slice(other * 16, other * 16 + 16)
            v1_hi[tap, at], v1_lo[tap, at] = halves(v1[tap, other // 4, other // 2 % 2, other % 2])

    def split_two(high, low):
        def body(other, _):
            for block in range(4):
                at = pl.ds(pl.multiple_of(block * LANES + other * 16, 16), 16)
                high[at], low[at] = halves(v2[other, block])

        lax.fori_loop(0, 8, body, None)

    def taps_forward(down):
        left, right = [], []
        for step in range(3):
            weight = jnp.concatenate([v1_hi[down * 3 + step], v1_lo[down * 3 + step]], axis=0)
            left.append(window(x_both, down, step))
            right += [weight, weight]
        out = mul(
            jnp.concatenate(left, axis=1), jnp.concatenate(right, axis=1), ((1,), (1,))
        )
        flow[...] += (out[:, :LANES] + out[:, LANES:]).reshape(flow.shape)

    def part_of_second(maps, high, low, half):
        at = pl.ds(pl.multiple_of(half * 256, 256), 256)

        def body(down, _):
            left, right = [], []
            for step in range(3):
                lanes = tap_lanes(down * 3 + step, LANES)
                seen = window(maps, down, step)
                weight_hi, weight_lo = high[at, lanes], low[at, lanes]
                left += [seen, seen[:, :LANES]]
                right += [weight_hi, weight_hi, weight_lo]
            out = mul(
                jnp.concatenate(left, axis=1), jnp.concatenate(right, axis=1), ((1,), (1,))
            )
            partial[half * 2] += out[:, :LANES].reshape(flow.shape)
            partial[half * 2 + 1] += out[:, LANES:].reshape(flow.shape)

        lax.fori_loop(0, 3, body, None)

    def up(block, half):
        at = pl.ds(half * 8, 8)
        return remote(
            partial.at[block, at],
            from_low.at[block, at],
            up_send.at[block, half],
            up_recv.at[block, half],
            part_peer(part + 1),
        )

    def down(block, half):
        at = pl.ds(half * 8, 8)
        return remote(
            partial.at[block, at],
            from_high.at[block, at],
            down_send.at[block, half],
            down_recv.at[block, half],
            part_peer(part - 1),
        )

    def scatter(maps, high, low, aside):
        near = jnp.where(part < 2, 1, 0)
        part_of_second(maps, high, low, near)

        @pl.when(part == 0)
        def _():
            for block in (3, 2):
                for half in range(2):
                    up(block, half).start()

        @pl.when(part == last)
        def _():
            for block in (0, 1):
                for half in range(2):
                    down(block, half).start()

        part_of_second(maps, high, low, 1 - near)
        for block in (3, 2, 1):
            goal = last - block

            for half in range(2):
                at = slice(half * 8, half * 8 + 8)

                @pl.when((part < block) & (part > 0))
                def _():
                    up(block, half).wait_recv()
                    partial[block, at] += from_low[block, at]
                    up(block, half).start()

                @pl.when((part > goal) & (part < last))
                def _():
                    down(goal, half).wait_recv()
                    partial[goal, at] += from_high[goal, at]
                    down(goal, half).start()

                if block == 1:

                    @pl.when(part == 0)
                    def _():
                        up(1, half).start()

                    @pl.when(part == last)
                    def _():
                        down(2, half).start()

            aside(3 - block)
        aside(3)
        for block in range(4):

            @pl.when(part == block)
            def _():
                for half in range(2):
                    at = slice(half * 8, half * 8 + 8)
                    total = partial[block, at]
                    if block > 0:
                        up(block, half).wait_recv()
                        total = total + from_low[block, at]
                    if block < last:
                        down(block, half).wait_recv()
                        total = total + from_high[block, at]
                    flow[at] = total

        for block in (3, 2, 1):
            goal = last - block
            for half in range(2):

                @pl.when(part < block)
                def _():
                    up(block, half).wait_send()

                @pl.when(part > goal)
                def _():
                    down(goal, half).wait_send()

    def turn_block(block, left, turned_block):
        value = slots[block].reshape(16 * count, LANES)
        left[...] = jnp.concatenate(halves(value), axis=1)
        turned_block[...] = jnp.concatenate(halves(value.T), axis=0)

    def use_block(block, left, turned_block, high, low, maps):
        at = pl.ds(pl.multiple_of(block * LANES, LANES), LANES)

        def body(down, _):
            right = []
            for step in range(3):
                lanes = tap_lanes(down * 3 + step, LANES)
                weight = jnp.concatenate([high[at, lanes], low[at, lanes]], axis=1)
                right.append(jnp.concatenate([weight, weight], axis=0))
            out = mul(left[...], jnp.concatenate(right, axis=1))
            for step in range(3):
                first = 2 * step * LANES
                fold_sum[pl.ds(down, 4), step : step + 4] += (
                    out[:, first : first + LANES] + out[:, first + LANES : first + 2 * LANES]
                ).reshape(4, 4, count, LANES)
            out = mul(
                turned_block[...],
                jnp.concatenate([window(maps, down, step) for step in range(3)], axis=1),
            )
            out = out[:LANES] + out[LANES:]
            for step in range(3):
                first = 2 * step * LANES
                sum_two[block, :, :, :, tap_lanes(down * 3 + step, LANES)] += (
                    out[:, first : first + LANES] + out[:, first + LANES : first + 2 * LANES]
                ).reshape(4, 2, 16, LANES)

        lax.fori_loop(0, 3, body, None)

    def pair_two(block):
        return remote(
            sum_two.at[block, :, 1 - core],
            half_two.at[block],
            pair_send.at[block],
            pair_recv.at[block],
            pair,
        )

    def plane_two(block, step):
        other = place ^ step
        return remote(
            half_two.at[block, other],
            piece_two.at[step, block],
            plane_send.at[block, step],
            plane_recv.at[block, step],
            row_peer(other * 2 + core),
        )

    def plane_two_go(block):
        pair_two(block).wait()
        for place_of in range(4):
            half_two[block, place_of] += sum_two[block, place_of, core]
        for step in range(1, 4):
            plane_two(block, step).start()

    def step_two(block, new_of, more):
        for step in range(1, 4):
            plane_two(block, step).wait()
        change = half_two[block, place] + piece_two[1, block] + piece_two[2, block] + piece_two[3, block]
        new = new_of(v2[me, block], change, d2[block])
        v2[me, block] = new
        series_two[block] += new

        @pl.when(more)
        def _():
            back_start((block,))

    def back_forward_when(block, more):
        @pl.when(more)
        def _():
            back_forward((block,))

    def gather_and_use(block_of, new_of, more):
        ring_start(slots, ring_send, ring_recv)
        block_of(order[0])
        pair_two(order[0]).start()
        ring_step(slots, ring_send, ring_recv, 1)
        block_of(order[1])
        pair_two(order[1]).start()
        plane_two_go(order[0])
        ring_step(slots, ring_send, ring_recv, 2)
        step_two(order[0], new_of, more)
        block_of(order[2])
        pair_two(order[2]).start()
        plane_two_go(order[1])
        ring_step(slots, ring_send, ring_recv, 3)
        step_two(order[1], new_of, more)
        block_of(order[3])
        pair_two(order[3]).start()
        plane_two_go(order[2])
        back_forward_when(order[0], more)
        ring_end(slots, ring_send, ring_recv)

    def rest_of_two(new_of, more):
        plane_two_go(order[3])
        step_two(order[2], new_of, more)
        back_forward_when(order[1], more)

    def end_of_two(new_of, more):
        step_two(order[3], new_of, more)
        back_forward_when(order[2], more)

    def pair_one(group):
        return remote(
            sum_one.at[pl.ds(group * 3, 3), :, :, 1 - core],
            half_one.at[pl.ds(group * 3, 3)],
            pair_send.at[4 + group],
            pair_recv.at[4 + group],
            pair,
        )

    across_x, across_y = row_peer(me ^ copies), row_peer(me ^ 2)
    lower, upper = pl.ds(0, channels // 2), pl.ds(channels // 2, channels // 2)

    def taps_of(group):
        return pl.ds(group * 3, 3)

    def fold_one(group, step):
        taps = taps_of(group)
        source, goal, device = (
            (half_one.at[taps, 1 - member, :, :, lower], first_low.at[taps], across_x),
            (half_one.at[taps, :, 1 - line, :, upper], first_up.at[taps], across_y),
            (half_one.at[taps, member, 1 - line, :, lower], second_low.at[taps], across_y),
            (half_one.at[taps, 1 - member, line, :, upper], second_up.at[taps], across_x),
        )[step]
        return remote(source, goal, fold_send.at[group, step], fold_recv.at[group, step], device)

    def spread_one(group, step, arriving=False):
        taps = taps_of(group)
        x, y = member, line
        if arriving:
            x, y = (x, 1 - y) if step in (0, 3) else (1 - x, y)
        piece = (
            v1.at[taps, x, y, core, :, lower],
            v1.at[taps, x, y, core, :, upper],
            v1.at[taps, x, :, core, :, lower],
            v1.at[taps, :, y, core, :, upper],
        )[step]
        device = across_y if step in (0, 3) else across_x
        return remote(piece, piece, open_send.at[group, step], open_recv.at[group, step], device)

    def share_one(group, step, arriving=False):
        taps = taps_of(group)
        side = 1 - core if arriving else core
        piece = (
            v1.at[taps, member, line, side],
            v1.at[taps, member, 1 - line, side, :, lower],
            v1.at[taps, 1 - member, line, side, :, upper],
            v1.at[taps, 1 - member, :, side, :, lower],
            v1.at[taps, :, 1 - line, side, :, upper],
        )[step]
        return remote(piece, piece, share_send.at[group, step], share_recv.at[group, step], pair)

    def open_first(group):
        spread_one(group, 0).start()
        spread_one(group, 1).start()
        share_one(group, 0).start()

    def open_second(group):
        spread_one(group, 0, True).wait_recv()
        spread_one(group, 2).start()
        spread_one(group, 1, True).wait_recv()
        spread_one(group, 3).start()
        share_one(group, 1).start()
        share_one(group, 2).start()

    def open_third(group):
        spread_one(group, 2, True).wait_recv()
        share_one(group, 3).start()
        spread_one(group, 3, True).wait_recv()
        share_one(group, 4).start()

    def open_arrived(group):
        for step in range(5):
            share_one(group, step, True).wait_recv()

    def open_end(group):
        for step in range(4):
            spread_one(group, step).wait_send()
        for step in range(5):
            share_one(group, step).wait_send()

    def pair_add(group):
        pair_one(group).wait()

        def body(tap, _):
            half_one[tap] += sum_one[tap, :, :, core]

        lax.fori_loop(group * 3, group * 3 + 3, body, None)
        fold_one(group, 0).start()
        fold_one(group, 1).start()

    def fold_add(group):
        fold_one(group, 0).wait()
        fold_one(group, 1).wait()

        def body(tap, _):
            half_one[tap, member, :, :, lower] += first_low[tap]
            half_one[tap, :, line, :, upper] += first_up[tap]

        lax.fori_loop(group * 3, group * 3 + 3, body, None)
        fold_one(group, 2).start()
        fold_one(group, 3).start()

    def first_gradient():
        def taps_weight(down):
            out = mul(
                turned[...],
                jnp.concatenate(
                    [window(x_both, down, step, slice(0, channels)) for step in range(3)], axis=1
                ),
            )
            out = out + mul(
                turned[...],
                jnp.concatenate(
                    [
                        window(x_both, down, step, slice(channels, 2 * channels))
                        for step in range(3)
                    ],
                    axis=1,
                ),
            )
            out = out[:LANES] + out[LANES:]
            for step in range(3):
                sum_one[down * 3 + step] = out[:, step * channels : (step + 1) * channels].reshape(
                    sum_one.shape[1:]
                )

        for group in range(GROUPS):
            taps_weight(group)
            pair_one(group).start()
            if group > 0:
                pair_add(group - 1)
            if group > 1:
                fold_add(group - 2)
        pair_add(GROUPS - 1)
        fold_add(GROUPS - 2)

    def step_group(group, new_of):
        fold_one(group, 2).wait()
        fold_one(group, 3).wait()

        def body(tap, _):
            change = half_one[tap, member, line] + jnp.concatenate(
                [second_low[tap], second_up[tap]], axis=1
            )
            new = new_of(v1[tap, member, line, core], change, d1[tap])
            v1[tap, member, line, core] = new
            series_one[:, tap_lanes(tap, channels)] += new

        lax.fori_loop(group * 3, group * 3 + 3, body, None)

    def no_aside(index):
        pass

    series_one[...] = jnp.zeros_like(series_one)
    series_two[...] = jnp.zeros_like(series_two)

    def first_vector(old, change, decay):
        return change + decay * old

    def next_vector(old, change, decay):
        return old - neumann_rate * (change + decay * old)

    for load in k1_loads + d1_loads:
        load.wait()
    for move in k1_moves:
        move.wait()
    lax.fori_loop(0, TAPS, split_one, None)
    ring_step(x_box, x_send, x_recv, 2)
    cut_end(0)
    for block in range(4):
        back_start((block,))
    ring_step(x_box, x_send, x_recv, 3)
    ring_end(x_box, x_send, x_recv)

    def place_images(cell, _):
        for block in range(4):
            x_row[block * own_count : (block + 1) * own_count] = x_box[block, cell]
        high, low = halves(x_row[...])
        x_both[cell // 4 + 1, cell % 4 + 1, :, 0:channels] = high
        x_both[cell // 4 + 1, cell % 4 + 1, :, channels : 2 * channels] = low
        x_own[cell] = x_row[:, pl.ds(pl.multiple_of(part * LANES, LANES), LANES)]

    each_cell(place_images)
    flow[...] = jnp.zeros_like(flow)
    lax.fori_loop(0, 3, lambda down, _: taps_forward(down), None)

    def sums_primal(cell, carry):
        value = flow[cell]
        return carry[0] + value, carry[1] + value * value

    put_sums(0, *each_cell(sums_primal, (zero, zero)))
    stats_own[0, 2:3, :] = jnp.sum(valid, axis=0, keepdims=True)
    moves = sum_start(0, 8)
    for block in range(4):
        back_forward((block,))
    cut_end(1)
    for block in range(4):
        back_arrived((block,))
        back_end((block,))
    split_two(k_hi, k_lo)
    partial[...] = jnp.zeros_like(partial)
    total = sum_end(0, 8, moves)
    label_total = total[2:3]
    average = total[0:1] * inverse
    scale = lax.rsqrt(total[1:2] * inverse - average * average + norm_eps)
    gain, shift = row(move_norm, 0), row(move_norm, 1)
    gain2, shift2 = row(move_norm, 2), row(move_norm, 3)

    def first_primal(cell, _):
        normal = (flow[cell] - average) * scale
        value, slope, bend = silu_pieces(normal * gain + shift)
        n1[cell] = normal
        s1[cell] = slope
        pb1[cell] = bend
        a_both[cell // 4 + 1, cell % 4 + 1] = jnp.concatenate(halves(value), axis=1)

    each_cell(first_primal)
    scatter(a_both, k_hi, k_lo, no_aside)
    put_sums(1, *each_cell(sums_primal, (zero, zero)))
    total = sum_end(1, 8, sum_start(1, 8))
    average = total[0:1] * inverse
    scale2 = lax.rsqrt(total[1:2] * inverse - average * average + norm_eps)

    def second_primal(cell, carry):
        normal = (flow[cell] - average) * scale2
        value, slope, bend = silu_pieces(normal * gain2 + shift2 + x_own[cell])
        n2[cell] = normal
        s2[cell] = slope
        pb2[cell] = bend
        return carry + value

    pooled[...] = each_cell(second_primal, zero) * (1.0 / 16.0)
    logits = sum_parts(mul_exact(pooled[...], head[...], ((1,), (1,))))
    real = lax.broadcasted_iota(jnp.int32, logits.shape, 1) < classes
    highest = jnp.max(jnp.where(real, logits, -jnp.inf), axis=1, keepdims=True)
    powers = jnp.where(real, jnp.exp(logits - highest), 0.0)
    sum_powers = jnp.sum(powers, axis=1, keepdims=True)
    chances[...] = powers / sum_powers
    target_logit = jnp.sum(chosen * logits, axis=1, keepdims=True)
    cross = (highest + jnp.log(sum_powers) - target_logit) * valid
    weights[...] = valid / label_total
    pull_logits[...] = weights[...] * (chances[...] - chosen)
    out_head = mul_exact(pull_logits[...], pooled[...], ((0,), (0,)))
    pull_block = mul_exact(pull_logits[...], head[...]) * (1.0 / 16.0)

    def back_two_primal(cell, carry):
        pull = pull_block * s2[cell]
        pull2[cell] = pull
        pb2[cell] = pull_block * pb2[cell]
        return carry[0] + pull * n2[cell], carry[1] + pull

    put_sums(2, *each_cell(back_two_primal, (zero, zero)))
    stats_own[2, 2:3, :] = jnp.sum(cross, axis=0, keepdims=True)
    stats_own[2, 8:24, :] = out_head[0:16]
    total = sum_end(2, 24, sum_start(2, 24))
    grad_small[0:1, :] = total[2:3]
    grad_small[1:2, :] = label_total
    grad_small[2:8, :] = jnp.zeros((6, LANES), jnp.float32)
    grad_small[16:32, :] = total[8:24]
    out_gain2, out_shift2 = total[0:1], total[1:2]
    factor2 = scale2 * gain2

    def pull_two_primal(cell, _):
        centred = pull2[cell] - out_shift2 * inverse - n2[cell] * (out_gain2 * inverse)
        c2[cell] = centred
        slots[part, cell] = factor2 * centred

    each_cell(pull_two_primal)
    fold_sum[...] = jnp.zeros_like(fold_sum)
    sum_two[...] = jnp.zeros_like(sum_two)

    def primal_block(block):
        turn_block(block, g_left.at[block], g_turned.at[block])
        use_block(block, g_left.at[block], g_turned.at[block], k_hi, k_lo, a_both)

    gather_and_use(primal_block, first_vector, True)

    def back_one_primal(cell, carry):
        seen = fold_sum[cell // 4 + 1, cell % 4 + 1]
        pull = seen * s1[cell]
        pull1[cell] = pull
        pb1[cell] = seen * pb1[cell]
        return carry[0] + pull * n1[cell], carry[1] + pull

    put_sums(3, *each_cell(back_one_primal, (zero, zero)))
    moves = sum_start(3, 8)
    rest_of_two(first_vector, True)
    total = sum_end(3, 8, moves)
    out_gain, out_shift = total[0:1], total[1:2]
    factor = scale * gain

    def pull_one_primal(cell, _):
        centred = pull1[cell] - out_shift * inverse - n1[cell] * (out_gain * inverse)
        c1[cell] = centred
        flow[cell] = factor * centred

    each_cell(pull_one_primal)
    turned[...] = jnp.concatenate(halves(flow[...].reshape(16 * count, LANES).T), axis=0)

    channel[0:1, :] = scale
    channel[1:2, :] = gain
    channel[2:3, :] = scale2
    channel[3:4, :] = gain2
    channel[4:5, :] = out_gain * inverse
    channel[5:6, :] = out_gain2 * inverse
    move_norm[0:1, :] = out_gain
    move_norm[1:2, :] = out_shift
    move_norm[2:3, :] = out_gain2
    move_norm[3:4, :] = out_shift2
    grad_small[8:16, :] = move_norm[...]
    move_head[0:16] = grad_small[16:32, :]

    first_gradient()
    end_of_two(first_vector, True)
    fold_add(GROUPS - 1)
    back_forward((order[3],))

    def deliver_move(which, source, other):
        return remote(
            source.at[other],
            row_parts.at[which, part],
            row_send.at[which, other],
            row_recv.at[which, part],
            part_peer(other),
        )

    def deliver_start(which, source):
        for other in range(4):

            @pl.when(part != other)
            def _():
                deliver_move(which, source, other).start()

        row_parts[which, part] = source[part]

    def deliver_end(which, source, result):
        for other in range(4):

            @pl.when(part != other)
            def _():
                deliver_move(which, source, other).wait_send()
                remote(
                    source.at[other],
                    row_parts.at[which, other],
                    row_send.at[which, other],
                    row_recv.at[which, other],
                    part_peer(other),
                ).wait_recv()

        for other in range(4):
            for tap in range(TAPS):
                start = tap * channels + other * LANES
                result[copy, :, start : start + LANES] = row_parts[
                    which, other, :, tap * LANES : (tap + 1) * LANES
                ]

    across, corner = row_peer(me ^ 2), copy ^ 2

    def spread_move(which, result, step, block, device):
        return remote(
            result.at[block], result.at[block], own_send.at[which, step], own_recv.at[which, step], device
        )

    def spread_start(which, result):
        spread_move(which, result, 0, copy, across).start()
        spread_move(which, result, 1, copy, pair).start()

    def spread_forward(which, result):
        spread_move(which, result, 0, corner, across).wait_recv()
        spread_move(which, result, 2, corner, pair).start()

    def spread_end(which, result):
        spread_move(which, result, 1, copy ^ 1, pair).wait_recv()
        spread_move(which, result, 2, copy ^ 3, pair).wait_recv()
        spread_move(which, result, 0, copy, across).wait_send()
        spread_move(which, result, 1, copy, pair).wait_send()
        spread_move(which, result, 2, corner, pair).wait_send()

    grad_source[...] = series_two[...]
    deliver_start(0, grad_source)
    for group in range(GROUPS):
        step_group(group, first_vector)
        open_first(group)

    def turn_body(turn, nothing):
        flow[...] = jnp.zeros_like(flow)

        def forward_group(group):
            open_arrived(group)
            lax.fori_loop(group * 3, group * 3 + 3, split_one, None)
            taps_forward(group)

        open_second(0)
        open_second(1)
        open_third(0)
        open_second(2)
        forward_group(0)
        open_third(1)
        forward_group(1)
        open_third(2)
        forward_group(2)
        for group in range(GROUPS):
            open_end(group)

        @pl.when(turn == 0)
        def _():
            for tap in range(TAPS):
                grads[0, :, :, tap * channels : (tap + 1) * channels] = v1[tap, member].reshape(
                    4, v1.shape[4], channels
                )

        def sums_forward(normal):
            def body(cell, carry):
                value = flow[cell]
                return carry[0] + value, carry[1] + value * normal[cell]

            return each_cell(body, (zero, zero))

        put_sums(0, *sums_forward(n1))
        moves = sum_start(0, 8)
        partial[...] = jnp.zeros_like(partial)
        fold_sum[...] = jnp.zeros_like(fold_sum)
        sum_two[...] = jnp.zeros_like(sum_two)
        for block in range(4):
            back_arrived((block,))
            back_end((block,))
        split_two(v2_hi, v2_lo)
        part_of_second(a_both, v2_hi, v2_lo, 0)
        part_of_second(a_both, v2_hi, v2_lo, 1)
        total = sum_end(0, 8, moves) * inverse
        average, cross = total[0:1], total[1:2]
        scale, gain = row(channel, 0), row(channel, 1)
        tan_scale_one = -scale * scale * cross
        move_gain, move_shift = row(move_norm, 0), row(move_norm, 1)

        def forward_one(cell, _):
            normal = n1[cell]
            tangent = scale * (flow[cell] - average - normal * cross)
            inner = move_gain * normal + gain * tangent + move_shift
            nt1[cell] = tangent
            in1[cell] = inner
            b_both[cell // 4 + 1, cell % 4 + 1] = jnp.concatenate(halves(s1[cell] * inner), axis=1)

        each_cell(forward_one)

        def aside(block):
            use_block(block, g_left.at[block], g_turned.at[block], v2_hi, v2_lo, b_both)

        scatter(b_both, k_hi, k_lo, aside)

        @pl.when(turn == 0)
        def _():
            deliver_end(0, grad_source, grads.at[1])
            spread_start(0, grads.at[1])

        @pl.when(turn == 1)
        def _():
            spread_forward(0, grads.at[1])


        put_sums(1, *sums_forward(n2))
        moves = sum_start(1, 8)
        early_logits = mul_exact(pooled[...], move_head[...], ((1,), (1,)))
        early_block = mul_exact(pull_logits[...], move_head[...])
        total = sum_end(1, 8, moves) * inverse
        average2, cross2 = total[0:1], total[1:2]
        scale2, gain2 = row(channel, 2), row(channel, 3)
        tan_scale_two = -scale2 * scale2 * cross2
        move_gain2, move_shift2 = row(move_norm, 2), row(move_norm, 3)

        def forward_two(cell, carry):
            normal = n2[cell]
            tangent = scale2 * (flow[cell] - average2 - normal * cross2)
            inner = move_gain2 * normal + gain2 * tangent + move_shift2
            nt2[cell] = tangent
            in2[cell] = inner
            return carry + s2[cell] * inner

        tan_pooled = each_cell(forward_two, zero) * (1.0 / 16.0)
        tan_logits = sum_parts(mul_exact(tan_pooled, head[...], ((1,), (1,))) + early_logits)
        chance = chances[...]
        tan_pull = (
            weights[...]
            * chance
            * (tan_logits - jnp.sum(chance * tan_logits, axis=1, keepdims=True))
        )
        tan_block = (mul_exact(tan_pull, head[...]) + early_block) * (1.0 / 16.0)

        def back_two(cell, carry):
            tangent = tan_block * s2[cell] + pb2[cell] * in2[cell]
            flow[cell] = tangent
            return (
                carry[0] + tangent * n2[cell] + pull2[cell] * nt2[cell],
                carry[1] + tangent,
            )

        put_sums(2, *each_cell(back_two, (zero, zero)))
        moves = sum_start(2, 8)
        out_head = mul_exact(pull_logits[...], tan_pooled, ((0,), (0,))) + mul_exact(
            tan_pull, pooled[...], ((0,), (0,))
        )
        stats_own[3, 8:24, :] = out_head[0:16]
        total = sum_end(2, 8, moves)
        out_gain2, out_shift2 = total[0:1], total[1:2]
        factor2 = scale2 * gain2
        tan_factor2 = tan_scale_two * gain2 + scale2 * move_gain2

        def pull_two_body(cell, _):
            slots[part, cell] = tan_factor2 * c2[cell] + factor2 * (
                flow[cell]
                - out_shift2 * inverse
                - nt2[cell] * row(channel, 5)
                - n2[cell] * (out_gain2 * inverse)
            )

        each_cell(pull_two_body)

        def turn_of_block(block):
            turn_block(block, t_left, t_turned)
            use_block(block, t_left, t_turned, k_hi, k_lo, a_both)

        more = turn < NEUMANN - 1
        gather_and_use(turn_of_block, next_vector, more)

        def back_one(cell, carry):
            pull = fold_sum[cell // 4 + 1, cell % 4 + 1]
            tangent = pull * s1[cell] + pb1[cell] * in1[cell]
            flow[cell] = tangent
            return (
                carry[0] + tangent * n1[cell] + pull1[cell] * nt1[cell],
                carry[1] + tangent,
            )

        put_sums(3, *each_cell(back_one, (zero, zero)))
        moves = sum_start(3, 24)
        rest_of_two(next_vector, more)
        total = sum_end(3, 24, moves)
        move_head[0:16] = move_head[0:16] - neumann_rate * total[8:24]
        out_gain, out_shift = total[0:1], total[1:2]
        factor = scale * gain
        tan_factor = tan_scale_one * gain + scale * move_gain

        def pull_one_body(cell, _):
            flow[cell] = tan_factor * c1[cell] + factor * (
                flow[cell]
                - out_shift * inverse
                - nt1[cell] * row(channel, 4)
                - n1[cell] * (out_gain * inverse)
            )

        each_cell(pull_one_body)
        turned[...] = jnp.concatenate(halves(flow[...].reshape(16 * count, LANES).T), axis=0)
        move_norm[0:1, :] = move_gain - neumann_rate * out_gain
        move_norm[1:2, :] = move_shift - neumann_rate * out_shift
        move_norm[2:3, :] = move_gain2 - neumann_rate * out_gain2
        move_norm[3:4, :] = move_shift2 - neumann_rate * out_shift2
        first_gradient()
        end_of_two(next_vector, more)
        fold_add(GROUPS - 1)
        back_forward_when(order[3], more)

        @pl.when(turn == NEUMANN - 1)
        def _():
            deliver_start(1, series_two)

        for group in range(GROUPS):
            step_group(group, next_vector)

            @pl.when(more)
            def _():
                open_first(group)

    lax.fori_loop(0, NEUMANN, turn_body, None)

    series[0, copy] = series_one[...]
    spread_start(1, series.at[0])
    deliver_end(1, series_two, series.at[1])
    spread_start(2, series.at[1])
    spread_forward(1, series.at[0])
    spread_forward(2, series.at[1])
    spread_end(0, grads.at[1])
    spread_end(1, series.at[0])
    spread_end(2, series.at[1])


def step_fused(
    links,
    rows,
    source,
    index_map,
    crop_offsets,
    flip_flags,
    labels,
    valid_mask,
    conv_weights,
    norm_params,
    head_weights,
    decay_rates,
):
    own_count, channels = source.shape[0], source.shape[3]
    cells, count = MAP * MAP, own_count * 4
    width, group = channels // 4, 8
    piece, block = width // group, channels // group
    classes = head_weights.shape[1]
    f32, b16 = jnp.float32, jnp.bfloat16
    small = jnp.concatenate(
        [
            norm_params,
            jnp.zeros((4, block), f32),
            head_weights.T,
            jnp.zeros((16 - classes, block), f32),
        ]
    )
    lane = links.member * block
    here = jnp.arange(2, dtype=jnp.int32)[None, :, None] == links.member
    operands = (
        source,
        index_map,
        crop_offsets,
        flip_flags,
        labels,
        valid_mask,
        conv_weights.reshape(2, 2, 2, piece, TAPS * channels),
        decay_rates.reshape(2, 2, 2, piece, TAPS * channels),
        jnp.where(here, small[:, None, :], 0.0).reshape(24, width),
    )
    vmem = pl.BlockSpec(memory_space=pltpu.VMEM)
    anywhere = pl.BlockSpec(memory_space=pl.ANY)
    row_map = pltpu.VMEM((cells, count, width), f32)
    four_maps = pltpu.VMEM((4, cells, count, width), f32)
    inner_piece = pltpu.VMEM((4, piece, TAPS * width), f32)
    inner_half = pltpu.VMEM((4, 4, piece, TAPS * width), f32)
    inner_part = pltpu.VMEM((channels, TAPS * width), b16)
    outer_part = pltpu.VMEM((TAPS, width, channels), b16)
    both = pltpu.VMEM((MAP + 2, MAP + 2, count, 2 * width), b16)
    logit = pltpu.VMEM((count, LANES), f32)
    dma = pltpu.SemaphoreType.DMA
    scratch = [
        pltpu.VMEM((piece, TAPS * channels), f32),
        inner_piece,
        inner_piece,
        pltpu.VMEM((2, 4, piece, TAPS * width), f32),
        pltpu.VMEM((2, piece, TAPS * channels), f32),
        pltpu.VMEM((2, 4, piece, TAPS * width), f32),
        pltpu.VMEM((TAPS, piece, channels), f32),
        inner_piece,
        pltpu.VMEM((TAPS, 2, 2, 2, piece, channels), f32),
        pltpu.VMEM((group, 4, piece, TAPS * width), f32),
        outer_part,
        outer_part,
        inner_part,
        inner_part,
        inner_part,
        inner_part,
        pltpu.VMEM(source.shape, f32),
        pltpu.VMEM((4, cells, own_count, channels), f32),
        pltpu.VMEM((count, channels), f32),
        pltpu.VMEM((MAP + 2, MAP + 2, count, 2 * channels), b16),
        row_map,
        both,
        both,
        pltpu.VMEM((4, cells * count, 2 * width), b16),
        pltpu.VMEM((4, 2 * width, cells * count), b16),
        pltpu.VMEM((cells * count, 2 * width), b16),
        pltpu.VMEM((2 * width, cells * count), b16),
        four_maps,
        four_maps,
        four_maps,
        four_maps,
        *[row_map] * 15,
        pltpu.VMEM((MAP + 2, MAP + 2, count, width), f32),
        pltpu.VMEM((TAPS, 2, 2, 2, piece, channels), f32),
        pltpu.VMEM((4, 4, 2, piece, TAPS * width), f32),
        pltpu.VMEM((TAPS, 2, 2, piece, channels), f32),
        inner_half,
        *[pltpu.VMEM((TAPS, 2, piece, channels // 2), f32)] * 2,
        *[pltpu.VMEM((TAPS, piece, channels // 2), f32)] * 2,
        inner_half,
        pltpu.VMEM((4, 8, 24, width), f32),
        pltpu.VMEM((4, 24, width), f32),
        pltpu.VMEM((4, count, LANES), f32),
        logit,
        pltpu.VMEM((24, width), f32),
        pltpu.VMEM((4, 2 * count, LANES), f32),
        pltpu.VMEM((2 * width, cells * count), b16),
        pltpu.VMEM((8, width), f32),
        pltpu.VMEM((8, width), f32),
        pltpu.VMEM((LANES, width), f32),
        pltpu.VMEM((LANES, width), f32),
        logit,
        logit,
        logit,
        logit,
        dma(()),
        dma((2,)),
        dma((2,)),
        dma((TAPS,)),
        dma((TAPS,)),
        dma((TAPS,)),
        dma((TAPS,)),
        dma((2, 4)),
        dma((2, 4)),
        dma((4,)),
        dma((4,)),
        dma((2, 4, 2)),
        dma((4, 2)),
        dma((4, 8)),
        dma((4, 8)),
        dma((4,)),
        dma((4,)),
        dma((4, 2)),
        dma((4, 2)),
        dma((4, 2)),
        dma((4, 2)),
        dma((2, 4, 2)),
        dma((4, 2)),
        dma((GROUPS + 4,)),
        dma((GROUPS + 4,)),
        dma((4, 4)),
        dma((4, 4)),
        dma((4, 4)),
        dma((4, 4)),
        dma((4, 4)),
        dma((4, 4)),
        dma((GROUPS, 4)),
        dma((GROUPS, 4)),
        dma((GROUPS, 4)),
        dma((GROUPS, 4)),
        dma((GROUPS, 5)),
        dma((GROUPS, 5)),
        dma((2, 4)),
        dma((2, 4)),
        dma((3, 3)),
        dma((3, 3)),
    ]
    result = jax.ShapeDtypeStruct((2, 4, piece, TAPS * channels), f32)
    grads, series, grad_small = pl.pallas_call(
        functools.partial(step_kernel, rows, links.members, links.copies, classes),
        out_shape=(result, result, jax.ShapeDtypeStruct((32, width), f32)),
        in_specs=[anywhere] + [pl.BlockSpec(memory_space=pltpu.SMEM)] * 5 + [anywhere] * 2 + [vmem],
        out_specs=(vmem,) * 3,
        scratch_shapes=scratch,
        compiler_params=pltpu.CompilerParams(
            collective_id=1, has_side_effects=True, vmem_limit_bytes=63 * 1024 * 1024
        ),
        name="train_step",
    )(*operands)
    own = lax.dynamic_slice_in_dim(grad_small, lane, block, 1)
    return (
        grad_small[0, 0],
        grad_small[1, 0],
        grads.reshape(conv_weights.shape),
        own[8:12],
        own[16 : 16 + classes].T,
        series.reshape(conv_weights.shape),
    )


def adamw(weight, grad, first, second, rate):
    first = beta_first * first + (1.0 - beta_first) * grad
    second = beta_second * second + (1.0 - beta_second) * grad * grad
    first_hat = first / (1.0 - beta_first**STEP)
    second_hat = second / (1.0 - beta_second**STEP)
    update = first_hat / (jnp.sqrt(second_hat) + adam_eps) + decoupled * weight
    return (weight - rate * update, first, second)


def silu_parts(value):
    gate = jax.nn.sigmoid(value)
    slope = gate * (1.0 - gate)
    first = gate + value * slope
    second = slope * (2.0 + value * (1.0 - 2.0 * gate))
    return value * gate, first, second


class Links:
    def __init__(self):
        self.shards = lax.axis_size("shard")
        self.copies = lax.axis_size("dp")
        self.parts = 4 if self.shards % 4 == 0 else 1
        self.members = self.shards // self.parts
        index = lax.axis_index("shard")
        self.part = index // self.members
        self.member = index % self.members
        self.across = [
            [p * self.members + m for p in range(self.parts)] for m in range(self.members)
        ]
        self.within = [
            [p * self.members + m for m in range(self.members)] for p in range(self.parts)
        ]

    def sum_rows(self, value):
        value = lax.psum(value, "dp")
        gathered = lax.all_gather(value, "shard", axis_index_groups=self.within)
        return jnp.sum(gathered, axis=0)

    def sum_parts(self, value):
        return jnp.sum(lax.all_gather(value, "shard", axis_index_groups=self.across), axis=0)

    def gather_parts(self, value, axis):
        return lax.all_gather(value, "shard", axis_index_groups=self.across, axis=axis, tiled=True)

    def gather_members(self, value, axis):
        return lax.all_gather(value, "shard", axis_index_groups=self.within, axis=axis, tiled=True)

    def scatter_parts(self, value, axis):
        return lax.psum_scatter(
            value, "shard", axis_index_groups=self.across, scatter_dimension=axis, tiled=True
        )

    def to_inner(self, value):
        rows, channels = value.shape[0], value.shape[1] // TAPS
        width = channels // self.parts
        cut = value.reshape(rows, TAPS, self.parts, width).transpose(2, 0, 1, 3)
        moved = lax.all_to_all(cut, "shard", 0, 0, axis_index_groups=self.across, tiled=True)
        whole = self.gather_members(moved, 1)
        return whole.reshape(channels, TAPS * width)

    def to_outer(self, value):
        channels, width = value.shape[0], value.shape[1] // TAPS
        rows = channels // self.shards
        cut = value.reshape(self.parts, self.members, rows, TAPS * width)
        cut = lax.dynamic_index_in_dim(cut, self.member, 1, keepdims=False)
        moved = lax.all_to_all(cut, "shard", 0, 0, axis_index_groups=self.across, tiled=True)
        moved = moved.reshape(self.parts, rows, TAPS, width).transpose(1, 2, 0, 3)
        return moved.reshape(rows, TAPS * channels)

    def own_rows(self, value, axis=0):
        size = value.shape[axis] // self.members
        return lax.dynamic_slice_in_dim(value, self.member * size, size, axis)


def moments(hidden, rows, links):
    totals = links.sum_rows(jnp.stack([jnp.sum(hidden, axis=0), jnp.sum(hidden * hidden, axis=0)]))
    average = totals[0] / rows
    scale = lax.rsqrt(totals[1] / rows - average * average + norm_eps)
    return (hidden - average) * scale, scale


def moments_tangent(normal, scale, tangent, rows, links):
    totals = links.sum_rows(
        jnp.stack([jnp.sum(tangent, axis=0), jnp.sum(tangent * normal, axis=0)])
    )
    average, cross = totals[0] / rows, totals[1] / rows
    return scale * (tangent - average - normal * cross), -scale * scale * cross


def step_general(
    links,
    rows,
    source,
    index_map,
    crop_offsets,
    flip_flags,
    labels,
    valid_mask,
    conv_weights,
    norm_params,
    head_weights,
    decay_rates,
):
    images = jax.vmap(crop_image)(source[index_map], crop_offsets, flip_flags)
    images = images.transpose(1, 2, 0, 3)
    valid = valid_mask.astype(jnp.float32)
    own_images, channels = images.shape[2:]
    count = own_images * links.parts
    width = channels // links.parts
    first_column = links.part * width
    label_total = lax.psum(jnp.sum(valid), ("shard", "dp"))
    images = links.gather_parts(images, 2)
    labels = links.gather_parts(labels, 0)
    valid = links.gather_parts(valid, 0)

    kernel_one = links.gather_members(conv_weights[0], 0)
    kernel_two = links.to_inner(conv_weights[1])
    decay_one = links.gather_members(decay_rates[0], 0)
    decay_two = links.to_inner(decay_rates[1])
    norms = links.gather_members(norm_params, 1)
    head = links.gather_members(head_weights, 0)
    gain_one, shift_one, gain_two, shift_two = norms[0], norms[1], norms[2], norms[3]

    def pool(value):
        return jnp.sum(value.reshape(MAP * MAP, count, width), axis=0) / (MAP * MAP)

    def spread(value):
        whole = jnp.broadcast_to(value[None] / (MAP * MAP), (MAP * MAP, count, width))
        return whole.reshape(MAP * MAP * count, width)

    columns = patches(images)
    own_columns = lax.dynamic_slice_in_dim(
        images.reshape(MAP * MAP * count, channels), first_column, width, 1
    )

    hidden_one = dot(columns, kernel_one, ((1,), (1,)))
    normal_one, scale_one = moments(hidden_one, rows, links)
    active, slope_one, bend_one = silu_parts(normal_one * gain_one + shift_one)
    active_columns = patches(active.reshape(MAP, MAP, count, width))
    hidden_two = links.scatter_parts(dot(active_columns, kernel_two, ((1,), (1,))), 1)
    normal_two, scale_two = moments(hidden_two, rows, links)
    block, slope_two, bend_two = silu_parts(normal_two * gain_two + shift_two + own_columns)
    pooled = pool(block)
    logits = links.sum_parts(dot(pooled, head, ((1,), (0,))))
    highest = jnp.max(logits, axis=1, keepdims=True)
    powers = jnp.exp(logits - highest)
    total = jnp.sum(powers, axis=1, keepdims=True)
    chances = powers / total
    classes = jnp.arange(logits.shape[1], dtype=jnp.int32)
    chosen = (labels[:, None] == classes[None, :]).astype(jnp.float32)
    cross = highest[:, 0] + jnp.log(total[:, 0]) - jnp.sum(chosen * logits, axis=1)
    loss_sum = links.sum_rows(jnp.sum(valid * cross)[None])[0]
    weights = (valid / label_total)[:, None]
    pull_logits = weights * (chances - chosen)
    grad_head = dot(pooled, pull_logits, ((0,), (0,)))
    pull_block = spread(dot(pull_logits, head, ((1,), (1,))))
    pull_two = pull_block * slope_two
    sums_two = links.sum_rows(
        jnp.stack([jnp.sum(pull_two * normal_two, axis=0), jnp.sum(pull_two, axis=0)])
    )
    centred_two = pull_two - sums_two[1] / rows - normal_two * (sums_two[0] / rows)
    factor_two = scale_two * gain_two
    pull_hidden_two = links.gather_parts(factor_two * centred_two, 1)
    grad_two = dot(pull_hidden_two, active_columns, ((0,), (0,)))
    pull_active = fold(dot(pull_hidden_two, kernel_two, ((1,), (0,))), count)
    pull_one = pull_active * slope_one
    sums_one = links.sum_rows(
        jnp.stack([jnp.sum(pull_one * normal_one, axis=0), jnp.sum(pull_one, axis=0)])
    )
    centred_one = pull_one - sums_one[1] / rows - normal_one * (sums_one[0] / rows)
    factor_one = scale_one * gain_one
    grad_one = dot(factor_one * centred_one, columns, ((0,), (0,)))

    grad_one = links.sum_rows(grad_one) + decay_one * kernel_one
    grad_two = links.sum_rows(grad_two) + decay_two * kernel_two
    grad_head = links.sum_rows(grad_head)
    grad_norm = jnp.concatenate([sums_one, sums_two])

    def product(vector):
        move_one, move_two, move_norm, move_head = vector
        tan_hidden = dot(columns, move_one, ((1,), (1,)))
        tan_normal_one, tan_scale_one = moments_tangent(
            normal_one, scale_one, tan_hidden, rows, links
        )
        tan_inner = move_norm[0] * normal_one + gain_one * tan_normal_one + move_norm[1]
        tan_active = slope_one * tan_inner
        tan_columns = patches(tan_active.reshape(MAP, MAP, count, width))
        tan_hidden = links.scatter_parts(
            dot(tan_columns, kernel_two, ((1,), (1,))) + dot(active_columns, move_two, ((1,), (1,))),
            1,
        )
        tan_normal_two, tan_scale_two = moments_tangent(
            normal_two, scale_two, tan_hidden, rows, links
        )
        tan_outer = move_norm[2] * normal_two + gain_two * tan_normal_two + move_norm[3]
        tan_pooled = pool(slope_two * tan_outer)
        tan_logits = links.sum_parts(
            dot(tan_pooled, head, ((1,), (0,))) + dot(pooled, move_head, ((1,), (0,)))
        )
        tan_chances = chances * (tan_logits - jnp.sum(chances * tan_logits, axis=1, keepdims=True))
        tan_pull = weights * tan_chances
        out_head = dot(tan_pooled, pull_logits, ((0,), (0,))) + dot(pooled, tan_pull, ((0,), (0,)))
        tan_block = spread(
            dot(tan_pull, head, ((1,), (1,))) + dot(pull_logits, move_head, ((1,), (1,)))
        )
        tan_two = tan_block * slope_two + pull_block * bend_two * tan_outer
        tan_sums_two = links.sum_rows(
            jnp.stack(
                [
                    jnp.sum(tan_two * normal_two + pull_two * tan_normal_two, axis=0),
                    jnp.sum(tan_two, axis=0),
                ]
            )
        )
        tan_factor = tan_scale_two * gain_two + scale_two * move_norm[2]
        tan_hidden = tan_factor * centred_two + factor_two * (
            tan_two
            - tan_sums_two[1] / rows
            - tan_normal_two * (sums_two[0] / rows)
            - normal_two * (tan_sums_two[0] / rows)
        )
        tan_hidden = links.gather_parts(tan_hidden, 1)
        out_two = dot(tan_hidden, active_columns, ((0,), (0,))) + dot(
            pull_hidden_two, tan_columns, ((0,), (0,))
        )
        tan_pull_active = fold(
            dot(tan_hidden, kernel_two, ((1,), (0,))) + dot(pull_hidden_two, move_two, ((1,), (0,))),
            count,
        )
        tan_one = tan_pull_active * slope_one + pull_active * bend_one * tan_inner
        tan_sums_one = links.sum_rows(
            jnp.stack(
                [
                    jnp.sum(tan_one * normal_one + pull_one * tan_normal_one, axis=0),
                    jnp.sum(tan_one, axis=0),
                ]
            )
        )
        tan_factor = tan_scale_one * gain_one + scale_one * move_norm[0]
        tan_hidden = tan_factor * centred_one + factor_one * (
            tan_one
            - tan_sums_one[1] / rows
            - tan_normal_one * (sums_one[0] / rows)
            - normal_one * (tan_sums_one[0] / rows)
        )
        out_one = dot(tan_hidden, columns, ((0,), (0,)))
        return (
            links.sum_rows(out_one) + decay_one * move_one,
            links.sum_rows(out_two) + decay_two * move_two,
            jnp.concatenate([tan_sums_one, tan_sums_two]),
            links.sum_rows(out_head),
        )

    vector = (grad_one, grad_two, grad_norm, grad_head)
    series_one, series_two = grad_one, grad_two
    for turn in range(NEUMANN):
        change = product(vector)
        vector = tuple(
            previous - neumann_rate * moved for previous, moved in zip(vector, change)
        )
        series_one, series_two = series_one + vector[0], series_two + vector[1]

    series = jnp.stack([links.own_rows(series_one), links.to_outer(series_two)])
    grads = jnp.stack([links.own_rows(grad_one), links.to_outer(grad_two)])
    return (
        loss_sum,
        label_total,
        grads,
        links.own_rows(grad_norm, 1),
        links.own_rows(grad_head),
        series,
    )


def shards(
    source,
    index_map,
    crop_offsets,
    flip_flags,
    labels,
    valid_mask,
    conv_weights,
    norm_params,
    head_weights,
    decay_rates,
    conv_first,
    conv_second,
    norm_first,
    norm_second,
    head_first,
    head_second,
):
    links = Links()
    rows = float(source.shape[0] * MAP * MAP * links.shards * links.copies)
    fused = links.members * links.copies == 8 and links.members == 2 and links.parts == 4
    loss_sum, label_total, grads, grad_norm, grad_head, series = (
        step_fused if fused else step_general
    )(
        links,
        rows,
        source,
        index_map,
        crop_offsets,
        flip_flags,
        labels,
        valid_mask,
        conv_weights,
        norm_params,
        head_weights,
        decay_rates,
    )
    hyper_gradient = -neumann_rate * conv_weights * series
    conv_new, conv_one, conv_two = adamw(conv_weights, grads, conv_first, conv_second, 0.015)
    norm_new, norm_one, norm_two = adamw(
        norm_params, grad_norm, norm_first, norm_second, 0.3
    )
    head_new, head_one, head_two = adamw(
        head_weights, grad_head, head_first, head_second, 0.13
    )
    return (
        loss_sum,
        label_total,
        conv_new,
        conv_one,
        conv_two,
        norm_new,
        norm_one,
        norm_two,
        head_new,
        head_one,
        head_two,
        hyper_gradient,
    )


def solution(mesh):
    images = P(("shard", "dp"))
    rows = P(None, "shard")
    head = P("shard")
    in_specs = (images,) * 6 + (rows, rows, head, rows, rows, rows, rows, rows, head, head)
    out_specs = (P(), P()) + (rows,) * 6 + (head,) * 3 + (rows,)
    return jax.shard_map(shards, mesh=mesh, in_specs=in_specs, out_specs=out_specs, check_vma=False)
```

```python
import functools

import jax
import jax.numpy as jnp
from jax import lax
from jax.experimental import pallas as pl
from jax.experimental.pallas import tpu as pltpu
from jax.sharding import PartitionSpec as P

MAP = 4
NEUMANN = 3
STEP = 5
TAPS = 9

norm_eps = 1e-05
neumann_rate = 10.0
beta_first = 0.5
beta_second = 0.5
adam_eps = 1e-08
decoupled = 0.01
HIGH = lax.Precision.HIGH


def crop_image(single, offsets, flipped):
    window = lax.dynamic_slice(
        single, (offsets[0], offsets[1], jnp.int32(0)), (MAP, MAP, single.shape[2])
    )
    return jnp.where(flipped == 1, window[:, ::-1, :], window)


def patches(maps):
    count, width = maps.shape[2:]
    padded = jnp.pad(maps, ((1, 1), (1, 1), (0, 0), (0, 0)))
    taps = [padded[dy : dy + MAP, dx : dx + MAP] for dy in range(3) for dx in range(3)]
    return jnp.concatenate(taps, axis=3).reshape(MAP * MAP * count, TAPS * width)


def fold(columns, count):
    width = columns.shape[1] // TAPS
    whole = columns.reshape(MAP, MAP, count, TAPS, width)
    padded = jnp.pad(whole, ((1, 1), (1, 1), (0, 0), (0, 0), (0, 0)))
    total = 0.0
    for dy in range(3):
        for dx in range(3):
            total = total + padded[2 - dy : 2 - dy + MAP, 2 - dx : 2 - dx + MAP, :, dy * 3 + dx]
    return total.reshape(MAP * MAP * count, width)


def dot(left, right, dims):
    return lax.dot_general(
        left, right, ((dims[0], dims[1]), ((), ())), precision=HIGH, preferred_element_type=jnp.float32
    )


MESH_ID = pl.DeviceIdType.MESH
LANES = 128
GROUPS = 3


def halves(value):
    high = value.astype(jnp.bfloat16)
    return high, (value - high.astype(jnp.float32)).astype(jnp.bfloat16)


def mul(left, right, dims=((1,), (0,))):
    return lax.dot_general(left, right, (dims, ((), ())), preferred_element_type=jnp.float32)


def mul_exact(left, right, dims=((1,), (0,))):
    return lax.dot_general(
        left,
        right,
        (dims, ((), ())),
        precision=lax.Precision.HIGHEST,
        preferred_element_type=jnp.float32,
    )


def silu_pieces(value):
    gate = 1.0 / (1.0 + jnp.exp(-value))
    slope = gate * (1.0 - gate)
    return value * gate, gate + value * slope, slope * (2.0 + value * (1.0 - 2.0 * gate))


def step_kernel(
    rows,
    members,
    copies,
    classes,
    source,
    index_map,
    crop_offsets,
    flip_flags,
    labels,
    valid_mask,
    weights_in,
    decay_in,
    pair_in,
    grads,
    series,
    grad_small,
    series_one,
    series_two,
    grad_source,
    row_parts,
    row_box,
    cut_box,
    d1,
    d2,
    v1,
    v2,
    v1_hi,
    v1_lo,
    v2_hi,
    v2_lo,
    k_hi,
    k_lo,
    source_box,
    x_box,
    x_row,
    x_both,
    x_own,
    a_both,
    b_both,
    g_left,
    g_turned,
    t_left,
    t_turned,
    slots,
    partial,
    from_low,
    from_high,
    flow,
    n1,
    s1,
    pb1,
    pull1,
    c1,
    n2,
    s2,
    pb2,
    pull2,
    c2,
    nt1,
    in1,
    nt2,
    in2,
    fold_sum,
    sum_one,
    sum_two,
    half_one,
    half_two,
    first_low,
    first_up,
    second_low,
    second_up,
    piece_two,
    stats_box,
    stats_own,
    logit_box,
    logit_own,
    pair_box,
    label_box,
    turned,
    channel,
    move_norm,
    move_head,
    head,
    pooled,
    chances,
    weights,
    pull_logits,
    x_load,
    pair_sem,
    cut_load,
    k1_load,
    d1_load,
    k1_send,
    k1_recv,
    half_send,
    half_recv,
    first_send,
    first_recv,
    label_send,
    label_recv,
    x_send,
    x_recv,
    stats_send,
    stats_recv,
    logit_send,
    logit_recv,
    up_send,
    up_recv,
    down_send,
    down_recv,
    ring_send,
    ring_recv,
    pair_send,
    pair_recv,
    plane_send,
    plane_recv,
    back_send,
    back_recv,
    swap_send,
    swap_recv,
    fold_send,
    fold_recv,
    open_send,
    open_recv,
    share_send,
    share_recv,
    row_send,
    row_recv,
    own_send,
    own_recv,
):
    shard = lax.axis_index("shard")
    copy = lax.axis_index("dp")
    part = shard // members
    member = shard % members
    me = member * copies + copy
    place, line, core = me // 2, (me // 2) % 2, me % 2
    last = 3
    count = flow.shape[1]
    own_count = source.shape[0]
    inverse = 1.0 / rows
    zero = jnp.zeros((count, LANES), jnp.float32)

    def row_peer(other):
        return (part * members + other // copies, other % copies)

    def part_peer(other):
        return (other * members + member, copy)

    def remote(source, target, send, recv, device):
        return pltpu.make_async_remote_copy(
            src_ref=source,
            dst_ref=target,
            send_sem=send,
            recv_sem=recv,
            device_id=device,
            device_id_type=MESH_ID,
        )

    def greet(device):
        pl.semaphore_signal(barrier, inc=1, device_id=device, device_id_type=MESH_ID)

    barrier = pltpu.get_barrier_semaphore()
    for step in range(1, 8):
        greet(row_peer(me ^ step))
    for step in range(1, 4):
        greet(part_peer(part ^ step))
    channels = source.shape[3]

    def tap_lanes(tap, width):
        return pl.ds(pl.multiple_of(tap * width, width), width)

    source_load = pltpu.make_async_copy(source, source_box, x_load)
    source_load.start()
    k1_loads = [
        pltpu.make_async_copy(
            weights_in.at[0, :, :, :, pl.ds(tap * channels, channels)],
            v1.at[tap, member],
            k1_load.at[tap],
        )
        for tap in range(TAPS)
    ]
    d1_loads = [
        pltpu.make_async_copy(
            decay_in.at[0, line, core, :, pl.ds(tap * channels, channels)], d1.at[tap], d1_load.at[tap]
        )
        for tap in range(TAPS)
    ]
    cut_loads = [
        pltpu.make_async_copy(weights_in.at[1, line, core], row_box.at[0], cut_load.at[0]),
        pltpu.make_async_copy(decay_in.at[1, line, core], row_box.at[1], cut_load.at[1]),
    ]
    for load in cut_loads + k1_loads + d1_loads:
        load.start()
    stats_own[...] = jnp.zeros_like(stats_own)
    channel[...] = jnp.zeros_like(channel)
    x_both[...] = jnp.zeros_like(x_both)
    a_both[...] = jnp.zeros_like(a_both)
    b_both[...] = jnp.zeros_like(b_both)
    label_box[0] = jnp.zeros(label_box.shape[1:], jnp.float32)
    lane = lax.broadcasted_iota(jnp.int32, (1, LANES), 1)

    def tag_image(image, _):
        at = part * own_count + image
        label_box[0, pl.ds(at, 1), :] = (lane == labels[image]).astype(jnp.float32)
        label_box[0, pl.ds(count + at, 1), :] = jnp.full(
            (1, LANES), valid_mask[image].astype(jnp.float32)
        )

    lax.fori_loop(0, own_count, tag_image, None)
    source_load.wait()

    def crop(image, _):
        picked, flipped = index_map[image], flip_flags[image]
        top, left = crop_offsets[image, 0], crop_offsets[image, 1]
        for cell in range(16):
            column = left + jnp.where(flipped == 1, 3 - cell % 4, cell % 4)
            x_box[part, cell, pl.ds(image, 1), :] = source_box[
                picked, top + cell // 4, pl.ds(column, 1), :
            ]

    lax.fori_loop(0, own_count, crop, None)
    for load in cut_loads:
        load.wait()
    for which in range(2):
        for other in range(4):
            for tap in range(TAPS):
                start = tap * channels + other * LANES
                cut_box[which, other, :, tap * LANES : (tap + 1) * LANES] = row_box[
                    which, :, start : start + LANES
                ]
    v2[me, part] = cut_box[0, part]
    d2[part] = cut_box[1, part]
    pl.semaphore_wait(barrier, 10)

    def ring_move(box, send, recv, block, step, way, half):
        at = pl.ds(half * 8, 8)
        return remote(
            box.at[block, at],
            box.at[block, at],
            send.at[0 if way > 0 else 1, step, half],
            recv.at[block, half],
            part_peer(part + way),
        )

    def ring_start(box, send, recv):
        for half in range(2):

            @pl.when(part < last)
            def _():
                ring_move(box, send, recv, part, 0, 1, half).start()

            @pl.when(part > 0)
            def _():
                ring_move(box, send, recv, part, 0, -1, half).start()

    def ring_step(box, send, recv, step):
        for half in range(2):

            @pl.when(part >= step)
            def _():
                ring_move(box, send, recv, part - step, step, -1, half).wait_recv()

                @pl.when(part < last)
                def _():
                    ring_move(box, send, recv, part - step, step, 1, half).start()

            @pl.when(part + step <= last)
            def _():
                ring_move(box, send, recv, part + step, step, 1, half).wait_recv()

                @pl.when(part > 0)
                def _():
                    ring_move(box, send, recv, part + step, step, -1, half).start()

    def ring_end(box, send, recv):
        for step in range(0, 3):
            for half in range(2):

                @pl.when((part >= step) & (part < last))
                def _():
                    ring_move(box, send, recv, part - step, step, 1, half).wait_send()

                @pl.when((part + step <= last) & (part > 0))
                def _():
                    ring_move(box, send, recv, part + step, step, -1, half).wait_send()

    order = (
        part,
        jnp.where(part == 0, 1, part - 1),
        jnp.where(part == 3, 1, jnp.where(part == 2, 3, 2)),
        jnp.where(part < 2, 3, 0),
    )

    def cut_move(which, other):
        box = v2.at[me, part] if which == 0 else d2.at[part]
        return remote(
            cut_box.at[which, other],
            box,
            first_send.at[which, other],
            first_recv.at[which, part],
            part_peer(other),
        )

    def cut_start(which):
        for other in range(4):

            @pl.when(part != other)
            def _():
                cut_move(which, other).start()

    def cut_end(which):
        for other in range(4):

            @pl.when(part != other)
            def _():
                cut_move(which, other).wait_send()
                box = v2.at[me, other] if which == 0 else d2.at[other]
                remote(
                    cut_box.at[which, other],
                    box,
                    first_send.at[which, other],
                    first_recv.at[which, other],
                    part_peer(other),
                ).wait_recv()

    pair = row_peer(me ^ 1)
    cut_start(0)
    ring_start(x_box, x_send, x_recv)
    partner = row_peer(me ^ copies)
    k1_moves = [
        remote(
            weights_in.at[0, :, core, :, pl.ds(tap * channels, channels)],
            v1.at[tap, member, :, core],
            k1_send.at[tap],
            k1_recv.at[tap],
            partner,
        )
        for tap in range(TAPS)
    ]
    for move in k1_moves:
        move.start()

    def k1_share(group, arriving=False):
        piece = v1.at[pl.ds(group * 3, 3), 1 - member, :, 1 - core if arriving else core]
        return remote(piece, piece, half_send.at[group], half_recv.at[group], pair)

    pair_move = remote(pair_in, pair_box, pair_sem.at[0], pair_sem.at[1], partner)
    pair_move.start()
    label_moves = [
        remote(
            label_box.at[0],
            label_box.at[step],
            label_send.at[step],
            label_recv.at[step],
            part_peer(part ^ step),
        )
        for step in range(1, 4)
    ]
    for move in label_moves:
        move.start()

    cut_start(1)

    def piece_of(which, other):
        return v2.at[other, which[0]]

    def lane_of(which):
        return which[0]

    def to_plane(which, step):
        piece, at = piece_of(which, me), lane_of(which)
        return remote(
            piece, piece, back_send.at[at, step], back_recv.at[at, step], row_peer(me ^ (2 * step))
        )

    def from_plane(which, step):
        piece, at = piece_of(which, me ^ (2 * step)), lane_of(which)
        return remote(piece, piece, back_send.at[at, step], back_recv.at[at, step], pair)

    def to_pair(which, step):
        piece, at = piece_of(which, me ^ (2 * step)), lane_of(which)
        return remote(piece, piece, swap_send.at[at, step], swap_recv.at[at, step], pair)

    def from_pair(which, step):
        piece, at = piece_of(which, me ^ 1 ^ (2 * step)), lane_of(which)
        return remote(piece, piece, swap_send.at[at, step], swap_recv.at[at, step], pair)

    def back_start(which):
        for step in range(1, 4):
            to_plane(which, step).start()
        to_pair(which, 0).start()

    def back_forward(which):
        for step in range(1, 4):
            from_plane(which, step).wait_recv()
            to_pair(which, step).start()

    def back_arrived(which):
        for step in range(0, 4):
            from_pair(which, step).wait_recv()

    def back_end(which):
        for step in range(1, 4):
            to_plane(which, step).wait_send()
        for step in range(0, 4):
            to_pair(which, step).wait_send()

    cut_end(0)
    for block in range(4):
        back_start((block,))
    ring_step(x_box, x_send, x_recv, 1)
    pair_move.wait()
    small = pair_in[...] + pair_box[...]
    move_norm[...] = small[0:8]
    head[...] = jnp.zeros_like(head)
    move_head[...] = jnp.zeros_like(move_head)
    head[0:16] = small[8:24]
    for move in label_moves:
        move.wait()
    tags = label_box[0] + label_box[1] + label_box[2] + label_box[3]
    chosen, valid = tags[:count], tags[count:]

    def each_cell(body, init=None):
        return lax.fori_loop(0, 16, body, init)

    def window(ref, down, right, lanes=slice(None), first=0, after=4):
        seen = ref[pl.ds(down + first, after - first), right : right + 4, :, lanes]
        return seen.reshape(4 * (after - first) * seen.shape[2], seen.shape[3])

    def reach(down):
        return (1 if down == 0 else 0), (3 if down == 2 else 4)

    def row(ref, index):
        return ref[index : index + 1, :]

    def put_sums(site, first, second):
        stats_own[site, 0:1, :] = jnp.sum(first, axis=0, keepdims=True)
        stats_own[site, 1:2, :] = jnp.sum(second, axis=0, keepdims=True)

    def sum_start(site, size):
        moves = []
        for step in range(1, 8):
            move = remote(
                stats_own.at[site, pl.ds(0, size)],
                stats_box.at[site, step, pl.ds(0, size)],
                stats_send.at[site, step],
                stats_recv.at[site, step],
                row_peer(me ^ step),
            )
            move.start()
            moves.append(move)
        stats_box[site, 0, pl.ds(0, size)] = stats_own[site, pl.ds(0, size)]
        return moves

    def sum_end(site, size, moves):
        for move in moves:
            move.wait()
        total = stats_box[site, me, pl.ds(0, size)]
        for other in range(1, 8):
            total = total + stats_box[site, other ^ me, pl.ds(0, size)]
        return total

    def sum_parts(value):
        logit_own[...] = value
        moves = []
        for step in range(1, 4):
            move = remote(
                logit_own,
                logit_box.at[step],
                logit_send.at[step],
                logit_recv.at[step],
                part_peer(part ^ step),
            )
            move.start()
            moves.append(move)
        logit_box[0] = value
        for move in moves:
            move.wait()
        total = logit_box[part]
        for other in range(1, 4):
            total = total + logit_box[other ^ part]
        return total

    def split_one(tap, _):
        for other in range(8):
            at = slice(other * 16, other * 16 + 16)
            v1_hi[tap, at], v1_lo[tap, at] = halves(v1[tap, other // 4, other // 2 % 2, other % 2])

    def split_two(high, low):
        def body(other, _):
            for block in range(4):
                at = pl.ds(pl.multiple_of(block * LANES + other * 16, 16), 16)
                high[at], low[at] = halves(v2[other, block])

        lax.fori_loop(0, 8, body, None)

    def taps_forward(row_of_taps):
        left, right = [], []
        for step in range(3):
            tap = row_of_taps * 3 + step
            weight = jnp.concatenate([v1_hi[tap], v1_lo[tap]], axis=0)
            left.append(window(x_both, row_of_taps, step))
            right += [weight, weight]
        out = mul(jnp.concatenate(left, axis=1), jnp.concatenate(right, axis=1), ((1,), (1,)))
        flow[...] += (out[:, :LANES] + out[:, LANES:]).reshape(flow.shape)

    def part_of_second(maps, high, low, half, add):
        at = pl.ds(pl.multiple_of(half * 256, 256), 256)

        for row_of_taps in (1, 0, 2):
            left, right = [], []
            first, after = reach(row_of_taps)
            for step in range(3):
                tap = row_of_taps * 3 + step
                lanes = slice(tap * LANES, (tap + 1) * LANES)
                seen = window(maps, row_of_taps, step, slice(None), first, after)
                weight_hi, weight_lo = high[at, lanes], low[at, lanes]
                left += [seen, seen[:, :LANES]]
                right += [weight_hi, weight_hi, weight_lo]
            out = mul(
                jnp.concatenate(left, axis=1), jnp.concatenate(right, axis=1), ((1,), (1,))
            )
            lines = slice(first * 4, after * 4)
            for side in range(2):
                value = out[:, side * LANES : (side + 1) * LANES].reshape(-1, count, LANES)
                if add or row_of_taps != 1:
                    partial[half * 2 + side, lines] += value
                else:
                    partial[half * 2 + side, lines] = value

    def up(block, half):
        at = pl.ds(half * 8, 8)
        return remote(
            partial.at[block, at],
            from_low.at[block, at],
            up_send.at[block, half],
            up_recv.at[block, half],
            part_peer(part + 1),
        )

    def down(block, half):
        at = pl.ds(half * 8, 8)
        return remote(
            partial.at[block, at],
            from_high.at[block, at],
            down_send.at[block, half],
            down_recv.at[block, half],
            part_peer(part - 1),
        )

    def scatter(maps, high, low, add, aside):
        near = jnp.where(part < 2, 1, 0)

        def half_body(index, _):
            part_of_second(maps, high, low, jnp.where(index == 0, near, 1 - near), add)

            @pl.when((index == 0) & (part == 0))
            def _():
                for block in (3, 2):
                    for half in range(2):
                        up(block, half).start()

            @pl.when((index == 0) & (part == last))
            def _():
                for block in (0, 1):
                    for half in range(2):
                        down(block, half).start()

        lax.fori_loop(0, 2, half_body, None)
        for block in (3, 2, 1):
            goal = last - block

            for half in range(2):
                at = slice(half * 8, half * 8 + 8)

                @pl.when((part < block) & (part > 0))
                def _():
                    up(block, half).wait_recv()
                    partial[block, at] += from_low[block, at]
                    up(block, half).start()

                @pl.when((part > goal) & (part < last))
                def _():
                    down(goal, half).wait_recv()
                    partial[goal, at] += from_high[goal, at]
                    down(goal, half).start()

                if block == 1:

                    @pl.when(part == 0)
                    def _():
                        up(1, half).start()

                    @pl.when(part == last)
                    def _():
                        down(2, half).start()

        aside()
        for block in range(4):

            @pl.when(part == block)
            def _():
                for half in range(2):
                    at = slice(half * 8, half * 8 + 8)
                    total = partial[block, at]
                    if block > 0:
                        up(block, half).wait_recv()
                        total = total + from_low[block, at]
                    if block < last:
                        down(block, half).wait_recv()
                        total = total + from_high[block, at]
                    flow[at] = total

        for block in (3, 2, 1):
            goal = last - block
            for half in range(2):

                @pl.when(part < block)
                def _():
                    up(block, half).wait_send()

                @pl.when(part > goal)
                def _():
                    down(goal, half).wait_send()

    def turn_block(block, left, turned_block):
        value = slots[block].reshape(16 * count, LANES)
        left[...] = jnp.concatenate(halves(value), axis=1)
        turned_block[...] = jnp.concatenate(halves(value.T), axis=0)

    def use_block(block, left, turned_block, high, low, maps):
        at = pl.ds(pl.multiple_of(block * LANES, LANES), LANES)

        for down in range(3):
            right = []
            first, after = reach(down)
            taps = [slice((down * 3 + step) * LANES, (down * 3 + step + 1) * LANES) for step in range(3)]
            for lanes in taps:
                weight = jnp.concatenate([high[at, lanes], low[at, lanes]], axis=1)
                right.append(jnp.concatenate([weight, weight], axis=0))
            out = mul(
                left[first * 4 * count : after * 4 * count], jnp.concatenate(right, axis=1)
            )
            for step in range(3):
                start = 2 * step * LANES
                fold_sum[down + first : down + after, step : step + 4] += (
                    out[:, start : start + LANES] + out[:, start + LANES : start + 2 * LANES]
                ).reshape(after - first, 4, count, LANES)
            out = mul(
                turned_block[...],
                jnp.concatenate([window(maps, down, step) for step in range(3)], axis=1),
            )
            out = out[:LANES] + out[LANES:]
            for step, lanes in enumerate(taps):
                start = 2 * step * LANES
                sum_two[block, :, :, :, lanes] += (
                    out[:, start : start + LANES] + out[:, start + LANES : start + 2 * LANES]
                ).reshape(4, 2, 16, LANES)

    def pair_two(block):
        return remote(
            sum_two.at[block, :, 1 - core],
            half_two.at[block],
            pair_send.at[block],
            pair_recv.at[block],
            pair,
        )

    def plane_two(block, step):
        other = place ^ step
        return remote(
            half_two.at[block, other],
            piece_two.at[step, block],
            plane_send.at[block, step],
            plane_recv.at[block, step],
            row_peer(other * 2 + core),
        )

    def plane_two_go(block):
        pair_two(block).wait()
        for place_of in range(4):
            half_two[block, place_of] += sum_two[block, place_of, core]
        for step in range(1, 4):
            plane_two(block, step).start()

    def step_two(block, new_of, more):
        for step in range(1, 4):
            plane_two(block, step).wait()
        change = half_two[block, place] + piece_two[1, block] + piece_two[2, block] + piece_two[3, block]
        new = new_of(v2[me, block], change, d2[block])
        v2[me, block] = new
        series_two[block] += new

        @pl.when(more)
        def _():
            back_start((block,))

    def back_forward_when(block, more):
        @pl.when(more)
        def _():
            back_forward((block,))

    def gather_and_use(block_of, new_of, more):
        ring_start(slots, ring_send, ring_recv)

        def order_at(index):
            first = jnp.where(index == 0, order[0], order[1])
            return jnp.where(index < 2, first, jnp.where(index == 2, order[2], order[3]))

        def body(index, _):
            @pl.when(index > 0)
            def _():
                ring_step(slots, ring_send, ring_recv, index)

            @pl.when(index == 2)
            def _():
                step_two(order[0], new_of, more)

            block = order_at(index)
            block_of(block)
            pair_two(block).start()

            @pl.when((index == 1) | (index == 2))
            def _():
                plane_two_go(order_at(index - 1))

        lax.fori_loop(0, 4, body, None)

    def beside_sums(new_of, more):
        step_two(order[1], new_of, more)
        plane_two_go(order[2])
        back_forward_when(order[0], more)
        ring_end(slots, ring_send, ring_recv)
        plane_two_go(order[3])

    def pair_one(group):
        return remote(
            sum_one.at[pl.ds(group * 3, 3), :, :, 1 - core],
            half_one.at[pl.ds(group * 3, 3)],
            pair_send.at[4 + group],
            pair_recv.at[4 + group],
            pair,
        )

    across_x, across_y = row_peer(me ^ copies), row_peer(me ^ 2)
    lower, upper = pl.ds(0, channels // 2), pl.ds(channels // 2, channels // 2)

    def taps_of(group):
        return pl.ds(group * 3, 3)

    def fold_one(group, step):
        taps = taps_of(group)
        source, goal, device = (
            (half_one.at[taps, 1 - member, :, :, lower], first_low.at[taps], across_x),
            (half_one.at[taps, :, 1 - line, :, upper], first_up.at[taps], across_y),
            (half_one.at[taps, member, 1 - line, :, lower], second_low.at[taps], across_y),
            (half_one.at[taps, 1 - member, line, :, upper], second_up.at[taps], across_x),
        )[step]
        return remote(source, goal, fold_send.at[group, step], fold_recv.at[group, step], device)

    def spread_one(group, step, arriving=False):
        taps = taps_of(group)
        x, y = member, line
        if arriving:
            x, y = (x, 1 - y) if step in (0, 3) else (1 - x, y)
        piece = (
            v1.at[taps, x, y, core, :, lower],
            v1.at[taps, x, y, core, :, upper],
            v1.at[taps, x, :, core, :, lower],
            v1.at[taps, :, y, core, :, upper],
        )[step]
        device = across_y if step in (0, 3) else across_x
        return remote(piece, piece, open_send.at[group, step], open_recv.at[group, step], device)

    def share_one(group, step, arriving=False):
        taps = taps_of(group)
        side = 1 - core if arriving else core
        piece = (
            v1.at[taps, member, line, side],
            v1.at[taps, member, 1 - line, side, :, lower],
            v1.at[taps, 1 - member, line, side, :, upper],
            v1.at[taps, 1 - member, :, side, :, lower],
            v1.at[taps, :, 1 - line, side, :, upper],
        )[step]
        return remote(piece, piece, share_send.at[group, step], share_recv.at[group, step], pair)

    def open_first(group):
        spread_one(group, 0).start()
        spread_one(group, 1).start()
        share_one(group, 0).start()

    def open_second(group):
        spread_one(group, 0, True).wait_recv()
        spread_one(group, 2).start()
        spread_one(group, 1, True).wait_recv()
        spread_one(group, 3).start()
        share_one(group, 1).start()
        share_one(group, 2).start()

    def open_third(group):
        spread_one(group, 2, True).wait_recv()
        share_one(group, 3).start()
        spread_one(group, 3, True).wait_recv()
        share_one(group, 4).start()

    def open_arrived(group):
        for step in range(5):
            share_one(group, step, True).wait_recv()

    def open_end(group):
        for step in range(4):
            spread_one(group, step).wait_send()
        for step in range(5):
            share_one(group, step).wait_send()

    def pair_add(group):
        pair_one(group).wait()

        def body(tap, _):
            half_one[tap] += sum_one[tap, :, :, core]

        lax.fori_loop(group * 3, group * 3 + 3, body, None)
        fold_one(group, 0).start()
        fold_one(group, 1).start()

    def fold_add(group):
        fold_one(group, 0).wait()
        fold_one(group, 1).wait()

        def body(tap, _):
            half_one[tap, member, :, :, lower] += first_low[tap]
            half_one[tap, :, line, :, upper] += first_up[tap]

        lax.fori_loop(group * 3, group * 3 + 3, body, None)
        fold_one(group, 2).start()
        fold_one(group, 3).start()

    def first_gradient(new_of, more):
        def taps_weight(down):
            out = mul(
                turned[...],
                jnp.concatenate(
                    [window(x_both, down, step, slice(0, channels)) for step in range(3)], axis=1
                ),
            )
            out = out + mul(
                turned[...],
                jnp.concatenate(
                    [
                        window(x_both, down, step, slice(channels, 2 * channels))
                        for step in range(3)
                    ],
                    axis=1,
                ),
            )
            out = out[:LANES] + out[LANES:]
            for step in range(3):
                sum_one[down * 3 + step] = out[:, step * channels : (step + 1) * channels].reshape(
                    sum_one.shape[1:]
                )

        def body(group, _):
            taps_weight(group)
            pair_one(group).start()

            @pl.when(group == 0)
            def _():
                step_two(order[2], new_of, more)

            @pl.when(group > 0)
            def _():
                pair_add(group - 1)

            @pl.when(group > 1)
            def _():
                fold_add(group - 2)

        lax.fori_loop(0, GROUPS, body, None)
        pair_add(GROUPS - 1)
        back_forward_when(order[1], more)
        fold_add(GROUPS - 2)
        step_two(order[3], new_of, more)
        fold_add(GROUPS - 1)

    def step_group(group, new_of):
        fold_one(group, 2).wait()
        fold_one(group, 3).wait()

        def body(tap, _):
            change = half_one[tap, member, line] + jnp.concatenate(
                [second_low[tap], second_up[tap]], axis=1
            )
            new = new_of(v1[tap, member, line, core], change, d1[tap])
            v1[tap, member, line, core] = new
            series_one[:, tap_lanes(tap, channels)] += new

        lax.fori_loop(group * 3, group * 3 + 3, body, None)

    def no_aside():
        pass

    series_one[...] = jnp.zeros_like(series_one)
    series_two[...] = jnp.zeros_like(series_two)

    def first_vector(old, change, decay):
        return change + decay * old

    def next_vector(old, change, decay):
        return old - neumann_rate * (change + decay * old)

    for load in k1_loads + d1_loads:
        load.wait()
    for group in range(GROUPS):
        for move in k1_moves[group * 3 : group * 3 + 3]:
            move.wait()
        k1_share(group).start()
    ring_step(x_box, x_send, x_recv, 2)
    for block in range(4):
        back_forward((block,))
    for group in range(GROUPS):
        k1_share(group, True).wait_recv()
        lax.fori_loop(group * 3, group * 3 + 3, split_one, None)
    for group in range(GROUPS):
        k1_share(group).wait_send()
    ring_step(x_box, x_send, x_recv, 3)
    ring_end(x_box, x_send, x_recv)

    def place_images(cell, _):
        for block in range(4):
            x_row[block * own_count : (block + 1) * own_count] = x_box[block, cell]
        high, low = halves(x_row[...])
        x_both[cell // 4 + 1, cell % 4 + 1, :, 0:channels] = high
        x_both[cell // 4 + 1, cell % 4 + 1, :, channels : 2 * channels] = low
        x_own[cell] = x_row[:, pl.ds(pl.multiple_of(part * LANES, LANES), LANES)]

    each_cell(place_images)
    flow[...] = jnp.zeros_like(flow)
    lax.fori_loop(0, 3, lambda row_of_taps, _: taps_forward(row_of_taps), None)

    def sums_primal(cell, carry):
        value = flow[cell]
        return carry[0] + value, carry[1] + value * value

    put_sums(0, *each_cell(sums_primal, (zero, zero)))
    stats_own[0, 2:3, :] = jnp.sum(valid, axis=0, keepdims=True)
    moves = sum_start(0, 8)
    cut_end(1)
    for block in range(4):
        back_arrived((block,))
        back_end((block,))
    split_two(k_hi, k_lo)
    total = sum_end(0, 8, moves)
    label_total = total[2:3]
    average = total[0:1] * inverse
    scale = lax.rsqrt(total[1:2] * inverse - average * average + norm_eps)
    gain, shift = row(move_norm, 0), row(move_norm, 1)
    gain2, shift2 = row(move_norm, 2), row(move_norm, 3)

    def first_primal(cell, _):
        normal = (flow[cell] - average) * scale
        value, slope, bend = silu_pieces(normal * gain + shift)
        n1[cell] = normal
        s1[cell] = slope
        pb1[cell] = bend
        a_both[cell // 4 + 1, cell % 4 + 1] = jnp.concatenate(halves(value), axis=1)

    each_cell(first_primal)
    scatter(a_both, k_hi, k_lo, False, no_aside)
    put_sums(1, *each_cell(sums_primal, (zero, zero)))
    total = sum_end(1, 8, sum_start(1, 8))
    average = total[0:1] * inverse
    scale2 = lax.rsqrt(total[1:2] * inverse - average * average + norm_eps)

    def second_primal(cell, carry):
        normal = (flow[cell] - average) * scale2
        value, slope, bend = silu_pieces(normal * gain2 + shift2 + x_own[cell])
        n2[cell] = normal
        s2[cell] = slope
        pb2[cell] = bend
        return carry + value

    pooled[...] = each_cell(second_primal, zero) * (1.0 / 16.0)
    logits = sum_parts(mul_exact(pooled[...], head[...], ((1,), (1,))))
    real = lax.broadcasted_iota(jnp.int32, logits.shape, 1) < classes
    highest = jnp.max(jnp.where(real, logits, -jnp.inf), axis=1, keepdims=True)
    powers = jnp.where(real, jnp.exp(logits - highest), 0.0)
    sum_powers = jnp.sum(powers, axis=1, keepdims=True)
    chances[...] = powers / sum_powers
    target_logit = jnp.sum(chosen * logits, axis=1, keepdims=True)
    cross = (highest + jnp.log(sum_powers) - target_logit) * valid
    weights[...] = valid / label_total
    pull_logits[...] = weights[...] * (chances[...] - chosen)
    out_head = mul_exact(pull_logits[...], pooled[...], ((0,), (0,)))
    pull_block = mul_exact(pull_logits[...], head[...]) * (1.0 / 16.0)

    def back_two_primal(cell, carry):
        pull = pull_block * s2[cell]
        pull2[cell] = pull
        pb2[cell] = pull_block * pb2[cell]
        return carry[0] + pull * n2[cell], carry[1] + pull

    put_sums(2, *each_cell(back_two_primal, (zero, zero)))
    stats_own[2, 2:3, :] = jnp.sum(cross, axis=0, keepdims=True)
    stats_own[2, 8:24, :] = out_head[0:16]
    total = sum_end(2, 24, sum_start(2, 24))
    grad_small[0:1, :] = total[2:3]
    grad_small[1:2, :] = label_total
    grad_small[2:8, :] = jnp.zeros((6, LANES), jnp.float32)
    grad_small[16:32, :] = total[8:24]
    out_gain2, out_shift2 = total[0:1], total[1:2]
    factor2 = scale2 * gain2

    def pull_two_primal(cell, _):
        centred = pull2[cell] - out_shift2 * inverse - n2[cell] * (out_gain2 * inverse)
        c2[cell] = centred
        slots[part, cell] = factor2 * centred

    each_cell(pull_two_primal)
    fold_sum[...] = jnp.zeros_like(fold_sum)
    sum_two[...] = jnp.zeros_like(sum_two)

    def primal_block(block):
        turn_block(block, g_left.at[block], g_turned.at[block])
        use_block(block, g_left.at[block], g_turned.at[block], k_hi, k_lo, a_both)

    gather_and_use(primal_block, first_vector, True)

    def back_one_primal(cell, carry):
        seen = fold_sum[cell // 4 + 1, cell % 4 + 1]
        pull = seen * s1[cell]
        pull1[cell] = pull
        pb1[cell] = seen * pb1[cell]
        return carry[0] + pull * n1[cell], carry[1] + pull

    put_sums(3, *each_cell(back_one_primal, (zero, zero)))
    moves = sum_start(3, 8)
    beside_sums(first_vector, True)
    total = sum_end(3, 8, moves)
    out_gain, out_shift = total[0:1], total[1:2]
    factor = scale * gain

    def pull_one_primal(cell, _):
        centred = pull1[cell] - out_shift * inverse - n1[cell] * (out_gain * inverse)
        c1[cell] = centred
        flow[cell] = factor * centred

    each_cell(pull_one_primal)
    turned[...] = jnp.concatenate(halves(flow[...].reshape(16 * count, LANES).T), axis=0)

    channel[0:1, :] = scale
    channel[1:2, :] = gain
    channel[2:3, :] = scale2
    channel[3:4, :] = gain2
    channel[4:5, :] = out_gain * inverse
    channel[5:6, :] = out_gain2 * inverse
    move_norm[0:1, :] = out_gain
    move_norm[1:2, :] = out_shift
    move_norm[2:3, :] = out_gain2
    move_norm[3:4, :] = out_shift2
    grad_small[8:16, :] = move_norm[...]
    move_head[0:16] = grad_small[16:32, :]

    first_gradient(first_vector, True)

    def deliver_move(which, source, other):
        return remote(
            source.at[other],
            row_parts.at[which, part],
            row_send.at[which, other],
            row_recv.at[which, part],
            part_peer(other),
        )

    def deliver_start(which, source):
        for other in range(4):

            @pl.when(part != other)
            def _():
                deliver_move(which, source, other).start()

        row_parts[which, part] = source[part]

    def deliver_end(which, source, result):
        for other in range(4):

            @pl.when(part != other)
            def _():
                deliver_move(which, source, other).wait_send()
                remote(
                    source.at[other],
                    row_parts.at[which, other],
                    row_send.at[which, other],
                    row_recv.at[which, other],
                    part_peer(other),
                ).wait_recv()

        for other in range(4):
            for tap in range(TAPS):
                start = tap * channels + other * LANES
                result[copy, :, start : start + LANES] = row_parts[
                    which, other, :, tap * LANES : (tap + 1) * LANES
                ]

    across, corner = row_peer(me ^ 2), copy ^ 2

    def spread_move(which, result, step, block, device):
        return remote(
            result.at[block], result.at[block], own_send.at[which, step], own_recv.at[which, step], device
        )

    def spread_start(which, result):
        spread_move(which, result, 0, copy, across).start()
        spread_move(which, result, 1, copy, pair).start()

    def spread_forward(which, result):
        spread_move(which, result, 0, corner, across).wait_recv()
        spread_move(which, result, 2, corner, pair).start()

    def spread_end(which, result):
        spread_move(which, result, 1, copy ^ 1, pair).wait_recv()
        spread_move(which, result, 2, copy ^ 3, pair).wait_recv()
        spread_move(which, result, 0, copy, across).wait_send()
        spread_move(which, result, 1, copy, pair).wait_send()
        spread_move(which, result, 2, corner, pair).wait_send()

    grad_source[...] = series_two[...]
    deliver_start(0, grad_source)
    for group in range(GROUPS):
        step_group(group, first_vector)
        open_first(group)

    def turn_body(turn, nothing):
        flow[...] = jnp.zeros_like(flow)

        def forward_group(group, _):
            open_arrived(group)
            lax.fori_loop(group * 3, group * 3 + 3, split_one, None)
            taps_forward(group)

        fold_sum[...] = jnp.zeros_like(fold_sum)
        sum_two[...] = jnp.zeros_like(sum_two)
        open_second(0)
        open_second(1)
        back_forward((order[2],))
        back_forward((order[3],))
        for block in range(4):
            back_arrived((block,))
            back_end((block,))
        split_two(v2_hi, v2_lo)
        open_third(0)
        open_second(2)

        def vector_half(half, _):
            part_of_second(a_both, v2_hi, v2_lo, half, False)

            @pl.when(half == 0)
            def _():
                open_third(1)
                open_third(2)

        lax.fori_loop(0, 2, vector_half, None)
        lax.fori_loop(0, GROUPS, forward_group, None)
        for group in range(GROUPS):
            open_end(group)

        @pl.when(turn == 0)
        def _():
            for tap in range(TAPS):
                grads[0, :, :, tap * channels : (tap + 1) * channels] = v1[tap, member].reshape(
                    4, v1.shape[4], channels
                )

        def sums_forward(normal):
            def body(cell, carry):
                value = flow[cell]
                return carry[0] + value, carry[1] + value * normal[cell]

            return each_cell(body, (zero, zero))

        put_sums(0, *sums_forward(n1))
        moves = sum_start(0, 8)
        total = sum_end(0, 8, moves) * inverse
        average, cross = total[0:1], total[1:2]
        scale, gain = row(channel, 0), row(channel, 1)
        tan_scale_one = -scale * scale * cross
        move_gain, move_shift = row(move_norm, 0), row(move_norm, 1)

        def forward_one(cell, _):
            normal = n1[cell]
            tangent = scale * (flow[cell] - average - normal * cross)
            inner = move_gain * normal + gain * tangent + move_shift
            nt1[cell] = tangent
            in1[cell] = inner
            b_both[cell // 4 + 1, cell % 4 + 1] = jnp.concatenate(halves(s1[cell] * inner), axis=1)

        each_cell(forward_one)

        def aside():
            def body(block, _):
                use_block(block, g_left.at[block], g_turned.at[block], v2_hi, v2_lo, b_both)

            lax.fori_loop(0, 4, body, None)

        scatter(b_both, k_hi, k_lo, True, aside)

        @pl.when(turn == 0)
        def _():
            deliver_end(0, grad_source, grads.at[1])
            spread_start(0, grads.at[1])

        @pl.when(turn == 1)
        def _():
            spread_forward(0, grads.at[1])


        put_sums(1, *sums_forward(n2))
        moves = sum_start(1, 8)
        early_logits = mul_exact(pooled[...], move_head[...], ((1,), (1,)))
        early_block = mul_exact(pull_logits[...], move_head[...])
        total = sum_end(1, 8, moves) * inverse
        average2, cross2 = total[0:1], total[1:2]
        scale2, gain2 = row(channel, 2), row(channel, 3)
        tan_scale_two = -scale2 * scale2 * cross2
        move_gain2, move_shift2 = row(move_norm, 2), row(move_norm, 3)

        def forward_two(cell, carry):
            normal = n2[cell]
            tangent = scale2 * (flow[cell] - average2 - normal * cross2)
            inner = move_gain2 * normal + gain2 * tangent + move_shift2
            nt2[cell] = tangent
            in2[cell] = inner
            return carry + s2[cell] * inner

        tan_pooled = each_cell(forward_two, zero) * (1.0 / 16.0)
        tan_logits = sum_parts(mul_exact(tan_pooled, head[...], ((1,), (1,))) + early_logits)
        chance = chances[...]
        tan_pull = (
            weights[...]
            * chance
            * (tan_logits - jnp.sum(chance * tan_logits, axis=1, keepdims=True))
        )
        tan_block = (mul_exact(tan_pull, head[...]) + early_block) * (1.0 / 16.0)

        def back_two(cell, carry):
            tangent = tan_block * s2[cell] + pb2[cell] * in2[cell]
            flow[cell] = tangent
            return (
                carry[0] + tangent * n2[cell] + pull2[cell] * nt2[cell],
                carry[1] + tangent,
            )

        put_sums(2, *each_cell(back_two, (zero, zero)))
        moves = sum_start(2, 8)
        out_head = mul_exact(pull_logits[...], tan_pooled, ((0,), (0,))) + mul_exact(
            tan_pull, pooled[...], ((0,), (0,))
        )
        stats_own[3, 8:24, :] = out_head[0:16]
        total = sum_end(2, 8, moves)
        out_gain2, out_shift2 = total[0:1], total[1:2]
        factor2 = scale2 * gain2
        tan_factor2 = tan_scale_two * gain2 + scale2 * move_gain2

        def pull_two_body(cell, _):
            slots[part, cell] = tan_factor2 * c2[cell] + factor2 * (
                flow[cell]
                - out_shift2 * inverse
                - nt2[cell] * row(channel, 5)
                - n2[cell] * (out_gain2 * inverse)
            )

        each_cell(pull_two_body)

        def turn_of_block(block):
            turn_block(block, t_left, t_turned)
            use_block(block, t_left, t_turned, k_hi, k_lo, a_both)

        more = turn < NEUMANN - 1
        gather_and_use(turn_of_block, next_vector, more)

        def back_one(cell, carry):
            pull = fold_sum[cell // 4 + 1, cell % 4 + 1]
            tangent = pull * s1[cell] + pb1[cell] * in1[cell]
            flow[cell] = tangent
            return (
                carry[0] + tangent * n1[cell] + pull1[cell] * nt1[cell],
                carry[1] + tangent,
            )

        put_sums(3, *each_cell(back_one, (zero, zero)))
        moves = sum_start(3, 24)
        beside_sums(next_vector, more)
        total = sum_end(3, 24, moves)
        move_head[0:16] = move_head[0:16] - neumann_rate * total[8:24]
        out_gain, out_shift = total[0:1], total[1:2]
        factor = scale * gain
        tan_factor = tan_scale_one * gain + scale * move_gain

        def pull_one_body(cell, _):
            flow[cell] = tan_factor * c1[cell] + factor * (
                flow[cell]
                - out_shift * inverse
                - nt1[cell] * row(channel, 4)
                - n1[cell] * (out_gain * inverse)
            )

        each_cell(pull_one_body)
        turned[...] = jnp.concatenate(halves(flow[...].reshape(16 * count, LANES).T), axis=0)
        move_norm[0:1, :] = move_gain - neumann_rate * out_gain
        move_norm[1:2, :] = move_shift - neumann_rate * out_shift
        move_norm[2:3, :] = move_gain2 - neumann_rate * out_gain2
        move_norm[3:4, :] = move_shift2 - neumann_rate * out_shift2
        first_gradient(next_vector, more)

        @pl.when(turn == NEUMANN - 1)
        def _():
            deliver_start(1, series_two)

        for group in range(GROUPS):
            step_group(group, next_vector)

            @pl.when(more)
            def _():
                open_first(group)

    lax.fori_loop(0, NEUMANN, turn_body, None)

    series[0, copy] = series_one[...]
    spread_start(1, series.at[0])
    deliver_end(1, series_two, series.at[1])
    spread_start(2, series.at[1])
    spread_forward(1, series.at[0])
    spread_forward(2, series.at[1])
    spread_end(0, grads.at[1])
    spread_end(1, series.at[0])
    spread_end(2, series.at[1])


def step_fused(
    links,
    rows,
    source,
    index_map,
    crop_offsets,
    flip_flags,
    labels,
    valid_mask,
    conv_weights,
    norm_params,
    head_weights,
    decay_rates,
):
    own_count, channels = source.shape[0], source.shape[3]
    cells, count = MAP * MAP, own_count * 4
    width, group = channels // 4, 8
    piece, block = width // group, channels // group
    classes = head_weights.shape[1]
    f32, b16 = jnp.float32, jnp.bfloat16
    small = jnp.concatenate(
        [
            norm_params,
            jnp.zeros((4, block), f32),
            head_weights.T,
            jnp.zeros((16 - classes, block), f32),
        ]
    )
    lane = links.member * block
    here = jnp.arange(2, dtype=jnp.int32)[None, :, None] == links.member
    operands = (
        source,
        index_map,
        crop_offsets,
        flip_flags,
        labels,
        valid_mask,
        conv_weights.reshape(2, 2, 2, piece, TAPS * channels),
        decay_rates.reshape(2, 2, 2, piece, TAPS * channels),
        jnp.where(here, small[:, None, :], 0.0).reshape(24, width),
    )
    vmem = pl.BlockSpec(memory_space=pltpu.VMEM)
    anywhere = pl.BlockSpec(memory_space=pl.ANY)
    row_map = pltpu.VMEM((cells, count, width), f32)
    four_maps = pltpu.VMEM((4, cells, count, width), f32)
    inner_piece = pltpu.VMEM((4, piece, TAPS * width), f32)
    inner_half = pltpu.VMEM((4, 4, piece, TAPS * width), f32)
    inner_part = pltpu.VMEM((channels, TAPS * width), b16)
    outer_part = pltpu.VMEM((TAPS, width, channels), b16)
    both = pltpu.VMEM((MAP + 2, MAP + 2, count, 2 * width), b16)
    logit = pltpu.VMEM((count, LANES), f32)
    dma = pltpu.SemaphoreType.DMA
    scratch = [
        pltpu.VMEM((piece, TAPS * channels), f32),
        inner_piece,
        inner_piece,
        pltpu.VMEM((2, 4, piece, TAPS * width), f32),
        pltpu.VMEM((2, piece, TAPS * channels), f32),
        pltpu.VMEM((2, 4, piece, TAPS * width), f32),
        pltpu.VMEM((TAPS, piece, channels), f32),
        inner_piece,
        pltpu.VMEM((TAPS, 2, 2, 2, piece, channels), f32),
        pltpu.VMEM((group, 4, piece, TAPS * width), f32),
        outer_part,
        outer_part,
        inner_part,
        inner_part,
        inner_part,
        inner_part,
        pltpu.VMEM(source.shape, f32),
        pltpu.VMEM((4, cells, own_count, channels), f32),
        pltpu.VMEM((count, channels), f32),
        pltpu.VMEM((MAP + 2, MAP + 2, count, 2 * channels), b16),
        row_map,
        both,
        both,
        pltpu.VMEM((4, cells * count, 2 * width), b16),
        pltpu.VMEM((4, 2 * width, cells * count), b16),
        pltpu.VMEM((cells * count, 2 * width), b16),
        pltpu.VMEM((2 * width, cells * count), b16),
        four_maps,
        four_maps,
        four_maps,
        four_maps,
        *[row_map] * 15,
        pltpu.VMEM((MAP + 2, MAP + 2, count, width), f32),
        pltpu.VMEM((TAPS, 2, 2, 2, piece, channels), f32),
        pltpu.VMEM((4, 4, 2, piece, TAPS * width), f32),
        pltpu.VMEM((TAPS, 2, 2, piece, channels), f32),
        inner_half,
        *[pltpu.VMEM((TAPS, 2, piece, channels // 2), f32)] * 2,
        *[pltpu.VMEM((TAPS, piece, channels // 2), f32)] * 2,
        inner_half,
        pltpu.VMEM((4, 8, 24, width), f32),
        pltpu.VMEM((4, 24, width), f32),
        pltpu.VMEM((4, count, LANES), f32),
        logit,
        pltpu.VMEM((24, width), f32),
        pltpu.VMEM((4, 2 * count, LANES), f32),
        pltpu.VMEM((2 * width, cells * count), b16),
        pltpu.VMEM((8, width), f32),
        pltpu.VMEM((8, width), f32),
        pltpu.VMEM((LANES, width), f32),
        pltpu.VMEM((LANES, width), f32),
        logit,
        logit,
        logit,
        logit,
        dma(()),
        dma((2,)),
        dma((2,)),
        dma((TAPS,)),
        dma((TAPS,)),
        dma((TAPS,)),
        dma((TAPS,)),
        dma((GROUPS,)),
        dma((GROUPS,)),
        dma((2, 4)),
        dma((2, 4)),
        dma((4,)),
        dma((4,)),
        dma((2, 4, 2)),
        dma((4, 2)),
        dma((4, 8)),
        dma((4, 8)),
        dma((4,)),
        dma((4,)),
        dma((4, 2)),
        dma((4, 2)),
        dma((4, 2)),
        dma((4, 2)),
        dma((2, 4, 2)),
        dma((4, 2)),
        dma((GROUPS + 4,)),
        dma((GROUPS + 4,)),
        dma((4, 4)),
        dma((4, 4)),
        dma((4, 4)),
        dma((4, 4)),
        dma((4, 4)),
        dma((4, 4)),
        dma((GROUPS, 4)),
        dma((GROUPS, 4)),
        dma((GROUPS, 4)),
        dma((GROUPS, 4)),
        dma((GROUPS, 5)),
        dma((GROUPS, 5)),
        dma((2, 4)),
        dma((2, 4)),
        dma((3, 3)),
        dma((3, 3)),
    ]
    result = jax.ShapeDtypeStruct((2, 4, piece, TAPS * channels), f32)
    grads, series, grad_small = pl.pallas_call(
        functools.partial(step_kernel, rows, links.members, links.copies, classes),
        out_shape=(result, result, jax.ShapeDtypeStruct((32, width), f32)),
        in_specs=[anywhere] + [pl.BlockSpec(memory_space=pltpu.SMEM)] * 5 + [anywhere] * 2 + [vmem],
        out_specs=(vmem,) * 3,
        scratch_shapes=scratch,
        compiler_params=pltpu.CompilerParams(
            collective_id=1, has_side_effects=True, vmem_limit_bytes=63 * 1024 * 1024
        ),
        name="train_step",
    )(*operands)
    own = lax.dynamic_slice_in_dim(grad_small, lane, block, 1)
    return (
        grad_small[0, 0],
        grad_small[1, 0],
        grads.reshape(conv_weights.shape),
        own[8:12],
        own[16 : 16 + classes].T,
        series.reshape(conv_weights.shape),
    )


def adamw(weight, grad, first, second, rate):
    first = beta_first * first + (1.0 - beta_first) * grad
    second = beta_second * second + (1.0 - beta_second) * grad * grad
    first_hat = first / (1.0 - beta_first**STEP)
    second_hat = second / (1.0 - beta_second**STEP)
    update = first_hat / (jnp.sqrt(second_hat) + adam_eps) + decoupled * weight
    return (weight - rate * update, first, second)


def silu_parts(value):
    gate = jax.nn.sigmoid(value)
    slope = gate * (1.0 - gate)
    first = gate + value * slope
    second = slope * (2.0 + value * (1.0 - 2.0 * gate))
    return value * gate, first, second


class Links:
    def __init__(self):
        self.shards = lax.axis_size("shard")
        self.copies = lax.axis_size("dp")
        self.parts = 4 if self.shards % 4 == 0 else 1
        self.members = self.shards // self.parts
        index = lax.axis_index("shard")
        self.part = index // self.members
        self.member = index % self.members
        self.across = [
            [p * self.members + m for p in range(self.parts)] for m in range(self.members)
        ]
        self.within = [
            [p * self.members + m for m in range(self.members)] for p in range(self.parts)
        ]

    def sum_rows(self, value):
        value = lax.psum(value, "dp")
        gathered = lax.all_gather(value, "shard", axis_index_groups=self.within)
        return jnp.sum(gathered, axis=0)

    def sum_parts(self, value):
        return jnp.sum(lax.all_gather(value, "shard", axis_index_groups=self.across), axis=0)

    def gather_parts(self, value, axis):
        return lax.all_gather(value, "shard", axis_index_groups=self.across, axis=axis, tiled=True)

    def gather_members(self, value, axis):
        return lax.all_gather(value, "shard", axis_index_groups=self.within, axis=axis, tiled=True)

    def scatter_parts(self, value, axis):
        return lax.psum_scatter(
            value, "shard", axis_index_groups=self.across, scatter_dimension=axis, tiled=True
        )

    def to_inner(self, value):
        rows, channels = value.shape[0], value.shape[1] // TAPS
        width = channels // self.parts
        cut = value.reshape(rows, TAPS, self.parts, width).transpose(2, 0, 1, 3)
        moved = lax.all_to_all(cut, "shard", 0, 0, axis_index_groups=self.across, tiled=True)
        whole = self.gather_members(moved, 1)
        return whole.reshape(channels, TAPS * width)

    def to_outer(self, value):
        channels, width = value.shape[0], value.shape[1] // TAPS
        rows = channels // self.shards
        cut = value.reshape(self.parts, self.members, rows, TAPS * width)
        cut = lax.dynamic_index_in_dim(cut, self.member, 1, keepdims=False)
        moved = lax.all_to_all(cut, "shard", 0, 0, axis_index_groups=self.across, tiled=True)
        moved = moved.reshape(self.parts, rows, TAPS, width).transpose(1, 2, 0, 3)
        return moved.reshape(rows, TAPS * channels)

    def own_rows(self, value, axis=0):
        size = value.shape[axis] // self.members
        return lax.dynamic_slice_in_dim(value, self.member * size, size, axis)


def moments(hidden, rows, links):
    totals = links.sum_rows(jnp.stack([jnp.sum(hidden, axis=0), jnp.sum(hidden * hidden, axis=0)]))
    average = totals[0] / rows
    scale = lax.rsqrt(totals[1] / rows - average * average + norm_eps)
    return (hidden - average) * scale, scale


def moments_tangent(normal, scale, tangent, rows, links):
    totals = links.sum_rows(
        jnp.stack([jnp.sum(tangent, axis=0), jnp.sum(tangent * normal, axis=0)])
    )
    average, cross = totals[0] / rows, totals[1] / rows
    return scale * (tangent - average - normal * cross), -scale * scale * cross


def step_general(
    links,
    rows,
    source,
    index_map,
    crop_offsets,
    flip_flags,
    labels,
    valid_mask,
    conv_weights,
    norm_params,
    head_weights,
    decay_rates,
):
    images = jax.vmap(crop_image)(source[index_map], crop_offsets, flip_flags)
    images = images.transpose(1, 2, 0, 3)
    valid = valid_mask.astype(jnp.float32)
    own_images, channels = images.shape[2:]
    count = own_images * links.parts
    width = channels // links.parts
    first_column = links.part * width
    label_total = lax.psum(jnp.sum(valid), ("shard", "dp"))
    images = links.gather_parts(images, 2)
    labels = links.gather_parts(labels, 0)
    valid = links.gather_parts(valid, 0)

    kernel_one = links.gather_members(conv_weights[0], 0)
    kernel_two = links.to_inner(conv_weights[1])
    decay_one = links.gather_members(decay_rates[0], 0)
    decay_two = links.to_inner(decay_rates[1])
    norms = links.gather_members(norm_params, 1)
    head = links.gather_members(head_weights, 0)
    gain_one, shift_one, gain_two, shift_two = norms[0], norms[1], norms[2], norms[3]

    def pool(value):
        return jnp.sum(value.reshape(MAP * MAP, count, width), axis=0) / (MAP * MAP)

    def spread(value):
        whole = jnp.broadcast_to(value[None] / (MAP * MAP), (MAP * MAP, count, width))
        return whole.reshape(MAP * MAP * count, width)

    columns = patches(images)
    own_columns = lax.dynamic_slice_in_dim(
        images.reshape(MAP * MAP * count, channels), first_column, width, 1
    )

    hidden_one = dot(columns, kernel_one, ((1,), (1,)))
    normal_one, scale_one = moments(hidden_one, rows, links)
    active, slope_one, bend_one = silu_parts(normal_one * gain_one + shift_one)
    active_columns = patches(active.reshape(MAP, MAP, count, width))
    hidden_two = links.scatter_parts(dot(active_columns, kernel_two, ((1,), (1,))), 1)
    normal_two, scale_two = moments(hidden_two, rows, links)
    block, slope_two, bend_two = silu_parts(normal_two * gain_two + shift_two + own_columns)
    pooled = pool(block)
    logits = links.sum_parts(dot(pooled, head, ((1,), (0,))))
    highest = jnp.max(logits, axis=1, keepdims=True)
    powers = jnp.exp(logits - highest)
    total = jnp.sum(powers, axis=1, keepdims=True)
    chances = powers / total
    classes = jnp.arange(logits.shape[1], dtype=jnp.int32)
    chosen = (labels[:, None] == classes[None, :]).astype(jnp.float32)
    cross = highest[:, 0] + jnp.log(total[:, 0]) - jnp.sum(chosen * logits, axis=1)
    loss_sum = links.sum_rows(jnp.sum(valid * cross)[None])[0]
    weights = (valid / label_total)[:, None]
    pull_logits = weights * (chances - chosen)
    grad_head = dot(pooled, pull_logits, ((0,), (0,)))
    pull_block = spread(dot(pull_logits, head, ((1,), (1,))))
    pull_two = pull_block * slope_two
    sums_two = links.sum_rows(
        jnp.stack([jnp.sum(pull_two * normal_two, axis=0), jnp.sum(pull_two, axis=0)])
    )
    centred_two = pull_two - sums_two[1] / rows - normal_two * (sums_two[0] / rows)
    factor_two = scale_two * gain_two
    pull_hidden_two = links.gather_parts(factor_two * centred_two, 1)
    grad_two = dot(pull_hidden_two, active_columns, ((0,), (0,)))
    pull_active = fold(dot(pull_hidden_two, kernel_two, ((1,), (0,))), count)
    pull_one = pull_active * slope_one
    sums_one = links.sum_rows(
        jnp.stack([jnp.sum(pull_one * normal_one, axis=0), jnp.sum(pull_one, axis=0)])
    )
    centred_one = pull_one - sums_one[1] / rows - normal_one * (sums_one[0] / rows)
    factor_one = scale_one * gain_one
    grad_one = dot(factor_one * centred_one, columns, ((0,), (0,)))

    grad_one = links.sum_rows(grad_one) + decay_one * kernel_one
    grad_two = links.sum_rows(grad_two) + decay_two * kernel_two
    grad_head = links.sum_rows(grad_head)
    grad_norm = jnp.concatenate([sums_one, sums_two])

    def product(vector):
        move_one, move_two, move_norm, move_head = vector
        tan_hidden = dot(columns, move_one, ((1,), (1,)))
        tan_normal_one, tan_scale_one = moments_tangent(
            normal_one, scale_one, tan_hidden, rows, links
        )
        tan_inner = move_norm[0] * normal_one + gain_one * tan_normal_one + move_norm[1]
        tan_active = slope_one * tan_inner
        tan_columns = patches(tan_active.reshape(MAP, MAP, count, width))
        tan_hidden = links.scatter_parts(
            dot(tan_columns, kernel_two, ((1,), (1,))) + dot(active_columns, move_two, ((1,), (1,))),
            1,
        )
        tan_normal_two, tan_scale_two = moments_tangent(
            normal_two, scale_two, tan_hidden, rows, links
        )
        tan_outer = move_norm[2] * normal_two + gain_two * tan_normal_two + move_norm[3]
        tan_pooled = pool(slope_two * tan_outer)
        tan_logits = links.sum_parts(
            dot(tan_pooled, head, ((1,), (0,))) + dot(pooled, move_head, ((1,), (0,)))
        )
        tan_chances = chances * (tan_logits - jnp.sum(chances * tan_logits, axis=1, keepdims=True))
        tan_pull = weights * tan_chances
        out_head = dot(tan_pooled, pull_logits, ((0,), (0,))) + dot(pooled, tan_pull, ((0,), (0,)))
        tan_block = spread(
            dot(tan_pull, head, ((1,), (1,))) + dot(pull_logits, move_head, ((1,), (1,)))
        )
        tan_two = tan_block * slope_two + pull_block * bend_two * tan_outer
        tan_sums_two = links.sum_rows(
            jnp.stack(
                [
                    jnp.sum(tan_two * normal_two + pull_two * tan_normal_two, axis=0),
                    jnp.sum(tan_two, axis=0),
                ]
            )
        )
        tan_factor = tan_scale_two * gain_two + scale_two * move_norm[2]
        tan_hidden = tan_factor * centred_two + factor_two * (
            tan_two
            - tan_sums_two[1] / rows
            - tan_normal_two * (sums_two[0] / rows)
            - normal_two * (tan_sums_two[0] / rows)
        )
        tan_hidden = links.gather_parts(tan_hidden, 1)
        out_two = dot(tan_hidden, active_columns, ((0,), (0,))) + dot(
            pull_hidden_two, tan_columns, ((0,), (0,))
        )
        tan_pull_active = fold(
            dot(tan_hidden, kernel_two, ((1,), (0,))) + dot(pull_hidden_two, move_two, ((1,), (0,))),
            count,
        )
        tan_one = tan_pull_active * slope_one + pull_active * bend_one * tan_inner
        tan_sums_one = links.sum_rows(
            jnp.stack(
                [
                    jnp.sum(tan_one * normal_one + pull_one * tan_normal_one, axis=0),
                    jnp.sum(tan_one, axis=0),
                ]
            )
        )
        tan_factor = tan_scale_one * gain_one + scale_one * move_norm[0]
        tan_hidden = tan_factor * centred_one + factor_one * (
            tan_one
            - tan_sums_one[1] / rows
            - tan_normal_one * (sums_one[0] / rows)
            - normal_one * (tan_sums_one[0] / rows)
        )
        out_one = dot(tan_hidden, columns, ((0,), (0,)))
        return (
            links.sum_rows(out_one) + decay_one * move_one,
            links.sum_rows(out_two) + decay_two * move_two,
            jnp.concatenate([tan_sums_one, tan_sums_two]),
            links.sum_rows(out_head),
        )

    vector = (grad_one, grad_two, grad_norm, grad_head)
    series_one, series_two = grad_one, grad_two
    for turn in range(NEUMANN):
        change = product(vector)
        vector = tuple(
            previous - neumann_rate * moved for previous, moved in zip(vector, change)
        )
        series_one, series_two = series_one + vector[0], series_two + vector[1]

    series = jnp.stack([links.own_rows(series_one), links.to_outer(series_two)])
    grads = jnp.stack([links.own_rows(grad_one), links.to_outer(grad_two)])
    return (
        loss_sum,
        label_total,
        grads,
        links.own_rows(grad_norm, 1),
        links.own_rows(grad_head),
        series,
    )


def shards(
    source,
    index_map,
    crop_offsets,
    flip_flags,
    labels,
    valid_mask,
    conv_weights,
    norm_params,
    head_weights,
    decay_rates,
    conv_first,
    conv_second,
    norm_first,
    norm_second,
    head_first,
    head_second,
):
    links = Links()
    rows = float(source.shape[0] * MAP * MAP * links.shards * links.copies)
    fused = links.members * links.copies == 8 and links.members == 2 and links.parts == 4
    loss_sum, label_total, grads, grad_norm, grad_head, series = (
        step_fused if fused else step_general
    )(
        links,
        rows,
        source,
        index_map,
        crop_offsets,
        flip_flags,
        labels,
        valid_mask,
        conv_weights,
        norm_params,
        head_weights,
        decay_rates,
    )
    hyper_gradient = -neumann_rate * conv_weights * series
    conv_new, conv_one, conv_two = adamw(conv_weights, grads, conv_first, conv_second, 0.015)
    norm_new, norm_one, norm_two = adamw(
        norm_params, grad_norm, norm_first, norm_second, 0.3
    )
    head_new, head_one, head_two = adamw(
        head_weights, grad_head, head_first, head_second, 0.13
    )
    return (
        loss_sum,
        label_total,
        conv_new,
        conv_one,
        conv_two,
        norm_new,
        norm_one,
        norm_two,
        head_new,
        head_one,
        head_two,
        hyper_gradient,
    )


def solution(mesh):
    images = P(("shard", "dp"))
    rows = P(None, "shard")
    head = P("shard")
    in_specs = (images,) * 6 + (rows, rows, head, rows, rows, rows, rows, rows, head, head)
    out_specs = (P(), P()) + (rows,) * 6 + (head,) * 3 + (rows,)
    return jax.shard_map(shards, mesh=mesh, in_specs=in_specs, out_specs=out_specs, check_vma=False)
```

```python
import functools

import jax
import jax.numpy as jnp
from jax import lax
from jax.experimental import pallas as pl
from jax.experimental.pallas import tpu as pltpu
from jax.sharding import PartitionSpec as P

MAP = 4
NEUMANN = 3
STEP = 5
TAPS = 9

norm_eps = 1e-05
neumann_rate = 10.0
beta_first = 0.5
beta_second = 0.5
adam_eps = 1e-08
decoupled = 0.01
HIGH = lax.Precision.HIGH


def crop_image(single, offsets, flipped):
    window = lax.dynamic_slice(
        single, (offsets[0], offsets[1], jnp.int32(0)), (MAP, MAP, single.shape[2])
    )
    return jnp.where(flipped == 1, window[:, ::-1, :], window)


def patches(maps):
    count, width = maps.shape[2:]
    padded = jnp.pad(maps, ((1, 1), (1, 1), (0, 0), (0, 0)))
    taps = [padded[dy : dy + MAP, dx : dx + MAP] for dy in range(3) for dx in range(3)]
    return jnp.concatenate(taps, axis=3).reshape(MAP * MAP * count, TAPS * width)


def fold(columns, count):
    width = columns.shape[1] // TAPS
    whole = columns.reshape(MAP, MAP, count, TAPS, width)
    padded = jnp.pad(whole, ((1, 1), (1, 1), (0, 0), (0, 0), (0, 0)))
    total = 0.0
    for dy in range(3):
        for dx in range(3):
            total = total + padded[2 - dy : 2 - dy + MAP, 2 - dx : 2 - dx + MAP, :, dy * 3 + dx]
    return total.reshape(MAP * MAP * count, width)


def dot(left, right, dims):
    return lax.dot_general(
        left, right, ((dims[0], dims[1]), ((), ())), precision=HIGH, preferred_element_type=jnp.float32
    )


MESH_ID = pl.DeviceIdType.MESH
LANES = 128
GROUPS = 3


def halves(value):
    high = value.astype(jnp.bfloat16)
    return high, (value - high.astype(jnp.float32)).astype(jnp.bfloat16)


def mul(left, right, dims=((1,), (0,))):
    return lax.dot_general(left, right, (dims, ((), ())), preferred_element_type=jnp.float32)


def mul_exact(left, right, dims=((1,), (0,))):
    return lax.dot_general(
        left,
        right,
        (dims, ((), ())),
        precision=lax.Precision.HIGHEST,
        preferred_element_type=jnp.float32,
    )


def silu_pieces(value):
    gate = 1.0 / (1.0 + jnp.exp(-value))
    slope = gate * (1.0 - gate)
    return value * gate, gate + value * slope, slope * (2.0 + value * (1.0 - 2.0 * gate))


def step_kernel(
    rows,
    members,
    copies,
    classes,
    source,
    index_map,
    crop_offsets,
    flip_flags,
    labels,
    valid_mask,
    weights_in,
    decay_in,
    pair_in,
    grads,
    series,
    grad_small,
    series_one,
    series_two,
    grad_source,
    row_parts,
    row_box,
    cut_box,
    d1,
    d2,
    v1,
    v2,
    v1_hi,
    v1_lo,
    v2_hi,
    v2_lo,
    k_hi,
    k_lo,
    source_box,
    x_box,
    x_row,
    x_both,
    x_own,
    a_both,
    b_both,
    g_left,
    g_turned,
    t_left,
    t_turned,
    slots,
    partial,
    from_low,
    from_high,
    flow,
    n1,
    s1,
    pb1,
    pull1,
    c1,
    n2,
    s2,
    pb2,
    pull2,
    c2,
    nt1,
    in1,
    nt2,
    in2,
    fold_sum,
    sum_one,
    sum_two,
    half_one,
    half_two,
    first_low,
    first_up,
    second_low,
    second_up,
    piece_two,
    stats_box,
    stats_own,
    logit_box,
    logit_own,
    pair_box,
    label_box,
    turned,
    channel,
    move_norm,
    move_head,
    head,
    pooled,
    chances,
    weights,
    pull_logits,
    x_load,
    pair_sem,
    cut_load,
    k1_load,
    d1_load,
    k1_send,
    k1_recv,
    half_send,
    half_recv,
    first_send,
    first_recv,
    label_send,
    label_recv,
    x_send,
    x_recv,
    stats_send,
    stats_recv,
    logit_send,
    logit_recv,
    up_send,
    up_recv,
    down_send,
    down_recv,
    ring_send,
    ring_recv,
    pair_send,
    pair_recv,
    plane_send,
    plane_recv,
    back_send,
    back_recv,
    swap_send,
    swap_recv,
    fold_send,
    fold_recv,
    open_send,
    open_recv,
    share_send,
    share_recv,
    row_send,
    row_recv,
    own_send,
    own_recv,
):
    shard = lax.axis_index("shard")
    copy = lax.axis_index("dp")
    part = shard // members
    member = shard % members
    me = member * copies + copy
    place, line, core = me // 2, (me // 2) % 2, me % 2
    last = 3
    count = flow.shape[1]
    own_count = source.shape[0]
    inverse = 1.0 / rows
    zero = jnp.zeros((count, LANES), jnp.float32)

    def row_peer(other):
        return (part * members + other // copies, other % copies)

    def part_peer(other):
        return (other * members + member, copy)

    def remote(source, target, send, recv, device):
        return pltpu.make_async_remote_copy(
            src_ref=source,
            dst_ref=target,
            send_sem=send,
            recv_sem=recv,
            device_id=device,
            device_id_type=MESH_ID,
        )

    def greet(device):
        pl.semaphore_signal(barrier, inc=1, device_id=device, device_id_type=MESH_ID)

    barrier = pltpu.get_barrier_semaphore()
    for step in range(1, 8):
        greet(row_peer(me ^ step))
    for step in range(1, 4):
        greet(part_peer(part ^ step))
    channels = source.shape[3]

    def tap_lanes(tap, width):
        return pl.ds(pl.multiple_of(tap * width, width), width)

    source_load = pltpu.make_async_copy(source, source_box, x_load)
    source_load.start()
    k1_loads = [
        pltpu.make_async_copy(
            weights_in.at[0, :, :, :, pl.ds(tap * channels, channels)],
            v1.at[tap, member],
            k1_load.at[tap],
        )
        for tap in range(TAPS)
    ]
    d1_loads = [
        pltpu.make_async_copy(
            decay_in.at[0, line, core, :, pl.ds(tap * channels, channels)], d1.at[tap], d1_load.at[tap]
        )
        for tap in range(TAPS)
    ]
    cut_loads = [
        pltpu.make_async_copy(weights_in.at[1, line, core], row_box.at[0], cut_load.at[0]),
        pltpu.make_async_copy(decay_in.at[1, line, core], row_box.at[1], cut_load.at[1]),
    ]
    for load in cut_loads + k1_loads + d1_loads:
        load.start()
    stats_own[...] = jnp.zeros_like(stats_own)
    channel[...] = jnp.zeros_like(channel)
    label_box[0] = jnp.zeros(label_box.shape[1:], jnp.float32)
    lane = lax.broadcasted_iota(jnp.int32, (1, LANES), 1)

    def tag_image(image, _):
        at = part * own_count + image
        label_box[0, pl.ds(at, 1), :] = (lane == labels[image]).astype(jnp.float32)
        label_box[0, pl.ds(count + at, 1), :] = jnp.full(
            (1, LANES), valid_mask[image].astype(jnp.float32)
        )

    lax.fori_loop(0, own_count, tag_image, None)
    source_load.wait()

    def crop(image, _):
        picked, flipped = index_map[image], flip_flags[image]
        top, left = crop_offsets[image, 0], crop_offsets[image, 1]
        for cell in range(16):
            column = left + jnp.where(flipped == 1, 3 - cell % 4, cell % 4)
            x_box[part, pl.ds(cell * own_count + image, 1), :] = source_box[
                picked, top + cell // 4, pl.ds(column, 1), :
            ]

    lax.fori_loop(0, own_count, crop, None)
    for load in cut_loads:
        load.wait()
    for which in range(2):
        for other in range(4):
            for tap in range(TAPS):
                start = tap * channels + other * LANES
                cut_box[which, other, :, tap * LANES : (tap + 1) * LANES] = row_box[
                    which, :, start : start + LANES
                ]
    v2[me, part] = cut_box[0, part]
    d2[part] = cut_box[1, part]
    pl.semaphore_wait(barrier, 10)

    def ring_move(box, send, recv, block, step, way, half):
        size = box.shape[1] // 2
        at = pl.ds(half * size, size)
        return remote(
            box.at[block, at],
            box.at[block, at],
            send.at[0 if way > 0 else 1, step, half],
            recv.at[block, half],
            part_peer(part + way),
        )

    def ring_start(box, send, recv):
        for half in range(2):

            @pl.when(part < last)
            def _():
                ring_move(box, send, recv, part, 0, 1, half).start()

            @pl.when(part > 0)
            def _():
                ring_move(box, send, recv, part, 0, -1, half).start()

    def ring_step(box, send, recv, step):
        for half in range(2):

            @pl.when(part >= step)
            def _():
                ring_move(box, send, recv, part - step, step, -1, half).wait_recv()

                @pl.when(part < last)
                def _():
                    ring_move(box, send, recv, part - step, step, 1, half).start()

            @pl.when(part + step <= last)
            def _():
                ring_move(box, send, recv, part + step, step, 1, half).wait_recv()

                @pl.when(part > 0)
                def _():
                    ring_move(box, send, recv, part + step, step, -1, half).start()

    def ring_end(box, send, recv):
        for step in range(0, 3):
            for half in range(2):

                @pl.when((part >= step) & (part < last))
                def _():
                    ring_move(box, send, recv, part - step, step, 1, half).wait_send()

                @pl.when((part + step <= last) & (part > 0))
                def _():
                    ring_move(box, send, recv, part + step, step, -1, half).wait_send()

    order = (
        part,
        jnp.where(part == 0, 1, part - 1),
        jnp.where(part == 3, 1, jnp.where(part == 2, 3, 2)),
        jnp.where(part < 2, 3, 0),
    )

    def cut_move(which, other):
        box = v2.at[me, part] if which == 0 else d2.at[part]
        return remote(
            cut_box.at[which, other],
            box,
            first_send.at[which, other],
            first_recv.at[which, part],
            part_peer(other),
        )

    def cut_start(which):
        for other in range(4):

            @pl.when(part != other)
            def _():
                cut_move(which, other).start()

    def cut_end(which):
        for other in range(4):

            @pl.when(part != other)
            def _():
                cut_move(which, other).wait_send()
                box = v2.at[me, other] if which == 0 else d2.at[other]
                remote(
                    cut_box.at[which, other],
                    box,
                    first_send.at[which, other],
                    first_recv.at[which, other],
                    part_peer(other),
                ).wait_recv()

    pair = row_peer(me ^ 1)
    cut_start(0)
    ring_start(x_box, x_send, x_recv)
    partner = row_peer(me ^ copies)
    k1_moves = [
        remote(
            weights_in.at[0, :, core, :, pl.ds(tap * channels, channels)],
            v1.at[tap, member, :, core],
            k1_send.at[tap],
            k1_recv.at[tap],
            partner,
        )
        for tap in range(TAPS)
    ]
    for move in k1_moves:
        move.start()

    def k1_share(group, arriving=False):
        piece = v1.at[pl.ds(group * 3, 3), 1 - member, :, 1 - core if arriving else core]
        return remote(piece, piece, half_send.at[group], half_recv.at[group], pair)

    pair_move = remote(pair_in, pair_box, pair_sem.at[0], pair_sem.at[1], partner)
    pair_move.start()
    label_moves = [
        remote(
            label_box.at[0],
            label_box.at[step],
            label_send.at[step],
            label_recv.at[step],
            part_peer(part ^ step),
        )
        for step in range(1, 4)
    ]
    for move in label_moves:
        move.start()

    cut_start(1)

    def piece_of(which, other):
        return v2.at[other, which[0]]

    def lane_of(which):
        return which[0]

    def to_plane(which, step):
        piece, at = piece_of(which, me), lane_of(which)
        return remote(
            piece, piece, back_send.at[at, step], back_recv.at[at, step], row_peer(me ^ (2 * step))
        )

    def from_plane(which, step):
        piece, at = piece_of(which, me ^ (2 * step)), lane_of(which)
        return remote(piece, piece, back_send.at[at, step], back_recv.at[at, step], pair)

    def to_pair(which, step):
        piece, at = piece_of(which, me ^ (2 * step)), lane_of(which)
        return remote(piece, piece, swap_send.at[at, step], swap_recv.at[at, step], pair)

    def from_pair(which, step):
        piece, at = piece_of(which, me ^ 1 ^ (2 * step)), lane_of(which)
        return remote(piece, piece, swap_send.at[at, step], swap_recv.at[at, step], pair)

    def back_start(which):
        for step in range(1, 4):
            to_plane(which, step).start()
        to_pair(which, 0).start()

    def back_forward(which):
        for step in range(1, 4):
            from_plane(which, step).wait_recv()
            to_pair(which, step).start()

    def back_arrived(which):
        for step in range(0, 4):
            from_pair(which, step).wait_recv()

    def back_end(which):
        for step in range(1, 4):
            to_plane(which, step).wait_send()
        for step in range(0, 4):
            to_pair(which, step).wait_send()

    x_both[...] = jnp.zeros_like(x_both)
    a_both[...] = jnp.zeros_like(a_both)
    b_both[...] = jnp.zeros_like(b_both)
    cut_end(0)
    for block in range(4):
        back_start((block,))
    ring_step(x_box, x_send, x_recv, 1)
    pair_move.wait()
    small = pair_in[...] + pair_box[...]
    move_norm[...] = small[0:8]
    head[...] = jnp.zeros_like(head)
    move_head[...] = jnp.zeros_like(move_head)
    head[0:16] = small[8:24]
    for move in label_moves:
        move.wait()
    tags = label_box[0] + label_box[1] + label_box[2] + label_box[3]
    chosen, valid = tags[:count], tags[count:]

    def each_cell(body, init=None):
        return lax.fori_loop(0, 16, body, init, unroll=2)

    def window(ref, down, right, lanes=slice(None), first=0, after=4):
        seen = ref[pl.ds(down + first, after - first), right : right + 4, :, lanes]
        return seen.reshape(4 * (after - first) * seen.shape[2], seen.shape[3])

    def reach(down):
        return (1 if down == 0 else 0), (3 if down == 2 else 4)

    def row(ref, index):
        return ref[index : index + 1, :]

    def put_sums(site, first, second):
        stats_own[site, 0:1, :] = jnp.sum(first, axis=0, keepdims=True)
        stats_own[site, 1:2, :] = jnp.sum(second, axis=0, keepdims=True)

    def sum_start(site, size):
        moves = []
        for step in range(1, 8):
            move = remote(
                stats_own.at[site, pl.ds(0, size)],
                stats_box.at[site, step, pl.ds(0, size)],
                stats_send.at[site, step],
                stats_recv.at[site, step],
                row_peer(me ^ step),
            )
            move.start()
            moves.append(move)
        stats_box[site, 0, pl.ds(0, size)] = stats_own[site, pl.ds(0, size)]
        return moves

    def sum_end(site, size, moves):
        for move in moves:
            move.wait()
        total = stats_box[site, me, pl.ds(0, size)]
        for other in range(1, 8):
            total = total + stats_box[site, other ^ me, pl.ds(0, size)]
        return total

    def sum_parts(value):
        logit_own[...] = value
        moves = []
        for step in range(1, 4):
            move = remote(
                logit_own,
                logit_box.at[step],
                logit_send.at[step],
                logit_recv.at[step],
                part_peer(part ^ step),
            )
            move.start()
            moves.append(move)
        logit_box[0] = value
        for move in moves:
            move.wait()
        total = logit_box[part]
        for other in range(1, 4):
            total = total + logit_box[other ^ part]
        return total

    def split_one(tap, _):
        for other in range(8):
            at = slice(other * 16, other * 16 + 16)
            v1_hi[tap, at], v1_lo[tap, at] = halves(v1[tap, other // 4, other // 2 % 2, other % 2])

    def split_two(high, low):
        def body(other, _):
            for block in range(4):
                at = pl.ds(pl.multiple_of(block * LANES + other * 16, 16), 16)
                high[at], low[at] = halves(v2[other, block])

        lax.fori_loop(0, 8, body, None)

    def taps_forward(row_of_taps):
        left, right = [], []
        for step in range(3):
            tap = row_of_taps * 3 + step
            weight = jnp.concatenate([v1_hi[tap], v1_lo[tap]], axis=0)
            left.append(window(x_both, row_of_taps, step))
            right += [weight, weight]
        out = mul(jnp.concatenate(left, axis=1), jnp.concatenate(right, axis=1), ((1,), (1,)))
        flow[...] += (out[:, :LANES] + out[:, LANES:]).reshape(flow.shape)

    def part_of_second(maps, high, low, half, add):
        at = pl.ds(pl.multiple_of(half * 256, 256), 256)

        for row_of_taps in (1, 0, 2):
            left, right = [], []
            first, after = reach(row_of_taps)
            for step in range(3):
                tap = row_of_taps * 3 + step
                lanes = slice(tap * LANES, (tap + 1) * LANES)
                seen = window(maps, row_of_taps, step, slice(None), first, after)
                weight_hi, weight_lo = high[at, lanes], low[at, lanes]
                left += [seen, seen[:, :LANES]]
                right += [weight_hi, weight_hi, weight_lo]
            out = mul(
                jnp.concatenate(left, axis=1), jnp.concatenate(right, axis=1), ((1,), (1,))
            )
            lines = slice(first * 4, after * 4)
            for side in range(2):
                value = out[:, side * LANES : (side + 1) * LANES].reshape(-1, count, LANES)
                if add or row_of_taps != 1:
                    partial[half * 2 + side, lines] += value
                else:
                    partial[half * 2 + side, lines] = value

    def up(block, half):
        at = pl.ds(half * 8, 8)
        return remote(
            partial.at[block, at],
            from_low.at[block, at],
            up_send.at[block, half],
            up_recv.at[block, half],
            part_peer(part + 1),
        )

    def down(block, half):
        at = pl.ds(half * 8, 8)
        return remote(
            partial.at[block, at],
            from_high.at[block, at],
            down_send.at[block, half],
            down_recv.at[block, half],
            part_peer(part - 1),
        )

    def scatter(maps, high, low, add, aside):
        near = jnp.where(part < 2, 1, 0)

        def half_body(index, _):
            part_of_second(maps, high, low, jnp.where(index == 0, near, 1 - near), add)

            @pl.when((index == 0) & (part == 0))
            def _():
                for block in (3, 2):
                    for half in range(2):
                        up(block, half).start()

            @pl.when((index == 0) & (part == last))
            def _():
                for block in (0, 1):
                    for half in range(2):
                        down(block, half).start()

        lax.fori_loop(0, 2, half_body, None)
        for block in (3, 2, 1):
            goal = last - block

            for half in range(2):
                at = slice(half * 8, half * 8 + 8)

                @pl.when((part < block) & (part > 0))
                def _():
                    up(block, half).wait_recv()
                    partial[block, at] += from_low[block, at]
                    up(block, half).start()

                @pl.when((part > goal) & (part < last))
                def _():
                    down(goal, half).wait_recv()
                    partial[goal, at] += from_high[goal, at]
                    down(goal, half).start()

                if block == 1:

                    @pl.when(part == 0)
                    def _():
                        up(1, half).start()

                    @pl.when(part == last)
                    def _():
                        down(2, half).start()

        aside()
        for block in range(4):

            @pl.when(part == block)
            def _():
                for half in range(2):
                    at = slice(half * 8, half * 8 + 8)
                    total = partial[block, at]
                    if block > 0:
                        up(block, half).wait_recv()
                        total = total + from_low[block, at]
                    if block < last:
                        down(block, half).wait_recv()
                        total = total + from_high[block, at]
                    flow[at] = total

        for block in (3, 2, 1):
            goal = last - block
            for half in range(2):

                @pl.when(part < block)
                def _():
                    up(block, half).wait_send()

                @pl.when(part > goal)
                def _():
                    down(goal, half).wait_send()

    def turn_block(block, left, turned_block):
        value = slots[block].reshape(16 * count, LANES)
        left[...] = jnp.concatenate(halves(value), axis=1)
        turned_block[...] = jnp.concatenate(halves(value.T), axis=0)

    def use_block(block, left, turned_block, high, low, maps):
        at = pl.ds(pl.multiple_of(block * LANES, LANES), LANES)

        for down in range(3):
            right = []
            first, after = reach(down)
            taps = [slice((down * 3 + step) * LANES, (down * 3 + step + 1) * LANES) for step in range(3)]
            for lanes in taps:
                weight = jnp.concatenate([high[at, lanes], low[at, lanes]], axis=1)
                right.append(jnp.concatenate([weight, weight], axis=0))
            out = mul(
                left[first * 4 * count : after * 4 * count], jnp.concatenate(right, axis=1)
            )
            for step in range(3):
                start = 2 * step * LANES
                fold_sum[down + first : down + after, step : step + 4] += (
                    out[:, start : start + LANES] + out[:, start + LANES : start + 2 * LANES]
                ).reshape(after - first, 4, count, LANES)
            out = mul(
                turned_block[...],
                jnp.concatenate([window(maps, down, step) for step in range(3)], axis=1),
            )
            out = out[:LANES] + out[LANES:]
            for step, lanes in enumerate(taps):
                start = 2 * step * LANES
                sum_two[block, :, :, :, lanes] += (
                    out[:, start : start + LANES] + out[:, start + LANES : start + 2 * LANES]
                ).reshape(4, 2, 16, LANES)

    def pair_two(block):
        return remote(
            sum_two.at[block, :, 1 - core],
            half_two.at[block],
            pair_send.at[block],
            pair_recv.at[block],
            pair,
        )

    def plane_two(block, step):
        other = place ^ step
        return remote(
            half_two.at[block, other],
            piece_two.at[step, block],
            plane_send.at[block, step],
            plane_recv.at[block, step],
            row_peer(other * 2 + core),
        )

    def plane_two_go(block):
        pair_two(block).wait()
        for place_of in range(4):
            half_two[block, place_of] += sum_two[block, place_of, core]
        for step in range(1, 4):
            plane_two(block, step).start()

    def step_two(block, new_of, more):
        for step in range(1, 4):
            plane_two(block, step).wait()
        change = half_two[block, place] + piece_two[1, block] + piece_two[2, block] + piece_two[3, block]
        new = new_of(v2[me, block], change, d2[block])
        v2[me, block] = new
        series_two[block] += new

        @pl.when(more)
        def _():
            back_start((block,))

    def back_forward_when(block, more):
        @pl.when(more)
        def _():
            back_forward((block,))

    def gather_and_use(block_of, new_of, more):
        ring_start(slots, ring_send, ring_recv)

        def order_at(index):
            first = jnp.where(index == 0, order[0], order[1])
            return jnp.where(index < 2, first, jnp.where(index == 2, order[2], order[3]))

        def body(index, _):
            @pl.when(index > 0)
            def _():
                ring_step(slots, ring_send, ring_recv, index)

            @pl.when(index == 2)
            def _():
                step_two(order[0], new_of, more)

            block = order_at(index)
            block_of(block)
            pair_two(block).start()

            @pl.when((index == 1) | (index == 2))
            def _():
                plane_two_go(order_at(index - 1))

        lax.fori_loop(0, 4, body, None)

    def beside_sums(new_of, more):
        step_two(order[1], new_of, more)
        plane_two_go(order[2])
        back_forward_when(order[0], more)
        ring_end(slots, ring_send, ring_recv)
        plane_two_go(order[3])

    def pair_one(group):
        return remote(
            sum_one.at[pl.ds(group * 3, 3), :, :, 1 - core],
            half_one.at[pl.ds(group * 3, 3)],
            pair_send.at[4 + group],
            pair_recv.at[4 + group],
            pair,
        )

    across_x, across_y = row_peer(me ^ copies), row_peer(me ^ 2)
    lower, upper = pl.ds(0, channels // 2), pl.ds(channels // 2, channels // 2)

    def taps_of(group):
        return pl.ds(group * 3, 3)

    def fold_one(group, step):
        taps = taps_of(group)
        source, goal, device = (
            (half_one.at[taps, 1 - member, :, :, lower], first_low.at[taps], across_x),
            (half_one.at[taps, :, 1 - line, :, upper], first_up.at[taps], across_y),
            (half_one.at[taps, member, 1 - line, :, lower], second_low.at[taps], across_y),
            (half_one.at[taps, 1 - member, line, :, upper], second_up.at[taps], across_x),
        )[step]
        return remote(source, goal, fold_send.at[group, step], fold_recv.at[group, step], device)

    def spread_one(group, step, arriving=False):
        taps = taps_of(group)
        x, y = member, line
        if arriving:
            x, y = (x, 1 - y) if step in (0, 3) else (1 - x, y)
        piece = (
            v1.at[taps, x, y, core, :, lower],
            v1.at[taps, x, y, core, :, upper],
            v1.at[taps, x, :, core, :, lower],
            v1.at[taps, :, y, core, :, upper],
        )[step]
        device = across_y if step in (0, 3) else across_x
        return remote(piece, piece, open_send.at[group, step], open_recv.at[group, step], device)

    def share_one(group, step, arriving=False):
        taps = taps_of(group)
        side = 1 - core if arriving else core
        piece = (
            v1.at[taps, member, line, side],
            v1.at[taps, member, 1 - line, side, :, lower],
            v1.at[taps, 1 - member, line, side, :, upper],
            v1.at[taps, 1 - member, :, side, :, lower],
            v1.at[taps, :, 1 - line, side, :, upper],
        )[step]
        return remote(piece, piece, share_send.at[group, step], share_recv.at[group, step], pair)

    def open_first(group):
        spread_one(group, 0).start()
        spread_one(group, 1).start()
        share_one(group, 0).start()

    def open_second(group):
        spread_one(group, 0, True).wait_recv()
        spread_one(group, 2).start()
        spread_one(group, 1, True).wait_recv()
        spread_one(group, 3).start()
        share_one(group, 1).start()
        share_one(group, 2).start()

    def open_third(group):
        spread_one(group, 2, True).wait_recv()
        share_one(group, 3).start()
        spread_one(group, 3, True).wait_recv()
        share_one(group, 4).start()

    def open_arrived(group):
        for step in range(5):
            share_one(group, step, True).wait_recv()

    def open_end(group):
        for step in range(4):
            spread_one(group, step).wait_send()
        for step in range(5):
            share_one(group, step).wait_send()

    def pair_add(group):
        pair_one(group).wait()

        def body(tap, _):
            half_one[tap] += sum_one[tap, :, :, core]

        lax.fori_loop(group * 3, group * 3 + 3, body, None)
        fold_one(group, 0).start()
        fold_one(group, 1).start()

    def fold_add(group):
        fold_one(group, 0).wait()
        fold_one(group, 1).wait()

        def body(tap, _):
            half_one[tap, member, :, :, lower] += first_low[tap]
            half_one[tap, :, line, :, upper] += first_up[tap]

        lax.fori_loop(group * 3, group * 3 + 3, body, None)
        fold_one(group, 2).start()
        fold_one(group, 3).start()

    def first_gradient(new_of, more):
        def taps_weight(down):
            out = mul(
                turned[...],
                jnp.concatenate(
                    [window(x_both, down, step, slice(0, channels)) for step in range(3)], axis=1
                ),
            )
            out = out + mul(
                turned[...],
                jnp.concatenate(
                    [
                        window(x_both, down, step, slice(channels, 2 * channels))
                        for step in range(3)
                    ],
                    axis=1,
                ),
            )
            out = out[:LANES] + out[LANES:]
            for step in range(3):
                sum_one[down * 3 + step] = out[:, step * channels : (step + 1) * channels].reshape(
                    sum_one.shape[1:]
                )

        def body(group, _):
            taps_weight(group)
            pair_one(group).start()

            @pl.when(group == 0)
            def _():
                step_two(order[2], new_of, more)

            @pl.when(group > 0)
            def _():
                pair_add(group - 1)

            @pl.when(group > 1)
            def _():
                fold_add(group - 2)

        lax.fori_loop(0, GROUPS, body, None)
        pair_add(GROUPS - 1)
        back_forward_when(order[1], more)
        fold_add(GROUPS - 2)
        step_two(order[3], new_of, more)
        fold_add(GROUPS - 1)

    def step_group(group, new_of):
        fold_one(group, 2).wait()
        fold_one(group, 3).wait()

        def body(tap, _):
            change = half_one[tap, member, line] + jnp.concatenate(
                [second_low[tap], second_up[tap]], axis=1
            )
            new = new_of(v1[tap, member, line, core], change, d1[tap])
            v1[tap, member, line, core] = new
            series_one[:, tap_lanes(tap, channels)] += new

        lax.fori_loop(group * 3, group * 3 + 3, body, None)

    def no_aside():
        pass

    series_one[...] = jnp.zeros_like(series_one)
    series_two[...] = jnp.zeros_like(series_two)

    def first_vector(old, change, decay):
        return change + decay * old

    def next_vector(old, change, decay):
        return old - neumann_rate * (change + decay * old)

    for load in k1_loads + d1_loads:
        load.wait()
    ring_step(x_box, x_send, x_recv, 2)
    for group in range(GROUPS):
        for move in k1_moves[group * 3 : group * 3 + 3]:
            move.wait()
        k1_share(group).start()
    for block in range(4):
        back_forward((block,))
    ring_step(x_box, x_send, x_recv, 3)
    ring_end(x_box, x_send, x_recv)

    for cell in range(16):
        for block in range(4):
            x_row[block * own_count : (block + 1) * own_count] = x_box[
                block, cell * own_count : (cell + 1) * own_count
            ]
        high, low = halves(x_row[...])
        x_both[cell // 4 + 1, cell % 4 + 1, :, 0:channels] = high
        x_both[cell // 4 + 1, cell % 4 + 1, :, channels : 2 * channels] = low
        x_own[cell] = x_row[:, pl.ds(pl.multiple_of(part * LANES, LANES), LANES)]

    flow[...] = jnp.zeros_like(flow)

    def primal_group(group, _):
        k1_share(group, True).wait_recv()
        lax.fori_loop(group * 3, group * 3 + 3, split_one, None)
        taps_forward(group)

    lax.fori_loop(0, GROUPS, primal_group, None)
    for group in range(GROUPS):
        k1_share(group).wait_send()

    def sums_primal(cell, carry):
        value = flow[cell]
        return carry[0] + value, carry[1] + value * value

    put_sums(0, *each_cell(sums_primal, (zero, zero)))
    stats_own[0, 2:3, :] = jnp.sum(valid, axis=0, keepdims=True)
    moves = sum_start(0, 8)
    cut_end(1)
    for block in range(4):
        back_arrived((block,))
        back_end((block,))
    split_two(k_hi, k_lo)
    total = sum_end(0, 8, moves)
    label_total = total[2:3]
    average = total[0:1] * inverse
    scale = lax.rsqrt(total[1:2] * inverse - average * average + norm_eps)
    gain, shift = row(move_norm, 0), row(move_norm, 1)
    gain2, shift2 = row(move_norm, 2), row(move_norm, 3)

    def first_primal(cell, _):
        normal = (flow[cell] - average) * scale
        value, slope, bend = silu_pieces(normal * gain + shift)
        n1[cell] = normal
        s1[cell] = slope
        pb1[cell] = bend
        a_both[cell // 4 + 1, cell % 4 + 1] = jnp.concatenate(halves(value), axis=1)

    each_cell(first_primal)
    scatter(a_both, k_hi, k_lo, False, no_aside)
    put_sums(1, *each_cell(sums_primal, (zero, zero)))
    total = sum_end(1, 8, sum_start(1, 8))
    average = total[0:1] * inverse
    scale2 = lax.rsqrt(total[1:2] * inverse - average * average + norm_eps)

    def second_primal(cell, carry):
        normal = (flow[cell] - average) * scale2
        value, slope, bend = silu_pieces(normal * gain2 + shift2 + x_own[cell])
        n2[cell] = normal
        s2[cell] = slope
        pb2[cell] = bend
        return carry + value

    pooled[...] = each_cell(second_primal, zero) * (1.0 / 16.0)
    logits = sum_parts(mul_exact(pooled[...], head[...], ((1,), (1,))))
    real = lax.broadcasted_iota(jnp.int32, logits.shape, 1) < classes
    highest = jnp.max(jnp.where(real, logits, -jnp.inf), axis=1, keepdims=True)
    powers = jnp.where(real, jnp.exp(logits - highest), 0.0)
    sum_powers = jnp.sum(powers, axis=1, keepdims=True)
    chances[...] = powers / sum_powers
    target_logit = jnp.sum(chosen * logits, axis=1, keepdims=True)
    cross = (highest + jnp.log(sum_powers) - target_logit) * valid
    weights[...] = valid / label_total
    pull_logits[...] = weights[...] * (chances[...] - chosen)
    out_head = mul_exact(pull_logits[...], pooled[...], ((0,), (0,)))
    pull_block = mul_exact(pull_logits[...], head[...]) * (1.0 / 16.0)

    def back_two_primal(cell, carry):
        pull = pull_block * s2[cell]
        pull2[cell] = pull
        pb2[cell] = pull_block * pb2[cell]
        return carry[0] + pull * n2[cell], carry[1] + pull

    put_sums(2, *each_cell(back_two_primal, (zero, zero)))
    stats_own[2, 2:3, :] = jnp.sum(cross, axis=0, keepdims=True)
    stats_own[2, 8:24, :] = out_head[0:16]
    total = sum_end(2, 24, sum_start(2, 24))
    grad_small[0:1, :] = total[2:3]
    grad_small[1:2, :] = label_total
    grad_small[2:8, :] = jnp.zeros((6, LANES), jnp.float32)
    grad_small[16:32, :] = total[8:24]
    out_gain2, out_shift2 = total[0:1], total[1:2]
    factor2 = scale2 * gain2

    def pull_two_primal(cell, _):
        centred = pull2[cell] - out_shift2 * inverse - n2[cell] * (out_gain2 * inverse)
        c2[cell] = centred
        slots[part, cell] = factor2 * centred

    each_cell(pull_two_primal)
    fold_sum[...] = jnp.zeros_like(fold_sum)
    sum_two[...] = jnp.zeros_like(sum_two)

    def primal_block(block):
        turn_block(block, g_left.at[block], g_turned.at[block])
        use_block(block, g_left.at[block], g_turned.at[block], k_hi, k_lo, a_both)

    gather_and_use(primal_block, first_vector, True)

    def back_one_primal(cell, carry):
        seen = fold_sum[cell // 4 + 1, cell % 4 + 1]
        pull = seen * s1[cell]
        pull1[cell] = pull
        pb1[cell] = seen * pb1[cell]
        return carry[0] + pull * n1[cell], carry[1] + pull

    put_sums(3, *each_cell(back_one_primal, (zero, zero)))
    moves = sum_start(3, 8)
    beside_sums(first_vector, True)
    total = sum_end(3, 8, moves)
    out_gain, out_shift = total[0:1], total[1:2]
    factor = scale * gain

    def pull_one_primal(cell, _):
        centred = pull1[cell] - out_shift * inverse - n1[cell] * (out_gain * inverse)
        c1[cell] = centred
        flow[cell] = factor * centred

    each_cell(pull_one_primal)
    turned[...] = jnp.concatenate(halves(flow[...].reshape(16 * count, LANES).T), axis=0)

    channel[0:1, :] = scale
    channel[1:2, :] = gain
    channel[2:3, :] = scale2
    channel[3:4, :] = gain2
    channel[4:5, :] = out_gain * inverse
    channel[5:6, :] = out_gain2 * inverse
    move_norm[0:1, :] = out_gain
    move_norm[1:2, :] = out_shift
    move_norm[2:3, :] = out_gain2
    move_norm[3:4, :] = out_shift2
    grad_small[8:16, :] = move_norm[...]
    move_head[0:16] = grad_small[16:32, :]

    first_gradient(first_vector, True)

    def deliver_move(which, source, other):
        return remote(
            source.at[other],
            row_parts.at[which, part],
            row_send.at[which, other],
            row_recv.at[which, part],
            part_peer(other),
        )

    def deliver_start(which, source):
        for other in range(4):

            @pl.when(part != other)
            def _():
                deliver_move(which, source, other).start()

        row_parts[which, part] = source[part]

    def deliver_end(which, source, result):
        for other in range(4):

            @pl.when(part != other)
            def _():
                deliver_move(which, source, other).wait_send()
                remote(
                    source.at[other],
                    row_parts.at[which, other],
                    row_send.at[which, other],
                    row_recv.at[which, other],
                    part_peer(other),
                ).wait_recv()

        for other in range(4):
            for tap in range(TAPS):
                start = tap * channels + other * LANES
                result[copy, :, start : start + LANES] = row_parts[
                    which, other, :, tap * LANES : (tap + 1) * LANES
                ]

    across, corner = row_peer(me ^ 2), copy ^ 2

    def spread_move(which, result, step, block, device):
        return remote(
            result.at[block], result.at[block], own_send.at[which, step], own_recv.at[which, step], device
        )

    def spread_start(which, result):
        spread_move(which, result, 0, copy, across).start()
        spread_move(which, result, 1, copy, pair).start()

    def spread_forward(which, result):
        spread_move(which, result, 0, corner, across).wait_recv()
        spread_move(which, result, 2, corner, pair).start()

    def spread_end(which, result):
        spread_move(which, result, 1, copy ^ 1, pair).wait_recv()
        spread_move(which, result, 2, copy ^ 3, pair).wait_recv()
        spread_move(which, result, 0, copy, across).wait_send()
        spread_move(which, result, 1, copy, pair).wait_send()
        spread_move(which, result, 2, corner, pair).wait_send()

    grad_source[...] = series_two[...]
    deliver_start(0, grad_source)
    for group in range(GROUPS):
        step_group(group, first_vector)
        open_first(group)

    def turn_body(turn, nothing):
        flow[...] = jnp.zeros_like(flow)

        def forward_group(group, _):
            open_arrived(group)
            lax.fori_loop(group * 3, group * 3 + 3, split_one, None)
            taps_forward(group)

        fold_sum[...] = jnp.zeros_like(fold_sum)
        sum_two[...] = jnp.zeros_like(sum_two)
        open_second(0)
        open_second(1)
        back_forward((order[2],))
        back_forward((order[3],))
        for block in range(4):
            back_arrived((block,))
            back_end((block,))
        split_two(v2_hi, v2_lo)
        open_third(0)
        open_second(2)

        def vector_half(half, _):
            part_of_second(a_both, v2_hi, v2_lo, half, False)

            @pl.when(half == 0)
            def _():
                open_third(1)
                open_third(2)

        lax.fori_loop(0, 2, vector_half, None)
        lax.fori_loop(0, GROUPS, forward_group, None)
        for group in range(GROUPS):
            open_end(group)

        @pl.when(turn == 0)
        def _():
            for tap in range(TAPS):
                grads[0, :, :, tap * channels : (tap + 1) * channels] = v1[tap, member].reshape(
                    4, v1.shape[4], channels
                )

        def sums_forward(normal):
            def body(cell, carry):
                value = flow[cell]
                return carry[0] + value, carry[1] + value * normal[cell]

            return each_cell(body, (zero, zero))

        put_sums(0, *sums_forward(n1))
        moves = sum_start(0, 8)
        total = sum_end(0, 8, moves) * inverse
        average, cross = total[0:1], total[1:2]
        scale, gain = row(channel, 0), row(channel, 1)
        tan_scale_one = -scale * scale * cross
        move_gain, move_shift = row(move_norm, 0), row(move_norm, 1)

        def forward_one(cell, _):
            normal = n1[cell]
            tangent = scale * (flow[cell] - average - normal * cross)
            inner = move_gain * normal + gain * tangent + move_shift
            nt1[cell] = tangent
            in1[cell] = inner
            b_both[cell // 4 + 1, cell % 4 + 1] = jnp.concatenate(halves(s1[cell] * inner), axis=1)

        each_cell(forward_one)

        def aside():
            def body(block, _):
                use_block(block, g_left.at[block], g_turned.at[block], v2_hi, v2_lo, b_both)

            lax.fori_loop(0, 4, body, None)

        scatter(b_both, k_hi, k_lo, True, aside)

        @pl.when(turn == 0)
        def _():
            deliver_end(0, grad_source, grads.at[1])
            spread_start(0, grads.at[1])

        @pl.when(turn == 1)
        def _():
            spread_forward(0, grads.at[1])


        put_sums(1, *sums_forward(n2))
        moves = sum_start(1, 8)
        early_logits = mul_exact(pooled[...], move_head[...], ((1,), (1,)))
        early_block = mul_exact(pull_logits[...], move_head[...])
        total = sum_end(1, 8, moves) * inverse
        average2, cross2 = total[0:1], total[1:2]
        scale2, gain2 = row(channel, 2), row(channel, 3)
        tan_scale_two = -scale2 * scale2 * cross2
        move_gain2, move_shift2 = row(move_norm, 2), row(move_norm, 3)

        def forward_two(cell, carry):
            normal = n2[cell]
            tangent = scale2 * (flow[cell] - average2 - normal * cross2)
            inner = move_gain2 * normal + gain2 * tangent + move_shift2
            nt2[cell] = tangent
            in2[cell] = inner
            return carry + s2[cell] * inner

        tan_pooled = each_cell(forward_two, zero) * (1.0 / 16.0)
        tan_logits = sum_parts(mul_exact(tan_pooled, head[...], ((1,), (1,))) + early_logits)
        chance = chances[...]
        tan_pull = (
            weights[...]
            * chance
            * (tan_logits - jnp.sum(chance * tan_logits, axis=1, keepdims=True))
        )
        tan_block = (mul_exact(tan_pull, head[...]) + early_block) * (1.0 / 16.0)

        def back_two(cell, carry):
            tangent = tan_block * s2[cell] + pb2[cell] * in2[cell]
            flow[cell] = tangent
            return (
                carry[0] + tangent * n2[cell] + pull2[cell] * nt2[cell],
                carry[1] + tangent,
            )

        put_sums(2, *each_cell(back_two, (zero, zero)))
        moves = sum_start(2, 8)
        out_head = mul_exact(pull_logits[...], tan_pooled, ((0,), (0,))) + mul_exact(
            tan_pull, pooled[...], ((0,), (0,))
        )
        stats_own[3, 8:24, :] = out_head[0:16]
        total = sum_end(2, 8, moves)
        out_gain2, out_shift2 = total[0:1], total[1:2]
        factor2 = scale2 * gain2
        tan_factor2 = tan_scale_two * gain2 + scale2 * move_gain2

        def pull_two_body(cell, _):
            slots[part, cell] = tan_factor2 * c2[cell] + factor2 * (
                flow[cell]
                - out_shift2 * inverse
                - nt2[cell] * row(channel, 5)
                - n2[cell] * (out_gain2 * inverse)
            )

        each_cell(pull_two_body)

        def turn_of_block(block):
            turn_block(block, t_left, t_turned)
            use_block(block, t_left, t_turned, k_hi, k_lo, a_both)

        more = turn < NEUMANN - 1
        gather_and_use(turn_of_block, next_vector, more)

        def back_one(cell, carry):
            pull = fold_sum[cell // 4 + 1, cell % 4 + 1]
            tangent = pull * s1[cell] + pb1[cell] * in1[cell]
            flow[cell] = tangent
            return (
                carry[0] + tangent * n1[cell] + pull1[cell] * nt1[cell],
                carry[1] + tangent,
            )

        put_sums(3, *each_cell(back_one, (zero, zero)))
        moves = sum_start(3, 24)
        beside_sums(next_vector, more)
        total = sum_end(3, 24, moves)
        move_head[0:16] = move_head[0:16] - neumann_rate * total[8:24]
        out_gain, out_shift = total[0:1], total[1:2]
        factor = scale * gain
        tan_factor = tan_scale_one * gain + scale * move_gain

        def pull_one_body(cell, _):
            flow[cell] = tan_factor * c1[cell] + factor * (
                flow[cell]
                - out_shift * inverse
                - nt1[cell] * row(channel, 4)
                - n1[cell] * (out_gain * inverse)
            )

        each_cell(pull_one_body)
        turned[...] = jnp.concatenate(halves(flow[...].reshape(16 * count, LANES).T), axis=0)
        move_norm[0:1, :] = move_gain - neumann_rate * out_gain
        move_norm[1:2, :] = move_shift - neumann_rate * out_shift
        move_norm[2:3, :] = move_gain2 - neumann_rate * out_gain2
        move_norm[3:4, :] = move_shift2 - neumann_rate * out_shift2
        first_gradient(next_vector, more)

        @pl.when(turn == NEUMANN - 1)
        def _():
            deliver_start(1, series_two)

        for group in range(GROUPS):
            step_group(group, next_vector)

            @pl.when(more)
            def _():
                open_first(group)

    lax.fori_loop(0, NEUMANN, turn_body, None)

    series[0, copy] = series_one[...]
    spread_start(1, series.at[0])
    deliver_end(1, series_two, series.at[1])
    spread_start(2, series.at[1])
    spread_forward(1, series.at[0])
    spread_forward(2, series.at[1])
    spread_end(0, grads.at[1])
    spread_end(1, series.at[0])
    spread_end(2, series.at[1])


def step_fused(
    links,
    rows,
    source,
    index_map,
    crop_offsets,
    flip_flags,
    labels,
    valid_mask,
    conv_weights,
    norm_params,
    head_weights,
    decay_rates,
):
    own_count, channels = source.shape[0], source.shape[3]
    cells, count = MAP * MAP, own_count * 4
    width, group = channels // 4, 8
    piece, block = width // group, channels // group
    classes = head_weights.shape[1]
    f32, b16 = jnp.float32, jnp.bfloat16
    small = jnp.concatenate(
        [
            norm_params,
            jnp.zeros((4, block), f32),
            head_weights.T,
            jnp.zeros((16 - classes, block), f32),
        ]
    )
    lane = links.member * block
    here = jnp.arange(2, dtype=jnp.int32)[None, :, None] == links.member
    operands = (
        source,
        index_map,
        crop_offsets,
        flip_flags,
        labels,
        valid_mask,
        conv_weights.reshape(2, 2, 2, piece, TAPS * channels),
        decay_rates.reshape(2, 2, 2, piece, TAPS * channels),
        jnp.where(here, small[:, None, :], 0.0).reshape(24, width),
    )
    vmem = pl.BlockSpec(memory_space=pltpu.VMEM)
    anywhere = pl.BlockSpec(memory_space=pl.ANY)
    row_map = pltpu.VMEM((cells, count, width), f32)
    four_maps = pltpu.VMEM((4, cells, count, width), f32)
    inner_piece = pltpu.VMEM((4, piece, TAPS * width), f32)
    inner_half = pltpu.VMEM((4, 4, piece, TAPS * width), f32)
    inner_part = pltpu.VMEM((channels, TAPS * width), b16)
    outer_part = pltpu.VMEM((TAPS, width, channels), b16)
    both = pltpu.VMEM((MAP + 2, MAP + 2, count, 2 * width), b16)
    logit = pltpu.VMEM((count, LANES), f32)
    dma = pltpu.SemaphoreType.DMA
    scratch = [
        pltpu.VMEM((piece, TAPS * channels), f32),
        inner_piece,
        inner_piece,
        pltpu.VMEM((2, 4, piece, TAPS * width), f32),
        pltpu.VMEM((2, piece, TAPS * channels), f32),
        pltpu.VMEM((2, 4, piece, TAPS * width), f32),
        pltpu.VMEM((TAPS, piece, channels), f32),
        inner_piece,
        pltpu.VMEM((TAPS, 2, 2, 2, piece, channels), f32),
        pltpu.VMEM((group, 4, piece, TAPS * width), f32),
        outer_part,
        outer_part,
        inner_part,
        inner_part,
        inner_part,
        inner_part,
        pltpu.VMEM(source.shape, f32),
        pltpu.VMEM((4, cells * own_count, channels), f32),
        pltpu.VMEM((count, channels), f32),
        pltpu.VMEM((MAP + 2, MAP + 2, count, 2 * channels), b16),
        row_map,
        both,
        both,
        pltpu.VMEM((4, cells * count, 2 * width), b16),
        pltpu.VMEM((4, 2 * width, cells * count), b16),
        pltpu.VMEM((cells * count, 2 * width), b16),
        pltpu.VMEM((2 * width, cells * count), b16),
        four_maps,
        four_maps,
        four_maps,
        four_maps,
        *[row_map] * 15,
        pltpu.VMEM((MAP + 2, MAP + 2, count, width), f32),
        pltpu.VMEM((TAPS, 2, 2, 2, piece, channels), f32),
        pltpu.VMEM((4, 4, 2, piece, TAPS * width), f32),
        pltpu.VMEM((TAPS, 2, 2, piece, channels), f32),
        inner_half,
        *[pltpu.VMEM((TAPS, 2, piece, channels // 2), f32)] * 2,
        *[pltpu.VMEM((TAPS, piece, channels // 2), f32)] * 2,
        inner_half,
        pltpu.VMEM((4, 8, 24, width), f32),
        pltpu.VMEM((4, 24, width), f32),
        pltpu.VMEM((4, count, LANES), f32),
        logit,
        pltpu.VMEM((24, width), f32),
        pltpu.VMEM((4, 2 * count, LANES), f32),
        pltpu.VMEM((2 * width, cells * count), b16),
        pltpu.VMEM((8, width), f32),
        pltpu.VMEM((8, width), f32),
        pltpu.VMEM((LANES, width), f32),
        pltpu.VMEM((LANES, width), f32),
        logit,
        logit,
        logit,
        logit,
        dma(()),
        dma((2,)),
        dma((2,)),
        dma((TAPS,)),
        dma((TAPS,)),
        dma((TAPS,)),
        dma((TAPS,)),
        dma((GROUPS,)),
        dma((GROUPS,)),
        dma((2, 4)),
        dma((2, 4)),
        dma((4,)),
        dma((4,)),
        dma((2, 4, 2)),
        dma((4, 2)),
        dma((4, 8)),
        dma((4, 8)),
        dma((4,)),
        dma((4,)),
        dma((4, 2)),
        dma((4, 2)),
        dma((4, 2)),
        dma((4, 2)),
        dma((2, 4, 2)),
        dma((4, 2)),
        dma((GROUPS + 4,)),
        dma((GROUPS + 4,)),
        dma((4, 4)),
        dma((4, 4)),
        dma((4, 4)),
        dma((4, 4)),
        dma((4, 4)),
        dma((4, 4)),
        dma((GROUPS, 4)),
        dma((GROUPS, 4)),
        dma((GROUPS, 4)),
        dma((GROUPS, 4)),
        dma((GROUPS, 5)),
        dma((GROUPS, 5)),
        dma((2, 4)),
        dma((2, 4)),
        dma((3, 3)),
        dma((3, 3)),
    ]
    result = jax.ShapeDtypeStruct((2, 4, piece, TAPS * channels), f32)
    grads, series, grad_small = pl.pallas_call(
        functools.partial(step_kernel, rows, links.members, links.copies, classes),
        out_shape=(result, result, jax.ShapeDtypeStruct((32, width), f32)),
        in_specs=[anywhere] + [pl.BlockSpec(memory_space=pltpu.SMEM)] * 5 + [anywhere] * 2 + [vmem],
        out_specs=(vmem,) * 3,
        scratch_shapes=scratch,
        compiler_params=pltpu.CompilerParams(
            collective_id=1, has_side_effects=True, vmem_limit_bytes=63 * 1024 * 1024
        ),
        name="train_step",
    )(*operands)
    own = lax.dynamic_slice_in_dim(grad_small, lane, block, 1)
    return (
        grad_small[0, 0],
        grad_small[1, 0],
        grads.reshape(conv_weights.shape),
        own[8:12],
        own[16 : 16 + classes].T,
        series.reshape(conv_weights.shape),
    )


def adamw(weight, grad, first, second, rate):
    first = beta_first * first + (1.0 - beta_first) * grad
    second = beta_second * second + (1.0 - beta_second) * grad * grad
    first_hat = first / (1.0 - beta_first**STEP)
    second_hat = second / (1.0 - beta_second**STEP)
    update = first_hat / (jnp.sqrt(second_hat) + adam_eps) + decoupled * weight
    return (weight - rate * update, first, second)


def silu_parts(value):
    gate = jax.nn.sigmoid(value)
    slope = gate * (1.0 - gate)
    first = gate + value * slope
    second = slope * (2.0 + value * (1.0 - 2.0 * gate))
    return value * gate, first, second


class Links:
    def __init__(self):
        self.shards = lax.axis_size("shard")
        self.copies = lax.axis_size("dp")
        self.parts = 4 if self.shards % 4 == 0 else 1
        self.members = self.shards // self.parts
        index = lax.axis_index("shard")
        self.part = index // self.members
        self.member = index % self.members
        self.across = [
            [p * self.members + m for p in range(self.parts)] for m in range(self.members)
        ]
        self.within = [
            [p * self.members + m for m in range(self.members)] for p in range(self.parts)
        ]

    def sum_rows(self, value):
        value = lax.psum(value, "dp")
        gathered = lax.all_gather(value, "shard", axis_index_groups=self.within)
        return jnp.sum(gathered, axis=0)

    def sum_parts(self, value):
        return jnp.sum(lax.all_gather(value, "shard", axis_index_groups=self.across), axis=0)

    def gather_parts(self, value, axis):
        return lax.all_gather(value, "shard", axis_index_groups=self.across, axis=axis, tiled=True)

    def gather_members(self, value, axis):
        return lax.all_gather(value, "shard", axis_index_groups=self.within, axis=axis, tiled=True)

    def scatter_parts(self, value, axis):
        return lax.psum_scatter(
            value, "shard", axis_index_groups=self.across, scatter_dimension=axis, tiled=True
        )

    def to_inner(self, value):
        rows, channels = value.shape[0], value.shape[1] // TAPS
        width = channels // self.parts
        cut = value.reshape(rows, TAPS, self.parts, width).transpose(2, 0, 1, 3)
        moved = lax.all_to_all(cut, "shard", 0, 0, axis_index_groups=self.across, tiled=True)
        whole = self.gather_members(moved, 1)
        return whole.reshape(channels, TAPS * width)

    def to_outer(self, value):
        channels, width = value.shape[0], value.shape[1] // TAPS
        rows = channels // self.shards
        cut = value.reshape(self.parts, self.members, rows, TAPS * width)
        cut = lax.dynamic_index_in_dim(cut, self.member, 1, keepdims=False)
        moved = lax.all_to_all(cut, "shard", 0, 0, axis_index_groups=self.across, tiled=True)
        moved = moved.reshape(self.parts, rows, TAPS, width).transpose(1, 2, 0, 3)
        return moved.reshape(rows, TAPS * channels)

    def own_rows(self, value, axis=0):
        size = value.shape[axis] // self.members
        return lax.dynamic_slice_in_dim(value, self.member * size, size, axis)


def moments(hidden, rows, links):
    totals = links.sum_rows(jnp.stack([jnp.sum(hidden, axis=0), jnp.sum(hidden * hidden, axis=0)]))
    average = totals[0] / rows
    scale = lax.rsqrt(totals[1] / rows - average * average + norm_eps)
    return (hidden - average) * scale, scale


def moments_tangent(normal, scale, tangent, rows, links):
    totals = links.sum_rows(
        jnp.stack([jnp.sum(tangent, axis=0), jnp.sum(tangent * normal, axis=0)])
    )
    average, cross = totals[0] / rows, totals[1] / rows
    return scale * (tangent - average - normal * cross), -scale * scale * cross


def step_general(
    links,
    rows,
    source,
    index_map,
    crop_offsets,
    flip_flags,
    labels,
    valid_mask,
    conv_weights,
    norm_params,
    head_weights,
    decay_rates,
):
    images = jax.vmap(crop_image)(source[index_map], crop_offsets, flip_flags)
    images = images.transpose(1, 2, 0, 3)
    valid = valid_mask.astype(jnp.float32)
    own_images, channels = images.shape[2:]
    count = own_images * links.parts
    width = channels // links.parts
    first_column = links.part * width
    label_total = lax.psum(jnp.sum(valid), ("shard", "dp"))
    images = links.gather_parts(images, 2)
    labels = links.gather_parts(labels, 0)
    valid = links.gather_parts(valid, 0)

    kernel_one = links.gather_members(conv_weights[0], 0)
    kernel_two = links.to_inner(conv_weights[1])
    decay_one = links.gather_members(decay_rates[0], 0)
    decay_two = links.to_inner(decay_rates[1])
    norms = links.gather_members(norm_params, 1)
    head = links.gather_members(head_weights, 0)
    gain_one, shift_one, gain_two, shift_two = norms[0], norms[1], norms[2], norms[3]

    def pool(value):
        return jnp.sum(value.reshape(MAP * MAP, count, width), axis=0) / (MAP * MAP)

    def spread(value):
        whole = jnp.broadcast_to(value[None] / (MAP * MAP), (MAP * MAP, count, width))
        return whole.reshape(MAP * MAP * count, width)

    columns = patches(images)
    own_columns = lax.dynamic_slice_in_dim(
        images.reshape(MAP * MAP * count, channels), first_column, width, 1
    )

    hidden_one = dot(columns, kernel_one, ((1,), (1,)))
    normal_one, scale_one = moments(hidden_one, rows, links)
    active, slope_one, bend_one = silu_parts(normal_one * gain_one + shift_one)
    active_columns = patches(active.reshape(MAP, MAP, count, width))
    hidden_two = links.scatter_parts(dot(active_columns, kernel_two, ((1,), (1,))), 1)
    normal_two, scale_two = moments(hidden_two, rows, links)
    block, slope_two, bend_two = silu_parts(normal_two * gain_two + shift_two + own_columns)
    pooled = pool(block)
    logits = links.sum_parts(dot(pooled, head, ((1,), (0,))))
    highest = jnp.max(logits, axis=1, keepdims=True)
    powers = jnp.exp(logits - highest)
    total = jnp.sum(powers, axis=1, keepdims=True)
    chances = powers / total
    classes = jnp.arange(logits.shape[1], dtype=jnp.int32)
    chosen = (labels[:, None] == classes[None, :]).astype(jnp.float32)
    cross = highest[:, 0] + jnp.log(total[:, 0]) - jnp.sum(chosen * logits, axis=1)
    loss_sum = links.sum_rows(jnp.sum(valid * cross)[None])[0]
    weights = (valid / label_total)[:, None]
    pull_logits = weights * (chances - chosen)
    grad_head = dot(pooled, pull_logits, ((0,), (0,)))
    pull_block = spread(dot(pull_logits, head, ((1,), (1,))))
    pull_two = pull_block * slope_two
    sums_two = links.sum_rows(
        jnp.stack([jnp.sum(pull_two * normal_two, axis=0), jnp.sum(pull_two, axis=0)])
    )
    centred_two = pull_two - sums_two[1] / rows - normal_two * (sums_two[0] / rows)
    factor_two = scale_two * gain_two
    pull_hidden_two = links.gather_parts(factor_two * centred_two, 1)
    grad_two = dot(pull_hidden_two, active_columns, ((0,), (0,)))
    pull_active = fold(dot(pull_hidden_two, kernel_two, ((1,), (0,))), count)
    pull_one = pull_active * slope_one
    sums_one = links.sum_rows(
        jnp.stack([jnp.sum(pull_one * normal_one, axis=0), jnp.sum(pull_one, axis=0)])
    )
    centred_one = pull_one - sums_one[1] / rows - normal_one * (sums_one[0] / rows)
    factor_one = scale_one * gain_one
    grad_one = dot(factor_one * centred_one, columns, ((0,), (0,)))

    grad_one = links.sum_rows(grad_one) + decay_one * kernel_one
    grad_two = links.sum_rows(grad_two) + decay_two * kernel_two
    grad_head = links.sum_rows(grad_head)
    grad_norm = jnp.concatenate([sums_one, sums_two])

    def product(vector):
        move_one, move_two, move_norm, move_head = vector
        tan_hidden = dot(columns, move_one, ((1,), (1,)))
        tan_normal_one, tan_scale_one = moments_tangent(
            normal_one, scale_one, tan_hidden, rows, links
        )
        tan_inner = move_norm[0] * normal_one + gain_one * tan_normal_one + move_norm[1]
        tan_active = slope_one * tan_inner
        tan_columns = patches(tan_active.reshape(MAP, MAP, count, width))
        tan_hidden = links.scatter_parts(
            dot(tan_columns, kernel_two, ((1,), (1,))) + dot(active_columns, move_two, ((1,), (1,))),
            1,
        )
        tan_normal_two, tan_scale_two = moments_tangent(
            normal_two, scale_two, tan_hidden, rows, links
        )
        tan_outer = move_norm[2] * normal_two + gain_two * tan_normal_two + move_norm[3]
        tan_pooled = pool(slope_two * tan_outer)
        tan_logits = links.sum_parts(
            dot(tan_pooled, head, ((1,), (0,))) + dot(pooled, move_head, ((1,), (0,)))
        )
        tan_chances = chances * (tan_logits - jnp.sum(chances * tan_logits, axis=1, keepdims=True))
        tan_pull = weights * tan_chances
        out_head = dot(tan_pooled, pull_logits, ((0,), (0,))) + dot(pooled, tan_pull, ((0,), (0,)))
        tan_block = spread(
            dot(tan_pull, head, ((1,), (1,))) + dot(pull_logits, move_head, ((1,), (1,)))
        )
        tan_two = tan_block * slope_two + pull_block * bend_two * tan_outer
        tan_sums_two = links.sum_rows(
            jnp.stack(
                [
                    jnp.sum(tan_two * normal_two + pull_two * tan_normal_two, axis=0),
                    jnp.sum(tan_two, axis=0),
                ]
            )
        )
        tan_factor = tan_scale_two * gain_two + scale_two * move_norm[2]
        tan_hidden = tan_factor * centred_two + factor_two * (
            tan_two
            - tan_sums_two[1] / rows
            - tan_normal_two * (sums_two[0] / rows)
            - normal_two * (tan_sums_two[0] / rows)
        )
        tan_hidden = links.gather_parts(tan_hidden, 1)
        out_two = dot(tan_hidden, active_columns, ((0,), (0,))) + dot(
            pull_hidden_two, tan_columns, ((0,), (0,))
        )
        tan_pull_active = fold(
            dot(tan_hidden, kernel_two, ((1,), (0,))) + dot(pull_hidden_two, move_two, ((1,), (0,))),
            count,
        )
        tan_one = tan_pull_active * slope_one + pull_active * bend_one * tan_inner
        tan_sums_one = links.sum_rows(
            jnp.stack(
                [
                    jnp.sum(tan_one * normal_one + pull_one * tan_normal_one, axis=0),
                    jnp.sum(tan_one, axis=0),
                ]
            )
        )
        tan_factor = tan_scale_one * gain_one + scale_one * move_norm[0]
        tan_hidden = tan_factor * centred_one + factor_one * (
            tan_one
            - tan_sums_one[1] / rows
            - tan_normal_one * (sums_one[0] / rows)
            - normal_one * (tan_sums_one[0] / rows)
        )
        out_one = dot(tan_hidden, columns, ((0,), (0,)))
        return (
            links.sum_rows(out_one) + decay_one * move_one,
            links.sum_rows(out_two) + decay_two * move_two,
            jnp.concatenate([tan_sums_one, tan_sums_two]),
            links.sum_rows(out_head),
        )

    vector = (grad_one, grad_two, grad_norm, grad_head)
    series_one, series_two = grad_one, grad_two
    for turn in range(NEUMANN):
        change = product(vector)
        vector = tuple(
            previous - neumann_rate * moved for previous, moved in zip(vector, change)
        )
        series_one, series_two = series_one + vector[0], series_two + vector[1]

    series = jnp.stack([links.own_rows(series_one), links.to_outer(series_two)])
    grads = jnp.stack([links.own_rows(grad_one), links.to_outer(grad_two)])
    return (
        loss_sum,
        label_total,
        grads,
        links.own_rows(grad_norm, 1),
        links.own_rows(grad_head),
        series,
    )


def shards(
    source,
    index_map,
    crop_offsets,
    flip_flags,
    labels,
    valid_mask,
    conv_weights,
    norm_params,
    head_weights,
    decay_rates,
    conv_first,
    conv_second,
    norm_first,
    norm_second,
    head_first,
    head_second,
):
    links = Links()
    rows = float(source.shape[0] * MAP * MAP * links.shards * links.copies)
    fused = links.members * links.copies == 8 and links.members == 2 and links.parts == 4
    loss_sum, label_total, grads, grad_norm, grad_head, series = (
        step_fused if fused else step_general
    )(
        links,
        rows,
        source,
        index_map,
        crop_offsets,
        flip_flags,
        labels,
        valid_mask,
        conv_weights,
        norm_params,
        head_weights,
        decay_rates,
    )
    hyper_gradient = -neumann_rate * conv_weights * series
    conv_new, conv_one, conv_two = adamw(conv_weights, grads, conv_first, conv_second, 0.015)
    norm_new, norm_one, norm_two = adamw(
        norm_params, grad_norm, norm_first, norm_second, 0.3
    )
    head_new, head_one, head_two = adamw(
        head_weights, grad_head, head_first, head_second, 0.13
    )
    return (
        loss_sum,
        label_total,
        conv_new,
        conv_one,
        conv_two,
        norm_new,
        norm_one,
        norm_two,
        head_new,
        head_one,
        head_two,
        hyper_gradient,
    )


def solution(mesh):
    images = P(("shard", "dp"))
    rows = P(None, "shard")
    head = P("shard")
    in_specs = (images,) * 6 + (rows, rows, head, rows, rows, rows, rows, rows, head, head)
    out_specs = (P(), P()) + (rows,) * 6 + (head,) * 3 + (rows,)
    return jax.shard_map(shards, mesh=mesh, in_specs=in_specs, out_specs=out_specs, check_vma=False)
```

```python
import functools

import jax
import jax.numpy as jnp
from jax import lax
from jax.experimental import pallas as pl
from jax.experimental.pallas import tpu as pltpu
from jax.sharding import PartitionSpec as P

MAP = 4
NEUMANN = 3
STEP = 5
TAPS = 9

norm_eps = 1e-05
neumann_rate = 10.0
beta_first = 0.5
beta_second = 0.5
adam_eps = 1e-08
decoupled = 0.01
HIGH = lax.Precision.HIGH


def crop_image(single, offsets, flipped):
    window = lax.dynamic_slice(
        single, (offsets[0], offsets[1], jnp.int32(0)), (MAP, MAP, single.shape[2])
    )
    return jnp.where(flipped == 1, window[:, ::-1, :], window)


def patches(maps):
    count, width = maps.shape[2:]
    padded = jnp.pad(maps, ((1, 1), (1, 1), (0, 0), (0, 0)))
    taps = [padded[dy : dy + MAP, dx : dx + MAP] for dy in range(3) for dx in range(3)]
    return jnp.concatenate(taps, axis=3).reshape(MAP * MAP * count, TAPS * width)


def fold(columns, count):
    width = columns.shape[1] // TAPS
    whole = columns.reshape(MAP, MAP, count, TAPS, width)
    padded = jnp.pad(whole, ((1, 1), (1, 1), (0, 0), (0, 0), (0, 0)))
    total = 0.0
    for dy in range(3):
        for dx in range(3):
            total = total + padded[2 - dy : 2 - dy + MAP, 2 - dx : 2 - dx + MAP, :, dy * 3 + dx]
    return total.reshape(MAP * MAP * count, width)


def dot(left, right, dims):
    return lax.dot_general(
        left, right, ((dims[0], dims[1]), ((), ())), precision=HIGH, preferred_element_type=jnp.float32
    )


MESH_ID = pl.DeviceIdType.MESH
LANES = 128
GROUPS = 3


def halves(value):
    high = value.astype(jnp.bfloat16)
    return high, (value - high.astype(jnp.float32)).astype(jnp.bfloat16)


def mul(left, right, dims=((1,), (0,))):
    return lax.dot_general(left, right, (dims, ((), ())), preferred_element_type=jnp.float32)


def mul_exact(left, right, dims=((1,), (0,))):
    return lax.dot_general(
        left,
        right,
        (dims, ((), ())),
        precision=lax.Precision.HIGHEST,
        preferred_element_type=jnp.float32,
    )


def silu_pieces(value):
    gate = 1.0 / (1.0 + jnp.exp(-value))
    slope = gate * (1.0 - gate)
    return value * gate, gate + value * slope, slope * (2.0 + value * (1.0 - 2.0 * gate))


def step_kernel(
    rows,
    members,
    copies,
    classes,
    source,
    index_map,
    crop_offsets,
    flip_flags,
    labels,
    valid_mask,
    weights_in,
    decay_in,
    pair_in,
    grads,
    series,
    grad_small,
    series_one,
    series_two,
    grad_source,
    row_parts,
    row_box,
    cut_box,
    d1,
    d2,
    v1,
    v2,
    v1_hi,
    v1_lo,
    v2_hi,
    v2_lo,
    k_hi,
    k_lo,
    source_box,
    x_box,
    x_row,
    x_both,
    x_own,
    a_both,
    b_both,
    g_left,
    g_turned,
    t_left,
    t_turned,
    slots,
    partial,
    from_low,
    from_high,
    flow,
    n1,
    s1,
    pb1,
    pull1,
    c1,
    n2,
    s2,
    pb2,
    pull2,
    c2,
    nt1,
    in1,
    nt2,
    in2,
    fold_sum,
    sum_one,
    sum_two,
    half_one,
    half_two,
    first_low,
    first_up,
    second_low,
    second_up,
    piece_two,
    stats_box,
    stats_own,
    logit_box,
    logit_own,
    pair_box,
    label_box,
    turned,
    channel,
    move_norm,
    move_head,
    head,
    pooled,
    chances,
    weights,
    pull_logits,
    x_load,
    pair_sem,
    cut_load,
    k1_load,
    d1_load,
    k1_send,
    k1_recv,
    half_send,
    half_recv,
    first_send,
    first_recv,
    label_send,
    label_recv,
    x_send,
    x_recv,
    stats_send,
    stats_recv,
    logit_send,
    logit_recv,
    up_send,
    up_recv,
    down_send,
    down_recv,
    ring_send,
    ring_recv,
    pair_send,
    pair_recv,
    plane_send,
    plane_recv,
    back_send,
    back_recv,
    swap_send,
    swap_recv,
    fold_send,
    fold_recv,
    open_send,
    open_recv,
    share_send,
    share_recv,
    row_send,
    row_recv,
    own_send,
    own_recv,
):
    shard = lax.axis_index("shard")
    copy = lax.axis_index("dp")
    part = shard // members
    member = shard % members
    me = member * copies + copy
    place, line, core = me // 2, (me // 2) % 2, me % 2
    last = 3
    count = flow.shape[1]
    own_count = source.shape[0]
    inverse = 1.0 / rows
    zero = jnp.zeros((count, LANES), jnp.float32)

    def row_peer(other):
        return (part * members + other // copies, other % copies)

    def part_peer(other):
        return (other * members + member, copy)

    def remote(source, target, send, recv, device):
        return pltpu.make_async_remote_copy(
            src_ref=source,
            dst_ref=target,
            send_sem=send,
            recv_sem=recv,
            device_id=device,
            device_id_type=MESH_ID,
        )

    def greet(device):
        pl.semaphore_signal(barrier, inc=1, device_id=device, device_id_type=MESH_ID)

    barrier = pltpu.get_barrier_semaphore()
    for step in range(1, 8):
        greet(row_peer(me ^ step))
    for step in range(1, 4):
        greet(part_peer(part ^ step))
    channels = source.shape[3]

    def tap_lanes(tap, width):
        return pl.ds(pl.multiple_of(tap * width, width), width)

    source_load = pltpu.make_async_copy(source, source_box, x_load)
    source_load.start()
    k1_loads = [
        pltpu.make_async_copy(
            weights_in.at[0, :, :, :, pl.ds(tap * channels, channels)],
            v1.at[tap, member],
            k1_load.at[tap],
        )
        for tap in range(TAPS)
    ]
    d1_loads = [
        pltpu.make_async_copy(
            decay_in.at[0, line, core, :, pl.ds(tap * channels, channels)], d1.at[tap], d1_load.at[tap]
        )
        for tap in range(TAPS)
    ]
    cut_loads = [
        pltpu.make_async_copy(weights_in.at[1, line, core], row_box.at[0], cut_load.at[0]),
        pltpu.make_async_copy(decay_in.at[1, line, core], row_box.at[1], cut_load.at[1]),
    ]
    for load in cut_loads + k1_loads + d1_loads:
        load.start()
    stats_own[...] = jnp.zeros_like(stats_own)
    channel[...] = jnp.zeros_like(channel)
    label_box[0] = jnp.zeros(label_box.shape[1:], jnp.float32)
    lane = lax.broadcasted_iota(jnp.int32, (1, LANES), 1)

    def tag_image(image, _):
        at = part * own_count + image
        label_box[0, pl.ds(at, 1), :] = (lane == labels[image]).astype(jnp.float32)
        label_box[0, pl.ds(count + at, 1), :] = jnp.full(
            (1, LANES), valid_mask[image].astype(jnp.float32)
        )

    lax.fori_loop(0, own_count, tag_image, None)
    source_load.wait()

    def crop(image, _):
        picked, flipped = index_map[image], flip_flags[image]
        top, left = crop_offsets[image, 0], crop_offsets[image, 1]
        for cell in range(16):
            column = left + jnp.where(flipped == 1, 3 - cell % 4, cell % 4)
            x_box[part, pl.ds(cell * own_count + image, 1), :] = source_box[
                picked, top + cell // 4, pl.ds(column, 1), :
            ]

    lax.fori_loop(0, own_count, crop, None)
    for load in cut_loads:
        load.wait()
    for which in range(2):
        for other in range(4):
            for tap in range(TAPS):
                start = tap * channels + other * LANES
                cut_box[which, other, :, tap * LANES : (tap + 1) * LANES] = row_box[
                    which, :, start : start + LANES
                ]
    v2[me, part] = cut_box[0, part]
    d2[part] = cut_box[1, part]
    pl.semaphore_wait(barrier, 10)

    def ring_move(box, send, recv, block, step, way, half):
        size = box.shape[1] // 2
        at = pl.ds(half * size, size)
        return remote(
            box.at[block, at],
            box.at[block, at],
            send.at[0 if way > 0 else 1, step, half],
            recv.at[block, half],
            part_peer(part + way),
        )

    def ring_start(box, send, recv):
        for half in range(2):

            @pl.when(part < last)
            def _():
                ring_move(box, send, recv, part, 0, 1, half).start()

            @pl.when(part > 0)
            def _():
                ring_move(box, send, recv, part, 0, -1, half).start()

    def ring_step(box, send, recv, step):
        for half in range(2):

            @pl.when(part >= step)
            def _():
                ring_move(box, send, recv, part - step, step, -1, half).wait_recv()

                @pl.when(part < last)
                def _():
                    ring_move(box, send, recv, part - step, step, 1, half).start()

            @pl.when(part + step <= last)
            def _():
                ring_move(box, send, recv, part + step, step, 1, half).wait_recv()

                @pl.when(part > 0)
                def _():
                    ring_move(box, send, recv, part + step, step, -1, half).start()

    def ring_end(box, send, recv):
        for step in range(0, 3):
            for half in range(2):

                @pl.when((part >= step) & (part < last))
                def _():
                    ring_move(box, send, recv, part - step, step, 1, half).wait_send()

                @pl.when((part + step <= last) & (part > 0))
                def _():
                    ring_move(box, send, recv, part + step, step, -1, half).wait_send()

    order = (
        part,
        jnp.where(part == 0, 1, part - 1),
        jnp.where(part == 3, 1, jnp.where(part == 2, 3, 2)),
        jnp.where(part < 2, 3, 0),
    )

    def cut_move(which, other):
        box = v2.at[me, part] if which == 0 else d2.at[part]
        return remote(
            cut_box.at[which, other],
            box,
            first_send.at[which, other],
            first_recv.at[which, part],
            part_peer(other),
        )

    def cut_start(which):
        for other in range(4):

            @pl.when(part != other)
            def _():
                cut_move(which, other).start()

    def cut_end(which):
        for other in range(4):

            @pl.when(part != other)
            def _():
                cut_move(which, other).wait_send()
                box = v2.at[me, other] if which == 0 else d2.at[other]
                remote(
                    cut_box.at[which, other],
                    box,
                    first_send.at[which, other],
                    first_recv.at[which, other],
                    part_peer(other),
                ).wait_recv()

    pair = row_peer(me ^ 1)
    cut_start(0)
    ring_start(x_box, x_send, x_recv)
    partner = row_peer(me ^ copies)
    k1_moves = [
        remote(
            weights_in.at[0, :, core, :, pl.ds(tap * channels, channels)],
            v1.at[tap, member, :, core],
            k1_send.at[tap],
            k1_recv.at[tap],
            partner,
        )
        for tap in range(TAPS)
    ]
    for move in k1_moves:
        move.start()

    def k1_share(group, arriving=False):
        piece = v1.at[pl.ds(group * 3, 3), 1 - member, :, 1 - core if arriving else core]
        return remote(piece, piece, half_send.at[group], half_recv.at[group], pair)

    pair_move = remote(pair_in, pair_box, pair_sem.at[0], pair_sem.at[1], partner)
    pair_move.start()
    label_moves = [
        remote(
            label_box.at[0],
            label_box.at[step],
            label_send.at[step],
            label_recv.at[step],
            part_peer(part ^ step),
        )
        for step in range(1, 4)
    ]
    for move in label_moves:
        move.start()

    cut_start(1)

    def piece_of(which, other):
        return v2.at[other, which[0]]

    def lane_of(which):
        return which[0]

    def to_plane(which, step):
        piece, at = piece_of(which, me), lane_of(which)
        return remote(
            piece, piece, back_send.at[at, step], back_recv.at[at, step], row_peer(me ^ (2 * step))
        )

    def from_plane(which, step):
        piece, at = piece_of(which, me ^ (2 * step)), lane_of(which)
        return remote(piece, piece, back_send.at[at, step], back_recv.at[at, step], pair)

    def to_pair(which, step):
        piece, at = piece_of(which, me ^ (2 * step)), lane_of(which)
        return remote(piece, piece, swap_send.at[at, step], swap_recv.at[at, step], pair)

    def from_pair(which, step):
        piece, at = piece_of(which, me ^ 1 ^ (2 * step)), lane_of(which)
        return remote(piece, piece, swap_send.at[at, step], swap_recv.at[at, step], pair)

    def back_start(which):
        for step in range(1, 4):
            to_plane(which, step).start()
        to_pair(which, 0).start()

    def back_forward(which):
        for step in range(1, 4):
            from_plane(which, step).wait_recv()
            to_pair(which, step).start()

    def back_arrived(which):
        for step in range(0, 4):
            from_pair(which, step).wait_recv()

    def back_end(which):
        for step in range(1, 4):
            to_plane(which, step).wait_send()
        for step in range(0, 4):
            to_pair(which, step).wait_send()

    x_both[...] = jnp.zeros_like(x_both)
    a_both[...] = jnp.zeros_like(a_both)
    b_both[...] = jnp.zeros_like(b_both)
    cut_end(0)
    for block in range(4):
        back_start((block,))
    ring_step(x_box, x_send, x_recv, 1)
    pair_move.wait()
    small = pair_in[...] + pair_box[...]
    move_norm[...] = small[0:8]
    head[...] = jnp.zeros_like(head)
    move_head[...] = jnp.zeros_like(move_head)
    head[0:16] = small[8:24]
    for move in label_moves:
        move.wait()
    tags = label_box[0] + label_box[1] + label_box[2] + label_box[3]
    chosen, valid = tags[:count], tags[count:]

    def each_cell(body, init=None):
        return lax.fori_loop(0, 16, body, init, unroll=2)

    def window(ref, down, right, lanes=slice(None), first=0, after=4):
        seen = ref[pl.ds(down + first, after - first), right : right + 4, :, lanes]
        return seen.reshape(4 * (after - first) * seen.shape[2], seen.shape[3])

    def reach(down):
        return (1 if down == 0 else 0), (3 if down == 2 else 4)

    def row(ref, index):
        return ref[index : index + 1, :]

    def put_sums(site, first, second):
        stats_own[site, 0:1, :] = jnp.sum(first, axis=0, keepdims=True)
        stats_own[site, 1:2, :] = jnp.sum(second, axis=0, keepdims=True)

    def sum_start(site, size):
        moves = []
        for step in range(1, 8):
            move = remote(
                stats_own.at[site, pl.ds(0, size)],
                stats_box.at[site, step, pl.ds(0, size)],
                stats_send.at[site, step],
                stats_recv.at[site, step],
                row_peer(me ^ step),
            )
            move.start()
            moves.append(move)
        stats_box[site, 0, pl.ds(0, size)] = stats_own[site, pl.ds(0, size)]
        return moves

    def sum_end(site, size, moves):
        for move in moves:
            move.wait()
        total = stats_box[site, me, pl.ds(0, size)]
        for other in range(1, 8):
            total = total + stats_box[site, other ^ me, pl.ds(0, size)]
        return total

    def sum_parts(value):
        logit_own[...] = value
        moves = []
        for step in range(1, 4):
            move = remote(
                logit_own,
                logit_box.at[step],
                logit_send.at[step],
                logit_recv.at[step],
                part_peer(part ^ step),
            )
            move.start()
            moves.append(move)
        logit_box[0] = value
        for move in moves:
            move.wait()
        total = logit_box[part]
        for other in range(1, 4):
            total = total + logit_box[other ^ part]
        return total

    def split_one(tap, _):
        for other in range(8):
            at = slice(other * 16, other * 16 + 16)
            v1_hi[tap, at], v1_lo[tap, at] = halves(v1[tap, other // 4, other // 2 % 2, other % 2])

    def split_two(high, low):
        def body(other, _):
            for block in range(4):
                at = pl.ds(pl.multiple_of(block * LANES + other * 16, 16), 16)
                high[at], low[at] = halves(v2[other, block])

        lax.fori_loop(0, 8, body, None)

    def taps_forward(row_of_taps):
        left, right = [], []
        for step in range(3):
            tap = row_of_taps * 3 + step
            weight = jnp.concatenate([v1_hi[tap], v1_lo[tap]], axis=0)
            left.append(window(x_both, row_of_taps, step))
            right += [weight, weight]
        out = mul(jnp.concatenate(left, axis=1), jnp.concatenate(right, axis=1), ((1,), (1,)))
        flow[...] += (out[:, :LANES] + out[:, LANES:]).reshape(flow.shape)

    def part_of_second(maps, high, low, half, add):
        at = pl.ds(pl.multiple_of(half * 256, 256), 256)

        for row_of_taps in (1, 0, 2):
            left, right = [], []
            first, after = reach(row_of_taps)
            for step in range(3):
                tap = row_of_taps * 3 + step
                lanes = slice(tap * LANES, (tap + 1) * LANES)
                seen = window(maps, row_of_taps, step, slice(None), first, after)
                weight_hi, weight_lo = high[at, lanes], low[at, lanes]
                left += [seen, seen[:, :LANES]]
                right += [weight_hi, weight_hi, weight_lo]
            out = mul(
                jnp.concatenate(left, axis=1), jnp.concatenate(right, axis=1), ((1,), (1,))
            )
            lines = slice(first * 4, after * 4)
            for side in range(2):
                value = out[:, side * LANES : (side + 1) * LANES].reshape(-1, count, LANES)
                if add or row_of_taps != 1:
                    partial[half * 2 + side, lines] += value
                else:
                    partial[half * 2 + side, lines] = value

    def up(block, half):
        at = pl.ds(half * 8, 8)
        return remote(
            partial.at[block, at],
            from_low.at[block, at],
            up_send.at[block, half],
            up_recv.at[block, half],
            part_peer(part + 1),
        )

    def down(block, half):
        at = pl.ds(half * 8, 8)
        return remote(
            partial.at[block, at],
            from_high.at[block, at],
            down_send.at[block, half],
            down_recv.at[block, half],
            part_peer(part - 1),
        )

    def scatter(maps, high, low, add, aside):
        near = jnp.where(part < 2, 1, 0)

        def half_body(index, _):
            part_of_second(maps, high, low, jnp.where(index == 0, near, 1 - near), add)

            @pl.when((index == 0) & (part == 0))
            def _():
                for block in (3, 2):
                    for half in range(2):
                        up(block, half).start()

            @pl.when((index == 0) & (part == last))
            def _():
                for block in (0, 1):
                    for half in range(2):
                        down(block, half).start()

        lax.fori_loop(0, 2, half_body, None)
        for block in (3, 2, 1):
            goal = last - block

            for half in range(2):
                at = slice(half * 8, half * 8 + 8)

                @pl.when((part < block) & (part > 0))
                def _():
                    up(block, half).wait_recv()
                    partial[block, at] += from_low[block, at]
                    up(block, half).start()

                @pl.when((part > goal) & (part < last))
                def _():
                    down(goal, half).wait_recv()
                    partial[goal, at] += from_high[goal, at]
                    down(goal, half).start()

                if block == 1:

                    @pl.when(part == 0)
                    def _():
                        up(1, half).start()

                    @pl.when(part == last)
                    def _():
                        down(2, half).start()

        aside()
        for block in range(4):

            @pl.when(part == block)
            def _():
                for half in range(2):
                    at = slice(half * 8, half * 8 + 8)
                    total = partial[block, at]
                    if block > 0:
                        up(block, half).wait_recv()
                        total = total + from_low[block, at]
                    if block < last:
                        down(block, half).wait_recv()
                        total = total + from_high[block, at]
                    flow[at] = total

        for block in (3, 2, 1):
            goal = last - block
            for half in range(2):

                @pl.when(part < block)
                def _():
                    up(block, half).wait_send()

                @pl.when(part > goal)
                def _():
                    down(goal, half).wait_send()

    def turn_block(block, left, turned_block):
        value = slots[block].reshape(16 * count, LANES)
        left[...] = jnp.concatenate(halves(value), axis=1)
        turned_block[...] = jnp.concatenate(halves(value.T), axis=0)

    def use_block(block, left, turned_block, high, low, maps):
        at = pl.ds(pl.multiple_of(block * LANES, LANES), LANES)

        for down in range(3):
            right = []
            first, after = reach(down)
            taps = [slice((down * 3 + step) * LANES, (down * 3 + step + 1) * LANES) for step in range(3)]
            for lanes in taps:
                weight = jnp.concatenate([high[at, lanes], low[at, lanes]], axis=1)
                right.append(jnp.concatenate([weight, weight], axis=0))
            out = mul(
                left[first * 4 * count : after * 4 * count], jnp.concatenate(right, axis=1)
            )
            for step in range(3):
                start = 2 * step * LANES
                fold_sum[down + first : down + after, step : step + 4] += (
                    out[:, start : start + LANES] + out[:, start + LANES : start + 2 * LANES]
                ).reshape(after - first, 4, count, LANES)
            out = mul(
                turned_block[...],
                jnp.concatenate([window(maps, down, step) for step in range(3)], axis=1),
            )
            out = out[:LANES] + out[LANES:]
            for step, lanes in enumerate(taps):
                start = 2 * step * LANES
                sum_two[block, :, :, :, lanes] += (
                    out[:, start : start + LANES] + out[:, start + LANES : start + 2 * LANES]
                ).reshape(4, 2, 16, LANES)

    def pair_two(block):
        return remote(
            sum_two.at[block, :, 1 - core],
            half_two.at[block],
            pair_send.at[block],
            pair_recv.at[block],
            pair,
        )

    def plane_two(block, step):
        other = place ^ step
        return remote(
            half_two.at[block, other],
            piece_two.at[step, block],
            plane_send.at[block, step],
            plane_recv.at[block, step],
            row_peer(other * 2 + core),
        )

    def plane_two_go(block):
        pair_two(block).wait()
        for place_of in range(4):
            half_two[block, place_of] += sum_two[block, place_of, core]
        for step in range(1, 4):
            plane_two(block, step).start()

    def step_two(block, new_of, more):
        for step in range(1, 4):
            plane_two(block, step).wait()
        change = half_two[block, place] + piece_two[1, block] + piece_two[2, block] + piece_two[3, block]
        new = new_of(v2[me, block], change, d2[block])
        v2[me, block] = new
        series_two[block] += new

        @pl.when(more)
        def _():
            back_start((block,))

    def back_forward_when(block, more):
        @pl.when(more)
        def _():
            back_forward((block,))

    def gather_and_use(block_of, new_of, more):
        ring_start(slots, ring_send, ring_recv)

        def order_at(index):
            first = jnp.where(index == 0, order[0], order[1])
            return jnp.where(index < 2, first, jnp.where(index == 2, order[2], order[3]))

        def body(index, _):
            @pl.when(index > 0)
            def _():
                ring_step(slots, ring_send, ring_recv, index)

            @pl.when(index == 2)
            def _():
                step_two(order[0], new_of, more)

            block = order_at(index)
            block_of(block)
            pair_two(block).start()

            @pl.when((index == 1) | (index == 2))
            def _():
                plane_two_go(order_at(index - 1))

        lax.fori_loop(0, 4, body, None)

    def beside_sums(new_of, more):
        step_two(order[1], new_of, more)
        plane_two_go(order[2])
        back_forward_when(order[0], more)
        ring_end(slots, ring_send, ring_recv)
        plane_two_go(order[3])

    def pair_one(group):
        return remote(
            sum_one.at[pl.ds(group * 3, 3), :, :, 1 - core],
            half_one.at[pl.ds(group * 3, 3)],
            pair_send.at[4 + group],
            pair_recv.at[4 + group],
            pair,
        )

    across_x, across_y = row_peer(me ^ copies), row_peer(me ^ 2)
    lower, upper = pl.ds(0, channels // 2), pl.ds(channels // 2, channels // 2)

    def taps_of(group):
        return pl.ds(group * 3, 3)

    def fold_one(group, step):
        taps = taps_of(group)
        source, goal, device = (
            (half_one.at[taps, 1 - member, :, :, lower], first_low.at[taps], across_x),
            (half_one.at[taps, :, 1 - line, :, upper], first_up.at[taps], across_y),
            (half_one.at[taps, member, 1 - line, :, lower], second_low.at[taps], across_y),
            (half_one.at[taps, 1 - member, line, :, upper], second_up.at[taps], across_x),
        )[step]
        return remote(source, goal, fold_send.at[group, step], fold_recv.at[group, step], device)

    def spread_one(group, step, arriving=False):
        taps = taps_of(group)
        x, y = member, line
        if arriving:
            x, y = (x, 1 - y) if step in (0, 3) else (1 - x, y)
        piece = (
            v1.at[taps, x, y, core, :, lower],
            v1.at[taps, x, y, core, :, upper],
            v1.at[taps, x, :, core, :, lower],
            v1.at[taps, :, y, core, :, upper],
        )[step]
        device = across_y if step in (0, 3) else across_x
        return remote(piece, piece, open_send.at[group, step], open_recv.at[group, step], device)

    def share_one(group, step, arriving=False):
        taps = taps_of(group)
        side = 1 - core if arriving else core
        piece = (
            v1.at[taps, member, line, side],
            v1.at[taps, member, 1 - line, side, :, lower],
            v1.at[taps, 1 - member, line, side, :, upper],
            v1.at[taps, 1 - member, :, side, :, lower],
            v1.at[taps, :, 1 - line, side, :, upper],
        )[step]
        return remote(piece, piece, share_send.at[group, step], share_recv.at[group, step], pair)

    def open_first(group):
        spread_one(group, 0).start()
        spread_one(group, 1).start()
        share_one(group, 0).start()

    def open_second(group):
        spread_one(group, 0, True).wait_recv()
        spread_one(group, 2).start()
        spread_one(group, 1, True).wait_recv()
        spread_one(group, 3).start()
        share_one(group, 1).start()
        share_one(group, 2).start()

    def open_third(group):
        spread_one(group, 2, True).wait_recv()
        share_one(group, 3).start()
        spread_one(group, 3, True).wait_recv()
        share_one(group, 4).start()

    def open_arrived(group):
        for step in range(5):
            share_one(group, step, True).wait_recv()

    def open_end(group):
        for step in range(4):
            spread_one(group, step).wait_send()
        for step in range(5):
            share_one(group, step).wait_send()

    def pair_add(group):
        pair_one(group).wait()

        def body(tap, _):
            half_one[tap] += sum_one[tap, :, :, core]

        lax.fori_loop(group * 3, group * 3 + 3, body, None)
        fold_one(group, 0).start()
        fold_one(group, 1).start()

    def fold_add(group):
        fold_one(group, 0).wait()
        fold_one(group, 1).wait()

        def body(tap, _):
            half_one[tap, member, :, :, lower] += first_low[tap]
            half_one[tap, :, line, :, upper] += first_up[tap]

        lax.fori_loop(group * 3, group * 3 + 3, body, None)
        fold_one(group, 2).start()
        fold_one(group, 3).start()

    def first_gradient(new_of, more):
        def taps_weight(down):
            out = mul(
                turned[...],
                jnp.concatenate(
                    [window(x_both, down, step, slice(0, channels)) for step in range(3)], axis=1
                ),
            )
            out = out + mul(
                turned[...],
                jnp.concatenate(
                    [
                        window(x_both, down, step, slice(channels, 2 * channels))
                        for step in range(3)
                    ],
                    axis=1,
                ),
            )
            out = out[:LANES] + out[LANES:]
            for step in range(3):
                sum_one[down * 3 + step] = out[:, step * channels : (step + 1) * channels].reshape(
                    sum_one.shape[1:]
                )

        def body(group, _):
            taps_weight(group)
            pair_one(group).start()

            @pl.when(group == 0)
            def _():
                step_two(order[2], new_of, more)

            @pl.when(group > 0)
            def _():
                pair_add(group - 1)

            @pl.when(group > 1)
            def _():
                fold_add(group - 2)

        lax.fori_loop(0, GROUPS, body, None)
        pair_add(GROUPS - 1)
        back_forward_when(order[1], more)
        fold_add(GROUPS - 2)
        step_two(order[3], new_of, more)
        fold_add(GROUPS - 1)

    def step_group(group, new_of):
        fold_one(group, 2).wait()
        fold_one(group, 3).wait()

        def body(tap, _):
            change = half_one[tap, member, line] + jnp.concatenate(
                [second_low[tap], second_up[tap]], axis=1
            )
            new = new_of(v1[tap, member, line, core], change, d1[tap])
            v1[tap, member, line, core] = new
            series_one[:, tap_lanes(tap, channels)] += new

        lax.fori_loop(group * 3, group * 3 + 3, body, None)

    def no_aside():
        pass

    series_one[...] = jnp.zeros_like(series_one)
    series_two[...] = jnp.zeros_like(series_two)

    def first_vector(old, change, decay):
        return change + decay * old

    def next_vector(old, change, decay):
        return old - neumann_rate * (change + decay * old)

    for load in k1_loads + d1_loads:
        load.wait()
    ring_step(x_box, x_send, x_recv, 2)
    for group in range(GROUPS):
        for move in k1_moves[group * 3 : group * 3 + 3]:
            move.wait()
        k1_share(group).start()
    for block in range(4):
        back_forward((block,))
    ring_step(x_box, x_send, x_recv, 3)
    ring_end(x_box, x_send, x_recv)

    for cell in range(16):
        for block in range(4):
            x_row[block * own_count : (block + 1) * own_count] = x_box[
                block, cell * own_count : (cell + 1) * own_count
            ]
        high, low = halves(x_row[...])
        x_both[cell // 4 + 1, cell % 4 + 1, :, 0:channels] = high
        x_both[cell // 4 + 1, cell % 4 + 1, :, channels : 2 * channels] = low
        x_own[cell] = x_row[:, pl.ds(pl.multiple_of(part * LANES, LANES), LANES)]

    flow[...] = jnp.zeros_like(flow)

    def primal_group(group, _):
        k1_share(group, True).wait_recv()
        lax.fori_loop(group * 3, group * 3 + 3, split_one, None)
        taps_forward(group)

    lax.fori_loop(0, GROUPS, primal_group, None)
    for group in range(GROUPS):
        k1_share(group).wait_send()

    def sums_primal(cell, carry):
        value = flow[cell]
        return carry[0] + value, carry[1] + value * value

    put_sums(0, *each_cell(sums_primal, (zero, zero)))
    stats_own[0, 2:3, :] = jnp.sum(valid, axis=0, keepdims=True)
    moves = sum_start(0, 8)
    cut_end(1)
    for block in range(4):
        back_arrived((block,))
        back_end((block,))
    split_two(k_hi, k_lo)
    total = sum_end(0, 8, moves)
    label_total = total[2:3]
    average = total[0:1] * inverse
    scale = lax.rsqrt(total[1:2] * inverse - average * average + norm_eps)
    gain, shift = row(move_norm, 0), row(move_norm, 1)
    gain2, shift2 = row(move_norm, 2), row(move_norm, 3)

    def first_primal(cell, _):
        normal = (flow[cell] - average) * scale
        value, slope, bend = silu_pieces(normal * gain + shift)
        n1[cell] = normal
        s1[cell] = slope
        pb1[cell] = bend
        a_both[cell // 4 + 1, cell % 4 + 1] = jnp.concatenate(halves(value), axis=1)

    each_cell(first_primal)
    scatter(a_both, k_hi, k_lo, False, no_aside)
    put_sums(1, *each_cell(sums_primal, (zero, zero)))
    total = sum_end(1, 8, sum_start(1, 8))
    average = total[0:1] * inverse
    scale2 = lax.rsqrt(total[1:2] * inverse - average * average + norm_eps)

    def second_primal(cell, carry):
        normal = (flow[cell] - average) * scale2
        value, slope, bend = silu_pieces(normal * gain2 + shift2 + x_own[cell])
        n2[cell] = normal
        s2[cell] = slope
        pb2[cell] = bend
        return carry + value

    pooled[...] = each_cell(second_primal, zero) * (1.0 / 16.0)
    logits = sum_parts(mul_exact(pooled[...], head[...], ((1,), (1,))))
    real = lax.broadcasted_iota(jnp.int32, logits.shape, 1) < classes
    highest = jnp.max(jnp.where(real, logits, -jnp.inf), axis=1, keepdims=True)
    powers = jnp.where(real, jnp.exp(logits - highest), 0.0)
    sum_powers = jnp.sum(powers, axis=1, keepdims=True)
    chances[...] = powers / sum_powers
    target_logit = jnp.sum(chosen * logits, axis=1, keepdims=True)
    cross = (highest + jnp.log(sum_powers) - target_logit) * valid
    weights[...] = valid / label_total
    pull_logits[...] = weights[...] * (chances[...] - chosen)
    out_head = mul_exact(pull_logits[...], pooled[...], ((0,), (0,)))
    pull_block = mul_exact(pull_logits[...], head[...]) * (1.0 / 16.0)

    def back_two_primal(cell, carry):
        pull = pull_block * s2[cell]
        pull2[cell] = pull
        pb2[cell] = pull_block * pb2[cell]
        return carry[0] + pull * n2[cell], carry[1] + pull

    put_sums(2, *each_cell(back_two_primal, (zero, zero)))
    stats_own[2, 2:3, :] = jnp.sum(cross, axis=0, keepdims=True)
    stats_own[2, 8:24, :] = out_head[0:16]
    total = sum_end(2, 24, sum_start(2, 24))
    grad_small[0:1, :] = total[2:3]
    grad_small[1:2, :] = label_total
    grad_small[2:8, :] = jnp.zeros((6, LANES), jnp.float32)
    grad_small[16:32, :] = total[8:24]
    out_gain2, out_shift2 = total[0:1], total[1:2]
    factor2 = scale2 * gain2

    def pull_two_primal(cell, _):
        centred = pull2[cell] - out_shift2 * inverse - n2[cell] * (out_gain2 * inverse)
        c2[cell] = centred
        slots[part, cell] = factor2 * centred

    each_cell(pull_two_primal)
    fold_sum[...] = jnp.zeros_like(fold_sum)
    sum_two[...] = jnp.zeros_like(sum_two)

    def primal_block(block):
        turn_block(block, g_left.at[block], g_turned.at[block])
        use_block(block, g_left.at[block], g_turned.at[block], k_hi, k_lo, a_both)

    gather_and_use(primal_block, first_vector, True)

    def back_one_primal(cell, carry):
        seen = fold_sum[cell // 4 + 1, cell % 4 + 1]
        pull = seen * s1[cell]
        pull1[cell] = pull
        pb1[cell] = seen * pb1[cell]
        return carry[0] + pull * n1[cell], carry[1] + pull

    put_sums(3, *each_cell(back_one_primal, (zero, zero)))
    moves = sum_start(3, 8)
    beside_sums(first_vector, True)
    total = sum_end(3, 8, moves)
    out_gain, out_shift = total[0:1], total[1:2]
    factor = scale * gain

    def pull_one_primal(cell, _):
        centred = pull1[cell] - out_shift * inverse - n1[cell] * (out_gain * inverse)
        c1[cell] = centred
        flow[cell] = factor * centred

    each_cell(pull_one_primal)
    turned[...] = jnp.concatenate(halves(flow[...].reshape(16 * count, LANES).T), axis=0)

    channel[0:1, :] = scale
    channel[1:2, :] = gain
    channel[2:3, :] = scale2
    channel[3:4, :] = gain2
    channel[4:5, :] = out_gain * inverse
    channel[5:6, :] = out_gain2 * inverse
    move_norm[0:1, :] = out_gain
    move_norm[1:2, :] = out_shift
    move_norm[2:3, :] = out_gain2
    move_norm[3:4, :] = out_shift2
    grad_small[8:16, :] = move_norm[...]
    move_head[0:16] = grad_small[16:32, :]

    first_gradient(first_vector, True)

    def deliver_move(which, source, other):
        return remote(
            source.at[other],
            row_parts.at[which, part],
            row_send.at[which, other],
            row_recv.at[which, part],
            part_peer(other),
        )

    def deliver_start(which, source):
        for other in range(4):

            @pl.when(part != other)
            def _():
                deliver_move(which, source, other).start()

        row_parts[which, part] = source[part]

    def deliver_end(which, source, result):
        for other in range(4):

            @pl.when(part != other)
            def _():
                deliver_move(which, source, other).wait_send()
                remote(
                    source.at[other],
                    row_parts.at[which, other],
                    row_send.at[which, other],
                    row_recv.at[which, other],
                    part_peer(other),
                ).wait_recv()

        for other in range(4):
            for tap in range(TAPS):
                start = tap * channels + other * LANES
                result[copy, :, start : start + LANES] = row_parts[
                    which, other, :, tap * LANES : (tap + 1) * LANES
                ]

    across, corner = row_peer(me ^ 2), copy ^ 2

    def spread_move(which, result, step, block, device):
        return remote(
            result.at[block], result.at[block], own_send.at[which, step], own_recv.at[which, step], device
        )

    def spread_start(which, result):
        spread_move(which, result, 0, copy, across).start()
        spread_move(which, result, 1, copy, pair).start()

    def spread_forward(which, result):
        spread_move(which, result, 0, corner, across).wait_recv()
        spread_move(which, result, 2, corner, pair).start()

    def spread_end(which, result):
        spread_move(which, result, 1, copy ^ 1, pair).wait_recv()
        spread_move(which, result, 2, copy ^ 3, pair).wait_recv()
        spread_move(which, result, 0, copy, across).wait_send()
        spread_move(which, result, 1, copy, pair).wait_send()
        spread_move(which, result, 2, corner, pair).wait_send()

    grad_source[...] = series_two[...]
    deliver_start(0, grad_source)
    for group in range(GROUPS):
        step_group(group, first_vector)
        open_first(group)

    def turn_body(turn, nothing):
        flow[...] = jnp.zeros_like(flow)

        def forward_group(group, _):
            open_arrived(group)
            lax.fori_loop(group * 3, group * 3 + 3, split_one, None)
            taps_forward(group)

        fold_sum[...] = jnp.zeros_like(fold_sum)
        sum_two[...] = jnp.zeros_like(sum_two)
        open_second(0)
        open_second(1)
        back_forward((order[2],))
        back_forward((order[3],))
        for block in range(4):
            back_arrived((block,))
            back_end((block,))
        split_two(v2_hi, v2_lo)
        open_third(0)
        open_second(2)

        part_of_second(a_both, v2_hi, v2_lo, 0, False)
        open_third(1)
        open_third(2)
        lax.fori_loop(0, GROUPS, forward_group, None)
        for group in range(GROUPS):
            open_end(group)

        @pl.when(turn == 0)
        def _():
            for tap in range(TAPS):
                grads[0, :, :, tap * channels : (tap + 1) * channels] = v1[tap, member].reshape(
                    4, v1.shape[4], channels
                )

        def sums_forward(normal):
            def body(cell, carry):
                value = flow[cell]
                return carry[0] + value, carry[1] + value * normal[cell]

            return each_cell(body, (zero, zero))

        put_sums(0, *sums_forward(n1))
        moves = sum_start(0, 8)
        part_of_second(a_both, v2_hi, v2_lo, 1, False)
        total = sum_end(0, 8, moves) * inverse
        average, cross = total[0:1], total[1:2]
        scale, gain = row(channel, 0), row(channel, 1)
        tan_scale_one = -scale * scale * cross
        move_gain, move_shift = row(move_norm, 0), row(move_norm, 1)

        def forward_one(cell, _):
            normal = n1[cell]
            tangent = scale * (flow[cell] - average - normal * cross)
            inner = move_gain * normal + gain * tangent + move_shift
            nt1[cell] = tangent
            in1[cell] = inner
            b_both[cell // 4 + 1, cell % 4 + 1] = jnp.concatenate(halves(s1[cell] * inner), axis=1)

        each_cell(forward_one)

        def aside():
            def body(block, _):
                use_block(block, g_left.at[block], g_turned.at[block], v2_hi, v2_lo, b_both)

            lax.fori_loop(0, 4, body, None)

        scatter(b_both, k_hi, k_lo, True, aside)

        @pl.when(turn == 0)
        def _():
            deliver_end(0, grad_source, grads.at[1])
            spread_start(0, grads.at[1])

        @pl.when(turn == 1)
        def _():
            spread_forward(0, grads.at[1])


        put_sums(1, *sums_forward(n2))
        moves = sum_start(1, 8)
        early_logits = mul_exact(pooled[...], move_head[...], ((1,), (1,)))
        early_block = mul_exact(pull_logits[...], move_head[...])
        total = sum_end(1, 8, moves) * inverse
        average2, cross2 = total[0:1], total[1:2]
        scale2, gain2 = row(channel, 2), row(channel, 3)
        tan_scale_two = -scale2 * scale2 * cross2
        move_gain2, move_shift2 = row(move_norm, 2), row(move_norm, 3)

        def forward_two(cell, carry):
            normal = n2[cell]
            tangent = scale2 * (flow[cell] - average2 - normal * cross2)
            inner = move_gain2 * normal + gain2 * tangent + move_shift2
            nt2[cell] = tangent
            in2[cell] = inner
            return carry + s2[cell] * inner

        tan_pooled = each_cell(forward_two, zero) * (1.0 / 16.0)
        tan_logits = sum_parts(mul_exact(tan_pooled, head[...], ((1,), (1,))) + early_logits)
        chance = chances[...]
        tan_pull = (
            weights[...]
            * chance
            * (tan_logits - jnp.sum(chance * tan_logits, axis=1, keepdims=True))
        )
        tan_block = (mul_exact(tan_pull, head[...]) + early_block) * (1.0 / 16.0)

        def back_two(cell, carry):
            tangent = tan_block * s2[cell] + pb2[cell] * in2[cell]
            flow[cell] = tangent
            return (
                carry[0] + tangent * n2[cell] + pull2[cell] * nt2[cell],
                carry[1] + tangent,
            )

        put_sums(2, *each_cell(back_two, (zero, zero)))
        moves = sum_start(2, 8)
        out_head = mul_exact(pull_logits[...], tan_pooled, ((0,), (0,))) + mul_exact(
            tan_pull, pooled[...], ((0,), (0,))
        )
        stats_own[3, 8:24, :] = out_head[0:16]
        total = sum_end(2, 8, moves)
        out_gain2, out_shift2 = total[0:1], total[1:2]
        factor2 = scale2 * gain2
        tan_factor2 = tan_scale_two * gain2 + scale2 * move_gain2

        def pull_two_body(cell, _):
            slots[part, cell] = tan_factor2 * c2[cell] + factor2 * (
                flow[cell]
                - out_shift2 * inverse
                - nt2[cell] * row(channel, 5)
                - n2[cell] * (out_gain2 * inverse)
            )

        each_cell(pull_two_body)

        def turn_of_block(block):
            turn_block(block, t_left, t_turned)
            use_block(block, t_left, t_turned, k_hi, k_lo, a_both)

        more = turn < NEUMANN - 1
        gather_and_use(turn_of_block, next_vector, more)

        def back_one(cell, carry):
            pull = fold_sum[cell // 4 + 1, cell % 4 + 1]
            tangent = pull * s1[cell] + pb1[cell] * in1[cell]
            flow[cell] = tangent
            return (
                carry[0] + tangent * n1[cell] + pull1[cell] * nt1[cell],
                carry[1] + tangent,
            )

        put_sums(3, *each_cell(back_one, (zero, zero)))
        moves = sum_start(3, 24)
        beside_sums(next_vector, more)
        total = sum_end(3, 24, moves)
        move_head[0:16] = move_head[0:16] - neumann_rate * total[8:24]
        out_gain, out_shift = total[0:1], total[1:2]
        factor = scale * gain
        tan_factor = tan_scale_one * gain + scale * move_gain

        def pull_one_body(cell, _):
            flow[cell] = tan_factor * c1[cell] + factor * (
                flow[cell]
                - out_shift * inverse
                - nt1[cell] * row(channel, 4)
                - n1[cell] * (out_gain * inverse)
            )

        each_cell(pull_one_body)
        turned[...] = jnp.concatenate(halves(flow[...].reshape(16 * count, LANES).T), axis=0)
        move_norm[0:1, :] = move_gain - neumann_rate * out_gain
        move_norm[1:2, :] = move_shift - neumann_rate * out_shift
        move_norm[2:3, :] = move_gain2 - neumann_rate * out_gain2
        move_norm[3:4, :] = move_shift2 - neumann_rate * out_shift2
        first_gradient(next_vector, more)

        @pl.when(turn == NEUMANN - 1)
        def _():
            deliver_start(1, series_two)

        for group in range(GROUPS):
            step_group(group, next_vector)

            @pl.when(more)
            def _():
                open_first(group)

    lax.fori_loop(0, NEUMANN, turn_body, None)

    series[0, copy] = series_one[...]
    spread_start(1, series.at[0])
    deliver_end(1, series_two, series.at[1])
    spread_start(2, series.at[1])
    spread_forward(1, series.at[0])
    spread_forward(2, series.at[1])
    spread_end(0, grads.at[1])
    spread_end(1, series.at[0])
    spread_end(2, series.at[1])


def step_fused(
    links,
    rows,
    source,
    index_map,
    crop_offsets,
    flip_flags,
    labels,
    valid_mask,
    conv_weights,
    norm_params,
    head_weights,
    decay_rates,
):
    own_count, channels = source.shape[0], source.shape[3]
    cells, count = MAP * MAP, own_count * 4
    width, group = channels // 4, 8
    piece, block = width // group, channels // group
    classes = head_weights.shape[1]
    f32, b16 = jnp.float32, jnp.bfloat16
    small = jnp.concatenate(
        [
            norm_params,
            jnp.zeros((4, block), f32),
            head_weights.T,
            jnp.zeros((16 - classes, block), f32),
        ]
    )
    lane = links.member * block
    here = jnp.arange(2, dtype=jnp.int32)[None, :, None] == links.member
    operands = (
        source,
        index_map,
        crop_offsets,
        flip_flags,
        labels,
        valid_mask,
        conv_weights.reshape(2, 2, 2, piece, TAPS * channels),
        decay_rates.reshape(2, 2, 2, piece, TAPS * channels),
        jnp.where(here, small[:, None, :], 0.0).reshape(24, width),
    )
    vmem = pl.BlockSpec(memory_space=pltpu.VMEM)
    anywhere = pl.BlockSpec(memory_space=pl.ANY)
    row_map = pltpu.VMEM((cells, count, width), f32)
    four_maps = pltpu.VMEM((4, cells, count, width), f32)
    inner_piece = pltpu.VMEM((4, piece, TAPS * width), f32)
    inner_half = pltpu.VMEM((4, 4, piece, TAPS * width), f32)
    inner_part = pltpu.VMEM((channels, TAPS * width), b16)
    outer_part = pltpu.VMEM((TAPS, width, channels), b16)
    both = pltpu.VMEM((MAP + 2, MAP + 2, count, 2 * width), b16)
    logit = pltpu.VMEM((count, LANES), f32)
    dma = pltpu.SemaphoreType.DMA
    scratch = [
        pltpu.VMEM((piece, TAPS * channels), f32),
        inner_piece,
        inner_piece,
        pltpu.VMEM((2, 4, piece, TAPS * width), f32),
        pltpu.VMEM((2, piece, TAPS * channels), f32),
        pltpu.VMEM((2, 4, piece, TAPS * width), f32),
        pltpu.VMEM((TAPS, piece, channels), f32),
        inner_piece,
        pltpu.VMEM((TAPS, 2, 2, 2, piece, channels), f32),
        pltpu.VMEM((group, 4, piece, TAPS * width), f32),
        outer_part,
        outer_part,
        inner_part,
        inner_part,
        inner_part,
        inner_part,
        pltpu.VMEM(source.shape, f32),
        pltpu.VMEM((4, cells * own_count, channels), f32),
        pltpu.VMEM((count, channels), f32),
        pltpu.VMEM((MAP + 2, MAP + 2, count, 2 * channels), b16),
        row_map,
        both,
        both,
        pltpu.VMEM((4, cells * count, 2 * width), b16),
        pltpu.VMEM((4, 2 * width, cells * count), b16),
        pltpu.VMEM((cells * count, 2 * width), b16),
        pltpu.VMEM((2 * width, cells * count), b16),
        four_maps,
        four_maps,
        four_maps,
        four_maps,
        *[row_map] * 15,
        pltpu.VMEM((MAP + 2, MAP + 2, count, width), f32),
        pltpu.VMEM((TAPS, 2, 2, 2, piece, channels), f32),
        pltpu.VMEM((4, 4, 2, piece, TAPS * width), f32),
        pltpu.VMEM((TAPS, 2, 2, piece, channels), f32),
        inner_half,
        *[pltpu.VMEM((TAPS, 2, piece, channels // 2), f32)] * 2,
        *[pltpu.VMEM((TAPS, piece, channels // 2), f32)] * 2,
        inner_half,
        pltpu.VMEM((4, 8, 24, width), f32),
        pltpu.VMEM((4, 24, width), f32),
        pltpu.VMEM((4, count, LANES), f32),
        logit,
        pltpu.VMEM((24, width), f32),
        pltpu.VMEM((4, 2 * count, LANES), f32),
        pltpu.VMEM((2 * width, cells * count), b16),
        pltpu.VMEM((8, width), f32),
        pltpu.VMEM((8, width), f32),
        pltpu.VMEM((LANES, width), f32),
        pltpu.VMEM((LANES, width), f32),
        logit,
        logit,
        logit,
        logit,
        dma(()),
        dma((2,)),
        dma((2,)),
        dma((TAPS,)),
        dma((TAPS,)),
        dma((TAPS,)),
        dma((TAPS,)),
        dma((GROUPS,)),
        dma((GROUPS,)),
        dma((2, 4)),
        dma((2, 4)),
        dma((4,)),
        dma((4,)),
        dma((2, 4, 2)),
        dma((4, 2)),
        dma((4, 8)),
        dma((4, 8)),
        dma((4,)),
        dma((4,)),
        dma((4, 2)),
        dma((4, 2)),
        dma((4, 2)),
        dma((4, 2)),
        dma((2, 4, 2)),
        dma((4, 2)),
        dma((GROUPS + 4,)),
        dma((GROUPS + 4,)),
        dma((4, 4)),
        dma((4, 4)),
        dma((4, 4)),
        dma((4, 4)),
        dma((4, 4)),
        dma((4, 4)),
        dma((GROUPS, 4)),
        dma((GROUPS, 4)),
        dma((GROUPS, 4)),
        dma((GROUPS, 4)),
        dma((GROUPS, 5)),
        dma((GROUPS, 5)),
        dma((2, 4)),
        dma((2, 4)),
        dma((3, 3)),
        dma((3, 3)),
    ]
    result = jax.ShapeDtypeStruct((2, 4, piece, TAPS * channels), f32)
    grads, series, grad_small = pl.pallas_call(
        functools.partial(step_kernel, rows, links.members, links.copies, classes),
        out_shape=(result, result, jax.ShapeDtypeStruct((32, width), f32)),
        in_specs=[anywhere] + [pl.BlockSpec(memory_space=pltpu.SMEM)] * 5 + [anywhere] * 2 + [vmem],
        out_specs=(vmem,) * 3,
        scratch_shapes=scratch,
        compiler_params=pltpu.CompilerParams(
            collective_id=1, has_side_effects=True, vmem_limit_bytes=63 * 1024 * 1024
        ),
        name="train_step",
    )(*operands)
    own = lax.dynamic_slice_in_dim(grad_small, lane, block, 1)
    return (
        grad_small[0, 0],
        grad_small[1, 0],
        grads.reshape(conv_weights.shape),
        own[8:12],
        own[16 : 16 + classes].T,
        series.reshape(conv_weights.shape),
    )


def adamw(weight, grad, first, second, rate):
    first = beta_first * first + (1.0 - beta_first) * grad
    second = beta_second * second + (1.0 - beta_second) * grad * grad
    first_hat = first / (1.0 - beta_first**STEP)
    second_hat = second / (1.0 - beta_second**STEP)
    update = first_hat / (jnp.sqrt(second_hat) + adam_eps) + decoupled * weight
    return (weight - rate * update, first, second)


def silu_parts(value):
    gate = jax.nn.sigmoid(value)
    slope = gate * (1.0 - gate)
    first = gate + value * slope
    second = slope * (2.0 + value * (1.0 - 2.0 * gate))
    return value * gate, first, second


class Links:
    def __init__(self):
        self.shards = lax.axis_size("shard")
        self.copies = lax.axis_size("dp")
        self.parts = 4 if self.shards % 4 == 0 else 1
        self.members = self.shards // self.parts
        index = lax.axis_index("shard")
        self.part = index // self.members
        self.member = index % self.members
        self.across = [
            [p * self.members + m for p in range(self.parts)] for m in range(self.members)
        ]
        self.within = [
            [p * self.members + m for m in range(self.members)] for p in range(self.parts)
        ]

    def sum_rows(self, value):
        value = lax.psum(value, "dp")
        gathered = lax.all_gather(value, "shard", axis_index_groups=self.within)
        return jnp.sum(gathered, axis=0)

    def sum_parts(self, value):
        return jnp.sum(lax.all_gather(value, "shard", axis_index_groups=self.across), axis=0)

    def gather_parts(self, value, axis):
        return lax.all_gather(value, "shard", axis_index_groups=self.across, axis=axis, tiled=True)

    def gather_members(self, value, axis):
        return lax.all_gather(value, "shard", axis_index_groups=self.within, axis=axis, tiled=True)

    def scatter_parts(self, value, axis):
        return lax.psum_scatter(
            value, "shard", axis_index_groups=self.across, scatter_dimension=axis, tiled=True
        )

    def to_inner(self, value):
        rows, channels = value.shape[0], value.shape[1] // TAPS
        width = channels // self.parts
        cut = value.reshape(rows, TAPS, self.parts, width).transpose(2, 0, 1, 3)
        moved = lax.all_to_all(cut, "shard", 0, 0, axis_index_groups=self.across, tiled=True)
        whole = self.gather_members(moved, 1)
        return whole.reshape(channels, TAPS * width)

    def to_outer(self, value):
        channels, width = value.shape[0], value.shape[1] // TAPS
        rows = channels // self.shards
        cut = value.reshape(self.parts, self.members, rows, TAPS * width)
        cut = lax.dynamic_index_in_dim(cut, self.member, 1, keepdims=False)
        moved = lax.all_to_all(cut, "shard", 0, 0, axis_index_groups=self.across, tiled=True)
        moved = moved.reshape(self.parts, rows, TAPS, width).transpose(1, 2, 0, 3)
        return moved.reshape(rows, TAPS * channels)

    def own_rows(self, value, axis=0):
        size = value.shape[axis] // self.members
        return lax.dynamic_slice_in_dim(value, self.member * size, size, axis)


def moments(hidden, rows, links):
    totals = links.sum_rows(jnp.stack([jnp.sum(hidden, axis=0), jnp.sum(hidden * hidden, axis=0)]))
    average = totals[0] / rows
    scale = lax.rsqrt(totals[1] / rows - average * average + norm_eps)
    return (hidden - average) * scale, scale


def moments_tangent(normal, scale, tangent, rows, links):
    totals = links.sum_rows(
        jnp.stack([jnp.sum(tangent, axis=0), jnp.sum(tangent * normal, axis=0)])
    )
    average, cross = totals[0] / rows, totals[1] / rows
    return scale * (tangent - average - normal * cross), -scale * scale * cross


def step_general(
    links,
    rows,
    source,
    index_map,
    crop_offsets,
    flip_flags,
    labels,
    valid_mask,
    conv_weights,
    norm_params,
    head_weights,
    decay_rates,
):
    images = jax.vmap(crop_image)(source[index_map], crop_offsets, flip_flags)
    images = images.transpose(1, 2, 0, 3)
    valid = valid_mask.astype(jnp.float32)
    own_images, channels = images.shape[2:]
    count = own_images * links.parts
    width = channels // links.parts
    first_column = links.part * width
    label_total = lax.psum(jnp.sum(valid), ("shard", "dp"))
    images = links.gather_parts(images, 2)
    labels = links.gather_parts(labels, 0)
    valid = links.gather_parts(valid, 0)

    kernel_one = links.gather_members(conv_weights[0], 0)
    kernel_two = links.to_inner(conv_weights[1])
    decay_one = links.gather_members(decay_rates[0], 0)
    decay_two = links.to_inner(decay_rates[1])
    norms = links.gather_members(norm_params, 1)
    head = links.gather_members(head_weights, 0)
    gain_one, shift_one, gain_two, shift_two = norms[0], norms[1], norms[2], norms[3]

    def pool(value):
        return jnp.sum(value.reshape(MAP * MAP, count, width), axis=0) / (MAP * MAP)

    def spread(value):
        whole = jnp.broadcast_to(value[None] / (MAP * MAP), (MAP * MAP, count, width))
        return whole.reshape(MAP * MAP * count, width)

    columns = patches(images)
    own_columns = lax.dynamic_slice_in_dim(
        images.reshape(MAP * MAP * count, channels), first_column, width, 1
    )

    hidden_one = dot(columns, kernel_one, ((1,), (1,)))
    normal_one, scale_one = moments(hidden_one, rows, links)
    active, slope_one, bend_one = silu_parts(normal_one * gain_one + shift_one)
    active_columns = patches(active.reshape(MAP, MAP, count, width))
    hidden_two = links.scatter_parts(dot(active_columns, kernel_two, ((1,), (1,))), 1)
    normal_two, scale_two = moments(hidden_two, rows, links)
    block, slope_two, bend_two = silu_parts(normal_two * gain_two + shift_two + own_columns)
    pooled = pool(block)
    logits = links.sum_parts(dot(pooled, head, ((1,), (0,))))
    highest = jnp.max(logits, axis=1, keepdims=True)
    powers = jnp.exp(logits - highest)
    total = jnp.sum(powers, axis=1, keepdims=True)
    chances = powers / total
    classes = jnp.arange(logits.shape[1], dtype=jnp.int32)
    chosen = (labels[:, None] == classes[None, :]).astype(jnp.float32)
    cross = highest[:, 0] + jnp.log(total[:, 0]) - jnp.sum(chosen * logits, axis=1)
    loss_sum = links.sum_rows(jnp.sum(valid * cross)[None])[0]
    weights = (valid / label_total)[:, None]
    pull_logits = weights * (chances - chosen)
    grad_head = dot(pooled, pull_logits, ((0,), (0,)))
    pull_block = spread(dot(pull_logits, head, ((1,), (1,))))
    pull_two = pull_block * slope_two
    sums_two = links.sum_rows(
        jnp.stack([jnp.sum(pull_two * normal_two, axis=0), jnp.sum(pull_two, axis=0)])
    )
    centred_two = pull_two - sums_two[1] / rows - normal_two * (sums_two[0] / rows)
    factor_two = scale_two * gain_two
    pull_hidden_two = links.gather_parts(factor_two * centred_two, 1)
    grad_two = dot(pull_hidden_two, active_columns, ((0,), (0,)))
    pull_active = fold(dot(pull_hidden_two, kernel_two, ((1,), (0,))), count)
    pull_one = pull_active * slope_one
    sums_one = links.sum_rows(
        jnp.stack([jnp.sum(pull_one * normal_one, axis=0), jnp.sum(pull_one, axis=0)])
    )
    centred_one = pull_one - sums_one[1] / rows - normal_one * (sums_one[0] / rows)
    factor_one = scale_one * gain_one
    grad_one = dot(factor_one * centred_one, columns, ((0,), (0,)))

    grad_one = links.sum_rows(grad_one) + decay_one * kernel_one
    grad_two = links.sum_rows(grad_two) + decay_two * kernel_two
    grad_head = links.sum_rows(grad_head)
    grad_norm = jnp.concatenate([sums_one, sums_two])

    def product(vector):
        move_one, move_two, move_norm, move_head = vector
        tan_hidden = dot(columns, move_one, ((1,), (1,)))
        tan_normal_one, tan_scale_one = moments_tangent(
            normal_one, scale_one, tan_hidden, rows, links
        )
        tan_inner = move_norm[0] * normal_one + gain_one * tan_normal_one + move_norm[1]
        tan_active = slope_one * tan_inner
        tan_columns = patches(tan_active.reshape(MAP, MAP, count, width))
        tan_hidden = links.scatter_parts(
            dot(tan_columns, kernel_two, ((1,), (1,))) + dot(active_columns, move_two, ((1,), (1,))),
            1,
        )
        tan_normal_two, tan_scale_two = moments_tangent(
            normal_two, scale_two, tan_hidden, rows, links
        )
        tan_outer = move_norm[2] * normal_two + gain_two * tan_normal_two + move_norm[3]
        tan_pooled = pool(slope_two * tan_outer)
        tan_logits = links.sum_parts(
            dot(tan_pooled, head, ((1,), (0,))) + dot(pooled, move_head, ((1,), (0,)))
        )
        tan_chances = chances * (tan_logits - jnp.sum(chances * tan_logits, axis=1, keepdims=True))
        tan_pull = weights * tan_chances
        out_head = dot(tan_pooled, pull_logits, ((0,), (0,))) + dot(pooled, tan_pull, ((0,), (0,)))
        tan_block = spread(
            dot(tan_pull, head, ((1,), (1,))) + dot(pull_logits, move_head, ((1,), (1,)))
        )
        tan_two = tan_block * slope_two + pull_block * bend_two * tan_outer
        tan_sums_two = links.sum_rows(
            jnp.stack(
                [
                    jnp.sum(tan_two * normal_two + pull_two * tan_normal_two, axis=0),
                    jnp.sum(tan_two, axis=0),
                ]
            )
        )
        tan_factor = tan_scale_two * gain_two + scale_two * move_norm[2]
        tan_hidden = tan_factor * centred_two + factor_two * (
            tan_two
            - tan_sums_two[1] / rows
            - tan_normal_two * (sums_two[0] / rows)
            - normal_two * (tan_sums_two[0] / rows)
        )
        tan_hidden = links.gather_parts(tan_hidden, 1)
        out_two = dot(tan_hidden, active_columns, ((0,), (0,))) + dot(
            pull_hidden_two, tan_columns, ((0,), (0,))
        )
        tan_pull_active = fold(
            dot(tan_hidden, kernel_two, ((1,), (0,))) + dot(pull_hidden_two, move_two, ((1,), (0,))),
            count,
        )
        tan_one = tan_pull_active * slope_one + pull_active * bend_one * tan_inner
        tan_sums_one = links.sum_rows(
            jnp.stack(
                [
                    jnp.sum(tan_one * normal_one + pull_one * tan_normal_one, axis=0),
                    jnp.sum(tan_one, axis=0),
                ]
            )
        )
        tan_factor = tan_scale_one * gain_one + scale_one * move_norm[0]
        tan_hidden = tan_factor * centred_one + factor_one * (
            tan_one
            - tan_sums_one[1] / rows
            - tan_normal_one * (sums_one[0] / rows)
            - normal_one * (tan_sums_one[0] / rows)
        )
        out_one = dot(tan_hidden, columns, ((0,), (0,)))
        return (
            links.sum_rows(out_one) + decay_one * move_one,
            links.sum_rows(out_two) + decay_two * move_two,
            jnp.concatenate([tan_sums_one, tan_sums_two]),
            links.sum_rows(out_head),
        )

    vector = (grad_one, grad_two, grad_norm, grad_head)
    series_one, series_two = grad_one, grad_two
    for turn in range(NEUMANN):
        change = product(vector)
        vector = tuple(
            previous - neumann_rate * moved for previous, moved in zip(vector, change)
        )
        series_one, series_two = series_one + vector[0], series_two + vector[1]

    series = jnp.stack([links.own_rows(series_one), links.to_outer(series_two)])
    grads = jnp.stack([links.own_rows(grad_one), links.to_outer(grad_two)])
    return (
        loss_sum,
        label_total,
        grads,
        links.own_rows(grad_norm, 1),
        links.own_rows(grad_head),
        series,
    )


def shards(
    source,
    index_map,
    crop_offsets,
    flip_flags,
    labels,
    valid_mask,
    conv_weights,
    norm_params,
    head_weights,
    decay_rates,
    conv_first,
    conv_second,
    norm_first,
    norm_second,
    head_first,
    head_second,
):
    links = Links()
    rows = float(source.shape[0] * MAP * MAP * links.shards * links.copies)
    fused = links.members * links.copies == 8 and links.members == 2 and links.parts == 4
    loss_sum, label_total, grads, grad_norm, grad_head, series = (
        step_fused if fused else step_general
    )(
        links,
        rows,
        source,
        index_map,
        crop_offsets,
        flip_flags,
        labels,
        valid_mask,
        conv_weights,
        norm_params,
        head_weights,
        decay_rates,
    )
    hyper_gradient = -neumann_rate * conv_weights * series
    conv_new, conv_one, conv_two = adamw(conv_weights, grads, conv_first, conv_second, 0.015)
    norm_new, norm_one, norm_two = adamw(
        norm_params, grad_norm, norm_first, norm_second, 0.3
    )
    head_new, head_one, head_two = adamw(
        head_weights, grad_head, head_first, head_second, 0.13
    )
    return (
        loss_sum,
        label_total,
        conv_new,
        conv_one,
        conv_two,
        norm_new,
        norm_one,
        norm_two,
        head_new,
        head_one,
        head_two,
        hyper_gradient,
    )


def solution(mesh):
    images = P(("shard", "dp"))
    rows = P(None, "shard")
    head = P("shard")
    in_specs = (images,) * 6 + (rows, rows, head, rows, rows, rows, rows, rows, head, head)
    out_specs = (P(), P()) + (rows,) * 6 + (head,) * 3 + (rows,)
    return jax.shard_map(shards, mesh=mesh, in_specs=in_specs, out_specs=out_specs, check_vma=False)
```
